32 devices in a mesh: dp: 8 (over y, x, core), mp: 4 (over z).
Axes of the slice: x: 2, y: 2, z: 4, core: 2. Of those that a mesh axis runs over, the one named last changes fastest.
Arguments:
- latents: bfloat16 [8, 2, 1280, 32], P('dp', None, 'mp'), may hold values from -6 to 6
- noise_target: float32 [8, 2, 1280, 32], P('dp', None, 'mp'), may hold values from -6 to 6
- token_mask: int32 [8, 2, 1280], P('dp', None, 'mp'), may hold values from 0 to 1, as said below
- timesteps: int32 [8, 2, 4], P('dp'), may hold values from 0 to 999
- labels: int32 [8, 2, 4], P('dp'), may hold values from 0 to 599
- state_embed: float32 [3, 32, 1024], P(None, None, 'dp'), as said below
- state_head: float32 [3, 1024, 32], P(None, 'dp'), as said below
- state_time_in: float32 [3, 256, 1024], P(None, None, 'dp'), as said below
- state_time_out: float32 [3, 1024, 1024], P(None, 'dp'), as said below
- state_classes: float32 [3, 600, 1024], P(None, None, 'dp'), as said below
- state_adaptive: float32 [3, 1024, 6, 1024], P(None, 'dp'), as said below
- state_attention_in: float32 [3, 1024, 3, 1024], P(None, 'dp', None, 'mp'), as said below
- state_attention_out: float32 [3, 1024, 1024], P(None, 'mp', 'dp'), as said below
- state_expand: float32 [3, 1024, 4096], P(None, 'dp', 'mp'), as said below
- state_contract: float32 [3, 4096, 1024], P(None, 'mp', 'dp'), as said below
Outputs:
- loss_value: float32 [], replicated
- grad_norm: float32 [], replicated
- new_embed: float32 [32, 1024], P(None, 'dp')
- embed_moments: float32 [2, 32, 1024], P(None, None, 'dp')
- new_head: float32 [1024, 32], P('dp')
- head_moments: float32 [2, 1024, 32], P(None, 'dp')
- new_time_in: float32 [256, 1024], P(None, 'dp')
- time_in_moments: float32 [2, 256, 1024], P(None, None, 'dp')
- new_time_out: float32 [1024, 1024], P('dp')
- time_out_moments: float32 [2, 1024, 1024], P(None, 'dp')
- new_classes: float32 [600, 1024], P(None, 'dp')
- classes_moments: float32 [2, 600, 1024], P(None, None, 'dp')
- new_adaptive: float32 [1024, 6, 1024], P('dp')
- adaptive_moments: float32 [2, 1024, 6, 1024], P(None, 'dp')
- new_attention_in: float32 [1024, 3, 1024], P('dp', None, 'mp')
- attention_in_moments: float32 [2, 1024, 3, 1024], P(None, 'dp', None, 'mp')
- new_attention_out: float32 [1024, 1024], P('mp', 'dp')
- attention_out_moments: float32 [2, 1024, 1024], P(None, 'mp', 'dp')
- new_expand: float32 [1024, 4096], P('dp', 'mp')
- expand_moments: float32 [2, 1024, 4096], P(None, 'dp', 'mp')
- new_contract: float32 [4096, 1024], P('mp', 'dp')
- contract_moments: float32 [2, 4096, 1024], P(None, 'mp', 'dp')
The draws below stay inside these ranges and needn't reach their ends.
Inputs may be any that keep to these rules, and one draw needn't show every extreme that they name: `token_mask`: in every window a token is valid exactly where its column within the 8-wide patch rows lies below the window's valid width, which is 2 or more. `state_embed`: slice 0 holds the weight, slice 1 the first moment, slice 2 the positive root of the second moment. `state_head`: as for state_embed. `state_time_in`: as for state_embed. `state_time_out`: as for state_embed. `state_classes`: as for state_embed. `state_adaptive`: as for state_embed. `state_attention_in`: as for state_embed. `state_attention_out`: as for state_embed. `state_expand`: as for state_embed. `state_contract`: as for state_embed.
All inputs are finite; a program needn't handle non-finite values.
Results may differ from the reference program's by a relative error of at most 0.004.
The reference program's roundings to bfloat16 on the way (of `features`) count: a program that leaves them out, or rounds other values in their place, can miss the bound.
Values may be sent and summed in bfloat16 or wider, within the bound.
A program may use at most 320 MiB of HBM per device.

```python
import math
import jax
import jax.numpy as jnp
from jax import lax

D = 1024
HEADS = 16
HD = 64
FF = 4096
PATCH = 32
FREQ = 256
CLASSES = 600
WTOK = 320
NMB = 2
WMB = 4
TPM = 1280
GROUPS = 8


threshold = 0.002


def grad_scale():
    counted = 2 * PATCH * D + FREQ * D + D * D + CLASSES * D + 6 * D * D + 4 * D * D + 2 * D * FF
    return threshold / math.sqrt(counted)


def state_draw(key, shape, spread, tag):
    own_key = jax.random.fold_in(key, 100 + tag)
    key_weight, key_first, key_second = jax.random.split(own_key, 3)
    scale = grad_scale()
    master = jax.random.normal(key_weight, shape, jnp.float32) * spread
    first_moment = jax.random.normal(key_first, shape, jnp.float32) * (scale * 0.1 / 0.9)
    root_moment = jnp.sqrt(jax.random.uniform(key_second, shape, jnp.float32, 1.0, 4.0)) * (scale * math.sqrt(0.001 / 0.999))
    return jnp.stack([master, first_moment, root_moment])


def draw_token_mask(key, part):
    own_key = jax.random.fold_in(key, 7)
    widths = jax.random.randint(own_key, (GROUPS, NMB, WMB, 1), 2, 16)
    columns = jnp.arange(WTOK, dtype=jnp.int32) % 8
    valid = (columns[None, None, None, :] < widths).astype(jnp.int32)
    return valid.reshape(GROUPS, NMB, WMB * WTOK)


def draw_state_embed(key, part):
    return state_draw(key, (PATCH, D), PATCH ** (-0.5), 1)


def draw_state_head(key, part):
    return state_draw(key, (D, PATCH), D ** (-0.5), 2)


def draw_state_time_in(key, part):
    return state_draw(key, (FREQ, D), FREQ ** (-0.5), 3)


def draw_state_time_out(key, part):
    return state_draw(key, (D, D), D ** (-0.5), 4)


def draw_state_classes(key, part):
    return state_draw(key, (CLASSES, D), 0.2, 5)


def draw_state_adaptive(key, part):
    return state_draw(key, (D, 6, D), D ** (-0.5), 6)


def draw_state_attention_in(key, part):
    return state_draw(key, (D, 3, D), D ** (-0.5), 7)


def draw_state_attention_out(key, part):
    return state_draw(key, (D, D), (D // 64) ** (-0.5), 8)


def draw_state_expand(key, part):
    return state_draw(key, (D, FF), D ** (-0.5), 9)


def draw_state_contract(key, part):
    return state_draw(key, (FF, D), FF ** (-0.5), 10)


def touch_ends(array, key, least, top_value):
    index_at = [jax.random.randint(jax.random.fold_in(key, axis), (), 0, length) for axis, length in enumerate(array.shape)]
    main_axis = array.shape.index(max(array.shape))
    beside = index_at[:main_axis] + [(index_at[main_axis] + 1) % array.shape[main_axis]] + index_at[main_axis + 1:]
    return array.at[tuple(index_at)].set(least).at[tuple(beside)].set(top_value)


def level_of(stream_key, shape, cuts, low, largest):
    loudness = 1.0
    for dim, blocks in cuts:
        draws = jax.random.uniform(jax.random.fold_in(jax.random.fold_in(stream_key, 6), dim), (blocks,), jnp.float32, low / len(cuts), largest / len(cuts))
        loudness = loudness * jnp.repeat(jnp.exp(draws), shape[dim] // blocks).reshape((-1,) + (1,) * (len(shape) - 1 - dim))
    return loudness


def gaussian(stream_key, extent, scale, limit, cuts=(), kind=jnp.bfloat16):
    values = scale * jax.random.normal(stream_key, extent, jnp.float32)
    if cuts:
        values = values * level_of(stream_key, extent, cuts, -0.22, 0.18)
    return jnp.clip(values, -limit, limit).astype(kind)


def setup_inputs(seed: int = 0) -> dict:
    streams_of = jax.random.split(jax.random.key(seed), 16)
    latents = gaussian(streams_of[0], (GROUPS, NMB, TPM, PATCH), 1.0, 6.0, ((0, 8), (2, 4)))
    noise_target = gaussian(streams_of[1], (GROUPS, NMB, TPM, PATCH), 1.0, 6.0, ((0, 8), (2, 4)), jnp.float32)
    token_mask = draw_token_mask(jax.random.fold_in(streams_of[15], 71), 0)
    timesteps = touch_ends(jax.random.randint(streams_of[3], (GROUPS, NMB, WMB), 0, 1000), jax.random.fold_in(streams_of[3], 1), 0, 999).astype(jnp.int32)
    labels = touch_ends(jax.random.randint(streams_of[4], (GROUPS, NMB, WMB), 0, CLASSES), jax.random.fold_in(streams_of[4], 1), 0, CLASSES - 1).astype(jnp.int32)
    state_embed = draw_state_embed(jax.random.fold_in(streams_of[15], 71), 0)
    state_head = draw_state_head(jax.random.fold_in(streams_of[15], 71), 0)
    state_time_in = draw_state_time_in(jax.random.fold_in(streams_of[15], 71), 0)
    state_time_out = draw_state_time_out(jax.random.fold_in(streams_of[15], 71), 0)
    state_classes = draw_state_classes(jax.random.fold_in(streams_of[15], 71), 0)
    state_adaptive = draw_state_adaptive(jax.random.fold_in(streams_of[15], 71), 0)
    state_attention_in = draw_state_attention_in(jax.random.fold_in(streams_of[15], 71), 0)
    state_attention_out = draw_state_attention_out(jax.random.fold_in(streams_of[15], 71), 0)
    state_expand = draw_state_expand(jax.random.fold_in(streams_of[15], 71), 0)
    state_contract = draw_state_contract(jax.random.fold_in(streams_of[15], 71), 0)
    return {"latents": latents, "noise_target": noise_target, "token_mask": token_mask, "timesteps": timesteps, "labels": labels, "state_embed": state_embed, "state_head": state_head, "state_time_in": state_time_in, "state_time_out": state_time_out, "state_classes": state_classes, "state_adaptive": state_adaptive, "state_attention_in": state_attention_in, "state_attention_out": state_attention_out, "state_expand": state_expand, "state_contract": state_contract}


@jax.custom_vjp
def low(v):
    return lax.optimization_barrier(v.astype(jnp.bfloat16)).astype(jnp.float32)

@jax.custom_vjp
def low_back(v):
    return v

def low_keep(v):
    return (low(v), None)

def low_pass(kept, grad):
    return (grad,)

def back_keep(v):
    return (v, None)

def back_low(kept, grad):
    return (low(grad),)
low.defvjp(low_keep, low_pass)
low_back.defvjp(back_keep, back_low)
beta_one = 0.9
beta_two = 0.999
adam_eps = 1e-08
learn_rate = 0.15
weight_decay = 0.1
threshold = 0.002
step_count = 10.0
highest = lax.Precision.HIGHEST

def layer_norm(values):
    center = values - lax.optimization_barrier(jnp.mean(values, axis=-1, keepdims=True))
    return center * lax.rsqrt(lax.optimization_barrier(jnp.mean(center * center, axis=-1, keepdims=True)) + 1e-06)

def modulate(values, shift, scale):
    return layer_norm(values) * (1.0 + scale) + shift

def timestep_features(step_ids):
    half_width = FREQ // 2
    frequency = jnp.exp(-math.log(10000.0) * jnp.arange(half_width, dtype=jnp.float32) / half_width)
    angles = step_ids.astype(jnp.float32)[:, None] * frequency[None, :]
    return jnp.concatenate([jnp.cos(angles), jnp.sin(angles)], axis=-1)

def window_positions(places):
    half_width = D // 2
    frequency = jnp.exp(-math.log(10000.0) * jnp.arange(half_width, dtype=jnp.float32) / half_width)
    angles = places.astype(jnp.float32)[:, None] * frequency[None, :]
    return jnp.concatenate([jnp.sin(angles), jnp.cos(angles)], axis=-1)

def micro_loss(masters, latent_rows, noise_rows, mask_rows, step_ids, label_ids, token_total):
    embed_mat, head_mat, time_in_mat, time_out_mat, classes_mat, adaptive_mat, attend_in_mat, attend_out_mat, expand_mat, contract_mat = [low(master) for master in masters]
    features = low(timestep_features(step_ids))
    time_pre = low_back(jnp.dot(features, time_in_mat, precision=highest))
    time_hidden = low(jax.nn.silu(time_pre))
    label_pick = (label_ids[:, None] == jnp.arange(CLASSES)[None, :]).astype(jnp.float32)
    condition = low_back(jnp.dot(time_hidden, time_out_mat, precision=highest) + jnp.dot(label_pick, classes_mat, precision=highest))
    adaptive = low_back(jnp.dot(low(jax.nn.silu(condition)), adaptive_mat.reshape(D, 6 * D), precision=highest))
    adaptive = adaptive.reshape(WMB, 1, 6, D)
    residual = low_back(jnp.dot(latent_rows, embed_mat, precision=highest)) + window_positions(jnp.arange(TPM) % WTOK)
    residual = residual.reshape(WMB, WTOK, D)
    normed_one = low(modulate(residual, adaptive[:, :, 0], adaptive[:, :, 1]))
    qkv_rows = low(low_back(jnp.einsum('wtd,dcn->wtcn', normed_one, attend_in_mat, precision=highest)))
    query_rows = qkv_rows[:, :, 0].reshape(WMB, WTOK, HEADS, HD)
    key_rows = qkv_rows[:, :, 1].reshape(WMB, WTOK, HEADS, HD)
    value_rows = qkv_rows[:, :, 2].reshape(WMB, WTOK, HEADS, HD)
    scores = low_back(jnp.einsum('wqhe,wkhe->whqk', query_rows, key_rows, precision=highest) * HD ** (-0.5))
    scores = jnp.where(mask_rows.reshape(WMB, 1, 1, WTOK) > 0, scores, -1e+30)
    attn_weights = low(jax.nn.softmax(scores, axis=-1))
    mixed_heads = low(low_back(jnp.einsum('whqk,wkhe->wqhe', attn_weights, value_rows, precision=highest)))
    mixed_heads = mixed_heads.reshape(WMB, WTOK, D)
    branch_one = low_back(jnp.einsum('wtd,de->wte', mixed_heads, attend_out_mat, precision=highest))
    middle = residual + adaptive[:, :, 2] * branch_one
    normed_two = low(modulate(middle, adaptive[:, :, 3], adaptive[:, :, 4]))
    up_pre = low_back(jnp.einsum('wtd,df->wtf', normed_two, expand_mat, precision=highest))
    hidden_act = low(jax.nn.gelu(up_pre, approximate=False))
    branch_two = low_back(jnp.einsum('wtf,fd->wtd', hidden_act, contract_mat, precision=highest))
    final = middle + adaptive[:, :, 5] * branch_two
    prediction = low_back(jnp.einsum('wtd,dp->wtp', low(layer_norm(final)), head_mat, precision=highest))
    pred_error = prediction.reshape(TPM, PATCH) - noise_rows
    return jnp.sum(lax.optimization_barrier(jnp.mean(pred_error * pred_error, axis=-1)) * mask_rows) / token_total

def adam_update(state_in, gradient, factor):
    clipped = gradient * factor
    first_moment = beta_one * state_in[1] + (1.0 - beta_one) * clipped
    second_moment = beta_two * state_in[2] * state_in[2] + (1.0 - beta_two) * clipped * clipped
    root_moment = jnp.sqrt(second_moment)
    update = first_moment / (1.0 - beta_one ** step_count) / (root_moment / math.sqrt(1.0 - beta_two ** step_count) + adam_eps)
    new_weight = state_in[0] - learn_rate * (update + weight_decay * state_in[0])
    return (new_weight, jnp.stack([first_moment, root_moment]))

def reference(latents, noise_target, token_mask, timesteps, labels, state_embed, state_head, state_time_in, state_time_out, state_classes, state_adaptive, state_attention_in, state_attention_out, state_expand, state_contract):
    states = (state_embed, state_head, state_time_in, state_time_out, state_classes, state_adaptive, state_attention_in, state_attention_out, state_expand, state_contract)
    masters = tuple((state_in[0] for state_in in states))
    token_total = jnp.sum(token_mask).astype(jnp.float32)
    batches = GROUPS * NMB
    pieces = (latents.astype(jnp.float32).reshape(batches, TPM, PATCH), noise_target.reshape(batches, TPM, PATCH), token_mask.astype(jnp.float32).reshape(batches, TPM), timesteps.reshape(batches, WMB), labels.reshape(batches, WMB))
    checked = jax.checkpoint(micro_loss)

    def whole_loss(weights):

        def add_piece(running, piece):
            return (running + checked(weights, piece[0], piece[1], piece[2], piece[3], piece[4], token_total), None)
        return lax.scan(add_piece, jnp.zeros((), jnp.float32), pieces)[0]
    loss_value, pull = jax.vjp(whole_loss, masters)
    gradients = pull(jnp.ones((), jnp.float32))[0]
    squares = jnp.zeros((), jnp.float32)
    for gradient in gradients:
        squares = squares + jnp.sum(gradient * gradient)
    grad_norm = jnp.sqrt(squares)
    factor = jnp.minimum(1.0, threshold / grad_norm)
    results = [loss_value, grad_norm]
    for state_in, gradient in zip(states, gradients):
        new_weight, moments = adam_update(state_in, gradient, factor)
        results.append(new_weight)
        results.append(moments)
    return tuple(results)
```

```python
import functools
import math

import jax
import jax.numpy as jnp
from jax import lax
from jax.experimental import pallas as pl
from jax.experimental.pallas import tpu as pltpu
from jax.sharding import PartitionSpec as P

D = 1024
HEADS = 16
HD = 64
PATCH = 32
FREQ = 256
CLASSES = 600
WTOK = 320
NMB = 2
WMB = 4
TILE = 256
NJ = 12
ROWS = NMB * WTOK
MESH = pl.DeviceIdType.MESH
BF = jnp.bfloat16
F32 = jnp.float32


beta_one = 0.9
beta_two = 0.999
adam_eps = 1e-08
learn_rate = 0.15
weight_decay = 0.1
threshold = 0.002
step_count = 10.0


def timestep_features(step_ids):
    half_width = FREQ // 2
    frequency = jnp.exp(-math.log(10000.0) * jnp.arange(half_width, dtype=F32) / half_width)
    angles = step_ids.astype(F32)[:, None] * frequency[None, :]
    return jnp.concatenate([jnp.cos(angles), jnp.sin(angles)], axis=-1)


def window_positions(places):
    half_width = D // 2
    frequency = jnp.exp(-math.log(10000.0) * jnp.arange(half_width, dtype=F32) / half_width)
    angles = places.astype(F32)[:, None] * frequency[None, :]
    return jnp.concatenate([jnp.sin(angles), jnp.cos(angles)], axis=-1)


def dot_nn(a, b):
    return jnp.dot(a, b, preferred_element_type=F32)


def dot_nt(a, b):
    return lax.dot_general(a, b, (((1,), (1,)), ((), ())), preferred_element_type=F32)


def dot_tn(a, b):
    return lax.dot_general(a, b, (((0,), (0,)), ((), ())), preferred_element_type=F32)


def norm_parts(values):
    center = values - jnp.mean(values, axis=-1, keepdims=True)
    inverse = lax.rsqrt(jnp.mean(center * center, axis=-1, keepdims=True) + 1e-06)
    return center * inverse, inverse


def norm_back(grad, normed, inverse):
    mean_grad = jnp.mean(grad, axis=-1, keepdims=True)
    mean_prod = jnp.mean(grad * normed, axis=-1, keepdims=True)
    return inverse * (grad - mean_grad - normed * mean_prod)


def silu_slope(values):
    gate = jax.nn.sigmoid(values)
    return gate * (1.0 + values * (1.0 - gate))


def gelu_parts(up):
    cdf = 0.5 * (1.0 + lax.erf(up * math.sqrt(0.5)))
    pdf = jnp.exp(-0.5 * up * up) * (1.0 / math.sqrt(2.0 * math.pi))
    return up * cdf, cdf + up * pdf


def per_window(mod):
    return mod[:, None, :]


def tokens3(values):
    return values.reshape(NMB, WTOK, -1)


def spread(values, mod):
    return (tokens3(values) * mod[:, None, :]).reshape(ROWS, -1)


def modulated(normed, shift, scale):
    return (tokens3(normed) * (1.0 + scale[:, None, :]) + shift[:, None, :]).reshape(ROWS, -1)


def window_sum(values):
    return jnp.sum(tokens3(values), axis=1)


def split_heads(qkv):
    shaped = qkv.reshape(NMB, WTOK, 3, HEADS, HD)
    return shaped[:, :, 0], shaped[:, :, 1], shaped[:, :, 2]


def scores_of(query, key, flags):
    scores = jnp.einsum("wqhe,wkhe->whqk", query, key, preferred_element_type=F32) * HD ** (-0.5)
    return jnp.where(flags.reshape(NMB, 1, 1, WTOK) > 0, scores, -1e30)


def attend(qkv, flags):
    query, key, value = split_heads(qkv)
    attn = jax.nn.softmax(scores_of(query, key, flags), axis=-1).astype(BF)
    mixed = jnp.einsum("whqk,wkhe->wqhe", attn, value, preferred_element_type=F32)
    return mixed.astype(BF).reshape(ROWS, D)


def attend_back(grad_mixed, qkv, flags):
    query, key, value = split_heads(qkv)
    grad_heads = grad_mixed.reshape(NMB, WTOK, HEADS, HD)
    attn_full = jax.nn.softmax(scores_of(query, key, flags), axis=-1)
    attn = attn_full.astype(BF)
    grad_value = jnp.einsum("whqk,wqhe->wkhe", attn, grad_heads, preferred_element_type=F32)
    grad_attn = jnp.einsum("wqhe,wkhe->whqk", grad_heads, value, preferred_element_type=F32)
    grad_scores = attn_full * (grad_attn - jnp.sum(attn_full * grad_attn, axis=-1, keepdims=True))
    grad_scores = grad_scores.astype(BF)
    grad_query = jnp.einsum("whqk,wkhe->wqhe", grad_scores, key, preferred_element_type=F32)
    grad_key = jnp.einsum("whqk,wqhe->wkhe", grad_scores, query, preferred_element_type=F32)
    parts = jnp.stack([grad_query * HD ** (-0.5), grad_key * HD ** (-0.5), grad_value], axis=2)
    return parts.astype(BF).reshape(ROWS, 3, D)


def flip(bits, at):
    return [1 - bit if place == at else bit for place, bit in enumerate(bits)]


class Place:
    def __init__(self, nd, nm):
        self.nm = nm
        self.nb = nd.bit_length() - 2
        dp_id = lax.axis_index("dp")
        self.m = lax.axis_index("mp")
        self.core = dp_id % 2
        self.bits = [dp_id // (1 << (self.nb - at)) % 2 for at in range(self.nb)]
        self.sibling = {"dp": self.dp_of(self.bits, 1 - self.core), "mp": self.m}
        self.orders = (list(range(self.nb))[::-1], list(range(self.nb)))
        self.halves = (pl.ds(0, nm // 2), pl.ds(nm // 2, nm - nm // 2))

    def dp_of(self, bits, core):
        total = core
        for at, bit in enumerate(bits):
            total = total + bit * (1 << (self.nb - at))
        return total

    def across(self, at):
        return {"dp": self.dp_of(flip(self.bits, at), self.core), "mp": self.m}

    def along(self, hops):
        return {"dp": self.dp_of(self.bits, self.core), "mp": (self.m + hops) % self.nm}

    def pick(self, half, done, flipped=None):
        where = flip(self.bits, flipped)
        return (self.halves[half],) + tuple(
            pl.ds(0, 2) if at in done else pl.ds(where[at], 1) for at in range(self.nb)
        )

    def mine(self, m=None):
        return (self.m if m is None else m,) + tuple(self.bits)

    def greet(self):
        barrier = pltpu.get_barrier_semaphore()
        others = [self.sibling]
        others += [self.across(at) for at in range(self.nb)]
        others += [self.along(hops) for hops in range(1, self.nm)]
        for other in others:
            pl.semaphore_signal(barrier, inc=1, device_id=other, device_id_type=MESH)
        pl.semaphore_wait(barrier, len(others))


class Copies:
    def __init__(self, send_sems, recv_sems):
        self.send_sems, self.recv_sems = send_sems, recv_sems
        self.started = {}

    def start(self, step, slot, source, target, device):
        copy = pltpu.make_async_remote_copy(
            src_ref=source,
            dst_ref=target,
            send_sem=self.send_sems.at[step, slot],
            recv_sem=self.recv_sems.at[step, slot],
            device_id=device,
            device_id_type=MESH,
        )
        copy.start()
        self.started[step, slot] = copy

    def arrived(self, step, slot):
        self.started[step, slot].wait_recv()

    def drain(self):
        for copy in self.started.values():
            copy.wait_send()


def gather_kernel(nd, nm, shard, whole, send_sems, recv_sems, local_sems):
    place = Place(nd, nm)
    nb, core = place.nb, place.core
    copies = Copies(send_sems, recv_sems)
    z_slots = [hops - 1 for hops in range(1, nm)]
    stage_slot = lambda stage, half: nm - 1 + 2 * stage + half
    twin = nm - 1 + 2 * nb
    locals_ = {}
    place.greet()

    def begin(j):
        here = whole.at[(j,) + place.mine() + (core,)]
        locals_[j] = pltpu.make_async_copy(shard.at[j], here, local_sems.at[j])
        locals_[j].start()
        for hops in range(1, nm):
            copies.start(j, hops - 1, shard.at[j], here, place.along(hops))
        copies.start(j, 2 * twin, shard.at[j], here, place.sibling)

    def stage(j, step):
        if step == 0:
            locals_[j].wait()
            for hops in range(1, nm):
                copies.arrived(j, hops - 1)
        else:
            for half in range(2):
                copies.arrived(j, stage_slot(step - 1, half))
        if step < nb:
            for half in range(2):
                order = place.orders[half]
                block = whole.at[(j,) + place.pick(half, order[:step]) + (core,)]
                copies.start(j, stage_slot(step, half), block, block, place.across(order[step]))
        if step == 0:
            for hops in range(1, nm):
                block = whole.at[(j,) + place.mine((place.m + nm - hops) % nm) + (core,)]
                copies.start(j, twin + hops - 1, block, block, place.sibling)
        else:
            for half in range(2):
                order = place.orders[half]
                block = whole.at[
                    (j,) + place.pick(half, order[: step - 1], order[step - 1]) + (core,)
                ]
                copies.start(j, twin + stage_slot(step - 1, half), block, block, place.sibling)

    def finish(j):
        for slot in range(twin, 2 * twin + 1):
            copies.arrived(j, slot)

    for turn in range(NJ + nb + 2):
        if turn < NJ:
            begin(turn)
        for step in range(nb + 1):
            if 0 <= turn - 1 - step < NJ:
                stage(turn - 1 - step, step)
        if 0 <= turn - 2 - nb < NJ:
            finish(turn - 2 - nb)
    copies.drain()


def gather_blocks(shard):
    nd, nm = lax.axis_size("dp"), lax.axis_size("mp")
    nb = nd.bit_length() - 2
    rows = shard.shape[1]
    slots = 2 * (nm - 1 + 2 * nb) + 1
    whole = pl.pallas_call(
        functools.partial(gather_kernel, nd, nm),
        out_shape=jax.ShapeDtypeStruct((NJ, nm) + (2,) * nb + (2, rows, TILE), BF),
        in_specs=[pl.BlockSpec(memory_space=pl.ANY)],
        out_specs=pl.BlockSpec(memory_space=pl.ANY),
        scratch_shapes=[
            pltpu.SemaphoreType.DMA((NJ, slots)),
            pltpu.SemaphoreType.DMA((NJ, slots)),
            pltpu.SemaphoreType.DMA((NJ,)),
        ],
        compiler_params=pltpu.CompilerParams(collective_id=0, has_side_effects=True),
    )(shard)
    return whole.reshape(NJ, nm, nd * rows, TILE)


def reduce_kernel(nd, nm, partial, total, mine_ref, twin_ref, stage_refs, z_ref, send_sems, recv_sems, local_sems):
    place = Place(nd, nm)
    nb, core = place.nb, place.core
    copies = Copies(send_sems, recv_sems)
    orders = [order[::-1] for order in place.orders]
    locals_ = {}
    place.greet()
    slot_of = lambda step, half: 1 + 2 * step + half
    z_slot = 1 + 2 * nb

    def add_to(target, index, source):
        shape = source.shape[:-2]
        count = math.prod(shape)

        def body(at, carry):
            inner, places = at, []
            for size in shape[::-1]:
                places.append(inner % size)
                inner = inner // size
            places = places[::-1]
            spot = tuple(
                base.start + offset if isinstance(base, pl.Slice) else base
                for base, offset in zip(index, places)
            )
            target[spot] = (target[spot].astype(F32) + source[tuple(places)].astype(F32)).astype(BF)
            return carry

        lax.fori_loop(0, count, body, 0)

    def begin(j):
        every = (slice(None),) * (nb + 1)
        locals_[j] = pltpu.make_async_copy(
            partial.at[(j,) + every + (core,)], mine_ref.at[j], local_sems.at[j]
        )
        locals_[j].start()
        copies.start(
            j, 0, partial.at[(j,) + every + (1 - core,)], twin_ref.at[j], place.sibling
        )

    def stage(j, step):
        if step == 0:
            locals_[j].wait()
            copies.arrived(j, 0)
            add_to(mine_ref.at[j], (pl.ds(0, nm),) + (pl.ds(0, 2),) * nb, twin_ref.at[j])
        else:
            for half in range(2):
                copies.arrived(j, slot_of(step - 1, half))
                index = place.pick(half, orders[half][step:])
                add_to(mine_ref.at[j], index, stage_refs[step - 1].at[j, half])
        if step < nb:
            for half in range(2):
                order = orders[half]
                block = mine_ref.at[(j,) + place.pick(half, order[step + 1 :], order[step])]
                target = stage_refs[step].at[j, half]
                copies.start(j, slot_of(step, half), block, target, place.across(order[step]))
        else:
            for hops in range(1, nm):
                block = mine_ref.at[(j,) + place.mine((place.m + hops) % nm)]
                copies.start(j, z_slot + hops - 1, block, z_ref.at[j, hops - 1], place.along(hops))

    def finish(j):
        summed = mine_ref[(j,) + place.mine()].astype(F32)
        for hops in range(1, nm):
            copies.arrived(j, z_slot + hops - 1)
            summed = summed + z_ref[j, hops - 1].astype(F32)
        total[j] = summed

    for turn in range(NJ + nb + 2):
        if turn < NJ:
            begin(turn)
        for step in range(nb + 1):
            if 0 <= turn - 1 - step < NJ:
                stage(turn - 1 - step, step)
        if 0 <= turn - 2 - nb < NJ:
            finish(turn - 2 - nb)
    copies.drain()


def reduce_blocks(partial):
    nd, nm = lax.axis_size("dp"), lax.axis_size("mp")
    nb = nd.bit_length() - 2
    rows = partial.shape[2] // nd
    bits = (2,) * nb
    slots = 2 * nb + nm

    def kernel(partial, total, mine_ref, twin_ref, *rest):
        stage_refs = [HalfRefs(rest[2 * step], rest[2 * step + 1]) for step in range(nb)]
        reduce_kernel(nd, nm, partial, total, mine_ref, twin_ref, stage_refs, *rest[2 * nb :])

    stage_shapes = []
    for step in range(nb):
        low_first = tuple(1 if at <= step else 2 for at in range(nb))
        high_first = tuple(1 if nb - 1 - at <= step else 2 for at in range(nb))
        stage_shapes.append(pltpu.VMEM((NJ, nm // 2) + low_first + (rows, TILE), BF))
        stage_shapes.append(pltpu.VMEM((NJ, nm - nm // 2) + high_first + (rows, TILE), BF))
    total = pl.pallas_call(
        kernel,
        out_shape=jax.ShapeDtypeStruct((NJ, rows, TILE), F32),
        in_specs=[pl.BlockSpec(memory_space=pl.ANY)],
        out_specs=pl.BlockSpec(memory_space=pltpu.VMEM),
        scratch_shapes=[
            pltpu.VMEM((NJ, nm) + bits + (rows, TILE), BF),
            pltpu.VMEM((NJ, nm) + bits + (rows, TILE), BF),
            *stage_shapes,
            pltpu.VMEM((NJ, nm - 1, rows, TILE), BF),
            pltpu.SemaphoreType.DMA((NJ, slots)),
            pltpu.SemaphoreType.DMA((NJ, slots)),
            pltpu.SemaphoreType.DMA((NJ,)),
        ],
        compiler_params=pltpu.CompilerParams(
            collective_id=1, has_side_effects=True, vmem_limit_bytes=60 << 20
        ),
    )(partial.reshape((NJ, nm) + bits + (2, rows, TILE)))
    return total


class HalfRefs:
    def __init__(self, first, second):
        self.refs = (first, second)

    @property
    def at(self):
        return self

    def __getitem__(self, index):
        j, half = index
        return self.refs[half].at[j]


def adam_update(state_in, gradient, factor):
    clipped = gradient * factor
    first_moment = beta_one * state_in[1] + (1.0 - beta_one) * clipped
    second_moment = beta_two * state_in[2] * state_in[2] + (1.0 - beta_two) * clipped * clipped
    root_moment = jnp.sqrt(second_moment)
    update = (
        first_moment
        / (1.0 - beta_one**step_count)
        / (root_moment / math.sqrt(1.0 - beta_two**step_count) + adam_eps)
    )
    new_weight = state_in[0] - learn_rate * (update + weight_decay * state_in[0])
    return (new_weight, jnp.stack([first_moment, root_moment]))


def per_device(
    latents,
    noise_target,
    token_mask,
    timesteps,
    labels,
    state_embed,
    state_head,
    state_time_in,
    state_time_out,
    state_classes,
    state_adaptive,
    state_attention_in,
    state_attention_out,
    state_expand,
    state_contract,
):
    nd, nm = lax.axis_size("dp"), lax.axis_size("mp")
    dp_id, mp_id = lax.axis_index("dp"), lax.axis_index("mp")
    rows = state_attention_in.shape[1]
    attn_in_tiles = state_attention_in[0].transpose(1, 0, 2)
    expand_tiles = state_expand[0].reshape(rows, 4, TILE).transpose(1, 0, 2)
    contract_tiles = state_contract[0].reshape(4, TILE, rows).transpose(0, 2, 1)
    ff_tiles = jnp.stack([expand_tiles, contract_tiles], axis=1).reshape(8, rows, TILE)
    shard = jnp.concatenate(
        [attn_in_tiles, state_attention_out[0].T[None], ff_tiles], axis=0
    ).astype(BF)
    weights = gather_blocks(shard)

    mask = token_mask.astype(F32).reshape(ROWS)
    token_total = lax.psum(jnp.sum(mask), ("dp", "mp"))
    ends = jnp.stack([state_embed[0], state_head[0].T]).astype(BF)
    ends = lax.all_gather(ends, "dp", axis=2, tiled=True)
    embed_mat, head_t = ends[0], ends[1]

    both_ids = lax.all_gather(jnp.stack([timesteps, labels])[:, 0], "dp", axis=1, tiled=False)
    both_ids = both_ids.reshape(2, nd * NMB * WMB)
    features = timestep_features(both_ids[0]).astype(BF)
    pick = (both_ids[1][:, None] == jnp.arange(CLASSES)[None, :]).astype(BF)
    time_pre = dot_nn(features, state_time_in[0].astype(BF))
    time_hidden = jax.nn.silu(time_pre).astype(BF)
    time_out_part = state_time_out[0].astype(BF)
    condition = lax.psum_scatter(
        dot_nn(time_hidden, time_out_part), "dp", scatter_dimension=1, tiled=True
    ) + dot_nn(pick, state_classes[0].astype(BF))
    cond_act = jax.nn.silu(condition).astype(BF)
    adaptive_part = state_adaptive[0].astype(BF).reshape(rows, 6 * D)
    mine = lax.dynamic_index_in_dim(
        cond_act.reshape(nd * NMB, WMB, rows), mp_id, 1, keepdims=False
    )
    mod = lax.psum_scatter(dot_nn(mine, adaptive_part), "dp", scatter_dimension=0, tiled=True)
    mod = mod.reshape(NMB, 6, D)

    latent_rows = latents.reshape(ROWS, PATCH)
    noise_rows = noise_target.reshape(ROWS, PATCH)
    positions = window_positions(jnp.arange(WTOK, dtype=jnp.int32))
    residual = (tokens3(dot_nn(latent_rows, embed_mat)) + positions[None]).reshape(ROWS, D)
    ln_one, inv_one = norm_parts(residual)
    n_one = modulated(ln_one, mod[:, 0], mod[:, 1]).astype(BF)
    qkv = jnp.einsum("tk,jmkc->tjmc", n_one, weights[:3], preferred_element_type=F32).astype(BF)
    qkv = qkv.reshape(ROWS, 3, D)
    mixed = attend(qkv, mask)
    mixed_tiles = mixed.reshape(ROWS, nm, TILE)
    branch_one = jnp.einsum("tmc,mnc->tn", mixed_tiles, weights[3], preferred_element_type=F32)
    middle = residual + spread(branch_one, mod[:, 2])
    ln_two, inv_two = norm_parts(middle)
    n_two = modulated(ln_two, mod[:, 3], mod[:, 4]).astype(BF)
    up = jnp.einsum("tk,fmkc->tfmc", n_two, weights[4::2], preferred_element_type=F32)
    hidden, slope = gelu_parts(up)
    hidden = hidden.astype(BF)
    branch_two = jnp.einsum("tfmc,fmnc->tn", hidden, weights[5::2], preferred_element_type=F32)
    final = middle + spread(branch_two, mod[:, 5])
    ln_out, inv_out = norm_parts(final)
    ln_low = ln_out.astype(BF)
    prediction = dot_nt(ln_low, head_t)
    error = prediction - noise_rows
    loss_local = jnp.sum(jnp.mean(error * error, axis=-1) * mask) / token_total

    grad_pred = (2.0 / PATCH * error * mask[:, None] / token_total).astype(BF)
    head_grad = dot_tn(grad_pred, ln_low)
    grad_final = norm_back(dot_nn(grad_pred, head_t), ln_out, inv_out)
    gate_two = window_sum(grad_final * branch_two)
    g_two = spread(grad_final, mod[:, 5]).astype(BF)
    contract_grad = jnp.einsum("tn,tfmc->fmnc", g_two, hidden, preferred_element_type=F32)
    grad_hidden = jnp.einsum("tn,fmnc->tfmc", g_two, weights[5::2], preferred_element_type=F32)
    grad_up = (grad_hidden * slope).astype(BF)
    expand_grad = jnp.einsum("tk,tfmc->fmkc", n_two, grad_up, preferred_element_type=F32)
    grad_n_two = jnp.einsum("tfmc,fmkc->tk", grad_up, weights[4::2], preferred_element_type=F32)
    shift_two, scale_two = window_sum(grad_n_two), window_sum(grad_n_two * ln_two)
    grad_middle = grad_final + norm_back(spread(grad_n_two, 1.0 + mod[:, 4]), ln_two, inv_two)
    gate_one = window_sum(grad_middle * branch_one)
    g_one = spread(grad_middle, mod[:, 2]).astype(BF)
    out_grad = jnp.einsum("tn,tmc->mnc", g_one, mixed_tiles, preferred_element_type=F32)
    grad_mixed = jnp.einsum("tn,mnc->tmc", g_one, weights[3], preferred_element_type=F32)
    grad_qkv = attend_back(grad_mixed.astype(BF).reshape(ROWS, D), qkv, mask)
    grad_qkv = grad_qkv.reshape(ROWS, 3, nm, TILE)
    in_grad = jnp.einsum("tk,tjmc->jmkc", n_one, grad_qkv, preferred_element_type=F32)
    grad_n_one = jnp.einsum("tjmc,jmkc->tk", grad_qkv, weights[:3], preferred_element_type=F32)
    shift_one, scale_one = window_sum(grad_n_one), window_sum(grad_n_one * ln_one)
    grad_embedded = grad_middle + norm_back(spread(grad_n_one, 1.0 + mod[:, 1]), ln_one, inv_one)
    embed_grad = dot_tn(latent_rows, grad_embedded.astype(BF))
    ff_grad = jnp.stack([expand_grad, contract_grad], axis=1).reshape(8, nm, D, TILE)
    partial = jnp.concatenate([in_grad, out_grad[None], ff_grad], axis=0).astype(BF)
    reduced = reduce_blocks(partial)

    ends_grad = lax.psum(jnp.stack([embed_grad, head_grad]), ("dp", "mp"))
    ends_grad = lax.dynamic_slice_in_dim(ends_grad, dp_id * rows, rows, 2)
    grad_mod = jnp.stack([shift_one, scale_one, gate_one, shift_two, scale_two, gate_two], axis=1)
    grad_mod = grad_mod.astype(BF).reshape(NMB, 6 * D)
    grad_mod = lax.all_gather(grad_mod, ("dp", "mp"), axis=0, tiled=False)
    grad_mod = grad_mod.reshape(nd, nm, NMB, 6 * D).transpose(0, 2, 1, 3)
    grad_mod = grad_mod.reshape(nd * NMB * WMB, 6 * D)
    adaptive_grad = dot_tn(cond_act, grad_mod).reshape(rows, 6, D)
    grad_cond = (dot_nt(grad_mod, adaptive_part) * silu_slope(condition)).astype(BF)
    classes_grad = dot_tn(pick, grad_cond)
    grad_cond_all = lax.all_gather(grad_cond, "dp", axis=1, tiled=True)
    time_out_grad = dot_tn(time_hidden, grad_cond_all)
    grad_time = (dot_nt(grad_cond_all, time_out_part) * silu_slope(time_pre)).astype(BF)
    time_in_grad = dot_tn(features, grad_time)

    small_grads = (
        ends_grad[0],
        ends_grad[1].T,
        time_in_grad,
        time_out_grad,
        classes_grad,
        adaptive_grad,
    )
    square_small = sum(jnp.sum(gradient * gradient) for gradient in small_grads)
    square_local = jnp.sum(reduced * reduced) + square_small / nm
    loss_value, square_total = lax.psum((loss_local, square_local), ("dp", "mp"))
    grad_norm = jnp.sqrt(square_total)
    factor = jnp.minimum(1.0, threshold / grad_norm)
    ff_reduced = reduced[4:].reshape(4, 2, rows, TILE)
    block_grads = (
        reduced[:3].transpose(1, 0, 2),
        reduced[3].T,
        ff_reduced[:, 0].transpose(1, 0, 2).reshape(rows, 4 * TILE),
        ff_reduced[:, 1].transpose(0, 2, 1).reshape(4 * TILE, rows),
    )
    all_states = (
        state_embed,
        state_head,
        state_time_in,
        state_time_out,
        state_classes,
        state_adaptive,
        state_attention_in,
        state_attention_out,
        state_expand,
        state_contract,
    )
    results = [loss_value, grad_norm]
    for state_in, gradient in zip(all_states, small_grads + block_grads):
        new_weight, moments = adam_update(state_in, gradient, factor)
        results.append(new_weight)
        results.append(moments)
    return tuple(results)


def solution(mesh):
    in_specs = (
        P("dp", None, "mp", None),
        P("dp", None, "mp", None),
        P("dp", None, "mp"),
        P("dp", None, None),
        P("dp", None, None),
        P(None, None, "dp"),
        P(None, "dp", None),
        P(None, None, "dp"),
        P(None, "dp", None),
        P(None, None, "dp"),
        P(None, "dp", None, None),
        P(None, "dp", None, "mp"),
        P(None, "mp", "dp"),
        P(None, "dp", "mp"),
        P(None, "mp", "dp"),
    )
    out_specs = (
        P(),
        P(),
        P(None, "dp"),
        P(None, None, "dp"),
        P("dp", None),
        P(None, "dp", None),
        P(None, "dp"),
        P(None, None, "dp"),
        P("dp", None),
        P(None, "dp", None),
        P(None, "dp"),
        P(None, None, "dp"),
        P("dp", None, None),
        P(None, "dp", None, None),
        P("dp", None, "mp"),
        P(None, "dp", None, "mp"),
        P("mp", "dp"),
        P(None, "mp", "dp"),
        P("dp", "mp"),
        P(None, "dp", "mp"),
        P("mp", "dp"),
        P(None, "mp", "dp"),
    )
    return jax.shard_map(
        per_device, mesh=mesh, in_specs=in_specs, out_specs=out_specs, check_vma=False
    )
```

```python
import functools
import math

import jax
import jax.numpy as jnp
from jax import lax
from jax.experimental import pallas as pl
from jax.experimental.pallas import tpu as pltpu
from jax.sharding import PartitionSpec as P

D = 1024
HEADS = 16
HD = 64
PATCH = 32
FREQ = 256
CLASSES = 600
WTOK = 320
NMB = 2
WMB = 4
TILE = 256
NJ = 12
ROWS = NMB * WTOK
MESH = pl.DeviceIdType.MESH
BF = jnp.bfloat16
F32 = jnp.float32


beta_one = 0.9
beta_two = 0.999
adam_eps = 1e-08
learn_rate = 0.15
weight_decay = 0.1
threshold = 0.002
step_count = 10.0


def timestep_features(step_ids):
    half_width = FREQ // 2
    frequency = jnp.exp(-math.log(10000.0) * jnp.arange(half_width, dtype=F32) / half_width)
    angles = step_ids.astype(F32)[:, None] * frequency[None, :]
    return jnp.concatenate([jnp.cos(angles), jnp.sin(angles)], axis=-1)


def window_positions(places):
    half_width = D // 2
    frequency = jnp.exp(-math.log(10000.0) * jnp.arange(half_width, dtype=F32) / half_width)
    angles = places.astype(F32)[:, None] * frequency[None, :]
    return jnp.concatenate([jnp.sin(angles), jnp.cos(angles)], axis=-1)


def dot_nn(a, b):
    return jnp.dot(a, b, preferred_element_type=F32)


def dot_nt(a, b):
    return lax.dot_general(a, b, (((1,), (1,)), ((), ())), preferred_element_type=F32)


def dot_tn(a, b):
    return lax.dot_general(a, b, (((0,), (0,)), ((), ())), preferred_element_type=F32)


def norm_back(grad, normed, inverse):
    mean_grad = jnp.mean(grad, axis=-1, keepdims=True)
    mean_prod = jnp.mean(grad * normed, axis=-1, keepdims=True)
    return inverse * (grad - mean_grad - normed * mean_prod)


def silu_slope(values):
    gate = jax.nn.sigmoid(values)
    return gate * (1.0 + values * (1.0 - gate))


def gelu_parts(up):
    cdf = 0.5 * (1.0 + lax.erf(up * math.sqrt(0.5)))
    pdf = jnp.exp(-0.5 * up * up) * (1.0 / math.sqrt(2.0 * math.pi))
    return up * cdf, cdf + up * pdf


def tokens3(values):
    return values.reshape(NMB, WTOK, -1)


def flip(bits, at):
    return [1 - bit if place == at else bit for place, bit in enumerate(bits)]


class Place:
    def __init__(self, nd, nm):
        self.nm = nm
        self.nb = nd.bit_length() - 2
        dp_id = lax.axis_index("dp")
        self.m = lax.axis_index("mp")
        self.core = dp_id % 2
        self.bits = [dp_id // (1 << (self.nb - at)) % 2 for at in range(self.nb)]
        self.sibling = {"dp": self.dp_of(self.bits, 1 - self.core), "mp": self.m}
        self.orders = (list(range(self.nb))[::-1], list(range(self.nb)))
        self.halves = (pl.ds(0, nm // 2), pl.ds(nm // 2, nm - nm // 2))

    def dp_of(self, bits, core):
        total = core
        for at, bit in enumerate(bits):
            total = total + bit * (1 << (self.nb - at))
        return total

    def across(self, at):
        return {"dp": self.dp_of(flip(self.bits, at), self.core), "mp": self.m}

    def along(self, hops):
        return {"dp": self.dp_of(self.bits, self.core), "mp": (self.m + hops) % self.nm}

    def pick(self, half, done, flipped=None):
        where = flip(self.bits, flipped)
        return (self.halves[half],) + tuple(
            pl.ds(0, 2) if at in done else pl.ds(where[at], 1) for at in range(self.nb)
        )

    def mine(self, m=None):
        return (self.m if m is None else m,) + tuple(self.bits)

    def greet(self):
        barrier = pltpu.get_barrier_semaphore()
        others = [self.sibling]
        others += [self.across(at) for at in range(self.nb)]
        others += [self.along(hops) for hops in range(1, self.nm)]
        for other in others:
            pl.semaphore_signal(barrier, inc=1, device_id=other, device_id_type=MESH)
        pl.semaphore_wait(barrier, len(others))


class Copies:
    def __init__(self, send_sems, recv_sems):
        self.send_sems, self.recv_sems = send_sems, recv_sems
        self.started = {}

    def start(self, step, slot, source, target, device):
        copy = pltpu.make_async_remote_copy(
            src_ref=source,
            dst_ref=target,
            send_sem=self.send_sems.at[step, slot],
            recv_sem=self.recv_sems.at[step, slot],
            device_id=device,
            device_id_type=MESH,
        )
        copy.start()
        self.started[step, slot] = copy

    def arrived(self, step, slot):
        self.started[step, slot].wait_recv()

    def drain(self, step=None):
        for key in list(self.started):
            if step is None or key[0] == step:
                self.started.pop(key).wait_send()


def gather_steps(nd, nm, shard, whole, send_sems, recv_sems, local_sems, load, compute, last):
    place = Place(nd, nm)
    nb, core = place.nb, place.core
    copies = Copies(send_sems, recv_sems)
    z_slots = [hops - 1 for hops in range(1, nm)]
    stage_slot = lambda stage, half: nm - 1 + 2 * stage + half
    twin = nm - 1 + 2 * nb
    locals_ = {}
    place.greet()

    def begin(j):
        here = whole.at[(j,) + place.mine() + (core,)]
        locals_[j] = pltpu.make_async_copy(shard.at[j], here, local_sems.at[j])
        locals_[j].start()
        for hops in range(1, nm):
            copies.start(j, hops - 1, shard.at[j], here, place.along(hops))
        copies.start(j, 2 * twin, shard.at[j], here, place.sibling)

    def stage(j, step):
        if step == 0:
            locals_[j].wait()
            for hops in range(1, nm):
                copies.arrived(j, hops - 1)
        else:
            for half in range(2):
                copies.arrived(j, stage_slot(step - 1, half))
        if step < nb:
            for half in range(2):
                order = place.orders[half]
                block = whole.at[(j,) + place.pick(half, order[:step]) + (core,)]
                copies.start(j, stage_slot(step, half), block, block, place.across(order[step]))
        if step == 0:
            for hops in range(1, nm):
                block = whole.at[(j,) + place.mine((place.m + nm - hops) % nm) + (core,)]
                copies.start(j, twin + hops - 1, block, block, place.sibling)
        else:
            for half in range(2):
                order = place.orders[half]
                block = whole.at[
                    (j,) + place.pick(half, order[: step - 1], order[step - 1]) + (core,)
                ]
                copies.start(j, twin + stage_slot(step - 1, half), block, block, place.sibling)

    def finish(j):
        for slot in range(twin, 2 * twin + 1):
            copies.arrived(j, slot)
        load(j)

    for turn in range(max(NJ + nb + 2, last + nb)):
        if turn < NJ:
            begin(turn)
        for step in range(nb + 1):
            if 0 <= turn - 1 - step < NJ:
                stage(turn - 1 - step, step)
        if 0 <= turn - 2 - nb < NJ:
            finish(turn - 2 - nb)
        compute(turn + 2 - nb)
    copies.drain()


def row_norm(values):
    center = values - jnp.mean(values, axis=-1, keepdims=True)
    inverse = lax.rsqrt(jnp.mean(center * center, axis=-1, keepdims=True) + 1e-06)
    return center * inverse, inverse


def each(count, body):
    lax.fori_loop(0, count, lambda at, carry: (body(at), carry)[1], 0)


def span(at, size):
    return pl.ds(pl.multiple_of(at * size, size), size)


def head_lanes(head, dtype=F32):
    lanes = lax.broadcasted_iota(jnp.int32, (1, TILE), 1) // HD
    return (lanes == head).astype(dtype)


def soft_rows(query, key, key_bias):
    scores = dot_nt(query, key) * HD ** (-0.5)
    scores = jnp.where(key_bias > 0, scores, -1e30)
    exponents = jnp.exp(scores - jnp.max(scores, axis=-1, keepdims=True))
    return exponents / jnp.sum(exponents, axis=-1, keepdims=True)


BLOCK = 64
PER_WINDOW = WTOK // BLOCK
NBLOCK = ROWS // BLOCK
LANE_BLOCK = 128


def transpose_rows(source, target):
    def body(at):
        target[:, span(at, LANE_BLOCK)] = source[span(at, LANE_BLOCK), :].T

    each(ROWS // LANE_BLOCK, body)


FORWARD_TURNS = (
    (5, ("qkv", 0)),
    (6, ("qkv", 1)),
    (7, ("qkv", 2)),
    (7, ("attend", 0)),
    (8, ("attend", 1)),
    (9, ("attend", 2)),
    (10, ("attend", 3)),
    (10, ("out",)),
    (11, ("up", 0)),
    (12, ("down", 0)),
    (12, ("up", 1)),
    (13, ("down", 1)),
    (13, ("up", 2)),
    (14, ("down", 2)),
    (15, ("up", 3)),
    (16, ("down", 3)),
)


def forward_kernel(nd, nm, shard, residual, mod, flags, *refs):
    (whole, n_one_t, qkv_out, mixed_out, branch_one_out, middle_out, n_two_t, hidden_out, slope_out, branch_two_out) = refs[:10]
    (n_one, qkv, mixed, branch_one, middle, n_two, flipped, hidden, slope, branch_two, loaded) = refs[10:21]
    send_sems, recv_sems, local_sems, load_sems, spill_sems = refs[21:]
    spilled = {}

    def spill(name, source, target):
        copy = pltpu.make_async_copy(source, target, spill_sems.at[len(spilled)])
        copy.start()
        spilled[name] = copy

    loads = {}
    slots = loaded.shape[0]

    def load(j):
        loads[j] = pltpu.make_async_copy(whole.at[j], loaded.at[j % slots], load_sems.at[j])
        loads[j].start()

    def tile(j, m):
        return loaded.at[j % slots, m].reshape(D, TILE)

    def first_norm():
        def body(at):
            window, here = at // PER_WINDOW, span(at, BLOCK)
            normed, _ = row_norm(residual[here, :])
            normed = normed * (1.0 + mod[window, 1:2, :]) + mod[window, 0:1, :]
            n_one[here, :] = normed.astype(BF)

        each(NBLOCK, body)
        transpose_rows(n_one, flipped.at[0])
        spill("n_one", flipped.at[0], n_one_t)

    def qkv_unit(j):
        def body(m):
            qkv[j, m] = dot_nn(n_one[...], tile(j, m)[...]).astype(BF)

        each(nm, body)
        spill(("qkv", j), qkv.at[j], qkv_out.at[j])

    def attend_unit(m):
        def body(window):
            here = span(window, WTOK)
            query, key, value = qkv[0, m, here, :], qkv[1, m, here, :], qkv[2, m, here, :]
            total = jnp.zeros((WTOK, TILE), F32)
            for head in range(TILE // HD):
                lanes = head_lanes(head, BF)
                attn = soft_rows(query * lanes, key, flags[window]).astype(BF)
                total = total + dot_nn(attn, value * lanes)
            mixed[m, here, :] = total.astype(BF)

        each(NMB, body)
        if m == nm - 1:
            spill("mixed", mixed, mixed_out)

    def add_nt(source, j, target, fresh):
        def body(at):
            columns = span(at, TILE)
            total = dot_nt(source[0], tile(j, 0)[columns, :])
            for m in range(1, nm):
                total = total + dot_nt(source[m], tile(j, m)[columns, :])
            target[:, columns] = total if fresh else target[:, columns] + total

        each(D // TILE, body)

    def out_unit():
        add_nt(mixed, 3, branch_one, True)
        spill("branch_one", branch_one, branch_one_out)

        def body(at):
            window, here = at // PER_WINDOW, span(at, BLOCK)
            rows = residual[here, :] + mod[window, 2:3, :] * branch_one[here, :]
            middle[here, :] = rows
            normed, _ = row_norm(rows)
            normed = normed * (1.0 + mod[window, 4:5, :]) + mod[window, 3:4, :]
            n_two[here, :] = normed.astype(BF)

        each(NBLOCK, body)
        spill("middle", middle, middle_out)
        transpose_rows(n_two, flipped.at[1])
        spill("n_two", flipped.at[1], n_two_t)

    def up_unit(f):
        slot = f % 2
        if f >= 2:
            spilled["hidden", f - 2].wait()
            spilled["slope", f - 2].wait()

        def body(m):
            up = dot_nn(n_two[...], tile(4 + 2 * f, m)[...])
            value, grad = gelu_parts(up)
            hidden[slot, m] = value.astype(BF)
            slope[slot, :, span(m, TILE)] = grad

        each(nm, body)
        spill(("hidden", f), hidden.at[slot], hidden_out.at[f])
        spill(("slope", f), slope.at[slot], slope_out.at[f])

    def down_unit(f):
        add_nt(hidden.at[f % 2], 5 + 2 * f, branch_two, f == 0)
        if f == 3:
            spill("branch_two", branch_two, branch_two_out)

    units = {"qkv": qkv_unit, "attend": attend_unit, "out": out_unit, "up": up_unit, "down": down_unit}
    need = {"qkv": lambda j: j, "out": lambda: 3, "up": lambda f: 4 + 2 * f, "down": lambda f: 5 + 2 * f}

    def compute(turn):
        if turn == 1:
            first_norm()
        for when, (name, *args) in FORWARD_TURNS:
            if when == turn:
                if name in need:
                    loads[need[name](*args)].wait()
                units[name](*args)

    last = max(when for when, _ in FORWARD_TURNS)
    gather_steps(nd, nm, shard, whole, send_sems, recv_sems, local_sems, load, compute, last)
    for name, copy in spilled.items():
        if name not in [(kind, f) for kind in ("hidden", "slope") for f in (0, 1)]:
            copy.wait()


def forward_blocks(shard, residual, mod, flags):
    nd, nm = lax.axis_size("dp"), lax.axis_size("mp")
    nb = nd.bit_length() - 2
    rows = shard.shape[1]
    slots = 2 * (nm - 1 + 2 * nb) + 1
    shapes = [
        ((NJ, nm) + (2,) * nb + (2, rows, TILE), BF),
        ((D, ROWS), BF),
        ((3, nm, ROWS, TILE), BF),
        ((nm, ROWS, TILE), BF),
        ((ROWS, D), F32),
        ((ROWS, D), F32),
        ((D, ROWS), BF),
        ((4, nm, ROWS, TILE), BF),
        ((4, ROWS, D), F32),
        ((ROWS, D), F32),
    ]
    return pl.pallas_call(
        functools.partial(forward_kernel, nd, nm),
        out_shape=[jax.ShapeDtypeStruct(shape, dtype) for shape, dtype in shapes],
        in_specs=[pl.BlockSpec(memory_space=pl.ANY)] + [pl.BlockSpec(memory_space=pltpu.VMEM)] * 3,
        out_specs=[pl.BlockSpec(memory_space=pl.ANY)] * len(shapes),
        scratch_shapes=[
            pltpu.VMEM((ROWS, D), BF),
            pltpu.VMEM((3, nm, ROWS, TILE), BF),
            pltpu.VMEM((nm, ROWS, TILE), BF),
            pltpu.VMEM((ROWS, D), F32),
            pltpu.VMEM((ROWS, D), F32),
            pltpu.VMEM((ROWS, D), BF),
            pltpu.VMEM((2, D, ROWS), BF),
            pltpu.VMEM((2, nm, ROWS, TILE), BF),
            pltpu.VMEM((2, ROWS, D), F32),
            pltpu.VMEM((ROWS, D), F32),
            pltpu.VMEM((4, nm) + (2,) * nb + (2, rows, TILE), BF),
            pltpu.SemaphoreType.DMA((NJ, slots)),
            pltpu.SemaphoreType.DMA((NJ, slots)),
            pltpu.SemaphoreType.DMA((NJ,)),
            pltpu.SemaphoreType.DMA((NJ,)),
            pltpu.SemaphoreType.DMA((24,)),
        ],
        compiler_params=pltpu.CompilerParams(
            collective_id=0, has_side_effects=True, vmem_limit_bytes=60 << 20
        ),
    )(shard, residual, mod, flags)


PIECES = (5, 4, 7, 6, 9, 8, 11, 10, 3, 2, 1, 0)
BACKWARD_TURNS = (
    (0, ("head",)),
    (1, ("slope", 0)),
    (1, ("spread", 0)),
    (2, ("slope", 1)),
    (2, ("spread", 1)),
    (3, ("slope", 2)),
    (3, ("spread", 2)),
    (4, ("slope", 3)),
    (4, ("spread", 3)),
    (5, ("mid",)),
    (6, ("attend", 0)),
    (7, ("attend", 1)),
    (8, ("attend", 2)),
    (9, ("attend", 3)),
    (10, ("inward", 2)),
    (11, ("inward", 1)),
    (12, ("inward", 0)),
    (12, ("last",)),
)
HELD = 5
TWINS = 4


def backward_kernel(nd, nm, whole, n_one_t, qkv, mixed, branch_one, middle, n_two_t, hidden, slope, branch_two, residual, *refs):
    (mod, flags, row_mask, token_total, noise, latents, head_t) = refs[:7]
    (total, loss, ends, grad_mod) = refs[7:11]
    (partial, twin_ref, xa, xb, grad_rows, grad_in, grad_low, grad_low_t, normed_t, pool, loaded, z_ref) = refs[11:23]
    rest = refs[23:]
    place = Place(nd, nm)
    nb, core = place.nb, place.core
    stage_refs = [rest[2 * step : 2 * step + 2] for step in range(nb)]
    send_sems, recv_sems, free_sem, load_sems = rest[2 * nb :]
    copies = Copies(send_sems, recv_sems)
    orders = [order[::-1] for order in place.orders]
    place.greet()
    slot_of = lambda step, half: 1 + 2 * step + half
    z_slot = 1 + 2 * nb
    loads = {}

    def load(name, source, target):
        copy = pltpu.make_async_copy(source, target, load_sems.at[len(loads)])
        copy.start()
        loads[name] = copy

    def load_tiles(j, slot):
        load(("w", j), whole.at[j], loaded.at[slot])

    def tile(slot, m):
        return loaded.at[slot, m].reshape(D, TILE)

    HIDDEN, QUERY, MIXED_GRAD = 4, 5, 8

    load("branch_two", branch_two, xb)
    load("middle", middle, xa)
    load(("hidden", 0), hidden.at[0], pool.at[HIDDEN])
    load("n_two", n_two_t, normed_t)
    load_tiles(5, 0)
    load_tiles(4, 1)

    def add_to(target, index, source):
        shape = source.shape[:-2]

        def body(at):
            inner, places = at, []
            for size in shape[::-1]:
                places.append(inner % size)
                inner = inner // size
            places = places[::-1]
            spot = tuple(
                base.start + offset if isinstance(base, pl.Slice) else base
                for base, offset in zip(index, places)
            ) + (core,)
            target[spot] = (target[spot].astype(F32) + source[tuple(places)].astype(F32)).astype(BF)

        each(math.prod(shape), body)

    every = (slice(None),) * (nb + 1)

    def begin(s):
        if s >= TWINS:
            pl.semaphore_wait(free_sem, 1)
        source = partial.at[(s % HELD,) + every + (1 - core,)]
        copies.start(s, 0, source, twin_ref.at[s % TWINS], place.sibling)

    def stage(s, step):
        mine = partial.at[s % HELD]
        if step == 0:
            copies.arrived(s, 0)
            add_to(mine, (pl.ds(0, nm),) + (pl.ds(0, 2),) * nb, twin_ref.at[s % TWINS])
            if s + TWINS < NJ:
                pl.semaphore_signal(free_sem, inc=1, device_id=place.sibling, device_id_type=MESH)
        else:
            for half in range(2):
                copies.arrived(s, slot_of(step - 1, half))
                index = place.pick(half, orders[half][step:])
                add_to(mine, index, stage_refs[step - 1][half].at[s])
        if step < nb:
            for half in range(2):
                order = orders[half]
                block = mine.at[place.pick(half, order[step + 1 :], order[step]) + (core,)]
                target = stage_refs[step][half].at[s]
                copies.start(s, slot_of(step, half), block, target, place.across(order[step]))
        else:
            for hops in range(1, nm):
                block = mine.at[place.mine((place.m + hops) % nm) + (core,)]
                copies.start(s, z_slot + hops - 1, block, z_ref.at[s, hops - 1], place.along(hops))

    def finish(s):
        summed = partial[(s % HELD,) + place.mine() + (core,)].astype(F32)
        for hops in range(1, nm):
            copies.arrived(s, z_slot + hops - 1)
            summed = summed + z_ref[s, hops - 1].astype(F32)
        total[PIECES[s]] = summed
        copies.drain(s)

    def weight_grad(s):
        j = PIECES[s]
        if j >= 4 and j % 2 == 1:
            f = (j - 5) // 2
            loads["hidden", f].wait()
            left, right = grad_low_t, HIDDEN
        elif j >= 4:
            left, right = normed_t, (j - 4) // 2
        elif j == 3:
            loads["mixed"].wait()
            left, right = grad_low_t, HIDDEN
        else:
            if j == 2:
                loads["n_one"].wait()
            left, right = normed_t, j

        def body(m):
            grads = dot_nn(left[...], pool[right, m]).astype(BF)
            partial.at[s % HELD, m].reshape(D, TILE)[...] = grads

        each(nm, body)
        if j in (5, 7, 9):
            load(("hidden", f + 1), hidden.at[f + 1], pool.at[HIDDEN])
        if j == 11:
            load("mixed", mixed, pool.at[HIDDEN])
        if j == 10:
            load("n_one", n_one_t, normed_t)

    def rows_of(at):
        return at // PER_WINDOW, span(at, BLOCK)

    def add_mod(window, which, values):
        grad_mod[window, which : which + 1, :] += jnp.sum(values, axis=0, keepdims=True)

    def head_unit():
        loads["branch_two"].wait()
        loads["middle"].wait()
        loss[...] = jnp.zeros_like(loss)
        ends[...] = jnp.zeros_like(ends)
        grad_mod[...] = jnp.zeros_like(grad_mod)

        def body(at):
            window, here = rows_of(at)
            gate = mod[window, 5:6, :]
            branch = xb[here, :]
            normed, inverse = row_norm(xa[here, :] + gate * branch)
            low = normed.astype(BF)
            error = dot_nt(low, head_t[...]) - noise[here, :]
            mask = row_mask[here, :]
            share = jnp.sum(error * error, axis=-1, keepdims=True) * (1.0 / PATCH) * mask
            loss[...] += jnp.sum(share, axis=0, keepdims=True) / token_total[...]
            grad_pred = (2.0 / PATCH * error * mask / token_total[...]).astype(BF)
            ends[1] += dot_tn(grad_pred, low)
            grad = norm_back(dot_nn(grad_pred, head_t[...]), normed, inverse)
            add_mod(window, 5, grad * branch)
            grad_rows[here, :] = grad
            grad_low[here, :] = (grad * gate).astype(BF)

        each(NBLOCK, body)
        transpose_rows(grad_low, grad_low_t)
        load(("slope", 0), slope.at[0], xa)
        load(("slope", 1), slope.at[1], xb)

    def slope_unit(f):
        loads["slope", f].wait()
        loads["w", 5 + 2 * f].wait()
        slopes = xa if f % 2 == 0 else xb

        def body(m):
            grad = dot_nn(grad_low[...], tile(0, m)[...])
            pool[f, m] = (grad * slopes[:, span(m, TILE)]).astype(BF)

        each(nm, body)
        if f + 2 < 4:
            load(("slope", f + 2), slope.at[f + 2], slopes)
        elif f == 2:
            load("middle_again", middle, xa)
        else:
            load("branch_one", branch_one, xb)
        load_tiles(7 + 2 * f if f < 3 else 3, 0)

    def add_rows(right, slot, fresh):
        def body(at):
            columns = span(at, TILE)
            summed = dot_nt(pool[right, 0], tile(slot, 0)[columns, :])
            for m in range(1, nm):
                summed = summed + dot_nt(pool[right, m], tile(slot, m)[columns, :])
            grad_in[:, columns] = summed if fresh else grad_in[:, columns] + summed

        each(D // TILE, body)

    def spread_unit(f):
        loads["w", 4 + 2 * f].wait()
        add_rows(f, 1, f == 0)
        load_tiles(6 + 2 * f if f < 3 else 2, 1)
        if f == 3:
            for part in range(3):
                load(("qkv", part), qkv.at[part], pool.at[QUERY + part])

    def norm_unit(which, after):
        def body(at):
            window, here = rows_of(at)
            normed, inverse = row_norm(xa[here, :])
            grad = grad_in[here, :]
            add_mod(window, which, grad)
            add_mod(window, which + 1, grad * normed)
            grad = grad * (1.0 + mod[window, which + 1 : which + 2, :])
            after(window, here, grad_rows[here, :] + norm_back(grad, normed, inverse))

        each(NBLOCK, body)

    def mid_unit():
        loads["middle_again"].wait()
        loads["branch_one"].wait()

        def after(window, here, grad):
            add_mod(window, 2, grad * xb[here, :])
            grad_rows[here, :] = grad
            grad_low[here, :] = (grad * mod[window, 2:3, :]).astype(BF)

        norm_unit(3, after)
        load("residual", residual, xa)
        loads["w", 3].wait()

        def body(m):
            pool[MIXED_GRAD, m] = dot_nn(grad_low[...], tile(0, m)[...]).astype(BF)

        each(nm, body)
        load_tiles(1, 0)

    def attend_unit(m):
        if m == 0:
            for part in range(3):
                loads["qkv", part].wait()

        def body(window):
            here = span(window, WTOK)
            query, key, value = (pool[QUERY + part, m, here, :] for part in range(3))
            grad_mixed = pool[MIXED_GRAD, m, here, :]
            grads = [jnp.zeros((WTOK, TILE), F32) for _ in range(3)]
            for head in range(TILE // HD):
                lanes = head_lanes(head, BF)
                own_query, own_grad = query * lanes, grad_mixed * lanes
                attn = soft_rows(own_query, key, flags[window])
                grads[2] = grads[2] + dot_tn(attn.astype(BF), own_grad)
                grad_attn = dot_nt(own_grad, value)
                inner = jnp.sum(attn * grad_attn, axis=-1, keepdims=True)
                grad_scores = (attn * (grad_attn - inner)).astype(BF)
                grads[0] = grads[0] + dot_nn(grad_scores, key * lanes)
                grads[1] = grads[1] + dot_tn(grad_scores, own_query)
            pool[0, m, here, :] = (grads[0] * HD ** (-0.5)).astype(BF)
            pool[1, m, here, :] = (grads[1] * HD ** (-0.5)).astype(BF)
            pool[2, m, here, :] = grads[2].astype(BF)

        each(NMB, body)

    def inward_unit(j):
        slot = 1 if j != 1 else 0
        loads["w", j].wait()
        add_rows(j, slot, j == 2)
        if j == 2:
            load_tiles(0, 1)

    def last_unit():
        loads["residual"].wait()

        def after(window, here, grad):
            ends[0] += dot_tn(latents[here, :], grad.astype(BF))

        norm_unit(0, after)

    units = {
        "head": head_unit,
        "slope": slope_unit,
        "spread": spread_unit,
        "mid": mid_unit,
        "attend": attend_unit,
        "inward": inward_unit,
        "last": last_unit,
    }

    def compute(turn):
        for when, (name, *args) in BACKWARD_TURNS:
            if when == turn:
                units[name](*args)

    last = max(when for when, _ in BACKWARD_TURNS)
    for turn in range(max(NJ + nb + 2, last + 1)):
        if turn == 0:
            compute(turn)
        if 0 < turn <= last and turn in (1, 5, 9):
            compute(turn)
        if turn == 8:
            transpose_rows(grad_low, grad_low_t)
        if turn < NJ:
            if turn == 1:
                loads["n_two"].wait()
            weight_grad(turn)
            begin(turn)
        for step in range(nb + 1):
            if 0 <= turn - 1 - step < NJ:
                stage(turn - 1 - step, step)
        if 0 <= turn - 2 - nb < NJ:
            finish(turn - 2 - nb)
        if turn not in (0, 1, 5, 9):
            compute(turn)


def backward_blocks(saved, residual, mod, flags, row_mask, token_total, noise, latents, head_t):
    nd, nm = lax.axis_size("dp"), lax.axis_size("mp")
    nb = nd.bit_length() - 2
    rows = D // nd
    bits = (2,) * nb
    slots = 2 * nb + nm
    stage_shapes = []
    for step in range(nb):
        high_first = tuple(1 if at <= step else 2 for at in range(nb))
        stage_shapes.append(pltpu.VMEM((NJ, nm // 2) + high_first + (rows, TILE), BF))
        stage_shapes.append(pltpu.VMEM((NJ, nm - nm // 2) + high_first[::-1] + (rows, TILE), BF))
    in_hbm = (*saved, residual)
    in_vmem = (mod, flags, row_mask, token_total, noise, latents, head_t)
    return pl.pallas_call(
        functools.partial(backward_kernel, nd, nm),
        out_shape=[
            jax.ShapeDtypeStruct((NJ, rows, TILE), F32),
            jax.ShapeDtypeStruct((1, 1), F32),
            jax.ShapeDtypeStruct((2, PATCH, D), F32),
            jax.ShapeDtypeStruct((NMB, 6, D), F32),
        ],
        in_specs=[pl.BlockSpec(memory_space=pl.ANY)] * len(in_hbm)
        + [pl.BlockSpec(memory_space=pltpu.VMEM)] * len(in_vmem),
        out_specs=[pl.BlockSpec(memory_space=pltpu.VMEM)] * 4,
        scratch_shapes=[
            pltpu.VMEM((HELD, nm) + bits + (2, rows, TILE), BF),
            pltpu.VMEM((TWINS, nm) + bits + (rows, TILE), BF),
            pltpu.VMEM((ROWS, D), F32),
            pltpu.VMEM((ROWS, D), F32),
            pltpu.VMEM((ROWS, D), F32),
            pltpu.VMEM((ROWS, D), F32),
            pltpu.VMEM((ROWS, D), BF),
            pltpu.VMEM((D, ROWS), BF),
            pltpu.VMEM((D, ROWS), BF),
            pltpu.VMEM((9, nm, ROWS, TILE), BF),
            pltpu.VMEM((2, nm) + bits + (2, rows, TILE), BF),
            pltpu.VMEM((NJ, nm - 1, rows, TILE), BF),
            *stage_shapes,
            pltpu.SemaphoreType.DMA((NJ, slots)),
            pltpu.SemaphoreType.DMA((NJ, slots)),
            pltpu.SemaphoreType.REGULAR,
            pltpu.SemaphoreType.DMA((36,)),
        ],
        compiler_params=pltpu.CompilerParams(
            collective_id=1, has_side_effects=True, vmem_limit_bytes=61 << 20
        ),
    )(*in_hbm, *in_vmem)


def adam_update(state_in, gradient, factor):
    clipped = gradient * factor
    first_moment = beta_one * state_in[1] + (1.0 - beta_one) * clipped
    second_moment = beta_two * state_in[2] * state_in[2] + (1.0 - beta_two) * clipped * clipped
    root_moment = jnp.sqrt(second_moment)
    update = (
        first_moment
        / (1.0 - beta_one**step_count)
        / (root_moment / math.sqrt(1.0 - beta_two**step_count) + adam_eps)
    )
    new_weight = state_in[0] - learn_rate * (update + weight_decay * state_in[0])
    return (new_weight, jnp.stack([first_moment, root_moment]))


def per_device(
    latents,
    noise_target,
    token_mask,
    timesteps,
    labels,
    state_embed,
    state_head,
    state_time_in,
    state_time_out,
    state_classes,
    state_adaptive,
    state_attention_in,
    state_attention_out,
    state_expand,
    state_contract,
):
    nd, nm = lax.axis_size("dp"), lax.axis_size("mp")
    dp_id, mp_id = lax.axis_index("dp"), lax.axis_index("mp")
    rows = state_attention_in.shape[1]
    attn_in_tiles = state_attention_in[0].transpose(1, 0, 2)
    expand_tiles = state_expand[0].reshape(rows, 4, TILE).transpose(1, 0, 2)
    contract_tiles = state_contract[0].reshape(4, TILE, rows).transpose(0, 2, 1)
    ff_tiles = jnp.stack([expand_tiles, contract_tiles], axis=1).reshape(8, rows, TILE)
    shard = jnp.concatenate(
        [attn_in_tiles, state_attention_out[0].T[None], ff_tiles], axis=0
    ).astype(BF)

    mask = token_mask.astype(F32).reshape(ROWS)
    token_total = lax.psum(jnp.sum(mask), ("dp", "mp"))
    ends = jnp.stack([state_embed[0], state_head[0].T]).astype(BF)
    ends = lax.all_gather(ends, "dp", axis=2, tiled=True)
    embed_mat, head_t = ends[0], ends[1]

    both_ids = lax.all_gather(jnp.stack([timesteps, labels])[:, 0], "dp", axis=1, tiled=False)
    both_ids = both_ids.reshape(2, nd * NMB * WMB)
    features = timestep_features(both_ids[0]).astype(BF)
    pick = (both_ids[1][:, None] == jnp.arange(CLASSES)[None, :]).astype(BF)
    time_pre = dot_nn(features, state_time_in[0].astype(BF))
    time_hidden = jax.nn.silu(time_pre).astype(BF)
    time_out_part = state_time_out[0].astype(BF)
    condition = lax.psum_scatter(
        dot_nn(time_hidden, time_out_part), "dp", scatter_dimension=1, tiled=True
    ) + dot_nn(pick, state_classes[0].astype(BF))
    cond_act = jax.nn.silu(condition).astype(BF)
    adaptive_part = state_adaptive[0].astype(BF).reshape(rows, 6 * D)
    mine = lax.dynamic_index_in_dim(
        cond_act.reshape(nd * NMB, WMB, rows), mp_id, 1, keepdims=False
    )
    mod = lax.psum_scatter(dot_nn(mine, adaptive_part), "dp", scatter_dimension=0, tiled=True)
    mod = mod.reshape(NMB, 6, D)

    latent_rows = latents.reshape(ROWS, PATCH)
    noise_rows = noise_target.reshape(ROWS, PATCH)
    positions = window_positions(jnp.arange(WTOK, dtype=jnp.int32))
    residual = (tokens3(dot_nn(latent_rows, embed_mat)) + positions[None]).reshape(ROWS, D)
    flags = token_mask.reshape(NMB, 1, WTOK)
    saved = forward_blocks(shard, residual, mod, flags)
    reduced, loss_local, ends_grad, grad_mod = backward_blocks(
        saved,
        residual,
        mod,
        flags,
        mask[:, None],
        token_total.reshape(1, 1),
        noise_rows,
        latent_rows,
        head_t,
    )
    loss_local = loss_local[0, 0]
    ends_grad = lax.psum(ends_grad, ("dp", "mp"))
    ends_grad = lax.dynamic_slice_in_dim(ends_grad, dp_id * rows, rows, 2)
    grad_mod = grad_mod.astype(BF).reshape(NMB, 6 * D)
    grad_mod = lax.all_gather(grad_mod, ("dp", "mp"), axis=0, tiled=False)
    grad_mod = grad_mod.reshape(nd, nm, NMB, 6 * D).transpose(0, 2, 1, 3)
    grad_mod = grad_mod.reshape(nd * NMB * WMB, 6 * D)
    adaptive_grad = dot_tn(cond_act, grad_mod).reshape(rows, 6, D)
    grad_cond = (dot_nt(grad_mod, adaptive_part) * silu_slope(condition)).astype(BF)
    classes_grad = dot_tn(pick, grad_cond)
    grad_cond_all = lax.all_gather(grad_cond, "dp", axis=1, tiled=True)
    time_out_grad = dot_tn(time_hidden, grad_cond_all)
    grad_time = (dot_nt(grad_cond_all, time_out_part) * silu_slope(time_pre)).astype(BF)
    time_in_grad = dot_tn(features, grad_time)

    small_grads = (
        ends_grad[0],
        ends_grad[1].T,
        time_in_grad,
        time_out_grad,
        classes_grad,
        adaptive_grad,
    )
    square_small = sum(jnp.sum(gradient * gradient) for gradient in small_grads)
    square_local = jnp.sum(reduced * reduced) + square_small / nm
    loss_value, square_total = lax.psum((loss_local, square_local), ("dp", "mp"))
    grad_norm = jnp.sqrt(square_total)
    factor = jnp.minimum(1.0, threshold / grad_norm)
    ff_reduced = reduced[4:].reshape(4, 2, rows, TILE)
    block_grads = (
        reduced[:3].transpose(1, 0, 2),
        reduced[3].T,
        ff_reduced[:, 0].transpose(1, 0, 2).reshape(rows, 4 * TILE),
        ff_reduced[:, 1].transpose(0, 2, 1).reshape(4 * TILE, rows),
    )
    all_states = (
        state_embed,
        state_head,
        state_time_in,
        state_time_out,
        state_classes,
        state_adaptive,
        state_attention_in,
        state_attention_out,
        state_expand,
        state_contract,
    )
    results = [loss_value, grad_norm]
    for state_in, gradient in zip(all_states, small_grads + block_grads):
        new_weight, moments = adam_update(state_in, gradient, factor)
        results.append(new_weight)
        results.append(moments)
    return tuple(results)


def solution(mesh):
    in_specs = (
        P("dp", None, "mp", None),
        P("dp", None, "mp", None),
        P("dp", None, "mp"),
        P("dp", None, None),
        P("dp", None, None),
        P(None, None, "dp"),
        P(None, "dp", None),
        P(None, None, "dp"),
        P(None, "dp", None),
        P(None, None, "dp"),
        P(None, "dp", None, None),
        P(None, "dp", None, "mp"),
        P(None, "mp", "dp"),
        P(None, "dp", "mp"),
        P(None, "mp", "dp"),
    )
    out_specs = (
        P(),
        P(),
        P(None, "dp"),
        P(None, None, "dp"),
        P("dp", None),
        P(None, "dp", None),
        P(None, "dp"),
        P(None, None, "dp"),
        P("dp", None),
        P(None, "dp", None),
        P(None, "dp"),
        P(None, None, "dp"),
        P("dp", None, None),
        P(None, "dp", None, None),
        P("dp", None, "mp"),
        P(None, "dp", None, "mp"),
        P("mp", "dp"),
        P(None, "mp", "dp"),
        P("dp", "mp"),
        P(None, "dp", "mp"),
        P("mp", "dp"),
        P(None, "mp", "dp"),
    )
    return jax.shard_map(
        per_device, mesh=mesh, in_specs=in_specs, out_specs=out_specs, check_vma=False
    )
```

```python
import functools
import math

import jax
import jax.numpy as jnp
from jax import lax
from jax.experimental import pallas as pl
from jax.experimental.pallas import tpu as pltpu
from jax.sharding import PartitionSpec as P

D = 1024
HEADS = 16
HD = 64
PATCH = 32
FREQ = 256
CLASSES = 600
WTOK = 320
NMB = 2
WMB = 4
TILE = 256
NJ = 12
ROWS = NMB * WTOK
MESH = pl.DeviceIdType.MESH
BF = jnp.bfloat16
F32 = jnp.float32


beta_one = 0.9
beta_two = 0.999
adam_eps = 1e-08
learn_rate = 0.15
weight_decay = 0.1
threshold = 0.002
step_count = 10.0


def timestep_features(step_ids):
    half_width = FREQ // 2
    frequency = jnp.exp(-math.log(10000.0) * jnp.arange(half_width, dtype=F32) / half_width)
    angles = step_ids.astype(F32)[:, None] * frequency[None, :]
    return jnp.concatenate([jnp.cos(angles), jnp.sin(angles)], axis=-1)


def window_positions(places):
    half_width = D // 2
    frequency = jnp.exp(-math.log(10000.0) * jnp.arange(half_width, dtype=F32) / half_width)
    angles = places.astype(F32)[:, None] * frequency[None, :]
    return jnp.concatenate([jnp.sin(angles), jnp.cos(angles)], axis=-1)


def dot_general(a, b, a_dim, b_dim):
    return lax.dot_general(a, b, (((a_dim,), (b_dim,)), ((), ())), preferred_element_type=F32)


def dot_nn(a, b):
    return jnp.dot(a, b, preferred_element_type=F32)


def dot_nt(a, b):
    return dot_general(a, b, 1, 1)


def dot_tn(a, b):
    return dot_general(a, b, 0, 0)


def norm_back(grad, normed, inverse):
    mean_grad = jnp.mean(grad, axis=-1, keepdims=True)
    mean_prod = jnp.mean(grad * normed, axis=-1, keepdims=True)
    return inverse * (grad - mean_grad - normed * mean_prod)


def silu(values):
    return values * jax.nn.sigmoid(values)


def silu_slope(values):
    gate = jax.nn.sigmoid(values)
    return gate * (1.0 + values * (1.0 - gate))


def gelu_parts(up):
    cdf = 0.5 * (1.0 + lax.erf(up * math.sqrt(0.5)))
    pdf = jnp.exp(-0.5 * up * up) * (1.0 / math.sqrt(2.0 * math.pi))
    return up * cdf, cdf + up * pdf


def tokens3(values):
    return values.reshape(NMB, WTOK, -1)


def flip(bits, at):
    return [1 - bit if place == at else bit for place, bit in enumerate(bits)]


class Place:
    def __init__(self, nd, nm):
        self.nm = nm
        self.nb = nd.bit_length() - 2
        dp_id = lax.axis_index("dp")
        self.nd = nd
        self.dp_id = dp_id
        self.m = lax.axis_index("mp")
        self.core = dp_id % 2
        self.bits = [dp_id // (1 << (self.nb - at)) % 2 for at in range(self.nb)]
        self.sibling = {"dp": self.dp_of(self.bits, 1 - self.core), "mp": self.m}
        self.orders = (list(range(self.nb))[::-1], list(range(self.nb)))
        self.halves = (pl.ds(0, nm // 2), pl.ds(nm // 2, nm - nm // 2))

    def dp_of(self, bits, core):
        total = core
        for at, bit in enumerate(bits):
            total = total + bit * (1 << (self.nb - at))
        return total

    def across(self, at):
        return {"dp": self.dp_of(flip(self.bits, at), self.core), "mp": self.m}

    def along(self, hops):
        return {"dp": self.dp_of(self.bits, self.core), "mp": (self.m + hops) % self.nm}

    def beside(self, hops):
        return {"dp": (self.dp_id + hops) % self.nd, "mp": self.m}

    def pick(self, half, done, flipped=None):
        where = flip(self.bits, flipped)
        return (self.halves[half],) + tuple(
            pl.ds(0, 2) if at in done else pl.ds(where[at], 1) for at in range(self.nb)
        )

    def mine(self, m=None):
        return (self.m if m is None else m,) + tuple(self.bits)

    def greet(self, everyone=False):
        barrier = pltpu.get_barrier_semaphore()
        if everyone:
            others = [self.beside(hops) for hops in range(1, self.nd)]
        else:
            others = [self.sibling] + [self.across(at) for at in range(self.nb)]
        others += [self.along(hops) for hops in range(1, self.nm)]
        for other in others:
            pl.semaphore_signal(barrier, inc=1, device_id=other, device_id_type=MESH)
        pl.semaphore_wait(barrier, len(others))


class Copies:
    def __init__(self, send_sems, recv_sems):
        self.send_sems, self.recv_sems = send_sems, recv_sems
        self.started = {}

    def start(self, step, slot, source, target, device):
        copy = pltpu.make_async_remote_copy(
            src_ref=source,
            dst_ref=target,
            send_sem=self.send_sems.at[step, slot],
            recv_sem=self.recv_sems.at[step, slot],
            device_id=device,
            device_id_type=MESH,
        )
        copy.start()
        self.started[step, slot] = copy

    def arrived(self, step, slot):
        self.started[step, slot].wait_recv()

    def drain(self, step=None):
        for key in list(self.started):
            if step is None or key[0] == step:
                self.started.pop(key).wait_send()


class Exchange:
    def __init__(self, place, send_sems, recv_sems):
        self.place = place
        self.copies = Copies(send_sems, recv_sems)

    def dp_gather(self, group, source, target):
        for hops in range(1, self.place.nd):
            here = target.at[self.place.dp_id]
            self.copies.start(group, hops - 1, source, here, self.place.beside(hops))

    def dp_scatter(self, group, source, target):
        for hops in range(1, self.place.nd):
            block = source.at[(self.place.dp_id + hops) % self.place.nd]
            self.copies.start(group, hops - 1, block, target.at[hops - 1], self.place.beside(hops))

    def mp_gather(self, group, source, target):
        for hops in range(1, self.place.nm):
            here = target.at[self.place.m]
            self.copies.start(group, hops - 1, source, here, self.place.along(hops))

    def wait(self, group):
        for step, slot in list(self.copies.started):
            if step == group:
                self.copies.arrived(step, slot)

    def drain(self):
        self.copies.drain()


def gather_steps(place, shard, whole, send_sems, recv_sems, local_sems, load, compute, last):
    nm, nb, core = place.nm, place.nb, place.core
    copies = Copies(send_sems, recv_sems)
    stage_slot = lambda stage, half: nm - 1 + 2 * stage + half
    twin = nm - 1 + 2 * nb
    locals_ = {}

    def begin(j):
        here = whole.at[(j,) + place.mine() + (core,)]
        locals_[j] = pltpu.make_async_copy(shard.at[j], here, local_sems.at[j])
        locals_[j].start()
        for hops in range(1, nm):
            copies.start(j, hops - 1, shard.at[j], here, place.along(hops))
        copies.start(j, 2 * twin, shard.at[j], here, place.sibling)

    def stage(j, step):
        if step == 0:
            locals_[j].wait()
            for hops in range(1, nm):
                copies.arrived(j, hops - 1)
        else:
            for half in range(2):
                copies.arrived(j, stage_slot(step - 1, half))
        if step < nb:
            for half in range(2):
                order = place.orders[half]
                block = whole.at[(j,) + place.pick(half, order[:step]) + (core,)]
                copies.start(j, stage_slot(step, half), block, block, place.across(order[step]))
        if step == 0:
            for hops in range(1, nm):
                block = whole.at[(j,) + place.mine((place.m + nm - hops) % nm) + (core,)]
                copies.start(j, twin + hops - 1, block, block, place.sibling)
        else:
            for half in range(2):
                order = place.orders[half]
                block = whole.at[
                    (j,) + place.pick(half, order[: step - 1], order[step - 1]) + (core,)
                ]
                copies.start(j, twin + stage_slot(step - 1, half), block, block, place.sibling)

    def finish(j):
        for slot in range(twin, 2 * twin + 1):
            copies.arrived(j, slot)
        load(j)

    for turn in range(max(NJ + nb + 2, last + nb)):
        if turn < NJ:
            begin(turn)
        for step in range(nb + 1):
            if 0 <= turn - 1 - step < NJ:
                stage(turn - 1 - step, step)
        if 0 <= turn - 2 - nb < NJ:
            finish(turn - 2 - nb)
        compute(turn + 2 - nb)
    copies.drain()


def row_norm(values):
    center = values - jnp.mean(values, axis=-1, keepdims=True)
    inverse = lax.rsqrt(jnp.mean(center * center, axis=-1, keepdims=True) + 1e-06)
    return center * inverse, inverse


def each(count, body):
    lax.fori_loop(0, count, lambda at, carry: (body(at), carry)[1], 0)


def span(at, size):
    return pl.ds(pl.multiple_of(at * size, size), size)


def head_lanes(head, dtype=F32):
    lanes = lax.broadcasted_iota(jnp.int32, (1, TILE), 1) // HD
    return (lanes == head).astype(dtype)


def soft_rows(query, key, key_bias):
    scores = dot_nt(query, key) * HD ** (-0.5)
    scores = jnp.where(key_bias > 0, scores, -1e30)
    exponents = jnp.exp(scores - jnp.max(scores, axis=-1, keepdims=True))
    return exponents / jnp.sum(exponents, axis=-1, keepdims=True)


def label_pick(front, count):
    labels = front[:, :, FREQ : FREQ + 1].reshape(-1, 1)
    lanes = lax.broadcasted_iota(jnp.int32, (labels.shape[0], count), 1).astype(F32)
    return (lanes == labels).astype(BF)


PER_INDEX = NMB * WMB
BLOCK = 64
PER_WINDOW = WTOK // BLOCK
NBLOCK = ROWS // BLOCK
LANE_BLOCK = 128


def transpose_rows(source, target):
    def body(at):
        target[:, span(at, LANE_BLOCK)] = source[span(at, LANE_BLOCK), :].T

    each(ROWS // LANE_BLOCK, body)


FORWARD_TURNS = (
    (5, ("qkv", 0)),
    (6, ("qkv", 1)),
    (7, ("qkv", 2)),
    (7, ("attend", 0)),
    (8, ("attend", 1)),
    (9, ("attend", 2)),
    (10, ("attend", 3)),
    (10, ("out",)),
    (11, ("up", 0)),
    (12, ("down", 0)),
    (12, ("up", 1)),
    (13, ("down", 1)),
    (13, ("up", 2)),
    (14, ("down", 2)),
    (15, ("up", 3)),
    (16, ("down", 3)),
)


def forward_kernel(nd, nm, shard, flags, front_in, ends_in, latents, positions, time_in, time_out, classes, adaptive, *refs):
    (residual_out, mod, ends, front, time_pre, condition, token_total) = refs[:7]
    refs = refs[7:]
    (residual, parts, parts_in, mods, mods_in, rows_ref, counts, swap_send, swap_recv) = refs[-9:]
    refs = refs[:-9]
    place = Place(nd, nm)
    swap = Exchange(place, swap_send, swap_recv)
    place.greet(everyone=True)
    dp_id = place.dp_id
    windows = nd * PER_INDEX
    upright = parts.shape[1] == windows
    (whole, n_one_t, qkv_out, mixed_out, branch_one_out, middle_out, n_two_t, hidden_out, slope_out, branch_two_out) = refs[:10]
    (n_one, qkv, mixed, branch_one, middle, n_two, flipped, hidden, slope, branch_two, loaded) = refs[10:21]
    send_sems, recv_sems, local_sems, load_sems, spill_sems = refs[21:]
    spilled = {}

    def spill(name, source, target):
        copy = pltpu.make_async_copy(source, target, spill_sems.at[len(spilled)])
        copy.start()
        spilled[name] = copy

    loads = {}
    slots = loaded.shape[0]

    def load(j):
        loads[j] = pltpu.make_async_copy(whole.at[j], loaded.at[j % slots], load_sems.at[j])
        loads[j].start()

    def tile(j, m):
        return loaded.at[j % slots, m].reshape(D, TILE)

    def first_swap():
        front[dp_id] = front_in[...]
        for which in range(2):
            ends[which, dp_id] = ends_in[which]
        swap.dp_gather(0, front_in, front)
        swap.dp_gather(1, ends_in.at[0], ends.at[0])
        swap.dp_gather(2, ends_in.at[1], ends.at[1])

    def time_layers():
        swap.wait(0)
        features = front[:, :, :FREQ].reshape(windows, FREQ).astype(BF)
        time_pre[...] = dot_nn(features, time_in[...])
        time_hidden = silu(time_pre[...]).astype(BF)
        for index in range(nd):
            if upright:
                parts[index] = dot_nn(time_hidden, time_out[index])
            else:
                parts[index] = dot_general(time_out[index], time_hidden, 0, 1)
        swap.dp_scatter(3, parts, parts_in)
        counts[place.m] = jnp.sum(front[:, :, FREQ + 128 :], axis=0)
        swap.mp_gather(5, counts.at[place.m], counts)

    def condition_layers():
        swap.wait(3)
        total = parts[dp_id] + jnp.sum(parts_in[...], axis=0)
        total = total if upright else total.T
        total = total + dot_nn(label_pick(front, classes.shape[0]), classes[...])
        condition[...] = total
        row_ids = lax.broadcasted_iota(jnp.int32, (nd * NMB, windows), 0)
        column_ids = lax.broadcasted_iota(jnp.int32, (nd * NMB, windows), 1)
        wanted = row_ids // NMB * PER_INDEX + place.m * NMB + row_ids % NMB
        own = dot_nn((wanted == column_ids).astype(BF), silu(total).astype(BF)).astype(BF)
        for which in range(6):
            rows_ref[...] = dot_nn(own, adaptive[which])

            def move(row):
                mods[row // NMB, row % NMB, which : which + 1, :] = rows_ref[pl.ds(row, 1), :]

            each(nd * NMB, move)
        swap.dp_scatter(4, mods, mods_in)

    def modulation():
        swap.wait(4)
        for window in range(NMB):
            mod[window] = mods[dp_id, window] + jnp.sum(mods_in[:, window], axis=0)
        swap.wait(5)
        token_total[...] = jnp.sum(counts[...], axis=0)
        swap.wait(1)
        swap.wait(2)
        embed_mat = ends[0].reshape(D, PATCH)

        def body(window):
            here = span(window, WTOK)
            residual[here, :] = dot_nt(latents[here, :], embed_mat) + positions[...]

        each(NMB, body)
        spill("residual", residual, residual_out)

    def first_norm():
        def body(at):
            window, here = at // PER_WINDOW, span(at, BLOCK)
            normed, _ = row_norm(residual[here, :])
            normed = normed * (1.0 + mod[window, 1:2, :]) + mod[window, 0:1, :]
            n_one[here, :] = normed.astype(BF)

        each(NBLOCK, body)
        transpose_rows(n_one, flipped.at[0])
        spill("n_one", flipped.at[0], n_one_t)

    def qkv_unit(j):
        def body(m):
            qkv[j, m] = dot_nn(n_one[...], tile(j, m)[...]).astype(BF)

        each(nm, body)
        spill(("qkv", j), qkv.at[j], qkv_out.at[j])

    def attend_unit(m):
        def body(window):
            here = span(window, WTOK)
            query, key, value = qkv[0, m, here, :], qkv[1, m, here, :], qkv[2, m, here, :]
            total = jnp.zeros((WTOK, TILE), F32)
            for head in range(TILE // HD):
                lanes = head_lanes(head, BF)
                attn = soft_rows(query * lanes, key, flags[window]).astype(BF)
                total = total + dot_nn(attn, value * lanes)
            mixed[m, here, :] = total.astype(BF)

        each(NMB, body)
        if m == nm - 1:
            spill("mixed", mixed, mixed_out)

    def add_nt(source, j, target, fresh):
        def body(at):
            columns = span(at, TILE)
            total = dot_nt(source[0], tile(j, 0)[columns, :])
            for m in range(1, nm):
                total = total + dot_nt(source[m], tile(j, m)[columns, :])
            target[:, columns] = total if fresh else target[:, columns] + total

        each(D // TILE, body)

    def out_unit():
        add_nt(mixed, 3, branch_one, True)
        spill("branch_one", branch_one, branch_one_out)

        def body(at):
            window, here = at // PER_WINDOW, span(at, BLOCK)
            rows = residual[here, :] + mod[window, 2:3, :] * branch_one[here, :]
            middle[here, :] = rows
            normed, _ = row_norm(rows)
            normed = normed * (1.0 + mod[window, 4:5, :]) + mod[window, 3:4, :]
            n_two[here, :] = normed.astype(BF)

        each(NBLOCK, body)
        spill("middle", middle, middle_out)
        transpose_rows(n_two, flipped.at[1])
        spill("n_two", flipped.at[1], n_two_t)

    def up_unit(f):
        slot = f % 2
        if f >= 2:
            spilled["hidden", f - 2].wait()
            spilled["slope", f - 2].wait()

        def body(m):
            up = dot_nn(n_two[...], tile(4 + 2 * f, m)[...])
            value, grad = gelu_parts(up)
            hidden[slot, m] = value.astype(BF)
            slope[slot, :, span(m, TILE)] = grad

        each(nm, body)
        spill(("hidden", f), hidden.at[slot], hidden_out.at[f])
        spill(("slope", f), slope.at[slot], slope_out.at[f])

    def down_unit(f):
        add_nt(hidden.at[f % 2], 5 + 2 * f, branch_two, f == 0)
        if f == 3:
            spill("branch_two", branch_two, branch_two_out)

    units = {"qkv": qkv_unit, "attend": attend_unit, "out": out_unit, "up": up_unit, "down": down_unit}
    need = {"qkv": lambda j: j, "out": lambda: 3, "up": lambda f: 4 + 2 * f, "down": lambda f: 5 + 2 * f}

    def compute(turn):
        early = (first_swap, time_layers, condition_layers, modulation, first_norm)
        if turn < len(early):
            early[turn]()
        for when, (name, *args) in FORWARD_TURNS:
            if when == turn:
                if name in need:
                    loads[need[name](*args)].wait()
                units[name](*args)

    last = max(when for when, _ in FORWARD_TURNS)
    gather_steps(place, shard, whole, send_sems, recv_sems, local_sems, load, compute, last)
    for name, copy in spilled.items():
        if name not in [(kind, f) for kind in ("hidden", "slope") for f in (0, 1)]:
            copy.wait()
    swap.drain()


def forward_blocks(shard, *others):
    nd, nm = lax.axis_size("dp"), lax.axis_size("mp")
    nb = nd.bit_length() - 2
    rows = shard.shape[1]
    slots = 2 * (nm - 1 + 2 * nb) + 1
    windows = nd * PER_INDEX
    tall = windows <= rows
    small = [
        ((NMB, 6, D), F32),
        ((2, nd, rows, PATCH), BF),
        ((nd, PER_INDEX, FREQ + 256), F32),
        ((windows, rows), F32),
        ((windows, rows), F32),
        ((PER_INDEX, 128), F32),
    ]
    shapes = [
        ((NJ, nm) + (2,) * nb + (2, rows, TILE), BF),
        ((D, ROWS), BF),
        ((3, nm, ROWS, TILE), BF),
        ((nm, ROWS, TILE), BF),
        ((ROWS, D), F32),
        ((ROWS, D), F32),
        ((D, ROWS), BF),
        ((4, nm, ROWS, TILE), BF),
        ((4, ROWS, D), F32),
        ((ROWS, D), F32),
    ]
    return pl.pallas_call(
        functools.partial(forward_kernel, nd, nm),
        out_shape=[
            jax.ShapeDtypeStruct(shape, dtype) for shape, dtype in [((ROWS, D), F32)] + small + shapes
        ],
        in_specs=[pl.BlockSpec(memory_space=pl.ANY)]
        + [pl.BlockSpec(memory_space=pltpu.VMEM)] * len(others),
        out_specs=[pl.BlockSpec(memory_space=pl.ANY)]
        + [pl.BlockSpec(memory_space=pltpu.VMEM)] * len(small)
        + [pl.BlockSpec(memory_space=pl.ANY)] * len(shapes),
        scratch_shapes=[
            pltpu.VMEM((ROWS, D), BF),
            pltpu.VMEM((3, nm, ROWS, TILE), BF),
            pltpu.VMEM((nm, ROWS, TILE), BF),
            pltpu.VMEM((ROWS, D), F32),
            pltpu.VMEM((ROWS, D), F32),
            pltpu.VMEM((ROWS, D), BF),
            pltpu.VMEM((2, D, ROWS), BF),
            pltpu.VMEM((2, nm, ROWS, TILE), BF),
            pltpu.VMEM((2, ROWS, D), F32),
            pltpu.VMEM((ROWS, D), F32),
            pltpu.VMEM((4, nm) + (2,) * nb + (2, rows, TILE), BF),
            pltpu.SemaphoreType.DMA((NJ, slots)),
            pltpu.SemaphoreType.DMA((NJ, slots)),
            pltpu.SemaphoreType.DMA((NJ,)),
            pltpu.SemaphoreType.DMA((NJ,)),
            pltpu.SemaphoreType.DMA((24,)),
            pltpu.VMEM((ROWS, D), F32),
            pltpu.VMEM((nd, windows if tall else rows, rows if tall else windows), F32),
            pltpu.VMEM((nd - 1, windows if tall else rows, rows if tall else windows), F32),
            pltpu.VMEM((nd, NMB, 6, D), F32),
            pltpu.VMEM((nd - 1, NMB, 6, D), F32),
            pltpu.VMEM((nd * NMB, D), F32),
            pltpu.VMEM((nm, PER_INDEX, 128), F32),
            pltpu.SemaphoreType.DMA((6, max(nd, nm) - 1)),
            pltpu.SemaphoreType.DMA((6, max(nd, nm) - 1)),
        ],
        compiler_params=pltpu.CompilerParams(
            collective_id=0, has_side_effects=True, vmem_limit_bytes=60 << 20
        ),
    )(shard, *others)


PIECES = (5, 4, 7, 6, 9, 8, 11, 10, 3, 2, 1, 0)
BACKWARD_TURNS = (
    (0, ("head",)),
    (1, ("slope", 0)),
    (1, ("spread", 0)),
    (2, ("slope", 1)),
    (2, ("spread", 1)),
    (3, ("slope", 2)),
    (3, ("spread", 2)),
    (4, ("slope", 3)),
    (4, ("spread", 3)),
    (5, ("mid",)),
    (6, ("attend", 0)),
    (7, ("attend", 1)),
    (8, ("attend", 2)),
    (9, ("attend", 3)),
    (10, ("inward", 2)),
    (11, ("inward", 1)),
    (12, ("inward", 0)),
    (12, ("last",)),
)
HELD = 5
TWINS = 4


def backward_kernel(nd, nm, whole, n_one_t, qkv, mixed, branch_one, middle, n_two_t, hidden, slope, branch_two, residual, *refs):
    (mod, flags, row_mask, token_total_in, noise, latents, both_ends) = refs[:7]
    token_total = token_total_in[0:1, 0:1]
    head_mat = both_ends[1].reshape(D, PATCH)
    (total, loss, ends, grad_mod) = refs[7:11]
    (partial, twin_ref, xa, xb, grad_rows, grad_in, grad_low, grad_low_t, normed_t, pool, loaded, z_ref) = refs[11:23]
    rest = refs[23:]
    place = Place(nd, nm)
    nb, core = place.nb, place.core
    stage_refs = [rest[2 * step : 2 * step + 2] for step in range(nb)]
    send_sems, recv_sems, free_sem, load_sems = rest[2 * nb :]
    copies = Copies(send_sems, recv_sems)
    orders = [order[::-1] for order in place.orders]
    place.greet()
    slot_of = lambda step, half: 1 + 2 * step + half
    z_slot = 1 + 2 * nb
    loads = {}

    def load(name, source, target):
        copy = pltpu.make_async_copy(source, target, load_sems.at[len(loads)])
        copy.start()
        loads[name] = copy

    def load_tiles(j, slot):
        load(("w", j), whole.at[j], loaded.at[slot])

    def tile(slot, m):
        return loaded.at[slot, m].reshape(D, TILE)

    HIDDEN, QUERY, MIXED_GRAD = 4, 5, 8

    load("branch_two", branch_two, xb)
    load("middle", middle, xa)
    load(("hidden", 0), hidden.at[0], pool.at[HIDDEN])
    load("n_two", n_two_t, normed_t)
    load_tiles(5, 0)
    load_tiles(4, 1)

    def add_to(target, index, source):
        shape = source.shape[:-2]

        def body(at):
            inner, places = at, []
            for size in shape[::-1]:
                places.append(inner % size)
                inner = inner // size
            places = places[::-1]
            spot = tuple(
                base.start + offset if isinstance(base, pl.Slice) else base
                for base, offset in zip(index, places)
            ) + (core,)
            target[spot] = (target[spot].astype(F32) + source[tuple(places)].astype(F32)).astype(BF)

        each(math.prod(shape), body)

    every = (slice(None),) * (nb + 1)

    def begin(s):
        if s >= TWINS:
            pl.semaphore_wait(free_sem, 1)
        source = partial.at[(s % HELD,) + every + (1 - core,)]
        copies.start(s, 0, source, twin_ref.at[s % TWINS], place.sibling)

    def stage(s, step):
        mine = partial.at[s % HELD]
        if step == 0:
            copies.arrived(s, 0)
            add_to(mine, (pl.ds(0, nm),) + (pl.ds(0, 2),) * nb, twin_ref.at[s % TWINS])
            if s + TWINS < NJ:
                pl.semaphore_signal(free_sem, inc=1, device_id=place.sibling, device_id_type=MESH)
        else:
            for half in range(2):
                copies.arrived(s, slot_of(step - 1, half))
                index = place.pick(half, orders[half][step:])
                add_to(mine, index, stage_refs[step - 1][half].at[s])
        if step < nb:
            for half in range(2):
                order = orders[half]
                block = mine.at[place.pick(half, order[step + 1 :], order[step]) + (core,)]
                target = stage_refs[step][half].at[s]
                copies.start(s, slot_of(step, half), block, target, place.across(order[step]))
        else:
            for hops in range(1, nm):
                block = mine.at[place.mine((place.m + hops) % nm) + (core,)]
                copies.start(s, z_slot + hops - 1, block, z_ref.at[s, hops - 1], place.along(hops))

    def finish(s):
        summed = partial[(s % HELD,) + place.mine() + (core,)].astype(F32)
        for hops in range(1, nm):
            copies.arrived(s, z_slot + hops - 1)
            summed = summed + z_ref[s, hops - 1].astype(F32)
        total[PIECES[s]] = summed
        copies.drain(s)

    def weight_grad(s):
        j = PIECES[s]
        if j >= 4 and j % 2 == 1:
            f = (j - 5) // 2
            loads["hidden", f].wait()
            left, right = grad_low_t, HIDDEN
        elif j >= 4:
            left, right = normed_t, (j - 4) // 2
        elif j == 3:
            loads["mixed"].wait()
            left, right = grad_low_t, HIDDEN
        else:
            if j == 2:
                loads["n_one"].wait()
            left, right = normed_t, j

        def body(m):
            grads = dot_nn(left[...], pool[right, m]).astype(BF)
            partial.at[s % HELD, m].reshape(D, TILE)[...] = grads

        each(nm, body)
        if j in (5, 7, 9):
            load(("hidden", f + 1), hidden.at[f + 1], pool.at[HIDDEN])
        if j == 11:
            load("mixed", mixed, pool.at[HIDDEN])
        if j == 10:
            load("n_one", n_one_t, normed_t)

    def rows_of(at):
        return at // PER_WINDOW, span(at, BLOCK)

    def add_mod(window, which, values):
        grad_mod[window, which : which + 1, :] += jnp.sum(values, axis=0, keepdims=True)

    def head_unit():
        loads["branch_two"].wait()
        loads["middle"].wait()
        loss[...] = jnp.zeros_like(loss)
        ends[...] = jnp.zeros_like(ends)
        grad_mod[...] = jnp.zeros_like(grad_mod)

        def body(at):
            window, here = rows_of(at)
            gate = mod[window, 5:6, :]
            branch = xb[here, :]
            normed, inverse = row_norm(xa[here, :] + gate * branch)
            low = normed.astype(BF)
            error = dot_nn(low, head_mat) - noise[here, :]
            mask = row_mask[here, :]
            share = jnp.sum(error * error, axis=-1, keepdims=True) * (1.0 / PATCH) * mask
            loss[...] += jnp.sum(share, axis=0, keepdims=True) / token_total
            grad_pred = (2.0 / PATCH * error * mask / token_total).astype(BF)
            ends[:, PATCH:] += dot_tn(low, grad_pred)
            grad = norm_back(dot_nt(grad_pred, head_mat), normed, inverse)
            add_mod(window, 5, grad * branch)
            grad_rows[here, :] = grad
            grad_low[here, :] = (grad * gate).astype(BF)

        each(NBLOCK, body)
        transpose_rows(grad_low, grad_low_t)
        load(("slope", 0), slope.at[0], xa)
        load(("slope", 1), slope.at[1], xb)

    def slope_unit(f):
        loads["slope", f].wait()
        loads["w", 5 + 2 * f].wait()
        slopes = xa if f % 2 == 0 else xb

        def body(m):
            grad = dot_nn(grad_low[...], tile(0, m)[...])
            pool[f, m] = (grad * slopes[:, span(m, TILE)]).astype(BF)

        each(nm, body)
        if f + 2 < 4:
            load(("slope", f + 2), slope.at[f + 2], slopes)
        elif f == 2:
            load("middle_again", middle, xa)
        else:
            load("branch_one", branch_one, xb)
        load_tiles(7 + 2 * f if f < 3 else 3, 0)

    def add_rows(right, slot, fresh):
        def body(at):
            columns = span(at, TILE)
            summed = dot_nt(pool[right, 0], tile(slot, 0)[columns, :])
            for m in range(1, nm):
                summed = summed + dot_nt(pool[right, m], tile(slot, m)[columns, :])
            grad_in[:, columns] = summed if fresh else grad_in[:, columns] + summed

        each(D // TILE, body)

    def spread_unit(f):
        loads["w", 4 + 2 * f].wait()
        add_rows(f, 1, f == 0)
        load_tiles(6 + 2 * f if f < 3 else 2, 1)
        if f == 3:
            for part in range(3):
                load(("qkv", part), qkv.at[part], pool.at[QUERY + part])

    def norm_unit(which, after):
        def body(at):
            window, here = rows_of(at)
            normed, inverse = row_norm(xa[here, :])
            grad = grad_in[here, :]
            add_mod(window, which, grad)
            add_mod(window, which + 1, grad * normed)
            grad = grad * (1.0 + mod[window, which + 1 : which + 2, :])
            after(window, here, grad_rows[here, :] + norm_back(grad, normed, inverse))

        each(NBLOCK, body)

    def mid_unit():
        loads["middle_again"].wait()
        loads["branch_one"].wait()

        def after(window, here, grad):
            add_mod(window, 2, grad * xb[here, :])
            grad_rows[here, :] = grad
            grad_low[here, :] = (grad * mod[window, 2:3, :]).astype(BF)

        norm_unit(3, after)
        load("residual", residual, xa)
        loads["w", 3].wait()

        def body(m):
            pool[MIXED_GRAD, m] = dot_nn(grad_low[...], tile(0, m)[...]).astype(BF)

        each(nm, body)
        load_tiles(1, 0)

    def attend_unit(m):
        if m == 0:
            for part in range(3):
                loads["qkv", part].wait()

        def body(window):
            here = span(window, WTOK)
            query, key, value = (pool[QUERY + part, m, here, :] for part in range(3))
            grad_mixed = pool[MIXED_GRAD, m, here, :]
            grads = [jnp.zeros((WTOK, TILE), F32) for _ in range(3)]
            for head in range(TILE // HD):
                lanes = head_lanes(head, BF)
                own_query, own_grad = query * lanes, grad_mixed * lanes
                attn = soft_rows(own_query, key, flags[window])
                grads[2] = grads[2] + dot_tn(attn.astype(BF), own_grad)
                grad_attn = dot_nt(own_grad, value)
                inner = jnp.sum(attn * grad_attn, axis=-1, keepdims=True)
                grad_scores = (attn * (grad_attn - inner)).astype(BF)
                grads[0] = grads[0] + dot_nn(grad_scores, key * lanes)
                grads[1] = grads[1] + dot_tn(grad_scores, own_query)
            pool[0, m, here, :] = (grads[0] * HD ** (-0.5)).astype(BF)
            pool[1, m, here, :] = (grads[1] * HD ** (-0.5)).astype(BF)
            pool[2, m, here, :] = grads[2].astype(BF)

        each(NMB, body)

    def inward_unit(j):
        slot = 1 if j != 1 else 0
        loads["w", j].wait()
        add_rows(j, slot, j == 2)
        if j == 2:
            load_tiles(0, 1)

    def last_unit():
        loads["residual"].wait()

        def after(window, here, grad):
            ends[:, :PATCH] += dot_tn(grad.astype(BF), latents[here, :])

        norm_unit(0, after)

    units = {
        "head": head_unit,
        "slope": slope_unit,
        "spread": spread_unit,
        "mid": mid_unit,
        "attend": attend_unit,
        "inward": inward_unit,
        "last": last_unit,
    }

    def compute(turn):
        for when, (name, *args) in BACKWARD_TURNS:
            if when == turn:
                units[name](*args)

    last = max(when for when, _ in BACKWARD_TURNS)
    for turn in range(max(NJ + nb + 2, last + 1)):
        if turn == 0:
            compute(turn)
        if 0 < turn <= last and turn in (1, 5, 9):
            compute(turn)
        if turn == 8:
            transpose_rows(grad_low, grad_low_t)
        if turn < NJ:
            if turn == 1:
                loads["n_two"].wait()
            weight_grad(turn)
            begin(turn)
        for step in range(nb + 1):
            if 0 <= turn - 1 - step < NJ:
                stage(turn - 1 - step, step)
        if 0 <= turn - 2 - nb < NJ:
            finish(turn - 2 - nb)
        if turn not in (0, 1, 5, 9):
            compute(turn)


def backward_blocks(saved, residual, mod, flags, row_mask, token_total, noise, latents, ends):
    nd, nm = lax.axis_size("dp"), lax.axis_size("mp")
    nb = nd.bit_length() - 2
    rows = D // nd
    bits = (2,) * nb
    slots = 2 * nb + nm
    stage_shapes = []
    for step in range(nb):
        high_first = tuple(1 if at <= step else 2 for at in range(nb))
        stage_shapes.append(pltpu.VMEM((NJ, nm // 2) + high_first + (rows, TILE), BF))
        stage_shapes.append(pltpu.VMEM((NJ, nm - nm // 2) + high_first[::-1] + (rows, TILE), BF))
    in_hbm = (*saved, residual)
    in_vmem = (mod, flags, row_mask, token_total, noise, latents, ends)
    return pl.pallas_call(
        functools.partial(backward_kernel, nd, nm),
        out_shape=[
            jax.ShapeDtypeStruct((NJ, rows, TILE), F32),
            jax.ShapeDtypeStruct((1, 1), F32),
            jax.ShapeDtypeStruct((D, 2 * PATCH), F32),
            jax.ShapeDtypeStruct((NMB, 6, D), F32),
        ],
        in_specs=[pl.BlockSpec(memory_space=pl.ANY)] * len(in_hbm)
        + [pl.BlockSpec(memory_space=pltpu.VMEM)] * len(in_vmem),
        out_specs=[pl.BlockSpec(memory_space=pltpu.VMEM)] * 4,
        scratch_shapes=[
            pltpu.VMEM((HELD, nm) + bits + (2, rows, TILE), BF),
            pltpu.VMEM((TWINS, nm) + bits + (rows, TILE), BF),
            pltpu.VMEM((ROWS, D), F32),
            pltpu.VMEM((ROWS, D), F32),
            pltpu.VMEM((ROWS, D), F32),
            pltpu.VMEM((ROWS, D), F32),
            pltpu.VMEM((ROWS, D), BF),
            pltpu.VMEM((D, ROWS), BF),
            pltpu.VMEM((D, ROWS), BF),
            pltpu.VMEM((9, nm, ROWS, TILE), BF),
            pltpu.VMEM((2, nm) + bits + (2, rows, TILE), BF),
            pltpu.VMEM((NJ, nm - 1, rows, TILE), BF),
            *stage_shapes,
            pltpu.SemaphoreType.DMA((NJ, slots)),
            pltpu.SemaphoreType.DMA((NJ, slots)),
            pltpu.SemaphoreType.REGULAR,
            pltpu.SemaphoreType.DMA((36,)),
        ],
        compiler_params=pltpu.CompilerParams(
            collective_id=1, has_side_effects=True, vmem_limit_bytes=61 << 20
        ),
    )(*in_hbm, *in_vmem)


def tail_kernel(nd, nm, reduced, loss, ends, grad_mod, front, time_pre, condition, time_in, time_out, classes, adaptive, *refs):
    (ends_sum, adaptive_grad, time_in_grad, time_out_grad, classes_grad, sums) = refs[:6]
    (ends_in, ends_rows, mod_rows, mod_in, own_mod, all_mod, act_rows, cond_all, terms, term_rows, send_sems, recv_sems) = refs[6:]
    place = Place(nd, nm)
    swap = Exchange(place, send_sems, recv_sems)
    dp_id, m = place.dp_id, place.m
    windows, rows = time_pre.shape
    place.greet(everyone=True)
    mod_in[m] = grad_mod[...]
    swap.mp_gather(0, grad_mod, mod_in)
    swap.dp_scatter(1, ends, ends_in)

    swap.wait(0)
    for index in range(nm):
        for step in range(NMB):
            for which in range(6):
                row = index * NMB + step
                mod_rows[which, row : row + 1, :] = mod_in[index, step, which : which + 1, :]
    for pair in range(3):
        own_mod[pair] = mod_rows[2 * pair : 2 * pair + 2].reshape(2 * PER_INDEX, D).astype(BF)
        all_mod[dp_id, pair] = own_mod[pair]
    swap.dp_gather(2, own_mod, all_mod)
    swap.wait(1)
    ends_rows[m] = ends[dp_id] + jnp.sum(ends_in[...], axis=0)
    swap.mp_gather(3, ends_rows.at[m], ends_rows)
    cond_act = silu(condition[...]).reshape(nd, PER_INDEX, rows)
    act_rows[...] = jnp.zeros_like(act_rows)
    for side in range(2):
        act_rows[side, :, side * PER_INDEX : (side + 1) * PER_INDEX, :] = cond_act
    features = front[:, :, :FREQ].reshape(windows, FREQ).astype(BF)
    time_hidden = silu(time_pre[...]).astype(BF)
    pick = label_pick(front, classes.shape[0])
    squares = jnp.zeros((8, 128), F32)
    whole_squares = jnp.zeros((8, 128), F32)

    def square_sum(values):
        return jnp.sum(jnp.sum(values * values, axis=0, keepdims=True), axis=1, keepdims=True)

    for j in range(NJ):
        whole_squares = whole_squares + square_sum(reduced[j])
    swap.wait(2)
    grad_cond = jnp.zeros((windows, rows), F32)
    for which in range(6):
        pair, side = which // 2, which % 2
        block = all_mod[:, pair].reshape(nd * 2 * PER_INDEX, D)
        act = act_rows[side].reshape(nd * 2 * PER_INDEX, rows).astype(BF)
        gradient = dot_tn(act, block)
        adaptive_grad[which] = gradient
        squares = squares + square_sum(gradient)
        back = dot_nt(block, adaptive[which]).reshape(nd, 2, PER_INDEX, rows)
        grad_cond = grad_cond + back[:, side].reshape(windows, rows)
    grad_cond = (grad_cond * silu_slope(condition[...])).astype(BF)
    cond_all[dp_id] = grad_cond
    swap.dp_gather(4, cond_all.at[dp_id], cond_all)
    gradient = dot_tn(pick, grad_cond)
    classes_grad[...] = gradient
    squares = squares + square_sum(gradient)
    swap.wait(3)
    ends_sum[...] = jnp.sum(ends_rows[...], axis=0)
    squares = squares + square_sum(ends_sum[...])
    swap.wait(4)
    grad_time = jnp.zeros((windows, rows), F32)
    for index in range(nd):
        gradient = dot_tn(time_hidden, cond_all[index])
        time_out_grad[index] = gradient
        squares = squares + square_sum(gradient)
        grad_time = grad_time + dot_nt(cond_all[index], time_out[index])
    grad_time = (grad_time * silu_slope(time_pre[...])).astype(BF)
    gradient = dot_tn(features, grad_time)
    time_in_grad[...] = gradient
    squares = squares + square_sum(gradient)

    terms[dp_id, 0] = squares * (1.0 / nm) + whole_squares
    terms[dp_id, 1] = jnp.zeros((8, 128), F32) + loss[...]
    swap.dp_gather(5, terms.at[dp_id], terms)
    swap.wait(5)
    term_rows[m] = jnp.sum(terms[...], axis=0)
    swap.mp_gather(6, term_rows.at[m], term_rows)
    swap.wait(6)
    sums[...] = jnp.sum(term_rows[...], axis=0)
    swap.drain()


def tail_blocks(*operands):
    nd, nm = lax.axis_size("dp"), lax.axis_size("mp")
    rows = D // nd
    windows = nd * PER_INDEX
    classes = operands[-2].shape[0]
    shapes = [
        (rows, 2 * PATCH),
        (6, rows, D),
        (FREQ, rows),
        (nd, rows, rows),
        (classes, rows),
        (2, 8, 128),
    ]
    return pl.pallas_call(
        functools.partial(tail_kernel, nd, nm),
        out_shape=[jax.ShapeDtypeStruct(shape, F32) for shape in shapes],
        in_specs=[pl.BlockSpec(memory_space=pltpu.VMEM)] * len(operands),
        out_specs=[pl.BlockSpec(memory_space=pltpu.VMEM)] * len(shapes),
        scratch_shapes=[
            pltpu.VMEM((nd - 1, rows, 2 * PATCH), F32),
            pltpu.VMEM((nm, rows, 2 * PATCH), F32),
            pltpu.VMEM((6, PER_INDEX, D), F32),
            pltpu.VMEM((nm, NMB, 6, D), F32),
            pltpu.VMEM((3, 2 * PER_INDEX, D), BF),
            pltpu.VMEM((nd, 3, 2 * PER_INDEX, D), BF),
            pltpu.VMEM((2, nd, 2 * PER_INDEX, rows), F32),
            pltpu.VMEM((nd, windows, rows), BF),
            pltpu.VMEM((nd, 2, 8, 128), F32),
            pltpu.VMEM((nm, 2, 8, 128), F32),
            pltpu.SemaphoreType.DMA((7, max(nd, nm) - 1)),
            pltpu.SemaphoreType.DMA((7, max(nd, nm) - 1)),
        ],
        compiler_params=pltpu.CompilerParams(
            collective_id=2, has_side_effects=True, vmem_limit_bytes=40 << 20
        ),
    )(*operands)


def adam_update(state_in, gradient, factor):
    clipped = gradient * factor
    first_moment = beta_one * state_in[1] + (1.0 - beta_one) * clipped
    second_moment = beta_two * state_in[2] * state_in[2] + (1.0 - beta_two) * clipped * clipped
    root_moment = jnp.sqrt(second_moment)
    update = (
        first_moment
        / (1.0 - beta_one**step_count)
        / (root_moment / math.sqrt(1.0 - beta_two**step_count) + adam_eps)
    )
    new_weight = state_in[0] - learn_rate * (update + weight_decay * state_in[0])
    return (new_weight, jnp.stack([first_moment, root_moment]))


def per_device(
    latents,
    noise_target,
    token_mask,
    timesteps,
    labels,
    state_embed,
    state_head,
    state_time_in,
    state_time_out,
    state_classes,
    state_adaptive,
    state_attention_in,
    state_attention_out,
    state_expand,
    state_contract,
):
    nd = lax.axis_size("dp")
    rows = state_attention_in.shape[1]
    attn_in_tiles = state_attention_in[0].transpose(1, 0, 2)
    expand_tiles = state_expand[0].reshape(rows, 4, TILE).transpose(1, 0, 2)
    contract_tiles = state_contract[0].reshape(4, TILE, rows).transpose(0, 2, 1)
    ff_tiles = jnp.stack([expand_tiles, contract_tiles], axis=1).reshape(8, rows, TILE)
    shard = jnp.concatenate(
        [attn_in_tiles, state_attention_out[0].T[None], ff_tiles], axis=0
    ).astype(BF)

    mask = token_mask.astype(F32).reshape(ROWS)
    ends_shard = jnp.stack([state_embed[0].T, state_head[0]]).astype(BF)
    step_ids = timesteps[0].T.reshape(PER_INDEX)
    label_ids = labels[0].T.reshape(PER_INDEX, 1).astype(F32)
    features = timestep_features(step_ids).astype(BF).astype(F32)
    front = jnp.concatenate(
        [
            features,
            jnp.broadcast_to(label_ids, (PER_INDEX, 128)),
            jnp.broadcast_to(jnp.sum(mask), (PER_INDEX, 128)),
        ],
        axis=1,
    )
    time_in_part = state_time_in[0].astype(BF)
    time_out_part = state_time_out[0].astype(BF).reshape(rows, nd, rows).transpose(1, 0, 2)
    class_pad = -CLASSES % 128
    classes_part = jnp.pad(state_classes[0].astype(BF), ((0, class_pad), (0, 0)))
    adaptive_part = state_adaptive[0].astype(BF).transpose(1, 0, 2)
    weights = (time_in_part, time_out_part, classes_part, adaptive_part)
    latent_rows = latents.reshape(ROWS, PATCH)
    noise_rows = noise_target.reshape(ROWS, PATCH)
    positions = window_positions(jnp.arange(WTOK, dtype=jnp.int32))
    flags = token_mask.reshape(NMB, 1, WTOK)
    residual, mod, ends, front_all, time_pre, condition, token_total, *saved = forward_blocks(
        shard, flags, front, ends_shard, latent_rows, positions, *weights
    )
    reduced, loss_local, ends_grad, grad_mod = backward_blocks(
        saved, residual, mod, flags, mask[:, None], token_total, noise_rows, latent_rows, ends
    )
    ends_sum, adaptive_grad, time_in_grad, time_out_grad, classes_grad, sums = tail_blocks(
        reduced,
        loss_local,
        ends_grad.reshape(nd, rows, 2 * PATCH),
        grad_mod,
        front_all,
        time_pre,
        condition,
        *weights,
    )
    small_grads = (
        ends_sum[:, :PATCH].T,
        ends_sum[:, PATCH:],
        time_in_grad,
        time_out_grad.transpose(1, 0, 2).reshape(rows, D),
        classes_grad[:CLASSES],
        adaptive_grad.transpose(1, 0, 2),
    )
    square_total, loss_value = sums[0, 0, 0], sums[1, 0, 0]
    grad_norm = jnp.sqrt(square_total)
    factor = jnp.minimum(1.0, threshold / grad_norm)
    ff_reduced = reduced[4:].reshape(4, 2, rows, TILE)
    block_grads = (
        reduced[:3].transpose(1, 0, 2),
        reduced[3].T,
        ff_reduced[:, 0].transpose(1, 0, 2).reshape(rows, 4 * TILE),
        ff_reduced[:, 1].transpose(0, 2, 1).reshape(4 * TILE, rows),
    )
    all_states = (
        state_embed,
        state_head,
        state_time_in,
        state_time_out,
        state_classes,
        state_adaptive,
        state_attention_in,
        state_attention_out,
        state_expand,
        state_contract,
    )
    results = [loss_value, grad_norm]
    for state_in, gradient in zip(all_states, small_grads + block_grads):
        new_weight, moments = adam_update(state_in, gradient, factor)
        results.append(new_weight)
        results.append(moments)
    return tuple(results)


def solution(mesh):
    in_specs = (
        P("dp", None, "mp", None),
        P("dp", None, "mp", None),
        P("dp", None, "mp"),
        P("dp", None, None),
        P("dp", None, None),
        P(None, None, "dp"),
        P(None, "dp", None),
        P(None, None, "dp"),
        P(None, "dp", None),
        P(None, None, "dp"),
        P(None, "dp", None, None),
        P(None, "dp", None, "mp"),
        P(None, "mp", "dp"),
        P(None, "dp", "mp"),
        P(None, "mp", "dp"),
    )
    out_specs = (
        P(),
        P(),
        P(None, "dp"),
        P(None, None, "dp"),
        P("dp", None),
        P(None, "dp", None),
        P(None, "dp"),
        P(None, None, "dp"),
        P("dp", None),
        P(None, "dp", None),
        P(None, "dp"),
        P(None, None, "dp"),
        P("dp", None, None),
        P(None, "dp", None, None),
        P("dp", None, "mp"),
        P(None, "dp", None, "mp"),
        P("mp", "dp"),
        P(None, "mp", "dp"),
        P("dp", "mp"),
        P(None, "dp", "mp"),
        P("mp", "dp"),
        P(None, "mp", "dp"),
    )
    return jax.shard_map(
        per_device, mesh=mesh, in_specs=in_specs, out_specs=out_specs, check_vma=False
    )
```

```python
import functools
import math

import jax
import jax.numpy as jnp
import numpy as np
from jax import lax
from jax.experimental import pallas as pl
from jax.experimental.pallas import tpu as pltpu
from jax.sharding import PartitionSpec as P

D = 1024
HEADS = 16
HD = 64
PATCH = 32
FREQ = 256
CLASSES = 600
WTOK = 320
NMB = 2
WMB = 4
TILE = 256
NJ = 12
ROWS = NMB * WTOK
MESH = pl.DeviceIdType.MESH
BF = jnp.bfloat16
F32 = jnp.float32


beta_one = 0.9
beta_two = 0.999
adam_eps = 1e-08
learn_rate = 0.15
weight_decay = 0.1
threshold = 0.002
step_count = 10.0


def window_positions():
    half_width = D // 2
    steps = np.arange(half_width, dtype=np.float32)
    frequency = np.exp(np.float32(-math.log(10000.0)) * steps / np.float32(half_width))
    angles = np.arange(WTOK, dtype=np.float32)[:, None] * frequency.astype(np.float32)[None, :]
    table = np.concatenate([np.sin(angles), np.cos(angles)], axis=-1)
    return jnp.asarray(table.astype(np.float32))


def dot_general(a, b, a_dim, b_dim):
    return lax.dot_general(a, b, (((a_dim,), (b_dim,)), ((), ())), preferred_element_type=F32)


def dot_nn(a, b):
    return jnp.dot(a, b, preferred_element_type=F32)


def dot_nt(a, b):
    return dot_general(a, b, 1, 1)


def dot_tn(a, b):
    return dot_general(a, b, 0, 0)


def norm_back(grad, normed, inverse):
    mean_grad = jnp.mean(grad, axis=-1, keepdims=True)
    mean_prod = jnp.mean(grad * normed, axis=-1, keepdims=True)
    return inverse * (grad - mean_grad - normed * mean_prod)


def silu(values):
    return values * jax.nn.sigmoid(values)


def silu_slope(values):
    gate = jax.nn.sigmoid(values)
    return gate * (1.0 + values * (1.0 - gate))


def gelu_parts(up):
    cdf = 0.5 * (1.0 + lax.erf(up * math.sqrt(0.5)))
    pdf = jnp.exp(-0.5 * up * up) * (1.0 / math.sqrt(2.0 * math.pi))
    return up * cdf, cdf + up * pdf


def tokens3(values):
    return values.reshape(NMB, WTOK, -1)


def flip(bits, at):
    return [1 - bit if place == at else bit for place, bit in enumerate(bits)]


class Place:
    def __init__(self, nd, nm):
        self.nm = nm
        self.nb = nd.bit_length() - 2
        dp_id = lax.axis_index("dp")
        self.nd = nd
        self.dp_id = dp_id
        self.m = lax.axis_index("mp")
        self.core = dp_id % 2
        self.bits = [dp_id // (1 << (self.nb - at)) % 2 for at in range(self.nb)]
        self.sibling = {"dp": self.dp_of(self.bits, 1 - self.core), "mp": self.m}
        self.orders = (list(range(self.nb))[::-1], list(range(self.nb)))
        self.halves = (pl.ds(0, nm // 2), pl.ds(nm // 2, nm - nm // 2))

    def dp_of(self, bits, core):
        total = core
        for at, bit in enumerate(bits):
            total = total + bit * (1 << (self.nb - at))
        return total

    def across(self, at):
        return {"dp": self.dp_of(flip(self.bits, at), self.core), "mp": self.m}

    def along(self, hops):
        return {"dp": self.dp_of(self.bits, self.core), "mp": (self.m + hops) % self.nm}

    def beside(self, hops):
        return {"dp": (self.dp_id + hops) % self.nd, "mp": self.m}

    def pick(self, half, done, flipped=None):
        where = flip(self.bits, flipped)
        return (self.halves[half],) + tuple(
            pl.ds(0, 2) if at in done else pl.ds(where[at], 1) for at in range(self.nb)
        )

    def mine(self, m=None):
        return (self.m if m is None else m,) + tuple(self.bits)

    def greet(self, everyone=False):
        barrier = pltpu.get_barrier_semaphore()
        if everyone:
            others = [self.beside(hops) for hops in range(1, self.nd)]
        else:
            others = [self.sibling] + [self.across(at) for at in range(self.nb)]
        others += [self.along(hops) for hops in range(1, self.nm)]
        for other in others:
            pl.semaphore_signal(barrier, inc=1, device_id=other, device_id_type=MESH)
        pl.semaphore_wait(barrier, len(others))


class Copies:
    def __init__(self, send_sems, recv_sems):
        self.send_sems, self.recv_sems = send_sems, recv_sems
        self.started = {}

    def start(self, step, slot, source, target, device):
        copy = pltpu.make_async_remote_copy(
            src_ref=source,
            dst_ref=target,
            send_sem=self.send_sems.at[step, slot],
            recv_sem=self.recv_sems.at[step, slot],
            device_id=device,
            device_id_type=MESH,
        )
        copy.start()
        self.started[step, slot] = copy

    def arrived(self, step, slot):
        self.started[step, slot].wait_recv()

    def drain(self, step=None):
        for key in list(self.started):
            if step is None or key[0] == step:
                self.started.pop(key).wait_send()


class Exchange:
    def __init__(self, place, send_sems, recv_sems):
        self.place = place
        self.copies = Copies(send_sems, recv_sems)

    def dp_gather(self, group, source, target):
        for hops in range(1, self.place.nd):
            here = target.at[self.place.dp_id]
            self.copies.start(group, hops - 1, source, here, self.place.beside(hops))

    def dp_scatter(self, group, source, target):
        for hops in range(1, self.place.nd):
            block = source.at[(self.place.dp_id + hops) % self.place.nd]
            self.copies.start(group, hops - 1, block, target.at[hops - 1], self.place.beside(hops))

    def mp_gather(self, group, source, target):
        for hops in range(1, self.place.nm):
            here = target.at[self.place.m]
            self.copies.start(group, hops - 1, source, here, self.place.along(hops))

    def wait(self, group):
        for step, slot in list(self.copies.started):
            if step == group:
                self.copies.arrived(step, slot)

    def drain(self):
        self.copies.drain()


def gather_steps(
        place, shard, whole, send_sems, recv_sems, local_sems, prepare, load, compute, last
    ):
    nm, nb, core = place.nm, place.nb, place.core
    copies = Copies(send_sems, recv_sems)
    stage_slot = lambda stage, half: nm - 1 + 2 * stage + half
    twin = nm - 1 + 2 * nb
    locals_ = {}

    def begin(j):
        here = whole.at[(j,) + place.mine() + (core,)]
        locals_[j] = pltpu.make_async_copy(shard.at[j], here, local_sems.at[j])
        locals_[j].start()
        for hops in range(1, nm):
            copies.start(j, hops - 1, shard.at[j], here, place.along(hops))
        copies.start(j, 2 * twin, shard.at[j], here, place.sibling)

    def stage(j, step):
        if step == 0:
            locals_[j].wait()
            for hops in range(1, nm):
                copies.arrived(j, hops - 1)
        else:
            for half in range(2):
                copies.arrived(j, stage_slot(step - 1, half))
        if step < nb:
            for half in range(2):
                order = place.orders[half]
                block = whole.at[(j,) + place.pick(half, order[:step]) + (core,)]
                copies.start(j, stage_slot(step, half), block, block, place.across(order[step]))
        if step == 0:
            for hops in range(1, nm):
                block = whole.at[(j,) + place.mine((place.m + nm - hops) % nm) + (core,)]
                copies.start(j, twin + hops - 1, block, block, place.sibling)
        else:
            for half in range(2):
                order = place.orders[half]
                block = whole.at[
                    (j,) + place.pick(half, order[: step - 1], order[step - 1]) + (core,)
                ]
                copies.start(j, twin + stage_slot(step - 1, half), block, block, place.sibling)

    def finish(j):
        for slot in range(twin, 2 * twin + 1):
            copies.arrived(j, slot)
        load(j)

    for turn in range(max(NJ + nb + 2, last + nb)):
        if turn < NJ:
            begin(turn)
        for step in range(nb + 1):
            if 0 <= turn - 1 - step < NJ:
                stage(turn - 1 - step, step)
        if 0 <= turn - 2 - nb < NJ:
            finish(turn - 2 - nb)
        if turn + 2 < NJ:
            prepare(turn + 2)
        compute(turn + 2 - nb)
    copies.drain()


def row_norm(values):
    center = values - jnp.mean(values, axis=-1, keepdims=True)
    inverse = lax.rsqrt(jnp.mean(center * center, axis=-1, keepdims=True) + 1e-06)
    return center * inverse, inverse


def each(count, body):
    lax.fori_loop(0, count, lambda at, carry: (body(at), carry)[1], 0)


def span(at, size):
    return pl.ds(pl.multiple_of(at * size, size), size)


def head_lanes(head, dtype=F32):
    lanes = lax.broadcasted_iota(jnp.int32, (1, TILE), 1) // HD
    return (lanes == head).astype(dtype)


def soft_rows(query, key, key_bias):
    scores = dot_nt(query, key) * HD ** (-0.5)
    scores = jnp.where(key_bias > 0, scores, -1e30)
    exponents = jnp.exp(scores - jnp.max(scores, axis=-1, keepdims=True))
    return exponents / jnp.sum(exponents, axis=-1, keepdims=True)


def label_pick(front, count):
    labels = front[:, :, FREQ : FREQ + 1].reshape(-1, 1)
    lanes = lax.broadcasted_iota(jnp.int32, (labels.shape[0], count), 1).astype(F32)
    return (lanes == labels).astype(BF)


PER_INDEX = NMB * WMB
def soft_columns(key, query, key_mask):
    scores = dot_nt(key, query) * HD ** (-0.5)
    scores = jnp.where(key_mask > 0, scores, -1e30)
    exponents = jnp.exp(scores - jnp.max(scores, axis=0, keepdims=True))
    return exponents / jnp.sum(exponents, axis=0, keepdims=True)


BLOCK = 64
PER_WINDOW = WTOK // BLOCK
NBLOCK = ROWS // BLOCK
LANE_BLOCK = 128


def token_rows(source, target):
    for window in range(NMB):
        target[window * WTOK : (window + 1) * WTOK, :] = source[window].T


def mask_column(source, target):
    for window in range(NMB):
        row = jnp.broadcast_to(source[window : window + 1, :].astype(F32), (8, WTOK))
        target[window * WTOK : (window + 1) * WTOK, :] = row.T[:, 0:1]


def transpose_rows(source, target):
    def body(at):
        target[:, span(at, LANE_BLOCK)] = source[span(at, LANE_BLOCK), :].T

    each(ROWS // LANE_BLOCK, body)


FORWARD_TURNS = (
    (5, ("qkv", 0)),
    (6, ("qkv", 1)),
    (7, ("qkv", 2)),
    (7, ("attend", 0)),
    (8, ("attend", 1)),
    (9, ("attend", 2)),
    (10, ("attend", 3)),
    (10, ("out",)),
    (11, ("up", 0)),
    (12, ("down", 0)),
    (12, ("up", 1)),
    (13, ("down", 1)),
    (13, ("up", 2)),
    (14, ("down", 2)),
    (15, ("up", 3)),
    (16, ("down", 3)),
)


def forward_kernel(nd, nm, states, flags, times_in, latents_in, positions, time_out, *refs):
    (residual_out, mod, ends, front, time_pre, condition, token_total) = refs[:7]
    refs = refs[7:]
    (residual, parts, parts_in, mods, mods_in, rows_ref, counts, swap_send, swap_recv) = refs[-9:]
    (shard, held_in, held_out, held_up, held_down, adaptive, time_in, classes, held_embed, held_head, ends_in, front_in, latents, state_sems) = refs[-23:-9]
    refs = refs[:-23]
    place = Place(nd, nm)
    swap = Exchange(place, swap_send, swap_recv)
    state_loads = {}
    class_pad = classes.shape[0] - CLASSES
    wanted_states = {
        "attention_in": held_in,
        "embed": held_embed,
        "head": held_head,
        "time_in": time_in,
        "classes": classes.at[pl.ds(0, CLASSES)],
        "attention_out": held_out,
        "expand": held_up,
        "contract": held_down,
        "adaptive": adaptive,
    }
    for at, (name, target) in enumerate(wanted_states.items()):
        state_loads[name] = pltpu.make_async_copy(states[name].at[0], target, state_sems.at[at])
        state_loads[name].start()

    def state_ready(name):
        if name in state_loads:
            state_loads.pop(name).wait()

    def prepare(j):
        if j < 3:
            state_ready("attention_in")
            values = held_in[j]
        elif j == 3:
            state_ready("attention_out")
            values = held_out[...].T
        elif j % 2 == 0:
            state_ready("expand")
            values = held_up[:, (j - 4) // 2 * TILE : (j - 2) // 2 * TILE]
        else:
            state_ready("contract")
            values = held_down[(j - 5) // 2 * TILE : (j - 3) // 2 * TILE, :].T
        shard[j] = values.astype(BF)

    for j in range(2):
        prepare(j)
    place.greet(everyone=True)
    dp_id = place.dp_id
    windows = nd * PER_INDEX
    upright = parts.shape[1] == windows
    (whole, n_one_t, qkv_out, mixed_out, branch_one_out, middle_out, n_two_t, hidden_out, slope_out, branch_two_out) = refs[:10]
    (n_one, qkv, mixed, branch_one, middle, n_two, flipped, hidden, slope, branch_two, loaded) = refs[10:21]
    send_sems, recv_sems, local_sems, load_sems, spill_sems = refs[21:]
    spilled = {}

    def spill(name, source, target):
        copy = pltpu.make_async_copy(source, target, spill_sems.at[len(spilled)])
        copy.start()
        spilled[name] = copy

    loads = {}
    slots = loaded.shape[0]

    def load(j):
        loads[j] = pltpu.make_async_copy(whole.at[j], loaded.at[j % slots], load_sems.at[j])
        loads[j].start()

    def tile(j, m):
        return loaded.at[j % slots, m].reshape(D, TILE)

    def first_swap():
        state_ready("embed")
        state_ready("head")
        ends_in[0] = held_embed[...].T.astype(BF)
        ends_in[1] = held_head[...].T.astype(BF)
        front_in[:, : FREQ + 128] = times_in[...]
        count = jnp.sum(jnp.sum(flags[...].astype(F32), axis=0, keepdims=True), axis=1, keepdims=True)
        front_in[:, FREQ + 128 :] = jnp.broadcast_to(count, (PER_INDEX, 128))
        classes[CLASSES:, :] = jnp.zeros((class_pad, classes.shape[1]), F32)
        token_rows(latents_in, latents)
        front[dp_id] = front_in[...]
        for which in range(2):
            ends[which, dp_id] = ends_in[which]
        swap.dp_gather(0, front_in, front)
        swap.dp_gather(1, ends_in.at[0], ends.at[0])
        swap.dp_gather(2, ends_in.at[1], ends.at[1])

    def time_layers():
        swap.wait(0)
        features = front[:, :, :FREQ].reshape(windows, FREQ).astype(BF)
        state_ready("time_in")
        time_pre[...] = dot_nn(features, time_in[...].astype(BF))
        time_hidden = silu(time_pre[...]).astype(BF)
        for index in range(nd):
            if upright:
                parts[index] = dot_nn(time_hidden, time_out[index])
            else:
                parts[index] = dot_general(time_out[index], time_hidden, 0, 1)
        swap.dp_scatter(3, parts, parts_in)
        counts[place.m] = jnp.sum(front[:, :, FREQ + 128 :], axis=0)
        swap.mp_gather(5, counts.at[place.m], counts)

    def condition_layers():
        state_ready("classes")
        state_ready("adaptive")
        swap.wait(3)
        total = parts[dp_id] + jnp.sum(parts_in[...], axis=0)
        total = total if upright else total.T
        total = total + dot_nn(label_pick(front, classes.shape[0]), classes[...].astype(BF))
        condition[...] = total
        row_ids = lax.broadcasted_iota(jnp.int32, (nd * NMB, windows), 0)
        column_ids = lax.broadcasted_iota(jnp.int32, (nd * NMB, windows), 1)
        wanted = row_ids // NMB * PER_INDEX + place.m * NMB + row_ids % NMB
        own = dot_nn((wanted == column_ids).astype(BF), silu(total).astype(BF)).astype(BF)
        for which in range(6):
            rows_ref[...] = dot_nn(own, adaptive[which].astype(BF))

            def move(row):
                mods[row // NMB, row % NMB, which : which + 1, :] = rows_ref[pl.ds(row, 1), :]

            each(nd * NMB, move)
        swap.dp_scatter(4, mods, mods_in)

    def modulation():
        swap.wait(4)
        for window in range(NMB):
            mod[window] = mods[dp_id, window] + jnp.sum(mods_in[:, window], axis=0)
        swap.wait(5)
        token_total[...] = jnp.sum(counts[...], axis=0)
        swap.wait(1)
        swap.wait(2)
        embed_mat = ends[0].reshape(D, PATCH)

        def body(window):
            here = span(window, WTOK)
            residual[here, :] = dot_nt(latents[here, :], embed_mat) + positions[...]

        each(NMB, body)
        spill("residual", residual, residual_out)

    def first_norm():
        def body(at):
            window, here = at // PER_WINDOW, span(at, BLOCK)
            normed, _ = row_norm(residual[here, :])
            normed = normed * (1.0 + mod[window, 1:2, :]) + mod[window, 0:1, :]
            n_one[here, :] = normed.astype(BF)

        each(NBLOCK, body)
        transpose_rows(n_one, flipped.at[0])
        spill("n_one", flipped.at[0], n_one_t)

    def qkv_unit(j):
        def body(m):
            qkv[j, m] = dot_nn(n_one[...], tile(j, m)[...]).astype(BF)

        each(nm, body)
        spill(("qkv", j), qkv.at[j], qkv_out.at[j])

    def attend_unit(m):
        def body(window):
            here = span(window, WTOK)
            query, key, value = qkv[0, m, here, :], qkv[1, m, here, :], qkv[2, m, here, :]
            total = jnp.zeros((WTOK, TILE), F32)
            for head in range(TILE // HD):
                lanes = head_lanes(head, BF)
                attn = soft_rows(query * lanes, key, flags[pl.ds(window, 1), :]).astype(BF)
                total = total + dot_nn(attn, value * lanes)
            mixed[m, here, :] = total.astype(BF)

        each(NMB, body)
        if m == nm - 1:
            spill("mixed", mixed, mixed_out)

    def add_nt(source, j, target, fresh):
        def body(at):
            columns = span(at, TILE)
            total = dot_nt(source[0], tile(j, 0)[columns, :])
            for m in range(1, nm):
                total = total + dot_nt(source[m], tile(j, m)[columns, :])
            target[:, columns] = total if fresh else target[:, columns] + total

        each(D // TILE, body)

    def out_unit():
        add_nt(mixed, 3, branch_one, True)
        spill("branch_one", branch_one, branch_one_out)

        def body(at):
            window, here = at // PER_WINDOW, span(at, BLOCK)
            rows = residual[here, :] + mod[window, 2:3, :] * branch_one[here, :]
            middle[here, :] = rows
            normed, _ = row_norm(rows)
            normed = normed * (1.0 + mod[window, 4:5, :]) + mod[window, 3:4, :]
            n_two[here, :] = normed.astype(BF)

        each(NBLOCK, body)
        spill("middle", middle, middle_out)
        transpose_rows(n_two, flipped.at[1])
        spill("n_two", flipped.at[1], n_two_t)

    def up_unit(f):
        slot = f % 2
        if f >= 2:
            spilled["hidden", f - 2].wait()
            spilled["slope", f - 2].wait()

        def body(m):
            up = dot_nn(n_two[...], tile(4 + 2 * f, m)[...])
            value, grad = gelu_parts(up)
            hidden[slot, m] = value.astype(BF)
            slope[slot, :, span(m, TILE)] = grad

        each(nm, body)
        spill(("hidden", f), hidden.at[slot], hidden_out.at[f])
        spill(("slope", f), slope.at[slot], slope_out.at[f])

    def down_unit(f):
        add_nt(hidden.at[f % 2], 5 + 2 * f, branch_two, f == 0)
        if f == 3:
            spill("branch_two", branch_two, branch_two_out)

    units = {"qkv": qkv_unit, "attend": attend_unit, "out": out_unit, "up": up_unit, "down": down_unit}
    need = {"qkv": lambda j: j, "out": lambda: 3, "up": lambda f: 4 + 2 * f, "down": lambda f: 5 + 2 * f}

    def compute(turn):
        early = (first_swap, time_layers, condition_layers, modulation, first_norm)
        if turn < len(early):
            early[turn]()
        for when, (name, *args) in FORWARD_TURNS:
            if when == turn:
                if name in need:
                    loads[need[name](*args)].wait()
                units[name](*args)

    last = max(when for when, _ in FORWARD_TURNS)
    gather_steps(
        place, shard, whole, send_sems, recv_sems, local_sems, prepare, load, compute, last
    )
    for name, copy in spilled.items():
        if name not in [(kind, f) for kind in ("hidden", "slope") for f in (0, 1)]:
            copy.wait()
    swap.drain()


def forward_blocks(states, *others):
    nd, nm = lax.axis_size("dp"), lax.axis_size("mp")
    nb = nd.bit_length() - 2
    rows = D // nd
    names = list(states)
    slots = 2 * (nm - 1 + 2 * nb) + 1
    windows = nd * PER_INDEX
    tall = windows <= rows
    small = [
        ((NMB, 6, D), F32),
        ((2, nd, rows, PATCH), BF),
        ((nd, PER_INDEX, FREQ + 256), F32),
        ((windows, rows), F32),
        ((windows, rows), F32),
        ((PER_INDEX, 128), F32),
    ]
    shapes = [
        ((NJ, nm) + (2,) * nb + (2, rows, TILE), BF),
        ((D, ROWS), BF),
        ((3, nm, ROWS, TILE), BF),
        ((nm, ROWS, TILE), BF),
        ((ROWS, D), F32),
        ((ROWS, D), F32),
        ((D, ROWS), BF),
        ((4, nm, ROWS, TILE), BF),
        ((4, ROWS, D), F32),
        ((ROWS, D), F32),
    ]

    def kernel(*refs):
        named = dict(zip(names, refs))
        forward_kernel(nd, nm, named, *refs[len(names) :])

    return pl.pallas_call(
        kernel,
        out_shape=[
            jax.ShapeDtypeStruct(shape, dtype) for shape, dtype in [((ROWS, D), F32)] + small + shapes
        ],
        in_specs=[pl.BlockSpec(memory_space=pl.ANY)] * len(names)
        + [pl.BlockSpec(memory_space=pltpu.VMEM)] * len(others),
        out_specs=[pl.BlockSpec(memory_space=pl.ANY)]
        + [pl.BlockSpec(memory_space=pltpu.VMEM)] * len(small)
        + [pl.BlockSpec(memory_space=pl.ANY)] * len(shapes),
        scratch_shapes=[
            pltpu.VMEM((ROWS, D), BF),
            pltpu.VMEM((3, nm, ROWS, TILE), BF),
            pltpu.VMEM((nm, ROWS, TILE), BF),
            pltpu.VMEM((ROWS, D), F32),
            pltpu.VMEM((ROWS, D), F32),
            pltpu.VMEM((ROWS, D), BF),
            pltpu.VMEM((2, D, ROWS), BF),
            pltpu.VMEM((2, nm, ROWS, TILE), BF),
            pltpu.VMEM((2, ROWS, D), F32),
            pltpu.VMEM((ROWS, D), F32),
            pltpu.VMEM((4, nm) + (2,) * nb + (2, rows, TILE), BF),
            pltpu.SemaphoreType.DMA((NJ, slots)),
            pltpu.SemaphoreType.DMA((NJ, slots)),
            pltpu.SemaphoreType.DMA((NJ,)),
            pltpu.SemaphoreType.DMA((NJ,)),
            pltpu.SemaphoreType.DMA((24,)),
            pltpu.VMEM((NJ, rows, TILE), BF),
            pltpu.VMEM((3, rows, TILE), F32),
            pltpu.VMEM((TILE, rows), F32),
            pltpu.VMEM((rows, 4 * TILE), F32),
            pltpu.VMEM((4 * TILE, rows), F32),
            pltpu.VMEM((6, rows, D), F32),
            pltpu.VMEM((FREQ, rows), F32),
            pltpu.VMEM((CLASSES + -CLASSES % 128, rows), F32),
            pltpu.VMEM((PATCH, rows), F32),
            pltpu.VMEM((PATCH, rows), F32),
            pltpu.VMEM((2, rows, PATCH), BF),
            pltpu.VMEM((PER_INDEX, FREQ + 256), F32),
            pltpu.VMEM((ROWS, PATCH), BF),
            pltpu.SemaphoreType.DMA((9,)),
            pltpu.VMEM((ROWS, D), F32),
            pltpu.VMEM((nd, windows if tall else rows, rows if tall else windows), F32),
            pltpu.VMEM((nd - 1, windows if tall else rows, rows if tall else windows), F32),
            pltpu.VMEM((nd, NMB, 6, D), F32),
            pltpu.VMEM((nd - 1, NMB, 6, D), F32),
            pltpu.VMEM((nd * NMB, D), F32),
            pltpu.VMEM((nm, PER_INDEX, 128), F32),
            pltpu.SemaphoreType.DMA((6, max(nd, nm) - 1)),
            pltpu.SemaphoreType.DMA((6, max(nd, nm) - 1)),
        ],
        compiler_params=pltpu.CompilerParams(
            collective_id=0, has_side_effects=True, vmem_limit_bytes=60 << 20
        ),
    )(*states.values(), *others)


PIECES = (5, 4, 7, 6, 9, 8, 11, 10, 3, 2, 1, 0)
BACKWARD_TURNS = (
    (0, ("head",)),
    (1, ("slope", 0)),
    (1, ("spread", 0)),
    (2, ("slope", 1)),
    (2, ("spread", 1)),
    (3, ("slope", 2)),
    (3, ("spread", 2)),
    (4, ("slope", 3)),
    (4, ("spread", 3)),
    (5, ("mid",)),
    (6, ("attend", 0)),
    (7, ("attend", 1)),
    (8, ("attend", 2)),
    (9, ("attend", 3)),
    (10, ("inward", 2)),
    (11, ("inward", 1)),
    (12, ("inward", 0)),
    (12, ("last",)),
)
HELD = 5
TWINS = 3


def backward_kernel(nd, nm, whole, n_one_t, qkv, mixed, branch_one, middle, n_two_t, hidden, slope, branch_two, residual, *refs):
    (mod, mask_in, token_total_in, noise_in, latents_in, both_ends) = refs[:6]
    token_total = token_total_in[0:1, 0:1]
    head_mat = both_ends[1].reshape(D, PATCH)
    (total, loss, ends, grad_mod) = refs[6:10]
    (partial, twin_ref, xa, xb, grad_rows, grad_in, grad_low, grad_low_t, normed_t, pool, loaded, z_ref, noise, latents, row_mask, ends_rows) = refs[10:26]
    rest = refs[26:]
    place = Place(nd, nm)
    nb, core = place.nb, place.core
    stage_refs = [rest[2 * step : 2 * step + 2] for step in range(nb)]
    send_sems, recv_sems, free_sem, load_sems = rest[2 * nb :]
    copies = Copies(send_sems, recv_sems)
    orders = [order[::-1] for order in place.orders]
    place.greet()
    slot_of = lambda step, half: 1 + 2 * step + half
    z_slot = 1 + 2 * nb
    loads = {}

    def load(name, source, target):
        copy = pltpu.make_async_copy(source, target, load_sems.at[len(loads)])
        copy.start()
        loads[name] = copy

    def load_tiles(j, slot):
        load(("w", j), whole.at[j], loaded.at[slot])

    def tile(slot, m):
        return loaded.at[slot, m].reshape(D, TILE)

    HIDDEN, QUERY, MIXED_GRAD = 4, 5, 8

    token_rows(latents_in, latents)
    token_rows(noise_in, noise)
    mask_column(mask_in, row_mask)

    load("branch_two", branch_two, xb)
    load("middle", middle, xa)
    load(("hidden", 0), hidden.at[0], pool.at[HIDDEN])
    load("n_two", n_two_t, normed_t)
    load_tiles(5, 0)
    load_tiles(4, 1)

    def add_to(target, index, source):
        shape = source.shape[:-2]

        def body(at):
            inner, places = at, []
            for size in shape[::-1]:
                places.append(inner % size)
                inner = inner // size
            places = places[::-1]
            spot = tuple(
                base.start + offset if isinstance(base, pl.Slice) else base
                for base, offset in zip(index, places)
            ) + (core,)
            target[spot] = (target[spot].astype(F32) + source[tuple(places)].astype(F32)).astype(BF)

        each(math.prod(shape), body)

    every = (slice(None),) * (nb + 1)

    def begin(s):
        if s >= TWINS:
            pl.semaphore_wait(free_sem, 1)
        source = partial.at[(s % HELD,) + every + (1 - core,)]
        copies.start(s, 0, source, twin_ref.at[s % TWINS], place.sibling)

    def stage(s, step):
        mine = partial.at[s % HELD]
        if step == 0:
            copies.arrived(s, 0)
            add_to(mine, (pl.ds(0, nm),) + (pl.ds(0, 2),) * nb, twin_ref.at[s % TWINS])
            if s + TWINS < NJ:
                pl.semaphore_signal(free_sem, inc=1, device_id=place.sibling, device_id_type=MESH)
        else:
            for half in range(2):
                copies.arrived(s, slot_of(step - 1, half))
                index = place.pick(half, orders[half][step:])
                add_to(mine, index, stage_refs[step - 1][half].at[s])
        if step < nb:
            for half in range(2):
                order = orders[half]
                block = mine.at[place.pick(half, order[step + 1 :], order[step]) + (core,)]
                target = stage_refs[step][half].at[s]
                copies.start(s, slot_of(step, half), block, target, place.across(order[step]))
        else:
            for hops in range(1, nm):
                block = mine.at[place.mine((place.m + hops) % nm) + (core,)]
                copies.start(s, z_slot + hops - 1, block, z_ref.at[s, hops - 1], place.along(hops))

    def finish(s):
        summed = partial[(s % HELD,) + place.mine() + (core,)].astype(F32)
        for hops in range(1, nm):
            copies.arrived(s, z_slot + hops - 1)
            summed = summed + z_ref[s, hops - 1].astype(F32)
        total[PIECES[s]] = summed
        copies.drain(s)

    def weight_grad(s):
        j = PIECES[s]
        if j >= 4 and j % 2 == 1:
            f = (j - 5) // 2
            loads["hidden", f].wait()
            left, right = grad_low_t, HIDDEN
        elif j >= 4:
            left, right = normed_t, (j - 4) // 2
        elif j == 3:
            loads["mixed"].wait()
            left, right = grad_low_t, HIDDEN
        else:
            if j == 2:
                loads["n_one"].wait()
            left, right = normed_t, j

        def body(m):
            grads = dot_nn(left[...], pool[right, m]).astype(BF)
            partial.at[s % HELD, m].reshape(D, TILE)[...] = grads

        each(nm, body)
        if j in (5, 7, 9):
            load(("hidden", f + 1), hidden.at[f + 1], pool.at[HIDDEN])
        if j == 11:
            load("mixed", mixed, pool.at[HIDDEN])
        if j == 10:
            load("n_one", n_one_t, normed_t)

    def rows_of(at):
        return at // PER_WINDOW, span(at, BLOCK)

    def add_mod(window, which, values):
        grad_mod[window, which : which + 1, :] += jnp.sum(values, axis=0, keepdims=True)

    def head_unit():
        loads["branch_two"].wait()
        loads["middle"].wait()
        loss[...] = jnp.zeros_like(loss)
        ends_rows[...] = jnp.zeros_like(ends_rows)
        grad_mod[...] = jnp.zeros_like(grad_mod)

        def body(at):
            window, here = rows_of(at)
            gate = mod[window, 5:6, :]
            branch = xb[here, :]
            normed, inverse = row_norm(xa[here, :] + gate * branch)
            low = normed.astype(BF)
            error = dot_nn(low, head_mat) - noise[here, :]
            mask = row_mask[here, :]
            share = jnp.sum(error * error, axis=-1, keepdims=True) * (1.0 / PATCH) * mask
            loss[...] += jnp.sum(share, axis=0, keepdims=True) / token_total
            grad_pred = (2.0 / PATCH * error * mask / token_total).astype(BF)
            ends_rows[PATCH:, :] += dot_tn(grad_pred, low)
            grad = norm_back(dot_nt(grad_pred, head_mat), normed, inverse)
            add_mod(window, 5, grad * branch)
            grad_rows[here, :] = grad
            grad_low[here, :] = (grad * gate).astype(BF)

        each(NBLOCK, body)
        transpose_rows(grad_low, grad_low_t)
        load(("slope", 0), slope.at[0], xa)
        load(("slope", 1), slope.at[1], xb)

    def slope_unit(f):
        loads["slope", f].wait()
        loads["w", 5 + 2 * f].wait()
        slopes = xa if f % 2 == 0 else xb

        def body(m):
            grad = dot_nn(grad_low[...], tile(0, m)[...])
            pool[f, m] = (grad * slopes[:, span(m, TILE)]).astype(BF)

        each(nm, body)
        if f + 2 < 4:
            load(("slope", f + 2), slope.at[f + 2], slopes)
        elif f == 2:
            load("middle_again", middle, xa)
        else:
            load("branch_one", branch_one, xb)
        load_tiles(7 + 2 * f if f < 3 else 3, 0)

    def add_rows(right, slot, fresh):
        def body(at):
            columns = span(at, TILE)
            summed = dot_nt(pool[right, 0], tile(slot, 0)[columns, :])
            for m in range(1, nm):
                summed = summed + dot_nt(pool[right, m], tile(slot, m)[columns, :])
            grad_in[:, columns] = summed if fresh else grad_in[:, columns] + summed

        each(D // TILE, body)

    def spread_unit(f):
        loads["w", 4 + 2 * f].wait()
        add_rows(f, 1, f == 0)
        load_tiles(6 + 2 * f if f < 3 else 2, 1)
        if f == 3:
            for part in range(3):
                load(("qkv", part), qkv.at[part], pool.at[QUERY + part])

    def norm_unit(which, after):
        def body(at):
            window, here = rows_of(at)
            normed, inverse = row_norm(xa[here, :])
            grad = grad_in[here, :]
            add_mod(window, which, grad)
            add_mod(window, which + 1, grad * normed)
            grad = grad * (1.0 + mod[window, which + 1 : which + 2, :])
            after(window, here, grad_rows[here, :] + norm_back(grad, normed, inverse))

        each(NBLOCK, body)

    def mid_unit():
        loads["middle_again"].wait()
        loads["branch_one"].wait()

        def after(window, here, grad):
            add_mod(window, 2, grad * xb[here, :])
            grad_rows[here, :] = grad
            grad_low[here, :] = (grad * mod[window, 2:3, :]).astype(BF)

        norm_unit(3, after)
        load("residual", residual, xa)
        loads["w", 3].wait()

        def body(m):
            pool[MIXED_GRAD, m] = dot_nn(grad_low[...], tile(0, m)[...]).astype(BF)

        each(nm, body)
        load_tiles(1, 0)

    def attend_unit(m):
        if m == 0:
            for part in range(3):
                loads["qkv", part].wait()

        def body(window):
            here = span(window, WTOK)
            query, key, value = (pool[QUERY + part, m, here, :] for part in range(3))
            grad_mixed = pool[MIXED_GRAD, m, here, :]
            grads = [jnp.zeros((WTOK, TILE), F32) for _ in range(3)]
            for head in range(TILE // HD):
                lanes = head_lanes(head, BF)
                own_query, own_grad = query * lanes, grad_mixed * lanes
                attn = soft_columns(key, own_query, row_mask[here, :])
                grads[2] = grads[2] + dot_nn(attn.astype(BF), own_grad)
                grad_attn = dot_nt(value, own_grad)
                inner = jnp.sum(attn * grad_attn, axis=0, keepdims=True)
                grad_scores = (attn * (grad_attn - inner)).astype(BF)
                grads[0] = grads[0] + dot_tn(grad_scores, key * lanes)
                grads[1] = grads[1] + dot_nn(grad_scores, own_query)
            pool[0, m, here, :] = (grads[0] * HD ** (-0.5)).astype(BF)
            pool[1, m, here, :] = (grads[1] * HD ** (-0.5)).astype(BF)
            pool[2, m, here, :] = grads[2].astype(BF)

        each(NMB, body)

    def inward_unit(j):
        slot = 1 if j != 1 else 0
        loads["w", j].wait()
        add_rows(j, slot, j == 2)
        if j == 2:
            load_tiles(0, 1)

    def last_unit():
        loads["residual"].wait()

        def after(window, here, grad):
            ends_rows[:PATCH, :] += dot_tn(latents[here, :], grad.astype(BF))

        norm_unit(0, after)
        ends[...] = ends_rows[...].T

    units = {
        "head": head_unit,
        "slope": slope_unit,
        "spread": spread_unit,
        "mid": mid_unit,
        "attend": attend_unit,
        "inward": inward_unit,
        "last": last_unit,
    }

    def compute(turn):
        for when, (name, *args) in BACKWARD_TURNS:
            if when == turn:
                units[name](*args)

    last = max(when for when, _ in BACKWARD_TURNS)
    for turn in range(max(NJ + nb + 2, last + 1)):
        if turn == 0:
            compute(turn)
        if 0 < turn <= last and turn in (1, 5, 9):
            compute(turn)
        if turn == 8:
            transpose_rows(grad_low, grad_low_t)
        if turn < NJ:
            if turn == 1:
                loads["n_two"].wait()
            weight_grad(turn)
            begin(turn)
        for step in range(nb + 1):
            if 0 <= turn - 1 - step < NJ:
                stage(turn - 1 - step, step)
        if 0 <= turn - 2 - nb < NJ:
            finish(turn - 2 - nb)
        if turn not in (0, 1, 5, 9):
            compute(turn)


def backward_blocks(saved, residual, *in_vmem):
    nd, nm = lax.axis_size("dp"), lax.axis_size("mp")
    nb = nd.bit_length() - 2
    rows = D // nd
    bits = (2,) * nb
    slots = 2 * nb + nm
    stage_shapes = []
    for step in range(nb):
        high_first = tuple(1 if at <= step else 2 for at in range(nb))
        stage_shapes.append(pltpu.VMEM((NJ, nm // 2) + high_first + (rows, TILE), BF))
        stage_shapes.append(pltpu.VMEM((NJ, nm - nm // 2) + high_first[::-1] + (rows, TILE), BF))
    in_hbm = (*saved, residual)
    return pl.pallas_call(
        functools.partial(backward_kernel, nd, nm),
        out_shape=[
            jax.ShapeDtypeStruct((NJ, rows, TILE), F32),
            jax.ShapeDtypeStruct((1, 1), F32),
            jax.ShapeDtypeStruct((D, 2 * PATCH), F32),
            jax.ShapeDtypeStruct((NMB, 6, D), F32),
        ],
        in_specs=[pl.BlockSpec(memory_space=pl.ANY)] * len(in_hbm)
        + [pl.BlockSpec(memory_space=pltpu.VMEM)] * len(in_vmem),
        out_specs=[pl.BlockSpec(memory_space=pltpu.VMEM)] * 4,
        scratch_shapes=[
            pltpu.VMEM((HELD, nm) + bits + (2, rows, TILE), BF),
            pltpu.VMEM((TWINS, nm) + bits + (rows, TILE), BF),
            pltpu.VMEM((ROWS, D), F32),
            pltpu.VMEM((ROWS, D), F32),
            pltpu.VMEM((ROWS, D), F32),
            pltpu.VMEM((ROWS, D), F32),
            pltpu.VMEM((ROWS, D), BF),
            pltpu.VMEM((D, ROWS), BF),
            pltpu.VMEM((D, ROWS), BF),
            pltpu.VMEM((9, nm, ROWS, TILE), BF),
            pltpu.VMEM((2, nm) + bits + (2, rows, TILE), BF),
            pltpu.VMEM((NJ, nm - 1, rows, TILE), BF),
            pltpu.VMEM((ROWS, PATCH), F32),
            pltpu.VMEM((ROWS, PATCH), BF),
            pltpu.VMEM((ROWS, 1), F32),
            pltpu.VMEM((2 * PATCH, D), F32),
            *stage_shapes,
            pltpu.SemaphoreType.DMA((NJ, slots)),
            pltpu.SemaphoreType.DMA((NJ, slots)),
            pltpu.SemaphoreType.REGULAR,
            pltpu.SemaphoreType.DMA((36,)),
        ],
        compiler_params=pltpu.CompilerParams(
            collective_id=1, has_side_effects=True, vmem_limit_bytes=61 << 20
        ),
    )(*in_hbm, *in_vmem)


def tail_kernel(nd, nm, adaptive_state, reduced, loss, ends, grad_mod, front, time_pre, condition, time_out, *refs):
    (ends_sum, adaptive_grad, time_in_grad, time_out_grad, classes_grad, sums) = refs[:6]
    (ends_in, ends_rows, mod_rows, mod_in, own_mod, all_mod, act_rows, cond_all, terms, term_rows, adaptive, send_sems, recv_sems, state_sem) = refs[6:]
    state_load = pltpu.make_async_copy(adaptive_state.at[0], adaptive, state_sem)
    state_load.start()
    place = Place(nd, nm)
    swap = Exchange(place, send_sems, recv_sems)
    dp_id, m = place.dp_id, place.m
    windows, rows = time_pre.shape
    place.greet(everyone=True)
    mod_in[m] = grad_mod[...]
    swap.mp_gather(0, grad_mod, mod_in)
    swap.dp_scatter(1, ends, ends_in)

    swap.wait(0)
    for index in range(nm):
        for step in range(NMB):
            for which in range(6):
                row = index * NMB + step
                mod_rows[which, row : row + 1, :] = mod_in[index, step, which : which + 1, :]
    for pair in range(3):
        own_mod[pair] = mod_rows[2 * pair : 2 * pair + 2].reshape(2 * PER_INDEX, D).astype(BF)
        all_mod[dp_id, pair] = own_mod[pair]
    swap.dp_gather(2, own_mod, all_mod)
    swap.wait(1)
    ends_rows[m] = ends[dp_id] + jnp.sum(ends_in[...], axis=0)
    swap.mp_gather(3, ends_rows.at[m], ends_rows)
    cond_act = silu(condition[...]).reshape(nd, PER_INDEX, rows)
    act_rows[...] = jnp.zeros_like(act_rows)
    for side in range(2):
        act_rows[side, :, side * PER_INDEX : (side + 1) * PER_INDEX, :] = cond_act
    features = front[:, :, :FREQ].reshape(windows, FREQ).astype(BF)
    time_hidden = silu(time_pre[...]).astype(BF)
    pick = label_pick(front, classes_grad.shape[0])
    squares = jnp.zeros((8, 128), F32)
    whole_squares = jnp.zeros((8, 128), F32)

    def square_sum(values):
        return jnp.sum(jnp.sum(values * values, axis=0, keepdims=True), axis=1, keepdims=True)

    for j in range(NJ):
        whole_squares = whole_squares + square_sum(reduced[j])
    swap.wait(2)
    state_load.wait()
    grad_cond = jnp.zeros((windows, rows), F32)
    for which in range(6):
        pair, side = which // 2, which % 2
        block = all_mod[:, pair].reshape(nd * 2 * PER_INDEX, D)
        act = act_rows[side].reshape(nd * 2 * PER_INDEX, rows).astype(BF)
        gradient = dot_tn(act, block)
        adaptive_grad[which] = gradient
        squares = squares + square_sum(gradient)
        back = dot_nt(block, adaptive[which].astype(BF)).reshape(nd, 2, PER_INDEX, rows)
        grad_cond = grad_cond + back[:, side].reshape(windows, rows)
    grad_cond = (grad_cond * silu_slope(condition[...])).astype(BF)
    cond_all[dp_id] = grad_cond
    swap.dp_gather(4, cond_all.at[dp_id], cond_all)
    gradient = dot_tn(pick, grad_cond)
    classes_grad[...] = gradient
    squares = squares + square_sum(gradient)
    swap.wait(3)
    ends_sum[...] = jnp.sum(ends_rows[...], axis=0).T
    squares = squares + square_sum(ends_sum[...])
    swap.wait(4)
    grad_time = jnp.zeros((windows, rows), F32)
    for index in range(nd):
        gradient = dot_tn(time_hidden, cond_all[index])
        time_out_grad[index] = gradient
        squares = squares + square_sum(gradient)
        grad_time = grad_time + dot_nt(cond_all[index], time_out[index])
    grad_time = (grad_time * silu_slope(time_pre[...])).astype(BF)
    gradient = dot_tn(features, grad_time)
    time_in_grad[...] = gradient
    squares = squares + square_sum(gradient)

    terms[dp_id, 0] = squares * (1.0 / nm) + whole_squares
    terms[dp_id, 1] = jnp.zeros((8, 128), F32) + loss[...]
    swap.dp_gather(5, terms.at[dp_id], terms)
    swap.wait(5)
    term_rows[m] = jnp.sum(terms[...], axis=0)
    swap.mp_gather(6, term_rows.at[m], term_rows)
    swap.wait(6)
    sums[...] = jnp.sum(term_rows[...], axis=0)
    swap.drain()


def tail_blocks(*operands):
    nd, nm = lax.axis_size("dp"), lax.axis_size("mp")
    rows = D // nd
    windows = nd * PER_INDEX
    classes = CLASSES + -CLASSES % 128
    shapes = [
        (2 * PATCH, rows),
        (6, rows, D),
        (FREQ, rows),
        (nd, rows, rows),
        (classes, rows),
        (2, 8, 128),
    ]
    return pl.pallas_call(
        functools.partial(tail_kernel, nd, nm),
        out_shape=[jax.ShapeDtypeStruct(shape, F32) for shape in shapes],
        in_specs=[pl.BlockSpec(memory_space=pl.ANY)]
        + [pl.BlockSpec(memory_space=pltpu.VMEM)] * (len(operands) - 1),
        out_specs=[pl.BlockSpec(memory_space=pltpu.VMEM)] * len(shapes),
        scratch_shapes=[
            pltpu.VMEM((nd - 1, rows, 2 * PATCH), F32),
            pltpu.VMEM((nm, rows, 2 * PATCH), F32),
            pltpu.VMEM((6, PER_INDEX, D), F32),
            pltpu.VMEM((nm, NMB, 6, D), F32),
            pltpu.VMEM((3, 2 * PER_INDEX, D), BF),
            pltpu.VMEM((nd, 3, 2 * PER_INDEX, D), BF),
            pltpu.VMEM((2, nd, 2 * PER_INDEX, rows), F32),
            pltpu.VMEM((nd, windows, rows), BF),
            pltpu.VMEM((nd, 2, 8, 128), F32),
            pltpu.VMEM((nm, 2, 8, 128), F32),
            pltpu.VMEM((6, rows, D), F32),
            pltpu.SemaphoreType.DMA((7, max(nd, nm) - 1)),
            pltpu.SemaphoreType.DMA((7, max(nd, nm) - 1)),
            pltpu.SemaphoreType.DMA,
        ],
        compiler_params=pltpu.CompilerParams(
            collective_id=2, has_side_effects=True, vmem_limit_bytes=40 << 20
        ),
    )(*operands)


def adam_update(weight, first, root, gradient, factor):
    clipped = gradient * factor
    first = beta_one * first + (1.0 - beta_one) * clipped
    root = jnp.sqrt(beta_two * root * root + (1.0 - beta_two) * clipped * clipped)
    update = (
        first
        / (1.0 - beta_one**step_count)
        / (root / math.sqrt(1.0 - beta_two**step_count) + adam_eps)
    )
    return weight - learn_rate * (update + weight_decay * weight), first, root


def chunk_rows(rows, lanes):
    limit = max(16, 16384 // max(lanes, 128))
    return max(size for size in range(8, limit + 1, 8) if rows % size == 0)


def adam_kernel(names, *refs):
    count = len(names)
    states = dict(zip(names, refs[:count]))
    reduced, ends, time_in, time_out, classes, adaptive, sums = refs[count : count + 7]
    refs = refs[count + 7 :]
    targets = dict(zip(names, zip(refs[: 2 * count : 2], refs[1 : 2 * count : 2])))
    held = dict(zip(names, refs[2 * count : 3 * count]))
    load_sems, store_sems = refs[3 * count :]
    squares = sums[0, 0:1, 0:1]
    factor = jnp.minimum(1.0, threshold / jnp.sqrt(squares))
    loads, stores = {}, []

    def parts_of(name):
        lead = held[name].shape[1:-2]
        return [(at,) for at in range(lead[0])] if lead else [()]

    for name in names:
        for part in parts_of(name):
            every = (slice(None),) + part
            copy = pltpu.make_async_copy(
                states[name].at[every], held[name].at[every], load_sems.at[len(loads)]
            )
            copy.start()
            loads[name, part] = copy

    def apply(where, gradient):
        ref, part, rows, columns = where
        spot = lambda which: (which,) + part + (rows, columns)
        values = [ref[spot(which)] for which in range(3)]
        for which, value in enumerate(adam_update(*values, gradient, factor)):
            ref[spot(which)] = value

    def store(name, part):
        weight, moments = targets[name]
        copies = (
            (held[name].at[(0,) + part], weight.at[part] if part else weight),
            (held[name].at[(pl.ds(1, 2),) + part], moments.at[(slice(None),) + part]),
        )
        for source, target in copies:
            copy = pltpu.make_async_copy(source, target, store_sems.at[len(stores)])
            copy.start()
            stores.append(copy)

    def rowwise(name, part, source, first_row=0):
        rows, lanes = held[name].shape[-2:]
        size = chunk_rows(rows, lanes)

        def body(at):
            here = span(at, size)
            there = pl.ds(pl.multiple_of(first_row + at * size, 8), size)
            apply((held[name], part, here, slice(None)), source[there, :])

        each(rows // size, body)

    every = slice(None)
    for name in names:
        for part in parts_of(name):
            loads[name, part].wait()
            if name == "adaptive":
                rowwise(name, part, adaptive.at[part[0]])
            elif name == "attention_in":
                rowwise(name, part, reduced.at[part[0]])
            elif name == "expand":
                for f in range(4):
                    columns = slice(f * TILE, (f + 1) * TILE)
                    apply((held[name], part, every, columns), reduced[4 + 2 * f])
            elif name == "contract":
                for f in range(4):
                    rows = slice(f * TILE, (f + 1) * TILE)
                    apply((held[name], part, rows, every), reduced[5 + 2 * f].T)
            elif name == "attention_out":
                apply((held[name], part, every, every), reduced[3].T)
            elif name == "embed":
                rowwise(name, part, ends)
            elif name == "head":
                rowwise(name, part, ends, PATCH)
            else:
                rowwise(name, part, {"time_in": time_in, "time_out": time_out, "classes": classes}[name])
            store(name, part)
    for copy in stores:
        copy.wait()


def adam_blocks(states, *gradients):
    names = list(states)
    shapes = [states[name].shape for name in names]
    outs = []
    for shape in shapes:
        outs += [shape[1:], (2,) + shape[1:]]
    pieces = sum(shape[1] if len(shape) == 4 else 1 for shape in shapes)
    return pl.pallas_call(
        functools.partial(adam_kernel, names),
        out_shape=[jax.ShapeDtypeStruct(shape, F32) for shape in outs],
        in_specs=[pl.BlockSpec(memory_space=pl.ANY)] * len(names)
        + [pl.BlockSpec(memory_space=pltpu.VMEM)] * len(gradients),
        out_specs=[pl.BlockSpec(memory_space=pl.ANY)] * len(outs),
        scratch_shapes=[pltpu.VMEM(shape, F32) for shape in shapes]
        + [pltpu.SemaphoreType.DMA((pieces,)), pltpu.SemaphoreType.DMA((2 * pieces,))],
        compiler_params=pltpu.CompilerParams(vmem_limit_bytes=40 << 20),
    )(*states.values(), *gradients)


def per_device(
    latents,
    noise_target,
    token_mask,
    timesteps,
    labels,
    state_embed,
    state_head,
    state_time_in,
    state_time_out,
    state_classes,
    state_adaptive,
    state_attention_in,
    state_attention_out,
    state_expand,
    state_contract,
):
    nd = lax.axis_size("dp")
    rows = state_attention_in.shape[1]
    states = {
        "adaptive": state_adaptive.transpose(0, 2, 1, 3),
        "attention_in": state_attention_in.transpose(0, 2, 1, 3),
        "expand": state_expand,
        "contract": state_contract,
        "time_out": state_time_out,
        "classes": state_classes,
        "attention_out": state_attention_out,
        "time_in": state_time_in,
        "embed": state_embed,
        "head": state_head.transpose(0, 2, 1),
    }
    lanes = jnp.arange(FREQ + 128)[None, :]
    step_ids = timesteps[0].T.reshape(PER_INDEX, 1).astype(F32)
    label_ids = labels[0].T.reshape(PER_INDEX, 1).astype(F32)
    half_width = FREQ // 2
    frequency = jnp.exp(-math.log(10000.0) * (lanes % half_width).astype(F32) / half_width)
    angles = step_ids * frequency
    features = jnp.where(lanes < half_width, jnp.cos(angles), jnp.sin(angles))
    front = jnp.where(lanes < FREQ, features.astype(BF).astype(F32), label_ids)
    time_out_part = state_time_out[0].astype(BF).reshape(rows, nd, rows).transpose(1, 0, 2)
    flags = token_mask.reshape(NMB, WTOK)
    latent_columns = latents[0].transpose(0, 2, 1)
    noise_columns = noise_target[0].transpose(0, 2, 1)
    residual, mod, ends, front_all, time_pre, condition, token_total, *saved = forward_blocks(
        states, flags, front, latent_columns, window_positions(), time_out_part
    )
    reduced, loss_local, ends_grad, grad_mod = backward_blocks(
        saved, residual, mod, flags, token_total, noise_columns, latent_columns, ends
    )
    ends_sum, adaptive_grad, time_in_grad, time_out_grad, classes_grad, sums = tail_blocks(
        states["adaptive"],
        reduced,
        loss_local,
        ends_grad.reshape(nd, rows, 2 * PATCH),
        grad_mod,
        front_all,
        time_pre,
        condition,
        time_out_part,
    )
    updated = adam_blocks(
        states,
        reduced,
        ends_sum,
        time_in_grad,
        time_out_grad.transpose(1, 0, 2).reshape(rows, D),
        classes_grad,
        adaptive_grad,
        sums,
    )
    new = dict(zip(states, zip(updated[::2], updated[1::2])))
    back = {"adaptive": (1, 0, 2), "attention_in": (1, 0, 2), "head": (1, 0)}
    results = [sums[1, 0, 0], jnp.sqrt(sums[0, 0, 0])]
    order = ("embed", "head", "time_in", "time_out", "classes", "adaptive", "attention_in")
    for name in order + ("attention_out", "expand", "contract"):
        weight, moments = new[name]
        if name in back:
            axes = back[name]
            weight = weight.transpose(axes)
            moments = moments.transpose((0,) + tuple(1 + axis for axis in axes))
        results += [weight, moments]
    return tuple(results)


def solution(mesh):
    in_specs = (
        P("dp", None, "mp", None),
        P("dp", None, "mp", None),
        P("dp", None, "mp"),
        P("dp", None, None),
        P("dp", None, None),
        P(None, None, "dp"),
        P(None, "dp", None),
        P(None, None, "dp"),
        P(None, "dp", None),
        P(None, None, "dp"),
        P(None, "dp", None, None),
        P(None, "dp", None, "mp"),
        P(None, "mp", "dp"),
        P(None, "dp", "mp"),
        P(None, "mp", "dp"),
    )
    out_specs = (
        P(),
        P(),
        P(None, "dp"),
        P(None, None, "dp"),
        P("dp", None),
        P(None, "dp", None),
        P(None, "dp"),
        P(None, None, "dp"),
        P("dp", None),
        P(None, "dp", None),
        P(None, "dp"),
        P(None, None, "dp"),
        P("dp", None, None),
        P(None, "dp", None, None),
        P("dp", None, "mp"),
        P(None, "dp", None, "mp"),
        P("mp", "dp"),
        P(None, "mp", "dp"),
        P("dp", "mp"),
        P(None, "dp", "mp"),
        P("mp", "dp"),
        P(None, "mp", "dp"),
    )
    return jax.shard_map(
        per_device, mesh=mesh, in_specs=in_specs, out_specs=out_specs, check_vma=False
    )
```

```python
import functools
import math

import jax
import jax.numpy as jnp
import numpy as np
from jax import lax
from jax.experimental import pallas as pl
from jax.experimental.pallas import tpu as pltpu
from jax.sharding import PartitionSpec as P

D = 1024
HEADS = 16
HD = 64
PATCH = 32
FREQ = 256
CLASSES = 600
WTOK = 320
NMB = 2
WMB = 4
TILE = 256
NJ = 12
ROWS = NMB * WTOK
MESH = pl.DeviceIdType.MESH
BF = jnp.bfloat16
F32 = jnp.float32


beta_one = 0.9
beta_two = 0.999
adam_eps = 1e-08
learn_rate = 0.15
weight_decay = 0.1
threshold = 0.002
step_count = 10.0


def window_positions():
    half_width = D // 2
    steps = np.arange(half_width, dtype=np.float32)
    frequency = np.exp(np.float32(-math.log(10000.0)) * steps / np.float32(half_width))
    angles = np.arange(WTOK, dtype=np.float32)[:, None] * frequency.astype(np.float32)[None, :]
    table = np.concatenate([np.sin(angles), np.cos(angles)], axis=-1)
    return jnp.asarray(table.astype(np.float32))


def dot_general(a, b, a_dim, b_dim):
    return lax.dot_general(a, b, (((a_dim,), (b_dim,)), ((), ())), preferred_element_type=F32)


def dot_nn(a, b):
    return jnp.dot(a, b, preferred_element_type=F32)


def dot_nt(a, b):
    return dot_general(a, b, 1, 1)


def dot_tn(a, b):
    return dot_general(a, b, 0, 0)


def norm_back(grad, normed, inverse):
    mean_grad = jnp.mean(grad, axis=-1, keepdims=True)
    mean_prod = jnp.mean(grad * normed, axis=-1, keepdims=True)
    return inverse * (grad - mean_grad - normed * mean_prod)


def silu(values):
    return values * jax.nn.sigmoid(values)


def silu_slope(values):
    gate = jax.nn.sigmoid(values)
    return gate * (1.0 + values * (1.0 - gate))


def gelu_parts(up):
    cdf = 0.5 * (1.0 + lax.erf(up * math.sqrt(0.5)))
    pdf = jnp.exp(-0.5 * up * up) * (1.0 / math.sqrt(2.0 * math.pi))
    return up * cdf, cdf + up * pdf


def tokens3(values):
    return values.reshape(NMB, WTOK, -1)


def flip(bits, at):
    return [1 - bit if place == at else bit for place, bit in enumerate(bits)]


class Place:
    def __init__(self, nd, nm):
        self.nm = nm
        self.nb = nd.bit_length() - 2
        dp_id = lax.axis_index("dp")
        self.nd = nd
        self.dp_id = dp_id
        self.m = lax.axis_index("mp")
        self.core = dp_id % 2
        self.bits = [dp_id // (1 << (self.nb - at)) % 2 for at in range(self.nb)]
        self.sibling = {"dp": self.dp_of(self.bits, 1 - self.core), "mp": self.m}
        self.orders = (list(range(self.nb))[::-1], list(range(self.nb)))
        self.halves = (pl.ds(0, nm // 2), pl.ds(nm // 2, nm - nm // 2))

    def dp_of(self, bits, core):
        total = core
        for at, bit in enumerate(bits):
            total = total + bit * (1 << (self.nb - at))
        return total

    def across(self, at):
        return {"dp": self.dp_of(flip(self.bits, at), self.core), "mp": self.m}

    def along(self, hops):
        return {"dp": self.dp_of(self.bits, self.core), "mp": (self.m + hops) % self.nm}

    def facing(self, hops):
        return {"dp": self.chip(hops) * 2 + self.core, "mp": self.m}

    def chip(self, hops):
        return (self.dp_id // 2 + hops) % (self.nd // 2)

    def beside(self, hops):
        return {"dp": (self.dp_id + hops) % self.nd, "mp": self.m}

    def pick(self, half, done, flipped=None):
        where = flip(self.bits, flipped)
        return (self.halves[half],) + tuple(
            pl.ds(0, 2) if at in done else pl.ds(where[at], 1) for at in range(self.nb)
        )

    def mine(self, m=None):
        return (self.m if m is None else m,) + tuple(self.bits)

    def greet(self, everyone=False):
        barrier = pltpu.get_barrier_semaphore()
        if everyone:
            others = [self.beside(hops) for hops in range(1, self.nd)]
        else:
            others = [self.sibling] + [self.facing(hops) for hops in range(1, self.nd // 2)]
        others += [self.along(hops) for hops in range(1, self.nm)]
        for other in others:
            pl.semaphore_signal(barrier, inc=1, device_id=other, device_id_type=MESH)
        return lambda: pl.semaphore_wait(barrier, len(others))


class Copies:
    def __init__(self, send_sems, recv_sems):
        self.send_sems, self.recv_sems = send_sems, recv_sems
        self.started = {}

    def start(self, step, slot, source, target, device):
        copy = pltpu.make_async_remote_copy(
            src_ref=source,
            dst_ref=target,
            send_sem=self.send_sems.at[step, slot],
            recv_sem=self.recv_sems.at[step, slot],
            device_id=device,
            device_id_type=MESH,
        )
        copy.start()
        self.started[step, slot] = copy

    def arrived(self, step, slot):
        self.started[step, slot].wait_recv()

    def drain(self, step=None):
        for key in list(self.started):
            if step is None or key[0] == step:
                self.started.pop(key).wait_send()


class Exchange:
    def __init__(self, place, send_sems, recv_sems):
        self.place = place
        self.copies = Copies(send_sems, recv_sems)

    def dp_gather(self, group, source, target):
        for hops in range(1, self.place.nd):
            here = target.at[self.place.dp_id]
            self.copies.start(group, hops - 1, source, here, self.place.beside(hops))

    def to_sibling(self, group, source, target, slot=0):
        self.copies.start(group, slot, source, target, self.place.sibling)

    def chip_scatter(self, group, source, target):
        for hops in range(1, self.place.nd // 2):
            block = source.at[self.place.chip(hops), self.place.core]
            self.copies.start(group, hops - 1, block, target.at[hops - 1], self.place.facing(hops))

    def chip_gather(self, group, source, target):
        for hops in range(1, self.place.nd // 2):
            self.copies.start(group, hops - 1, source, target, self.place.facing(hops))

    def mp_gather(self, group, source, target):
        for hops in range(1, self.place.nm):
            here = target.at[self.place.m]
            self.copies.start(group, hops - 1, source, here, self.place.along(hops))

    def wait(self, group):
        for step, slot in list(self.copies.started):
            if step == group:
                self.copies.arrived(step, slot)

    def drain(self):
        self.copies.drain()


def gather_steps(
    place, shard, whole, send_sems, recv_sems, local_sems, all_here, prepare, load, compute, last
):
    nm, nb, core = place.nm, place.nb, place.core
    copies = Copies(send_sems, recv_sems)
    stage_slot = lambda stage, half: nm - 1 + 2 * stage + half
    twin = nm - 1 + 2 * nb
    wide = ARRIVALS[-1]
    count = NJ - 1
    late = 2 * twin + 1
    wide_z = lambda part, hops: (0 if part == 0 else late) + hops - 1
    wide_twin = lambda part, hops: (twin if part == 0 else late + nm - 1) + hops - 1
    locals_ = {}

    def begin_local(j):
        here = whole.at[(j,) + place.mine() + (core,)]
        locals_[j] = pltpu.make_async_copy(shard.at[j], here, local_sems.at[j])
        locals_[j].start()
        copies.start(j, 2 * twin, shard.at[j], here, place.sibling)

    def begin(j):
        here = whole.at[(j,) + place.mine() + (core,)]
        for hops in range(1, nm):
            copies.start(j, hops - 1, shard.at[j], here, place.along(hops))
        begin_local(j)

    def half_of_wide(half, bits):
        lanes = pl.ds(half * (TILE // 2), TILE // 2)
        return whole.at[(wide, place.m) + bits + (core, slice(None), lanes)]

    def wide_stage(step):
        if step == 1:
            locals_[wide].wait()
        for half in range(2):
            order = place.orders[half]
            if step > 0:
                copies.arrived(wide, stage_slot(step - 1, half))
            if step == 0:
                source = shard.at[wide, :, pl.ds(half * (TILE // 2), TILE // 2)]
                block = half_of_wide(half, tuple(place.bits))
                copies.start(wide, stage_slot(0, half), source, block, place.across(order[0]))
            elif step < nb:
                block = half_of_wide(half, place.pick(half, order[:step])[1:])
                copies.start(wide, stage_slot(step, half), block, block, place.across(order[step]))
            if step > 0:
                block = half_of_wide(half, place.pick(half, order[: step - 1], order[step - 1])[1:])
                copies.start(wide, twin + stage_slot(step - 1, half), block, block, place.sibling)

    def part_of_wide(part, m):
        return whole.at[(wide, m, pl.ds(part, 1)) + (pl.ds(0, 2),) * (nb - 1) + (core,)]

    def wide_send(part):
        block = part_of_wide(part, place.m)
        for hops in range(1, nm):
            copies.start(wide, wide_z(part, hops), block, block, place.along(hops))

    def wide_pass(part):
        for hops in range(1, nm):
            copies.arrived(wide, wide_z(part, hops))
            block = part_of_wide(part, (place.m + nm - hops) % nm)
            copies.start(wide, wide_twin(part, hops), block, block, place.sibling)

    def stage(j, step):
        if step == 0:
            locals_[j].wait()
            for hops in range(1, nm):
                copies.arrived(j, hops - 1)
        else:
            for half in range(2):
                copies.arrived(j, stage_slot(step - 1, half))
        if step < nb:
            for half in range(2):
                order = place.orders[half]
                block = whole.at[(j,) + place.pick(half, order[:step]) + (core,)]
                copies.start(j, stage_slot(step, half), block, block, place.across(order[step]))
        if step == 0:
            for hops in range(1, nm):
                block = whole.at[(j,) + place.mine((place.m + nm - hops) % nm) + (core,)]
                copies.start(j, twin + hops - 1, block, block, place.sibling)
        else:
            for half in range(2):
                order = place.orders[half]
                block = whole.at[
                    (j,) + place.pick(half, order[: step - 1], order[step - 1]) + (core,)
                ]
                copies.start(j, twin + stage_slot(step - 1, half), block, block, place.sibling)

    def finish(j):
        for slot in range(twin, 2 * twin + 1):
            copies.arrived(j, slot)
        if j == wide:
            for hops in range(1, nm):
                copies.arrived(j, wide_twin(1, hops))
        load(j)

    prepare(ARRIVALS[0])
    prepare(wide)
    all_here()
    begin(ARRIVALS[0])
    wide_stage(0)
    begin_local(wide)
    for at in range(1, 3):
        prepare(ARRIVALS[at])
        begin(ARRIVALS[at])
    prepare(ARRIVALS[3])
    for turn in range(max(NJ + nb + 1, last + nb - 1)):
        for step in range(nb + 1):
            if 0 <= turn - step < count:
                stage(ARRIVALS[turn - step], step)
        if 1 <= turn + 1 <= nb:
            wide_stage(turn + 1)
        if turn + 3 < count:
            begin(ARRIVALS[turn + 3])
        if turn in (nb, nb + 3):
            wide_send(0 if turn == nb else 1)
        if turn in (nb + 5, nb + 8):
            wide_pass(0 if turn == nb + 5 else 1)
        if turn == nb + 10:
            finish(wide)
        if 0 <= turn - 1 - nb < count:
            finish(ARRIVALS[turn - 1 - nb])
        if turn + 4 < count:
            prepare(ARRIVALS[turn + 4])
        compute(turn + 2 - nb)
    copies.drain()


def row_norm(values):
    center = values - jnp.mean(values, axis=-1, keepdims=True)
    inverse = lax.rsqrt(jnp.mean(center * center, axis=-1, keepdims=True) + 1e-06)
    return center * inverse, inverse


def each(count, body, unroll=1):
    lax.fori_loop(0, count, lambda at, carry: (body(at), carry)[1], 0, unroll=math.gcd(count, unroll))


def span(at, size):
    return pl.ds(pl.multiple_of(at * size, size), size)


def head_lanes(head, dtype=F32):
    lanes = lax.broadcasted_iota(jnp.int32, (1, TILE), 1) // HD
    return (lanes == head).astype(dtype)


def soft_rows(query, key, key_bias):
    scores = dot_nt(query, key) * HD ** (-0.5)
    scores = jnp.where(key_bias > 0, scores, -1e30)
    exponents = jnp.exp(scores - jnp.max(scores, axis=-1, keepdims=True))
    return exponents / jnp.sum(exponents, axis=-1, keepdims=True)


def label_pick(front, count):
    labels = front[:, :, FREQ : FREQ + 1].reshape(-1, 1)
    lanes = lax.broadcasted_iota(jnp.int32, (labels.shape[0], count), 1).astype(F32)
    return (lanes == labels).astype(BF)


PER_INDEX = NMB * WMB
def soft_columns(key, query, key_mask):
    scores = dot_nt(key, query) * HD ** (-0.5)
    scores = jnp.where(key_mask > 0, scores, -1e30)
    exponents = jnp.exp(scores - jnp.max(scores, axis=0, keepdims=True))
    return exponents / jnp.sum(exponents, axis=0, keepdims=True)


BLOCK = 64
PER_WINDOW = WTOK // BLOCK
NBLOCK = ROWS // BLOCK
LANE_BLOCK = 128


def token_rows(source, target):
    for window in range(NMB):
        target[window * WTOK : (window + 1) * WTOK, :] = source[window].T


def mask_column(source, target):
    for window in range(NMB):
        row = jnp.broadcast_to(source[window : window + 1, :].astype(F32), (8, WTOK))
        target[window * WTOK : (window + 1) * WTOK, :] = row.T[:, 0:1]


def transpose_rows(source, target):
    def body(at):
        target[:, span(at, LANE_BLOCK)] = source[span(at, LANE_BLOCK), :].T

    each(ROWS // LANE_BLOCK, body)


ARRIVALS = (0, 1, 2, 3, 4, 6, 8, 10, 5, 7, 9, 11)
FORWARD_TURNS = (
    (4, ("qkv", 0)),
    (5, ("qkv", 1)),
    (6, ("qkv", 2)),
    (6, ("attend", 0)),
    (7, ("attend", 1)),
    (7, ("attend", 2)),
    (7, ("attend", 3)),
    (8, ("out",)),
    (9, ("up", 0)),
    (9, ("up", 1)),
    (10, ("up", 2)),
    (11, ("up", 3)),
    (12, ("down", 0)),
    (13, ("down", 1)),
    (13, ("down", 3)),
    (14, ("down", 2)),
)


def forward_kernel(nd, nm, states, flags, times_in, latents_in, positions, time_out, *refs):
    (residual_out, mod, ends, front, time_pre, condition, token_total) = refs[:7]
    refs = refs[7:]
    (residual, parts, parts_twin, parts_in, mods, mods_twin, mods_in) = refs[-12:-5]
    (rows_ref, counts, ends_all, swap_send, swap_recv) = refs[-5:]
    (shard, held_in, held_out, held_up, held_down, adaptive, time_in, classes, held_embed, held_head, ends_in, front_in, latents, state_sems) = refs[-26:-12]
    refs = refs[:-26]
    place = Place(nd, nm)
    swap = Exchange(place, swap_send, swap_recv)
    all_here = place.greet(everyone=True)
    state_loads = {}
    class_pad = classes.shape[0] - CLASSES
    wanted_states = {
        "attention_in": held_in,
        "contract": held_down,
        "embed": held_embed,
        "head": held_head,
        "time_in": time_in,
        "classes": classes.at[pl.ds(0, CLASSES)],
        "adaptive": adaptive,
        "attention_out": held_out,
        "expand": held_up,
    }
    for at, (name, target) in enumerate(wanted_states.items()):
        state_loads[name] = pltpu.make_async_copy(states[name].at[0], target, state_sems.at[at])
        state_loads[name].start()

    def state_ready(name):
        if name in state_loads:
            state_loads.pop(name).wait()

    def prepare(j):
        if j < 3:
            state_ready("attention_in")
            values = held_in[j]
        elif j == 3:
            state_ready("attention_out")
            values = held_out[...].T
        elif j % 2 == 0:
            state_ready("expand")
            values = held_up[:, (j - 4) // 2 * TILE : (j - 2) // 2 * TILE]
        else:
            state_ready("contract")
            values = held_down[(j - 5) // 2 * TILE : (j - 3) // 2 * TILE, :].T
        shard[j] = values.astype(BF)

    dp_id = place.dp_id
    windows = nd * PER_INDEX
    upright = parts.shape[2] == windows
    (whole, n_one_t, qkv_out, mixed_out, branch_one_out, middle_out, n_two_t, hidden_out, slope_out, branch_two_out) = refs[:10]
    (n_one, qkv, mixed, branch_one, middle, n_two, flipped, hidden, slope, branch_two, loaded) = refs[10:21]
    send_sems, recv_sems, local_sems, load_sems, spill_sems = refs[21:]
    spilled, spill_count = {}, []

    def spill(name, source, target):
        copy = pltpu.make_async_copy(source, target, spill_sems.at[len(spill_count)])
        copy.start()
        spill_count.append(name)
        spilled[name] = copy

    loads = {}
    slots = loaded.shape[0]

    def load(j):
        loads[j] = pltpu.make_async_copy(whole.at[j], loaded.at[ARRIVALS.index(j) % slots], load_sems.at[j])
        loads[j].start()

    def tile(j, m):
        return loaded.at[ARRIVALS.index(j) % slots, m].reshape(D, TILE)

    def first_swap():
        state_ready("embed")
        state_ready("head")
        ends_in[0] = held_embed[...].astype(BF)
        ends_in[1] = held_head[...].astype(BF)
        front_in[:, : FREQ + 128] = times_in[...]
        count = jnp.sum(jnp.sum(flags[...].astype(F32), axis=0, keepdims=True), axis=1, keepdims=True)
        front_in[:, FREQ + 128 :] = jnp.broadcast_to(count, (PER_INDEX, 128))
        classes[CLASSES:, :] = jnp.zeros((class_pad, classes.shape[1]), F32)
        token_rows(latents_in, latents)
        front[dp_id] = front_in[...]
        ends_all[dp_id] = ends_in[...]
        swap.dp_gather(0, front_in, front)
        swap.dp_gather(1, ends_in, ends_all)

    def time_layers():
        swap.wait(0)
        features = front[:, :, :FREQ].reshape(windows, FREQ).astype(BF)
        state_ready("time_in")
        time_pre[...] = dot_nn(features, time_in[...].astype(BF))
        time_hidden = silu(time_pre[...]).astype(BF)
        for index in range(nd):
            if upright:
                parts[index // 2, index % 2] = dot_nn(time_hidden, time_out[index])
            else:
                parts[index // 2, index % 2] = dot_general(time_out[index], time_hidden, 0, 1)
        swap.to_sibling(2, parts.at[:, 1 - place.core], parts_twin)
        counts[place.m] = jnp.sum(front[:, :, FREQ + 128 :], axis=0)
        swap.mp_gather(5, counts.at[place.m], counts)
        swap.wait(2)
        for chip in range(nd // 2):
            parts[chip, place.core] += parts_twin[chip]
        swap.chip_scatter(3, parts, parts_in)

    def condition_layers():
        state_ready("classes")
        state_ready("adaptive")
        swap.wait(3)
        total = parts[dp_id // 2, place.core] + jnp.sum(parts_in[...], axis=0)
        total = total if upright else total.T
        total = total + dot_nn(label_pick(front, classes.shape[0]), classes[...].astype(BF))
        condition[...] = total
        row_ids = lax.broadcasted_iota(jnp.int32, (nd * NMB, windows), 0)
        column_ids = lax.broadcasted_iota(jnp.int32, (nd * NMB, windows), 1)
        wanted = row_ids // NMB * PER_INDEX + place.m * NMB + row_ids % NMB
        own = dot_nn((wanted == column_ids).astype(BF), silu(total).astype(BF)).astype(BF)
        for which in range(6):
            rows_ref[...] = dot_nn(own, adaptive[which].astype(BF))

            def move(row):
                index, window = row // NMB, row % NMB
                spot = (index // 2, index % 2, window, slice(which, which + 1))
                mods[spot] = rows_ref[pl.ds(row, 1), :]

            each(nd * NMB, move)
        swap.to_sibling(6, mods.at[:, 1 - place.core], mods_twin)
        swap.wait(6)
        for chip in range(nd // 2):
            for window in range(NMB):
                mods[chip, place.core, window] += mods_twin[chip, window]
        swap.chip_scatter(4, mods, mods_in)

    def modulation():
        swap.wait(4)
        for window in range(NMB):
            mod[window] = mods[dp_id // 2, place.core, window] + jnp.sum(mods_in[:, window], axis=0)
        swap.wait(5)
        token_total[...] = jnp.sum(counts[...], axis=0)
        swap.wait(1)

        def turn_ends(index):
            for which in range(2):
                ends[which, index] = ends_all[index, which].astype(F32).T.astype(BF)

        each(nd, turn_ends)
        embed_mat = ends[0].reshape(D, PATCH)

        def body(window):
            here = span(window, WTOK)
            residual[here, :] = dot_nt(latents[here, :], embed_mat) + positions[...]

        each(NMB, body)
        spill("residual", residual, residual_out)

    def first_norm():
        def body(at):
            window, here = at // PER_WINDOW, span(at, BLOCK)
            normed, _ = row_norm(residual[here, :])
            normed = normed * (1.0 + mod[window, 1:2, :]) + mod[window, 0:1, :]
            n_one[here, :] = normed.astype(BF)

        each(NBLOCK, body)
        transpose_rows(n_one, flipped.at[0])
        spill("n_one", flipped.at[0], n_one_t)

    def qkv_unit(j):
        def body(m):
            qkv[j, m] = dot_nn(n_one[...], tile(j, m)[...]).astype(BF)

        each(nm, body)
        spill(("qkv", j), qkv.at[j], qkv_out.at[j])

    def attend_unit(m):
        def body(window):
            here = span(window, WTOK)
            query, key, value = qkv[0, m, here, :], qkv[1, m, here, :], qkv[2, m, here, :]
            total = jnp.zeros((WTOK, TILE), F32)
            for head in range(TILE // HD):
                lanes = head_lanes(head, BF)
                attn = soft_rows(query * lanes, key, flags[pl.ds(window, 1), :]).astype(BF)
                total = total + dot_nn(attn, value * lanes)
            mixed[m, here, :] = total.astype(BF)

        each(NMB, body)
        if m == nm - 1:
            spill("mixed", mixed, mixed_out)

    def add_nt(source, j, target, fresh):
        def body(at):
            columns = span(at, TILE)
            left = jnp.concatenate([source[m] for m in range(nm)], axis=1)
            right = jnp.concatenate([tile(j, m)[columns, :] for m in range(nm)], axis=1)
            total = dot_nt(left, right)
            target[:, columns] = total if fresh else target[:, columns] + total

        each(D // TILE, body)

    def out_unit():
        add_nt(mixed, 3, branch_one, True)
        spill("branch_one", branch_one, branch_one_out)

        def body(at):
            window, here = at // PER_WINDOW, span(at, BLOCK)
            rows = residual[here, :] + mod[window, 2:3, :] * branch_one[here, :]
            middle[here, :] = rows
            normed, _ = row_norm(rows)
            normed = normed * (1.0 + mod[window, 4:5, :]) + mod[window, 3:4, :]
            n_two[here, :] = normed.astype(BF)

        each(NBLOCK, body)
        spill("middle", middle, middle_out)
        transpose_rows(n_two, flipped.at[1])
        spill("n_two", flipped.at[1], n_two_t)

    def up_unit(f):
        slot = f % 2
        if f >= 2:
            spilled.pop(("slope", f - 2)).wait()

        def body(m):
            up = dot_nn(n_two[...], tile(4 + 2 * f, m)[...])
            value, grad = gelu_parts(up)
            hidden[f, m] = value.astype(BF)
            slope[slot, :, span(m, TILE)] = grad

        each(nm, body)
        spill(("hidden", f), hidden.at[f], hidden_out.at[f])
        spill(("slope", f), slope.at[slot], slope_out.at[f])

    def down_unit(f):
        add_nt(hidden.at[f], 5 + 2 * f, branch_two, f == 0)
        if f == 2:
            spill("branch_two", branch_two, branch_two_out)

    units = {"qkv": qkv_unit, "attend": attend_unit, "out": out_unit, "up": up_unit, "down": down_unit}
    need = {"qkv": lambda j: j, "out": lambda: 3, "up": lambda f: 4 + 2 * f, "down": lambda f: 5 + 2 * f}

    def compute(turn):
        early = (first_swap, time_layers, condition_layers, modulation, first_norm)
        if turn < len(early):
            early[turn]()
        for when, (name, *args) in FORWARD_TURNS:
            if when == turn:
                if name in need:
                    loads[need[name](*args)].wait()
                units[name](*args)

    last = max(when for when, _ in FORWARD_TURNS)
    gather_steps(
        place,
        shard,
        whole,
        send_sems,
        recv_sems,
        local_sems,
        all_here,
        prepare,
        load,
        compute,
        last,
    )
    for copy in spilled.values():
        copy.wait()
    swap.drain()


def forward_blocks(states, *others):
    nd, nm = lax.axis_size("dp"), lax.axis_size("mp")
    nb = nd.bit_length() - 2
    rows = D // nd
    names = list(states)
    slots = 2 * (nm - 1 + 2 * nb) + 1 + 2 * (nm - 1)
    windows = nd * PER_INDEX
    chips = nd // 2
    part = (windows, rows) if windows <= rows else (rows, windows)
    small = [
        ((NMB, 6, D), F32),
        ((2, nd, rows, PATCH), BF),
        ((nd, PER_INDEX, FREQ + 256), F32),
        ((windows, rows), F32),
        ((windows, rows), F32),
        ((PER_INDEX, 128), F32),
    ]
    shapes = [
        ((NJ, nm) + (2,) * nb + (2, rows, TILE), BF),
        ((D, ROWS), BF),
        ((3, nm, ROWS, TILE), BF),
        ((nm, ROWS, TILE), BF),
        ((ROWS, D), F32),
        ((ROWS, D), F32),
        ((D, ROWS), BF),
        ((4, nm, ROWS, TILE), BF),
        ((4, ROWS, D), F32),
        ((ROWS, D), F32),
    ]

    def kernel(*refs):
        named = dict(zip(names, refs))
        forward_kernel(nd, nm, named, *refs[len(names) :])

    return pl.pallas_call(
        kernel,
        out_shape=[
            jax.ShapeDtypeStruct(shape, dtype) for shape, dtype in [((ROWS, D), F32)] + small + shapes
        ],
        in_specs=[pl.BlockSpec(memory_space=pl.ANY)] * len(names)
        + [pl.BlockSpec(memory_space=pltpu.VMEM)] * len(others),
        out_specs=[pl.BlockSpec(memory_space=pl.ANY)]
        + [pl.BlockSpec(memory_space=pltpu.VMEM)] * len(small)
        + [pl.BlockSpec(memory_space=pl.ANY)] * len(shapes),
        scratch_shapes=[
            pltpu.VMEM((ROWS, D), BF),
            pltpu.VMEM((3, nm, ROWS, TILE), BF),
            pltpu.VMEM((nm, ROWS, TILE), BF),
            pltpu.VMEM((ROWS, D), F32),
            pltpu.VMEM((ROWS, D), F32),
            pltpu.VMEM((ROWS, D), BF),
            pltpu.VMEM((2, D, ROWS), BF),
            pltpu.VMEM((4, nm, ROWS, TILE), BF),
            pltpu.VMEM((2, ROWS, D), F32),
            pltpu.VMEM((ROWS, D), F32),
            pltpu.VMEM((4, nm) + (2,) * nb + (2, rows, TILE), BF),
            pltpu.SemaphoreType.DMA((NJ, slots)),
            pltpu.SemaphoreType.DMA((NJ, slots)),
            pltpu.SemaphoreType.DMA((NJ,)),
            pltpu.SemaphoreType.DMA((NJ,)),
            pltpu.SemaphoreType.DMA((24,)),
            pltpu.VMEM((NJ, rows, TILE), BF),
            pltpu.VMEM((3, rows, TILE), F32),
            pltpu.VMEM((TILE, rows), F32),
            pltpu.VMEM((rows, 4 * TILE), F32),
            pltpu.VMEM((4 * TILE, rows), F32),
            pltpu.VMEM((6, rows, D), F32),
            pltpu.VMEM((FREQ, rows), F32),
            pltpu.VMEM((CLASSES + -CLASSES % 128, rows), F32),
            pltpu.VMEM((PATCH, rows), F32),
            pltpu.VMEM((PATCH, rows), F32),
            pltpu.VMEM((2, PATCH, rows), BF),
            pltpu.VMEM((PER_INDEX, FREQ + 256), F32),
            pltpu.VMEM((ROWS, PATCH), BF),
            pltpu.SemaphoreType.DMA((9,)),
            pltpu.VMEM((ROWS, D), F32),
            pltpu.VMEM((chips, 2) + part, F32),
            pltpu.VMEM((chips,) + part, F32),
            pltpu.VMEM((chips - 1,) + part, F32),
            pltpu.VMEM((chips, 2, NMB, 6, D), F32),
            pltpu.VMEM((chips, NMB, 6, D), F32),
            pltpu.VMEM((chips - 1, NMB, 6, D), F32),
            pltpu.VMEM((nd * NMB, D), F32),
            pltpu.VMEM((nm, PER_INDEX, 128), F32),
            pltpu.VMEM((nd, 2, PATCH, rows), BF),
            pltpu.SemaphoreType.DMA((7, max(nd, nm) - 1)),
            pltpu.SemaphoreType.DMA((7, max(nd, nm) - 1)),
        ],
        compiler_params=pltpu.CompilerParams(
            collective_id=0, has_side_effects=True, vmem_limit_bytes=60 << 20
        ),
    )(*states.values(), *others)


PIECES = (5, 4, 7, 6, 9, 8, 11, 10, 3, 2, 1, 0)
BACKWARD_TURNS = (
    (0, ("head",)),
    (1, ("slope", 0)),
    (1, ("spread", 0)),
    (2, ("slope", 1)),
    (2, ("spread", 1)),
    (3, ("slope", 2)),
    (3, ("spread", 2)),
    (4, ("slope", 3)),
    (4, ("spread", 3)),
    (5, ("mid",)),
    (6, ("attend", 0)),
    (7, ("attend", 1)),
    (8, ("attend", 2)),
    (9, ("attend", 3)),
    (10, ("inward", 2)),
    (10, ("inward", 1)),
    (11, ("inward", 0)),
    (11, ("last",)),
    (12, ("swap", 0)),
    (13, ("swap", 1)),
    (14, ("swap", 2)),
)
HELD = 5
TWINS = 3


def backward_kernel(nd, nm, whole, n_one_t, qkv, mixed, branch_one, middle, n_two_t, hidden, slope, branch_two, residual, *refs):
    (mod, mask_in, token_total_in, noise_in, latents_in, both_ends) = refs[:6]
    token_total = token_total_in[0:1, 0:1]
    head_mat = both_ends[1].reshape(D, PATCH)
    (total, loss, ends_sum, all_mod) = refs[6:10]
    (partial, twin_ref, xa, xb, grad_rows, grad_in, grad_low, grad_low_t, normed_t, pool, loaded, z_ref, noise, inverses, row_mask, ends_rows) = refs[10:26]
    rest = refs[26:]
    place = Place(nd, nm)
    nb, core = place.nb, place.core
    part_rows = D // nd
    stage_refs = [rest[2 * step : 2 * step + 2] for step in range(nb)]
    send_sems, recv_sems, free_sem, load_sems = rest[2 * nb : 2 * nb + 4]
    (grad_mod, mod_in, mod_rows, own_mod, ends, ends_twin, ends_in, ends_z) = rest[2 * nb + 4 : -3]
    swap_send, swap_recv, own_sem = rest[-3:]
    swap = Exchange(place, swap_send, swap_recv)
    copies = Copies(send_sems, recv_sems)
    orders = [order[::-1] for order in place.orders]
    all_here = place.greet()
    slot_of = lambda step, half: 1 + 2 * step + half
    z_slot = 1 + 2 * nb
    loads = {}

    def load(name, source, target):
        copy = pltpu.make_async_copy(source, target, load_sems.at[len(loads)])
        copy.start()
        loads[name] = copy

    def load_tiles(j, slot):
        load(("w", j), whole.at[j], loaded.at[slot])

    def tile(slot, m):
        return loaded.at[slot, m].reshape(D, TILE)

    HIDDEN, QUERY, MIXED_GRAD = 4, 5, 8

    load("branch_two", branch_two, xb)
    load("middle", middle, xa)
    load(("hidden", 0), hidden.at[0], pool.at[HIDDEN])
    load("n_two", n_two_t, normed_t)
    load_tiles(5, 0)
    load_tiles(4, 1)
    token_rows(noise_in, noise)
    mask_column(mask_in, row_mask)

    def add_to(target, index, source):
        shape = source.shape[:-2]

        def body(at):
            inner, places = at, []
            for size in shape[::-1]:
                places.append(inner % size)
                inner = inner // size
            places = places[::-1]
            spot = tuple(
                base.start + offset if isinstance(base, pl.Slice) else base
                for base, offset in zip(index, places)
            ) + (core,)
            target[spot] = (target[spot].astype(F32) + source[tuple(places)].astype(F32)).astype(BF)

        each(math.prod(shape), body, 4)

    every = (slice(None),) * (nb + 1)

    def begin(s):
        if s == 0:
            all_here()
        if s >= TWINS:
            pl.semaphore_wait(free_sem, 1)
        source = partial.at[(s % HELD,) + every + (1 - core,)]
        copies.start(s, 0, source, twin_ref.at[s % TWINS], place.sibling)

    def stage(s, step):
        mine = partial.at[s % HELD]
        if step == 0:
            copies.arrived(s, 0)
            add_to(mine, (pl.ds(0, nm),) + (pl.ds(0, 2),) * nb, twin_ref.at[s % TWINS])
            if s + TWINS < NJ:
                pl.semaphore_signal(free_sem, inc=1, device_id=place.sibling, device_id_type=MESH)
        else:
            for half in range(2):
                copies.arrived(s, slot_of(step - 1, half))
                index = place.pick(half, orders[half][step:])
                add_to(mine, index, stage_refs[step - 1][half].at[s])
        if step < nb:
            for half in range(2):
                order = orders[half]
                block = mine.at[place.pick(half, order[step + 1 :], order[step]) + (core,)]
                target = stage_refs[step][half].at[s]
                copies.start(s, slot_of(step, half), block, target, place.across(order[step]))
        else:
            for hops in range(1, nm):
                block = mine.at[place.mine((place.m + hops) % nm) + (core,)]
                copies.start(s, z_slot + hops - 1, block, z_ref.at[s, hops - 1], place.along(hops))

    def finish(s):
        summed = partial[(s % HELD,) + place.mine() + (core,)].astype(F32)
        for hops in range(1, nm):
            copies.arrived(s, z_slot + hops - 1)
            summed = summed + z_ref[s, hops - 1].astype(F32)
        total[PIECES[s]] = summed
        copies.drain(s)

    def weight_grad(s):
        j = PIECES[s]
        if j >= 4 and j % 2 == 1:
            f = (j - 5) // 2
            loads["hidden", f].wait()
            left, right = grad_low_t, HIDDEN
        elif j >= 4:
            left, right = normed_t, (j - 4) // 2
        elif j == 3:
            loads["mixed"].wait()
            left, right = grad_low_t, HIDDEN
        else:
            if j == 2:
                loads["n_one"].wait()
            left, right = normed_t, j

        def body(m):
            grads = dot_nn(left[...], pool[right, m]).astype(BF)
            partial.at[s % HELD, m].reshape(D, TILE)[...] = grads

        each(nm, body)
        if j in (5, 7, 9):
            load(("hidden", f + 1), hidden.at[f + 1], pool.at[HIDDEN])
        if j == 11:
            load("mixed", mixed, pool.at[HIDDEN])
        if j == 10:
            load("n_one", n_one_t, normed_t)

    def rows_of(at):
        return at // PER_WINDOW, span(at, BLOCK)

    def add_mod(window, which, values):
        grad_mod[window, which : which + 1, :] += jnp.sum(values, axis=0, keepdims=True)

    def head_unit():
        loads["branch_two"].wait()
        loads["middle"].wait()
        grad_mod[...] = jnp.zeros_like(grad_mod)

        def norms(at):
            window, here = rows_of(at)
            normed, inverse = row_norm(xa[here, :] + mod[window, 5:6, :] * xb[here, :])
            grad_rows[here, :] = normed
            inverses[here, :] = inverse
            grad_low[here, :] = normed.astype(BF)

        each(NBLOCK, norms)
        error = dot_nn(grad_low[...], head_mat) - noise[...]
        mask = row_mask[...]
        share = jnp.sum(error * error, axis=-1, keepdims=True) * (1.0 / PATCH) * mask
        loss[...] = jnp.sum(share, axis=0, keepdims=True) / token_total
        grad_pred = (2.0 / PATCH * error * mask / token_total).astype(BF)
        ends_rows[PATCH:, :] = dot_tn(grad_pred, grad_low[...])
        grad_in[...] = dot_nt(grad_pred, head_mat)

        def grads(at):
            window, here = rows_of(at)
            grad = norm_back(grad_in[here, :], grad_rows[here, :], inverses[here, :])
            add_mod(window, 5, grad * xb[here, :])
            grad_rows[here, :] = grad
            grad_low[here, :] = (grad * mod[window, 5:6, :]).astype(BF)

        each(NBLOCK, grads)
        transpose_rows(grad_low, grad_low_t)
        load(("slope", 0), slope.at[0], xa)
        load(("slope", 1), slope.at[1], xb)

    def slope_unit(f):
        loads["slope", f].wait()
        loads["w", 5 + 2 * f].wait()
        slopes = xa if f % 2 == 0 else xb

        def body(m):
            grad = dot_nn(grad_low[...], tile(0, m)[...])
            pool[f, m] = (grad * slopes[:, span(m, TILE)]).astype(BF)

        each(nm, body)
        if f + 2 < 4:
            load(("slope", f + 2), slope.at[f + 2], slopes)
        elif f == 2:
            load("middle_again", middle, xa)
        else:
            load("branch_one", branch_one, xb)
        load_tiles(7 + 2 * f if f < 3 else 3, 0)

    def add_rows(which, slot, fresh):
        def body(at):
            columns = span(at, TILE)
            left = jnp.concatenate([pool[which, m] for m in range(nm)], axis=1)
            right = jnp.concatenate([tile(slot, m)[columns, :] for m in range(nm)], axis=1)
            total = dot_nt(left, right)
            grad_in[:, columns] = total if fresh else grad_in[:, columns] + total

        each(D // TILE, body)

    def spread_unit(f):
        loads["w", 4 + 2 * f].wait()
        add_rows(f, 1, f == 0)
        load_tiles(6 + 2 * f if f < 3 else 2, 1)
        if f == 3:
            for part in range(3):
                load(("qkv", part), qkv.at[part], pool.at[QUERY + part])

    def norm_unit(which, after):
        def body(at):
            window, here = rows_of(at)
            normed, inverse = row_norm(xa[here, :])
            grad = grad_in[here, :]
            add_mod(window, which, grad)
            add_mod(window, which + 1, grad * normed)
            grad = grad * (1.0 + mod[window, which + 1 : which + 2, :])
            after(window, here, grad_rows[here, :] + norm_back(grad, normed, inverse))

        each(NBLOCK, body)

    def mid_unit():
        loads["middle_again"].wait()
        loads["branch_one"].wait()

        def after(window, here, grad):
            add_mod(window, 2, grad * xb[here, :])
            grad_rows[here, :] = grad
            grad_low[here, :] = (grad * mod[window, 2:3, :]).astype(BF)

        norm_unit(3, after)
        load("residual", residual, xa)
        loads["w", 3].wait()

        def body(m):
            pool[MIXED_GRAD, m] = dot_nn(grad_low[...], tile(0, m)[...]).astype(BF)

        each(nm, body)
        load_tiles(1, 0)

    def attend_unit(m):
        if m == 0:
            for part in range(3):
                loads["qkv", part].wait()

        def body(window):
            here = span(window, WTOK)
            query, key, value = (pool[QUERY + part, m, here, :] for part in range(3))
            grad_mixed = pool[MIXED_GRAD, m, here, :]
            grads = [jnp.zeros((WTOK, TILE), F32) for _ in range(3)]
            for head in range(TILE // HD):
                lanes = head_lanes(head, BF)
                own_query, own_grad = query * lanes, grad_mixed * lanes
                attn = soft_columns(key, own_query, row_mask[here, :])
                grads[2] = grads[2] + dot_nn(attn.astype(BF), own_grad)
                grad_attn = dot_nt(value, own_grad)
                inner = jnp.sum(attn * grad_attn, axis=0, keepdims=True)
                grad_scores = (attn * (grad_attn - inner)).astype(BF)
                grads[0] = grads[0] + dot_tn(grad_scores, key * lanes)
                grads[1] = grads[1] + dot_nn(grad_scores, own_query)
            pool[0, m, here, :] = (grads[0] * HD ** (-0.5)).astype(BF)
            pool[1, m, here, :] = (grads[1] * HD ** (-0.5)).astype(BF)
            pool[2, m, here, :] = grads[2].astype(BF)

        each(NMB, body)

    def inward_unit(j):
        slot = 1 if j != 1 else 0
        loads["w", j].wait()
        add_rows(j, slot, j == 2)
        if j == 2:
            load_tiles(0, 1)

    def last_unit():
        loads["residual"].wait()

        def after(window, here, grad):
            grad_low[here, :] = grad.astype(BF)

        norm_unit(0, after)
        embed_grad = jnp.zeros((PATCH, D), F32)
        for window in range(NMB):
            here = slice(window * WTOK, (window + 1) * WTOK)
            embed_grad = embed_grad + dot_nn(latents_in[window], grad_low[here, :])
        ends_rows[:PATCH, :] = embed_grad
        for index in range(nd):
            part = ends_rows[:, index * part_rows : (index + 1) * part_rows]
            ends[index // 2, index % 2] = part if part.shape == ends.shape[2:] else part.T
        mod_in[place.m] = grad_mod[...]
        swap.mp_gather(0, grad_mod, mod_in)
        swap.to_sibling(1, ends.at[:, 1 - core], ends_twin)

    own_copy = pltpu.make_async_copy(own_mod, all_mod.at[place.dp_id], own_sem)

    def swap_unit(step):
        if step == 0:
            swap.wait(0)
            for index in range(nm):
                for window in range(NMB):
                    for which in range(6):
                        row = index * NMB + window
                        mod_rows[which, row : row + 1, :] = mod_in[index, window, which : which + 1, :]
            for pair in range(3):
                both = mod_rows[2 * pair : 2 * pair + 2].reshape(2 * PER_INDEX, D)
                own_mod[pair] = both.astype(BF)
            own_copy.start()
            here = all_mod.at[place.dp_id]
            swap.chip_gather(2, own_mod, here)
            swap.to_sibling(3, own_mod, here, nd // 2 - 1)
            swap.wait(1)
            for chip in range(nd // 2):
                ends[chip, core] += ends_twin[chip]
            swap.chip_scatter(4, ends, ends_in)
        if step == 1:
            swap.wait(2)
            for hops in range(1, nd // 2):
                block = all_mod.at[place.chip(nd // 2 - hops) * 2 + core]
                swap.to_sibling(3, block, block, hops - 1)
            swap.wait(4)
            ends_z[place.m] = ends[place.dp_id // 2, core] + jnp.sum(ends_in[...], axis=0)
            swap.mp_gather(5, ends_z.at[place.m], ends_z)
        if step == 2:
            swap.wait(3)
            swap.wait(5)
            summed = jnp.sum(ends_z[...], axis=0)
            ends_sum[...] = summed if summed.shape == ends_sum.shape else summed.T
            own_copy.wait()
            swap.drain()

    units = {
        "head": head_unit,
        "slope": slope_unit,
        "spread": spread_unit,
        "mid": mid_unit,
        "attend": attend_unit,
        "inward": inward_unit,
        "last": last_unit,
        "swap": swap_unit,
    }

    def compute(turn):
        for when, (name, *args) in BACKWARD_TURNS:
            if when == turn:
                units[name](*args)

    last = max(when for when, _ in BACKWARD_TURNS)
    for turn in range(max(NJ + nb + 2, last + 1)):
        if turn == 0:
            compute(turn)
        if 0 < turn <= last and turn in (1, 5, 9):
            compute(turn)
        if turn == 8:
            transpose_rows(grad_low, grad_low_t)
        if turn < NJ:
            if turn == 1:
                loads["n_two"].wait()
            weight_grad(turn)
            begin(turn)
        for step in range(nb + 1):
            if 0 <= turn - 1 - step < NJ:
                stage(turn - 1 - step, step)
        if 0 <= turn - 2 - nb < NJ:
            finish(turn - 2 - nb)
        if turn not in (0, 1, 5, 9):
            compute(turn)


def backward_blocks(saved, residual, *in_vmem):
    nd, nm = lax.axis_size("dp"), lax.axis_size("mp")
    nb = nd.bit_length() - 2
    rows = D // nd
    bits = (2,) * nb
    slots = 2 * nb + nm
    stage_shapes = []
    for step in range(nb):
        high_first = tuple(1 if at <= step else 2 for at in range(nb))
        stage_shapes.append(pltpu.VMEM((NJ, nm // 2) + high_first + (rows, TILE), BF))
        stage_shapes.append(pltpu.VMEM((NJ, nm - nm // 2) + high_first[::-1] + (rows, TILE), BF))
    ends_part = (2 * PATCH, rows) if 2 * PATCH <= rows else (rows, 2 * PATCH)
    in_hbm = (*saved, residual)
    return pl.pallas_call(
        functools.partial(backward_kernel, nd, nm),
        out_shape=[
            jax.ShapeDtypeStruct((NJ, rows, TILE), F32),
            jax.ShapeDtypeStruct((1, 1), F32),
            jax.ShapeDtypeStruct((2 * PATCH, rows), F32),
            jax.ShapeDtypeStruct((nd, 3, 2 * PER_INDEX, D), BF),
        ],
        in_specs=[pl.BlockSpec(memory_space=pl.ANY)] * len(in_hbm)
        + [pl.BlockSpec(memory_space=pltpu.VMEM)] * len(in_vmem),
        out_specs=[pl.BlockSpec(memory_space=pltpu.VMEM)] * 3 + [pl.BlockSpec(memory_space=pl.ANY)],
        scratch_shapes=[
            pltpu.VMEM((HELD, nm) + bits + (2, rows, TILE), BF),
            pltpu.VMEM((TWINS, nm) + bits + (rows, TILE), BF),
            pltpu.VMEM((ROWS, D), F32),
            pltpu.VMEM((ROWS, D), F32),
            pltpu.VMEM((ROWS, D), F32),
            pltpu.VMEM((ROWS, D), F32),
            pltpu.VMEM((ROWS, D), BF),
            pltpu.VMEM((D, ROWS), BF),
            pltpu.VMEM((D, ROWS), BF),
            pltpu.VMEM((9, nm, ROWS, TILE), BF),
            pltpu.VMEM((2, nm) + bits + (2, rows, TILE), BF),
            pltpu.VMEM((NJ, nm - 1, rows, TILE), BF),
            pltpu.VMEM((ROWS, PATCH), F32),
            pltpu.VMEM((ROWS, 1), F32),
            pltpu.VMEM((ROWS, 1), F32),
            pltpu.VMEM((2 * PATCH, D), F32),
            *stage_shapes,
            pltpu.SemaphoreType.DMA((NJ, slots)),
            pltpu.SemaphoreType.DMA((NJ, slots)),
            pltpu.SemaphoreType.REGULAR,
            pltpu.SemaphoreType.DMA((36,)),
            pltpu.VMEM((NMB, 6, D), F32),
            pltpu.VMEM((nm, NMB, 6, D), F32),
            pltpu.VMEM((6, PER_INDEX, D), F32),
            pltpu.VMEM((3, 2 * PER_INDEX, D), BF),
            pltpu.VMEM((nd // 2, 2) + ends_part, F32),
            pltpu.VMEM((nd // 2,) + ends_part, F32),
            pltpu.VMEM((nd // 2 - 1,) + ends_part, F32),
            pltpu.VMEM((nm,) + ends_part, F32),
            pltpu.SemaphoreType.DMA((6, max(nd // 2, nm - 1))),
            pltpu.SemaphoreType.DMA((6, max(nd // 2, nm - 1))),
            pltpu.SemaphoreType.DMA,
        ],
        compiler_params=pltpu.CompilerParams(
            collective_id=1, has_side_effects=True, vmem_limit_bytes=63 << 20
        ),
    )(*in_hbm, *in_vmem)


def tail_kernel(nd, nm, adaptive_state, reduced_in, loss, ends_sum, all_mod_in, front, time_pre, condition, time_out, *refs):
    (adaptive_grad, time_in_grad, time_out_grad, classes_grad, sums) = refs[:5]
    (reduced, all_mod, act_rows, cond_all, terms, term_rows, adaptive) = refs[5:12]
    send_sems, recv_sems, load_sems = refs[12:]
    place = Place(nd, nm)
    swap = Exchange(place, send_sems, recv_sems)
    all_here = place.greet(everyone=True)
    loads = []
    pairs = ((all_mod_in, all_mod), (adaptive_state.at[0], adaptive), (reduced_in, reduced))
    for at, (source, target) in enumerate(pairs):
        loads.append(pltpu.make_async_copy(source, target, load_sems.at[at]))
        loads[at].start()
    dp_id, m = place.dp_id, place.m
    windows, rows = time_pre.shape
    cond_act = silu(condition[...]).reshape(nd, PER_INDEX, rows)
    act_rows[...] = jnp.zeros_like(act_rows)
    for side in range(2):
        act_rows[side, :, side * PER_INDEX : (side + 1) * PER_INDEX, :] = cond_act
    features = front[:, :, :FREQ].reshape(windows, FREQ).astype(BF)
    time_hidden = silu(time_pre[...]).astype(BF)
    pick = label_pick(front, classes_grad.shape[0])
    squares = jnp.zeros((8, 128), F32)
    whole_squares = jnp.zeros((8, 128), F32)

    def square_sum(values):
        return jnp.sum(jnp.sum(values * values, axis=0, keepdims=True), axis=1, keepdims=True)

    loads[0].wait()
    loads[1].wait()
    grad_cond = jnp.zeros((windows, rows), F32)
    for which in range(6):
        pair, side = which // 2, which % 2
        block = all_mod[:, pair].reshape(nd * 2 * PER_INDEX, D)
        act = act_rows[side].reshape(nd * 2 * PER_INDEX, rows).astype(BF)
        gradient = dot_tn(act, block)
        adaptive_grad[which] = gradient
        squares = squares + square_sum(gradient)
        back = dot_nt(block, adaptive[which].astype(BF)).reshape(nd, 2, PER_INDEX, rows)
        grad_cond = grad_cond + back[:, side].reshape(windows, rows)
    grad_cond = (grad_cond * silu_slope(condition[...])).astype(BF)
    cond_all[dp_id] = grad_cond
    all_here()
    swap.dp_gather(0, cond_all.at[dp_id], cond_all)
    gradient = dot_tn(pick, grad_cond)
    classes_grad[...] = gradient
    squares = squares + square_sum(gradient)
    squares = squares + square_sum(ends_sum[...])
    loads[2].wait()

    def add_squares(j, squares):
        return squares + square_sum(reduced[j])

    whole_squares = lax.fori_loop(0, NJ, add_squares, whole_squares)
    swap.wait(0)
    grad_time = jnp.zeros((windows, rows), F32)
    for index in range(nd):
        gradient = dot_tn(time_hidden, cond_all[index])
        time_out_grad[index] = gradient
        squares = squares + square_sum(gradient)
        grad_time = grad_time + dot_nt(cond_all[index], time_out[index])
    grad_time = (grad_time * silu_slope(time_pre[...])).astype(BF)
    gradient = dot_tn(features, grad_time)
    time_in_grad[...] = gradient
    squares = squares + square_sum(gradient)

    terms[dp_id, 0] = squares * (1.0 / nm) + whole_squares
    terms[dp_id, 1] = jnp.zeros((8, 128), F32) + loss[...]
    swap.dp_gather(1, terms.at[dp_id], terms)
    swap.wait(1)
    term_rows[m] = jnp.sum(terms[...], axis=0)
    swap.mp_gather(2, term_rows.at[m], term_rows)
    swap.wait(2)
    sums[...] = jnp.sum(term_rows[...], axis=0)
    swap.drain()


def tail_blocks(*operands):
    nd, nm = lax.axis_size("dp"), lax.axis_size("mp")
    rows = D // nd
    windows = nd * PER_INDEX
    classes = CLASSES + -CLASSES % 128
    shapes = [
        (6, rows, D),
        (FREQ, rows),
        (nd, rows, rows),
        (classes, rows),
        (2, 8, 128),
    ]
    return pl.pallas_call(
        functools.partial(tail_kernel, nd, nm),
        out_shape=[jax.ShapeDtypeStruct(shape, F32) for shape in shapes],
        in_specs=[
            pl.BlockSpec(memory_space=pltpu.HBM if at in (0, 1, 4) else pltpu.VMEM)
            for at in range(len(operands))
        ],
        out_specs=[pl.BlockSpec(memory_space=pltpu.VMEM)] * len(shapes),
        scratch_shapes=[
            pltpu.VMEM((NJ, rows, TILE), F32),
            pltpu.VMEM((nd, 3, 2 * PER_INDEX, D), BF),
            pltpu.VMEM((2, nd, 2 * PER_INDEX, rows), F32),
            pltpu.VMEM((nd, windows, rows), BF),
            pltpu.VMEM((nd, 2, 8, 128), F32),
            pltpu.VMEM((nm, 2, 8, 128), F32),
            pltpu.VMEM((6, rows, D), F32),
            pltpu.SemaphoreType.DMA((3, max(nd, nm) - 1)),
            pltpu.SemaphoreType.DMA((3, max(nd, nm) - 1)),
            pltpu.SemaphoreType.DMA((3,)),
        ],
        compiler_params=pltpu.CompilerParams(
            collective_id=2, has_side_effects=True, vmem_limit_bytes=40 << 20
        ),
    )(*operands)


def adam_update(weight, first, root, gradient, factor):
    clipped = gradient * factor
    first = beta_one * first + (1.0 - beta_one) * clipped
    root = jnp.sqrt(beta_two * root * root + (1.0 - beta_two) * clipped * clipped)
    update = (
        first
        / (1.0 - beta_one**step_count)
        / (root / math.sqrt(1.0 - beta_two**step_count) + adam_eps)
    )
    return weight - learn_rate * (update + weight_decay * weight), first, root


def chunk_rows(rows, lanes):
    limit = max(16, 16384 // max(lanes, 128))
    return max(size for size in range(8, limit + 1, 8) if rows % size == 0)


def adam_kernel(names, *refs):
    count = len(names)
    states = dict(zip(names, refs[:count]))
    reduced, ends, time_in, time_out, classes, adaptive, sums = refs[count : count + 7]
    refs = refs[count + 7 :]
    targets = dict(zip(names, zip(refs[: 2 * count : 2], refs[1 : 2 * count : 2])))
    held = dict(zip(names, refs[2 * count : 3 * count]))
    load_sems, store_sems = refs[3 * count :]
    squares = sums[0, 0:1, 0:1]
    factor = jnp.minimum(1.0, threshold / jnp.sqrt(squares))
    loads, stores = {}, []

    def parts_of(name):
        lead = held[name].shape[1:-2]
        return [(at,) for at in range(lead[0])] if lead else [()]

    for name in names:
        for part in parts_of(name):
            every = (slice(None),) + part
            copy = pltpu.make_async_copy(
                states[name].at[every], held[name].at[every], load_sems.at[len(loads)]
            )
            copy.start()
            loads[name, part] = copy

    def apply(where, gradient):
        ref, part, rows, columns = where
        spot = lambda which: (which,) + part + (rows, columns)
        values = [ref[spot(which)] for which in range(3)]
        for which, value in enumerate(adam_update(*values, gradient, factor)):
            ref[spot(which)] = value

    def store(name, part):
        weight, moments = targets[name]
        copies = (
            (held[name].at[(0,) + part], weight.at[part] if part else weight),
            (held[name].at[(pl.ds(1, 2),) + part], moments.at[(slice(None),) + part]),
        )
        for source, target in copies:
            copy = pltpu.make_async_copy(source, target, store_sems.at[len(stores)])
            copy.start()
            stores.append(copy)

    def rowwise(name, part, source, first_row=0):
        rows, lanes = held[name].shape[-2:]
        size = chunk_rows(rows, lanes)

        def body(at):
            here = span(at, size)
            there = pl.ds(pl.multiple_of(first_row + at * size, 8), size)
            apply((held[name], part, here, slice(None)), source[there, :])

        each(rows // size, body)

    every = slice(None)
    for name in names:
        for part in parts_of(name):
            loads[name, part].wait()
            if name == "adaptive":
                rowwise(name, part, adaptive.at[part[0]])
            elif name == "attention_in":
                rowwise(name, part, reduced.at[part[0]])
            elif name == "expand":
                for f in range(4):
                    columns = slice(f * TILE, (f + 1) * TILE)
                    apply((held[name], part, every, columns), reduced[4 + 2 * f])
            elif name == "contract":
                for f in range(4):
                    rows = slice(f * TILE, (f + 1) * TILE)
                    apply((held[name], part, rows, every), reduced[5 + 2 * f].T)
            elif name == "attention_out":
                apply((held[name], part, every, every), reduced[3].T)
            elif name == "embed":
                rowwise(name, part, ends)
            elif name == "head":
                rowwise(name, part, ends, PATCH)
            else:
                rowwise(name, part, {"time_in": time_in, "time_out": time_out, "classes": classes}[name])
            store(name, part)
    for copy in stores:
        copy.wait()


def adam_blocks(states, *gradients):
    names = list(states)
    shapes = [states[name].shape for name in names]
    outs = []
    for shape in shapes:
        outs += [shape[1:], (2,) + shape[1:]]
    pieces = sum(shape[1] if len(shape) == 4 else 1 for shape in shapes)
    return pl.pallas_call(
        functools.partial(adam_kernel, names),
        out_shape=[jax.ShapeDtypeStruct(shape, F32) for shape in outs],
        in_specs=[pl.BlockSpec(memory_space=pl.ANY)] * len(names)
        + [pl.BlockSpec(memory_space=pltpu.VMEM)] * len(gradients),
        out_specs=[pl.BlockSpec(memory_space=pl.ANY)] * len(outs),
        scratch_shapes=[pltpu.VMEM(shape, F32) for shape in shapes]
        + [pltpu.SemaphoreType.DMA((pieces,)), pltpu.SemaphoreType.DMA((2 * pieces,))],
        compiler_params=pltpu.CompilerParams(vmem_limit_bytes=40 << 20),
    )(*states.values(), *gradients)


def per_device(
    latents,
    noise_target,
    token_mask,
    timesteps,
    labels,
    state_embed,
    state_head,
    state_time_in,
    state_time_out,
    state_classes,
    state_adaptive,
    state_attention_in,
    state_attention_out,
    state_expand,
    state_contract,
):
    nd = lax.axis_size("dp")
    rows = state_attention_in.shape[1]
    states = {
        "adaptive": state_adaptive.transpose(0, 2, 1, 3),
        "attention_in": state_attention_in.transpose(0, 2, 1, 3),
        "expand": state_expand,
        "contract": state_contract,
        "time_out": state_time_out,
        "classes": state_classes,
        "attention_out": state_attention_out,
        "time_in": state_time_in,
        "embed": state_embed,
        "head": state_head.transpose(0, 2, 1),
    }
    lanes = jnp.arange(FREQ + 128)[None, :]
    step_ids = timesteps[0].T.reshape(PER_INDEX, 1).astype(F32)
    label_ids = labels[0].T.reshape(PER_INDEX, 1).astype(F32)
    half_width = FREQ // 2
    frequency = jnp.exp(-math.log(10000.0) * (lanes % half_width).astype(F32) / half_width)
    angles = step_ids * frequency
    features = jnp.where(lanes < half_width, jnp.cos(angles), jnp.sin(angles))
    front = jnp.where(lanes < FREQ, features.astype(BF).astype(F32), label_ids)
    time_out_part = state_time_out[0].astype(BF).reshape(rows, nd, rows).transpose(1, 0, 2)
    flags = token_mask.reshape(NMB, WTOK)
    latent_columns = latents[0].transpose(0, 2, 1)
    noise_columns = noise_target[0].transpose(0, 2, 1)
    residual, mod, ends, front_all, time_pre, condition, token_total, *saved = forward_blocks(
        states, flags, front, latent_columns, window_positions(), time_out_part
    )
    reduced, loss_local, ends_sum, all_mod = backward_blocks(
        saved, residual, mod, flags, token_total, noise_columns, latent_columns, ends
    )
    adaptive_grad, time_in_grad, time_out_grad, classes_grad, sums = tail_blocks(
        states["adaptive"],
        reduced,
        loss_local,
        ends_sum,
        all_mod,
        front_all,
        time_pre,
        condition,
        time_out_part,
    )
    updated = adam_blocks(
        states,
        reduced,
        ends_sum,
        time_in_grad,
        time_out_grad.transpose(1, 0, 2).reshape(rows, D),
        classes_grad,
        adaptive_grad,
        sums,
    )
    new = dict(zip(states, zip(updated[::2], updated[1::2])))
    back = {"adaptive": (1, 0, 2), "attention_in": (1, 0, 2), "head": (1, 0)}
    results = [sums[1, 0, 0], jnp.sqrt(sums[0, 0, 0])]
    order = ("embed", "head", "time_in", "time_out", "classes", "adaptive", "attention_in")
    for name in order + ("attention_out", "expand", "contract"):
        weight, moments = new[name]
        if name in back:
            axes = back[name]
            weight = weight.transpose(axes)
            moments = moments.transpose((0,) + tuple(1 + axis for axis in axes))
        results += [weight, moments]
    return tuple(results)


def solution(mesh):
    in_specs = (
        P("dp", None, "mp", None),
        P("dp", None, "mp", None),
        P("dp", None, "mp"),
        P("dp", None, None),
        P("dp", None, None),
        P(None, None, "dp"),
        P(None, "dp", None),
        P(None, None, "dp"),
        P(None, "dp", None),
        P(None, None, "dp"),
        P(None, "dp", None, None),
        P(None, "dp", None, "mp"),
        P(None, "mp", "dp"),
        P(None, "dp", "mp"),
        P(None, "mp", "dp"),
    )
    out_specs = (
        P(),
        P(),
        P(None, "dp"),
        P(None, None, "dp"),
        P("dp", None),
        P(None, "dp", None),
        P(None, "dp"),
        P(None, None, "dp"),
        P("dp", None),
        P(None, "dp", None),
        P(None, "dp"),
        P(None, None, "dp"),
        P("dp", None, None),
        P(None, "dp", None, None),
        P("dp", None, "mp"),
        P(None, "dp", None, "mp"),
        P("mp", "dp"),
        P(None, "mp", "dp"),
        P("dp", "mp"),
        P(None, "dp", "mp"),
        P("mp", "dp"),
        P(None, "mp", "dp"),
    )
    return jax.shard_map(
        per_device, mesh=mesh, in_specs=in_specs, out_specs=out_specs, check_vma=False
    )
```

```python
import functools
import math

import jax
import jax.numpy as jnp
import numpy as np
from jax import lax
from jax.experimental import pallas as pl
from jax.experimental.pallas import tpu as pltpu
from jax.sharding import PartitionSpec as P

D = 1024
HEADS = 16
HD = 64
PATCH = 32
FREQ = 256
CLASSES = 600
WTOK = 320
NMB = 2
WMB = 4
TILE = 256
NJ = 12
ROWS = NMB * WTOK
MESH = pl.DeviceIdType.MESH
BF = jnp.bfloat16
F32 = jnp.float32


beta_one = 0.9
beta_two = 0.999
adam_eps = 1e-08
learn_rate = 0.15
weight_decay = 0.1
threshold = 0.002
step_count = 10.0


def window_positions():
    half_width = D // 2
    steps = np.arange(half_width, dtype=np.float32)
    frequency = np.exp(np.float32(-math.log(10000.0)) * steps / np.float32(half_width))
    angles = np.arange(WTOK, dtype=np.float32)[:, None] * frequency.astype(np.float32)[None, :]
    table = np.concatenate([np.sin(angles), np.cos(angles)], axis=-1)
    return jnp.asarray(table.astype(np.float32))


def dot_general(a, b, a_dim, b_dim):
    return lax.dot_general(a, b, (((a_dim,), (b_dim,)), ((), ())), preferred_element_type=F32)


def dot_nn(a, b):
    return jnp.dot(a, b, preferred_element_type=F32)


def dot_nt(a, b):
    return dot_general(a, b, 1, 1)


def dot_tn(a, b):
    return dot_general(a, b, 0, 0)


def norm_back(grad, normed, inverse):
    mean_grad = jnp.mean(grad, axis=-1, keepdims=True)
    mean_prod = jnp.mean(grad * normed, axis=-1, keepdims=True)
    return inverse * (grad - mean_grad - normed * mean_prod)


def silu(values):
    return values * jax.nn.sigmoid(values)


def silu_slope(values):
    gate = jax.nn.sigmoid(values)
    return gate * (1.0 + values * (1.0 - gate))


def gelu_parts(up):
    cdf = 0.5 * (1.0 + lax.erf(up * math.sqrt(0.5)))
    pdf = jnp.exp(-0.5 * up * up) * (1.0 / math.sqrt(2.0 * math.pi))
    return up * cdf, cdf + up * pdf


def tokens3(values):
    return values.reshape(NMB, WTOK, -1)


def flip(bits, at):
    return [1 - bit if place == at else bit for place, bit in enumerate(bits)]


class Place:
    def __init__(self, nd, nm):
        self.nm = nm
        self.nb = nd.bit_length() - 2
        dp_id = lax.axis_index("dp")
        self.nd = nd
        self.dp_id = dp_id
        self.m = lax.axis_index("mp")
        self.core = dp_id % 2
        self.bits = [dp_id // (1 << (self.nb - at)) % 2 for at in range(self.nb)]
        self.sibling = {"dp": self.dp_of(self.bits, 1 - self.core), "mp": self.m}
        self.orders = (list(range(self.nb))[::-1], list(range(self.nb)))
        self.halves = (pl.ds(0, nm // 2), pl.ds(nm // 2, nm - nm // 2))

    def dp_of(self, bits, core):
        total = core
        for at, bit in enumerate(bits):
            total = total + bit * (1 << (self.nb - at))
        return total

    def across(self, at):
        return {"dp": self.dp_of(flip(self.bits, at), self.core), "mp": self.m}

    def along(self, hops):
        return {"dp": self.dp_of(self.bits, self.core), "mp": (self.m + hops) % self.nm}

    def facing(self, hops):
        return {"dp": self.chip(hops) * 2 + self.core, "mp": self.m}

    def chip(self, hops):
        return (self.dp_id // 2 + hops) % (self.nd // 2)

    def beside(self, hops):
        return {"dp": (self.dp_id + hops) % self.nd, "mp": self.m}

    def pick(self, half, done, flipped=None):
        where = flip(self.bits, flipped)
        return (self.halves[half],) + tuple(
            pl.ds(0, 2) if at in done else pl.ds(where[at], 1) for at in range(self.nb)
        )

    def mine(self, m=None):
        return (self.m if m is None else m,) + tuple(self.bits)

    def greet(self, everyone=False):
        barrier = pltpu.get_barrier_semaphore()
        if everyone:
            others = [self.beside(hops) for hops in range(1, self.nd)]
        else:
            others = [self.sibling] + [self.facing(hops) for hops in range(1, self.nd // 2)]
        others += [self.along(hops) for hops in range(1, self.nm)]
        for other in others:
            pl.semaphore_signal(barrier, inc=1, device_id=other, device_id_type=MESH)
        return lambda: pl.semaphore_wait(barrier, len(others))


class Copies:
    def __init__(self, send_sems, recv_sems):
        self.send_sems, self.recv_sems = send_sems, recv_sems
        self.started = {}

    def start(self, step, slot, source, target, device):
        copy = pltpu.make_async_remote_copy(
            src_ref=source,
            dst_ref=target,
            send_sem=self.send_sems.at[step, slot],
            recv_sem=self.recv_sems.at[step, slot],
            device_id=device,
            device_id_type=MESH,
        )
        copy.start()
        self.started[step, slot] = copy

    def arrived(self, step, slot):
        self.started[step, slot].wait_recv()

    def drain(self, step=None):
        for key in list(self.started):
            if step is None or key[0] == step:
                self.started.pop(key).wait_send()


class Exchange:
    def __init__(self, place, send_sems, recv_sems):
        self.place = place
        self.copies = Copies(send_sems, recv_sems)

    def dp_gather(self, group, source, target):
        for hops in range(1, self.place.nd):
            here = target.at[self.place.dp_id]
            self.copies.start(group, hops - 1, source, here, self.place.beside(hops))

    def to_sibling(self, group, source, target, slot=0):
        self.copies.start(group, slot, source, target, self.place.sibling)

    def chip_scatter(self, group, source, target):
        for hops in range(1, self.place.nd // 2):
            block = source.at[self.place.chip(hops), self.place.core]
            self.copies.start(group, hops - 1, block, target.at[hops - 1], self.place.facing(hops))

    def chip_gather(self, group, source, target):
        for hops in range(1, self.place.nd // 2):
            self.copies.start(group, hops - 1, source, target, self.place.facing(hops))

    def mp_gather(self, group, source, target):
        for hops in range(1, self.place.nm):
            here = target.at[self.place.m]
            self.copies.start(group, hops - 1, source, here, self.place.along(hops))

    def wait(self, group):
        for step, slot in list(self.copies.started):
            if step == group:
                self.copies.arrived(step, slot)

    def drain(self):
        self.copies.drain()


def gather_steps(
    place, shard, whole, send_sems, recv_sems, local_sems, all_here, prepare, load, compute, last
):
    nm, nb, core = place.nm, place.nb, place.core
    copies = Copies(send_sems, recv_sems)
    stage_slot = lambda stage, half: nm - 1 + 2 * stage + half
    twin = nm - 1 + 2 * nb
    wide = ARRIVALS[-1]
    count = NJ - 1
    late = 2 * twin + 1
    wide_z = lambda part, hops: (0 if part == 0 else late) + hops - 1
    wide_twin = lambda part, hops: (twin if part == 0 else late + nm - 1) + hops - 1
    locals_ = {}

    def begin_local(j):
        here = whole.at[(j,) + place.mine() + (core,)]
        locals_[j] = pltpu.make_async_copy(shard.at[j], here, local_sems.at[j])
        locals_[j].start()
        copies.start(j, 2 * twin, shard.at[j], here, place.sibling)

    def begin(j):
        here = whole.at[(j,) + place.mine() + (core,)]
        for hops in range(1, nm):
            copies.start(j, hops - 1, shard.at[j], here, place.along(hops))
        begin_local(j)

    def half_of_wide(half, bits):
        lanes = pl.ds(half * (TILE // 2), TILE // 2)
        return whole.at[(wide, place.m) + bits + (core, slice(None), lanes)]

    def wide_stage(step):
        if step == 1:
            locals_[wide].wait()
        for half in range(2):
            order = place.orders[half]
            if step > 0:
                copies.arrived(wide, stage_slot(step - 1, half))
            if step == 0:
                source = shard.at[wide, :, pl.ds(half * (TILE // 2), TILE // 2)]
                block = half_of_wide(half, tuple(place.bits))
                copies.start(wide, stage_slot(0, half), source, block, place.across(order[0]))
            elif step < nb:
                block = half_of_wide(half, place.pick(half, order[:step])[1:])
                copies.start(wide, stage_slot(step, half), block, block, place.across(order[step]))
            if step > 0:
                block = half_of_wide(half, place.pick(half, order[: step - 1], order[step - 1])[1:])
                copies.start(wide, twin + stage_slot(step - 1, half), block, block, place.sibling)

    def part_of_wide(part, m):
        return whole.at[(wide, m, pl.ds(part, 1)) + (pl.ds(0, 2),) * (nb - 1) + (core,)]

    def wide_send(part):
        block = part_of_wide(part, place.m)
        for hops in range(1, nm):
            copies.start(wide, wide_z(part, hops), block, block, place.along(hops))

    def wide_pass(part):
        for hops in range(1, nm):
            copies.arrived(wide, wide_z(part, hops))
            block = part_of_wide(part, (place.m + nm - hops) % nm)
            copies.start(wide, wide_twin(part, hops), block, block, place.sibling)

    def stage(j, step):
        if step == 0:
            locals_[j].wait()
            for hops in range(1, nm):
                copies.arrived(j, hops - 1)
        else:
            for half in range(2):
                copies.arrived(j, stage_slot(step - 1, half))
        if step < nb:
            for half in range(2):
                order = place.orders[half]
                block = whole.at[(j,) + place.pick(half, order[:step]) + (core,)]
                copies.start(j, stage_slot(step, half), block, block, place.across(order[step]))
        if step == 0:
            for hops in range(1, nm):
                block = whole.at[(j,) + place.mine((place.m + nm - hops) % nm) + (core,)]
                copies.start(j, twin + hops - 1, block, block, place.sibling)
        else:
            for half in range(2):
                order = place.orders[half]
                block = whole.at[
                    (j,) + place.pick(half, order[: step - 1], order[step - 1]) + (core,)
                ]
                copies.start(j, twin + stage_slot(step - 1, half), block, block, place.sibling)

    def finish(j):
        for slot in range(twin, 2 * twin + 1):
            copies.arrived(j, slot)
        if j == wide:
            for hops in range(1, nm):
                copies.arrived(j, wide_twin(1, hops))
        load(j)

    prepare(ARRIVALS[0])
    prepare(wide)
    all_here()
    begin(ARRIVALS[0])
    wide_stage(0)
    begin_local(wide)
    for at in range(1, 3):
        prepare(ARRIVALS[at])
        begin(ARRIVALS[at])
    prepare(ARRIVALS[3])
    for turn in range(max(NJ + nb + 1, last + nb - 1)):
        for step in range(nb + 1):
            if 0 <= turn - step < count:
                stage(ARRIVALS[turn - step], step)
        if 1 <= turn + 1 <= nb:
            wide_stage(turn + 1)
        if turn + 3 < count:
            begin(ARRIVALS[turn + 3])
        if turn in (nb, nb + 3):
            wide_send(0 if turn == nb else 1)
        if turn in (nb + 5, nb + 8):
            wide_pass(0 if turn == nb + 5 else 1)
        if turn == nb + 10:
            finish(wide)
        if 0 <= turn - 1 - nb < count:
            finish(ARRIVALS[turn - 1 - nb])
        if turn + 4 < count:
            prepare(ARRIVALS[turn + 4])
        compute(turn + 2 - nb)
    copies.drain()


def row_norm(values):
    center = values - jnp.mean(values, axis=-1, keepdims=True)
    inverse = lax.rsqrt(jnp.mean(center * center, axis=-1, keepdims=True) + 1e-06)
    return center * inverse, inverse


def each(count, body, unroll=1):
    lax.fori_loop(0, count, lambda at, carry: (body(at), carry)[1], 0, unroll=math.gcd(count, unroll))


def span(at, size):
    return pl.ds(pl.multiple_of(at * size, size), size)


def head_lanes(head, dtype=F32):
    lanes = lax.broadcasted_iota(jnp.int32, (1, TILE), 1) // HD
    return (lanes == head).astype(dtype)


def soft_rows(query, key, key_bias):
    scores = dot_nt(query, key)
    scores = jnp.where(key_bias > 0, scores, -1e30)
    exponents = jnp.exp(scores - jnp.max(scores, axis=-1, keepdims=True))
    return exponents * (1.0 / jnp.sum(exponents, axis=-1, keepdims=True))


def label_pick(front, count):
    labels = front[:, :, FREQ : FREQ + 1].reshape(-1, 1)
    lanes = lax.broadcasted_iota(jnp.int32, (labels.shape[0], count), 1).astype(F32)
    return (lanes == labels).astype(BF)


PER_INDEX = NMB * WMB
def soft_columns(key, query, key_mask):
    scores = dot_nt(key, query)
    scores = jnp.where(key_mask > 0, scores, -1e30)
    exponents = jnp.exp(scores - jnp.max(scores, axis=0, keepdims=True))
    return exponents * (1.0 / jnp.sum(exponents, axis=0, keepdims=True))


BLOCK = 64
PER_WINDOW = WTOK // BLOCK
NBLOCK = ROWS // BLOCK
LANE_BLOCK = 128


def token_rows(source, target):
    for window in range(NMB):
        target[window * WTOK : (window + 1) * WTOK, :] = source[window].T


def mask_column(source, target):
    for window in range(NMB):
        row = jnp.broadcast_to(source[window : window + 1, :].astype(F32), (8, WTOK))
        target[window * WTOK : (window + 1) * WTOK, :] = row.T[:, 0:1]


def square_sum(values):
    return jnp.sum(jnp.sum(values * values, axis=0, keepdims=True), axis=1, keepdims=True)


def transpose_rows(source, target):
    def body(at):
        target[:, span(at, LANE_BLOCK)] = source[span(at, LANE_BLOCK), :].T

    each(ROWS // LANE_BLOCK, body)


ARRIVALS = (0, 1, 2, 3, 4, 6, 8, 10, 5, 7, 9, 11)
FORWARD_TURNS = (
    (4, ("qkv", 0)),
    (5, ("qkv", 1)),
    (6, ("qkv", 2)),
    (6, ("attend", 0)),
    (7, ("attend", 1)),
    (7, ("attend", 2)),
    (7, ("attend", 3)),
    (8, ("out",)),
    (9, ("up", 0)),
    (9, ("up", 1)),
    (10, ("up", 2)),
    (11, ("up", 3)),
    (12, ("down", 0)),
    (13, ("down", 1)),
    (13, ("down", 3)),
    (14, ("down", 2)),
)


def forward_kernel(nd, nm, states, flags, times_in, latents_in, positions, *refs):
    (residual_out, mod, ends, front, time_pre, condition, token_total, time_out) = refs[:8]
    refs = refs[8:]
    (residual, parts, parts_twin, parts_in, mods, mods_twin, mods_in) = refs[-12:-5]
    (rows_ref, counts, ends_all, swap_send, swap_recv) = refs[-5:]
    (shard, held_in, held_out, held_up, held_down, adaptive, time_in, classes, held_embed, held_head, ends_in, front_in, latents, held_time, state_sems) = refs[-27:-12]
    refs = refs[:-27]
    place = Place(nd, nm)
    swap = Exchange(place, swap_send, swap_recv)
    all_here = place.greet(everyone=True)
    state_loads = {}
    class_pad = classes.shape[0] - CLASSES
    wanted_states = {
        "attn_in": held_in,
        "contract": held_down,
        "embed": held_embed,
        "head": held_head,
        "time_in": time_in,
        "time_out": held_time,
        "classes": classes.at[pl.ds(0, CLASSES)],
        "adapt": adaptive,
        "attn_out": held_out,
        "expand": held_up,
    }
    for at, (name, target) in enumerate(wanted_states.items()):
        state_loads[name] = pltpu.make_async_copy(states[name].at[0], target, state_sems.at[at])
        state_loads[name].start()

    def state_ready(name):
        if name in state_loads:
            state_loads.pop(name).wait()

    def prepare(j):
        if j < 3:
            state_ready("attn_in")
            values = held_in[j]
        elif j == 3:
            state_ready("attn_out")
            values = held_out[...].T
        elif j % 2 == 0:
            state_ready("expand")
            values = held_up[:, (j - 4) // 2 * TILE : (j - 2) // 2 * TILE]
        else:
            state_ready("contract")
            values = held_down[(j - 5) // 2 * TILE : (j - 3) // 2 * TILE, :].T
        shard[j] = values.astype(BF)

    dp_id = place.dp_id
    part_rows = D // nd
    windows = nd * PER_INDEX
    upright = parts.shape[2] == windows
    (whole, n_one_t, qkv_out, mixed_out, branch_one_out, middle_out, n_two_t, hidden_out, slope_out, branch_two_out) = refs[:10]
    (n_one, qkv, mixed, branch_one, middle, n_two, flipped, hidden, slope, branch_two, loaded) = refs[10:21]
    send_sems, recv_sems, local_sems, load_sems, spill_sems = refs[21:]
    spilled, spill_count = {}, []

    def spill(name, source, target):
        copy = pltpu.make_async_copy(source, target, spill_sems.at[len(spill_count)])
        copy.start()
        spill_count.append(name)
        spilled[name] = copy

    loads = {}
    slots = loaded.shape[0]

    def load(j):
        loads[j] = pltpu.make_async_copy(whole.at[j], loaded.at[ARRIVALS.index(j) % slots], load_sems.at[j])
        loads[j].start()

    def tile(j, m):
        return loaded.at[ARRIVALS.index(j) % slots, m].reshape(D, TILE)

    def first_swap():
        state_ready("embed")
        state_ready("head")
        ends_in[0] = held_embed[...].astype(BF)
        ends_in[1] = held_head[...].astype(BF)
        front_in[:, : FREQ + 128] = times_in[...]
        count = jnp.sum(jnp.sum(flags[...].astype(F32), axis=0, keepdims=True), axis=1, keepdims=True)
        front_in[:, FREQ + 128 :] = jnp.broadcast_to(count, (PER_INDEX, 128))
        classes[CLASSES:, :] = jnp.zeros((class_pad, classes.shape[1]), F32)
        token_rows(latents_in, latents)
        front[dp_id] = front_in[...]
        ends_all[dp_id] = ends_in[...]
        swap.dp_gather(0, front_in, front)
        swap.dp_gather(1, ends_in, ends_all)

    def time_layers():
        state_ready("time_out")
        for index in range(nd):
            time_out[index] = held_time[:, index * part_rows : (index + 1) * part_rows].astype(BF)
        swap.wait(0)
        features = front[:, :, :FREQ].reshape(windows, FREQ).astype(BF)
        state_ready("time_in")
        time_pre[...] = dot_nn(features, time_in[...].astype(BF))
        time_hidden = silu(time_pre[...]).astype(BF)
        for index in range(nd):
            if upright:
                parts[index // 2, index % 2] = dot_nn(time_hidden, time_out[index])
            else:
                parts[index // 2, index % 2] = dot_general(time_out[index], time_hidden, 0, 1)
        swap.to_sibling(2, parts.at[:, 1 - place.core], parts_twin)
        counts[place.m] = jnp.sum(front[:, :, FREQ + 128 :], axis=0)
        swap.mp_gather(5, counts.at[place.m], counts)
        swap.wait(2)
        for chip in range(nd // 2):
            parts[chip, place.core] += parts_twin[chip]
        swap.chip_scatter(3, parts, parts_in)

    def condition_layers():
        state_ready("classes")
        state_ready("adapt")
        swap.wait(3)
        total = parts[dp_id // 2, place.core] + jnp.sum(parts_in[...], axis=0)
        total = total if upright else total.T
        total = total + dot_nn(label_pick(front, classes.shape[0]), classes[...].astype(BF))
        condition[...] = total
        row_ids = lax.broadcasted_iota(jnp.int32, (nd * NMB, windows), 0)
        column_ids = lax.broadcasted_iota(jnp.int32, (nd * NMB, windows), 1)
        wanted = row_ids // NMB * PER_INDEX + place.m * NMB + row_ids % NMB
        own = dot_nn((wanted == column_ids).astype(BF), silu(total).astype(BF)).astype(BF)
        for which in range(6):
            rows_ref[...] = dot_nn(own, adaptive[which].astype(BF))

            def move(row):
                index, window = row // NMB, row % NMB
                spot = (index // 2, index % 2, window, slice(which, which + 1))
                mods[spot] = rows_ref[pl.ds(row, 1), :]

            each(nd * NMB, move)
        swap.to_sibling(6, mods.at[:, 1 - place.core], mods_twin)
        swap.wait(6)
        for chip in range(nd // 2):
            for window in range(NMB):
                mods[chip, place.core, window] += mods_twin[chip, window]
        swap.chip_scatter(4, mods, mods_in)

    def modulation():
        swap.wait(4)
        for window in range(NMB):
            mod[window] = mods[dp_id // 2, place.core, window] + jnp.sum(mods_in[:, window], axis=0)
        swap.wait(5)
        token_total[...] = jnp.sum(counts[...], axis=0)
        swap.wait(1)

        def turn_ends(index):
            for which in range(2):
                ends[which, index] = ends_all[index, which].astype(F32).T.astype(BF)

        each(nd, turn_ends)
        embed_mat = ends[0].reshape(D, PATCH)

        def body(window):
            here = span(window, WTOK)
            residual[here, :] = dot_nt(latents[here, :], embed_mat) + positions[...]

        each(NMB, body)
        spill("residual", residual, residual_out)

    def first_norm():
        def body(at):
            window, here = at // PER_WINDOW, span(at, BLOCK)
            normed, _ = row_norm(residual[here, :])
            normed = normed * (1.0 + mod[window, 1:2, :]) + mod[window, 0:1, :]
            n_one[here, :] = normed.astype(BF)

        each(NBLOCK, body)
        transpose_rows(n_one, flipped.at[0])
        spill("n_one", flipped.at[0], n_one_t)

    def qkv_unit(j):
        def body(m):
            qkv[j, m] = dot_nn(n_one[...], tile(j, m)[...]).astype(BF)

        each(nm, body)
        spill(("qkv", j), qkv.at[j], qkv_out.at[j])

    def attend_unit(m):
        def body(window):
            here = span(window, WTOK)
            query, key, value = qkv[0, m, here, :], qkv[1, m, here, :], qkv[2, m, here, :]
            total = jnp.zeros((WTOK, TILE), F32)
            for head in range(TILE // HD):
                lanes = head_lanes(head, BF)
                attn = soft_rows(query * (lanes * HD ** (-0.5)), key, flags[pl.ds(window, 1), :]).astype(BF)
                total = total + dot_nn(attn, value * lanes)
            mixed[m, here, :] = total.astype(BF)

        each(NMB, body)
        if m == nm - 1:
            spill("mixed", mixed, mixed_out)

    def add_nt(source, j, target, fresh):
        def body(at):
            columns = span(at, TILE)
            left = jnp.concatenate([source[m] for m in range(nm)], axis=1)
            right = jnp.concatenate([tile(j, m)[columns, :] for m in range(nm)], axis=1)
            total = dot_nt(left, right)
            target[:, columns] = total if fresh else target[:, columns] + total

        each(D // TILE, body)

    def out_unit():
        add_nt(mixed, 3, branch_one, True)
        spill("br_one", branch_one, branch_one_out)

        def body(at):
            window, here = at // PER_WINDOW, span(at, BLOCK)
            rows = residual[here, :] + mod[window, 2:3, :] * branch_one[here, :]
            middle[here, :] = rows
            normed, _ = row_norm(rows)
            normed = normed * (1.0 + mod[window, 4:5, :]) + mod[window, 3:4, :]
            n_two[here, :] = normed.astype(BF)

        each(NBLOCK, body)
        spill("middle", middle, middle_out)
        transpose_rows(n_two, flipped.at[1])
        spill("n_two", flipped.at[1], n_two_t)

    def up_unit(f):
        slot = f % 2
        if f >= 2:
            spilled.pop(("slope", f - 2)).wait()

        def body(m):
            up = dot_nn(n_two[...], tile(4 + 2 * f, m)[...])
            value, grad = gelu_parts(up)
            hidden[f, m] = value.astype(BF)
            slope[slot, :, span(m, TILE)] = grad

        each(nm, body)
        spill(("hidden", f), hidden.at[f], hidden_out.at[f])
        spill(("slope", f), slope.at[slot], slope_out.at[f])

    def down_unit(f):
        add_nt(hidden.at[f], 5 + 2 * f, branch_two, f == 0)
        if f == 2:
            spill("br_two", branch_two, branch_two_out)

    units = {"qkv": qkv_unit, "attend": attend_unit, "out": out_unit, "up": up_unit, "down": down_unit}
    need = {"qkv": lambda j: j, "out": lambda: 3, "up": lambda f: 4 + 2 * f, "down": lambda f: 5 + 2 * f}

    def compute(turn):
        early = (first_swap, time_layers, condition_layers, modulation, first_norm)
        if turn < len(early):
            early[turn]()
        for when, (name, *args) in FORWARD_TURNS:
            if when == turn:
                if name in need:
                    loads[need[name](*args)].wait()
                units[name](*args)

    last = max(when for when, _ in FORWARD_TURNS)
    gather_steps(
        place,
        shard,
        whole,
        send_sems,
        recv_sems,
        local_sems,
        all_here,
        prepare,
        load,
        compute,
        last,
    )
    for copy in spilled.values():
        copy.wait()
    swap.drain()


def forward_blocks(states, *others):
    nd, nm = lax.axis_size("dp"), lax.axis_size("mp")
    nb = nd.bit_length() - 2
    rows = D // nd
    names = list(states)
    slots = 2 * (nm - 1 + 2 * nb) + 1 + 2 * (nm - 1)
    windows = nd * PER_INDEX
    chips = nd // 2
    part = (windows, rows) if windows <= rows else (rows, windows)
    small = [
        ((NMB, 6, D), F32),
        ((2, nd, rows, PATCH), BF),
        ((nd, PER_INDEX, FREQ + 256), F32),
        ((windows, rows), F32),
        ((windows, rows), F32),
        ((PER_INDEX, 128), F32),
        ((nd, rows, rows), BF),
    ]
    shapes = [
        ((NJ, nm) + (2,) * nb + (2, rows, TILE), BF),
        ((D, ROWS), BF),
        ((3, nm, ROWS, TILE), BF),
        ((nm, ROWS, TILE), BF),
        ((ROWS, D), F32),
        ((ROWS, D), F32),
        ((D, ROWS), BF),
        ((4, nm, ROWS, TILE), BF),
        ((4, ROWS, D), F32),
        ((ROWS, D), F32),
    ]

    def kernel(*refs):
        named = dict(zip(names, refs))
        forward_kernel(nd, nm, named, *refs[len(names) :])

    return pl.pallas_call(
        kernel,
        out_shape=[
            jax.ShapeDtypeStruct(shape, dtype) for shape, dtype in [((ROWS, D), F32)] + small + shapes
        ],
        in_specs=[pl.BlockSpec(memory_space=pl.ANY)] * len(names)
        + [pl.BlockSpec(memory_space=pltpu.VMEM)] * len(others),
        out_specs=[pl.BlockSpec(memory_space=pl.ANY)]
        + [pl.BlockSpec(memory_space=pltpu.VMEM)] * len(small)
        + [pl.BlockSpec(memory_space=pl.ANY)] * len(shapes),
        scratch_shapes=[
            pltpu.VMEM((ROWS, D), BF),
            pltpu.VMEM((3, nm, ROWS, TILE), BF),
            pltpu.VMEM((nm, ROWS, TILE), BF),
            pltpu.VMEM((ROWS, D), F32),
            pltpu.VMEM((ROWS, D), F32),
            pltpu.VMEM((ROWS, D), BF),
            pltpu.VMEM((2, D, ROWS), BF),
            pltpu.VMEM((4, nm, ROWS, TILE), BF),
            pltpu.VMEM((2, ROWS, D), F32),
            pltpu.VMEM((ROWS, D), F32),
            pltpu.VMEM((4, nm) + (2,) * nb + (2, rows, TILE), BF),
            pltpu.SemaphoreType.DMA((NJ, slots)),
            pltpu.SemaphoreType.DMA((NJ, slots)),
            pltpu.SemaphoreType.DMA((NJ,)),
            pltpu.SemaphoreType.DMA((NJ,)),
            pltpu.SemaphoreType.DMA((24,)),
            pltpu.VMEM((NJ, rows, TILE), BF),
            pltpu.VMEM((3, rows, TILE), F32),
            pltpu.VMEM((TILE, rows), F32),
            pltpu.VMEM((rows, 4 * TILE), F32),
            pltpu.VMEM((4 * TILE, rows), F32),
            pltpu.VMEM((6, rows, D), F32),
            pltpu.VMEM((FREQ, rows), F32),
            pltpu.VMEM((CLASSES + -CLASSES % 128, rows), F32),
            pltpu.VMEM((PATCH, rows), F32),
            pltpu.VMEM((PATCH, rows), F32),
            pltpu.VMEM((2, PATCH, rows), BF),
            pltpu.VMEM((PER_INDEX, FREQ + 256), F32),
            pltpu.VMEM((ROWS, PATCH), BF),
            pltpu.VMEM((rows, D), F32),
            pltpu.SemaphoreType.DMA((10,)),
            pltpu.VMEM((ROWS, D), F32),
            pltpu.VMEM((chips, 2) + part, F32),
            pltpu.VMEM((chips,) + part, F32),
            pltpu.VMEM((chips - 1,) + part, F32),
            pltpu.VMEM((chips, 2, NMB, 6, D), F32),
            pltpu.VMEM((chips, NMB, 6, D), F32),
            pltpu.VMEM((chips - 1, NMB, 6, D), F32),
            pltpu.VMEM((nd * NMB, D), F32),
            pltpu.VMEM((nm, PER_INDEX, 128), F32),
            pltpu.VMEM((nd, 2, PATCH, rows), BF),
            pltpu.SemaphoreType.DMA((7, max(nd, nm) - 1)),
            pltpu.SemaphoreType.DMA((7, max(nd, nm) - 1)),
        ],
        compiler_params=pltpu.CompilerParams(
            collective_id=0, has_side_effects=True, vmem_limit_bytes=60 << 20
        ),
    )(*states.values(), *others)


PIECES = (5, 4, 7, 6, 9, 8, 11, 10, 3, 2, 1, 0)
BACKWARD_TURNS = (
    (0, ("head",)),
    (1, ("slope", 0)),
    (1, ("spread", 0)),
    (2, ("slope", 1)),
    (2, ("spread", 1)),
    (3, ("slope", 2)),
    (3, ("spread", 2)),
    (4, ("slope", 3)),
    (4, ("spread", 3)),
    (5, ("mid",)),
    (6, ("attend", 0)),
    (7, ("attend", 1)),
    (8, ("attend", 2)),
    (9, ("attend", 3)),
    (10, ("inward", 2)),
    (10, ("inward", 1)),
    (11, ("inward", 0)),
    (11, ("last",)),
    (12, ("swap", 0)),
    (13, ("swap", 1)),
    (14, ("swap", 2)),
)
HELD = 5
TWINS = 3


def backward_kernel(nd, nm, whole, n_one_t, qkv, mixed, branch_one, middle, n_two_t, hidden, slope, branch_two, residual, *refs):
    (mod, mask_in, token_total_in, noise_in, latents_in, both_ends) = refs[:6]
    token_total = token_total_in[0:1, 0:1]
    head_mat = both_ends[1].reshape(D, PATCH)
    (total, loss, squares, ends_sum, all_mod) = refs[6:11]
    (partial, twin_ref, xa, xb, grad_rows, grad_in, grad_low, grad_low_t, normed_t, pool, loaded, z_ref, noise, inverses, row_mask, ends_rows) = refs[11:27]
    rest = refs[27:]
    place = Place(nd, nm)
    nb, core = place.nb, place.core
    part_rows = D // nd
    stage_refs = [rest[2 * step : 2 * step + 2] for step in range(nb)]
    send_sems, recv_sems, free_sem, load_sems = rest[2 * nb : 2 * nb + 4]
    (grad_mod, mod_in, mod_rows, own_mod, ends, ends_twin, ends_in, ends_z) = rest[2 * nb + 4 : -3]
    swap_send, swap_recv, own_sem = rest[-3:]
    swap = Exchange(place, swap_send, swap_recv)
    copies = Copies(send_sems, recv_sems)
    orders = [order[::-1] for order in place.orders]
    all_here = place.greet()
    slot_of = lambda step, half: 1 + 2 * step + half
    z_slot = 1 + 2 * nb
    loads = {}

    def load(name, source, target):
        copy = pltpu.make_async_copy(source, target, load_sems.at[len(loads)])
        copy.start()
        loads[name] = copy

    def load_tiles(j, slot):
        load(("w", j), whole.at[j], loaded.at[slot])

    def tile(slot, m):
        return loaded.at[slot, m].reshape(D, TILE)

    HIDDEN, QUERY, MIXED_GRAD = 4, 5, 8

    load("br_two", branch_two, xb)
    load("middle", middle, xa)
    load(("hidden", 0), hidden.at[0], pool.at[HIDDEN])
    load("n_two", n_two_t, normed_t)
    load_tiles(5, 0)
    load_tiles(4, 1)
    token_rows(noise_in, noise)
    mask_column(mask_in, row_mask)

    def add_to(target, index, source):
        shape = source.shape[:-2]

        def body(at):
            inner, places = at, []
            for size in shape[::-1]:
                places.append(inner % size)
                inner = inner // size
            places = places[::-1]
            spot = tuple(
                base.start + offset if isinstance(base, pl.Slice) else base
                for base, offset in zip(index, places)
            ) + (core,)
            target[spot] = target[spot] + source[tuple(places)]

        each(math.prod(shape), body, 4)

    every = (slice(None),) * (nb + 1)

    def begin(s):
        if s == 0:
            all_here()
        if s >= TWINS:
            pl.semaphore_wait(free_sem, 1)
        source = partial.at[(s % HELD,) + every + (1 - core,)]
        copies.start(s, 0, source, twin_ref.at[s % TWINS], place.sibling)

    def stage(s, step):
        mine = partial.at[s % HELD]
        if step == 0:
            copies.arrived(s, 0)
            add_to(mine, (pl.ds(0, nm),) + (pl.ds(0, 2),) * nb, twin_ref.at[s % TWINS])
            if s + TWINS < NJ:
                pl.semaphore_signal(free_sem, inc=1, device_id=place.sibling, device_id_type=MESH)
        else:
            for half in range(2):
                copies.arrived(s, slot_of(step - 1, half))
                index = place.pick(half, orders[half][step:])
                add_to(mine, index, stage_refs[step - 1][half].at[s])
        if step < nb:
            for half in range(2):
                order = orders[half]
                block = mine.at[place.pick(half, order[step + 1 :], order[step]) + (core,)]
                target = stage_refs[step][half].at[s]
                copies.start(s, slot_of(step, half), block, target, place.across(order[step]))
        else:
            for hops in range(1, nm):
                block = mine.at[place.mine((place.m + hops) % nm) + (core,)]
                copies.start(s, z_slot + hops - 1, block, z_ref.at[s, hops - 1], place.along(hops))

    def finish(s):
        summed = partial[(s % HELD,) + place.mine() + (core,)].astype(F32)
        for hops in range(1, nm):
            copies.arrived(s, z_slot + hops - 1)
            summed = summed + z_ref[s, hops - 1].astype(F32)
        total[PIECES[s]] = summed
        squares[...] += square_sum(summed)
        copies.drain(s)

    def weight_grad(s):
        j = PIECES[s]
        if j >= 4 and j % 2 == 1:
            f = (j - 5) // 2
            loads["hidden", f].wait()
            left, right = grad_low_t, HIDDEN
        elif j >= 4:
            left, right = normed_t, (j - 4) // 2
        elif j == 3:
            loads["mixed"].wait()
            left, right = grad_low_t, HIDDEN
        else:
            if j == 2:
                loads["n_one"].wait()
            left, right = normed_t, j

        def body(m):
            grads = dot_nn(left[...], pool[right, m]).astype(BF)
            partial.at[s % HELD, m].reshape(D, TILE)[...] = grads

        each(nm, body)
        if j in (5, 7, 9):
            load(("hidden", f + 1), hidden.at[f + 1], pool.at[HIDDEN])
        if j == 11:
            load("mixed", mixed, pool.at[HIDDEN])
        if j == 10:
            load("n_one", n_one_t, normed_t)

    def rows_of(at):
        return at // PER_WINDOW, span(at, BLOCK)

    def add_mod(window, which, values):
        grad_mod[window, which : which + 1, :] += jnp.sum(values, axis=0, keepdims=True)

    def head_unit():
        loads["br_two"].wait()
        loads["middle"].wait()
        grad_mod[...] = jnp.zeros_like(grad_mod)
        squares[...] = jnp.zeros_like(squares)

        def norms(at):
            window, here = rows_of(at)
            normed, inverse = row_norm(xa[here, :] + mod[window, 5:6, :] * xb[here, :])
            grad_rows[here, :] = normed
            inverses[here, :] = inverse
            grad_low[here, :] = normed.astype(BF)

        each(NBLOCK, norms)
        error = dot_nn(grad_low[...], head_mat) - noise[...]
        mask = row_mask[...]
        share = jnp.sum(error * error, axis=-1, keepdims=True) * (1.0 / PATCH) * mask
        loss[...] = jnp.sum(share, axis=0, keepdims=True) / token_total
        grad_pred = (2.0 / PATCH * error * mask / token_total).astype(BF)
        ends_rows[PATCH:, :] = dot_tn(grad_pred, grad_low[...])
        grad_in[...] = dot_nt(grad_pred, head_mat)

        def grads(at):
            window, here = rows_of(at)
            grad = norm_back(grad_in[here, :], grad_rows[here, :], inverses[here, :])
            add_mod(window, 5, grad * xb[here, :])
            grad_rows[here, :] = grad
            grad_low[here, :] = (grad * mod[window, 5:6, :]).astype(BF)

        each(NBLOCK, grads)
        transpose_rows(grad_low, grad_low_t)
        load(("slope", 0), slope.at[0], xa)
        load(("slope", 1), slope.at[1], xb)

    def slope_unit(f):
        loads["slope", f].wait()
        loads["w", 5 + 2 * f].wait()
        slopes = xa if f % 2 == 0 else xb

        def body(m):
            grad = dot_nn(grad_low[...], tile(0, m)[...])
            pool[f, m] = (grad * slopes[:, span(m, TILE)]).astype(BF)

        each(nm, body)
        if f + 2 < 4:
            load(("slope", f + 2), slope.at[f + 2], slopes)
        elif f == 2:
            load("middle2", middle, xa)
        else:
            load("br_one", branch_one, xb)
        load_tiles(7 + 2 * f if f < 3 else 3, 0)

    def add_rows(which, slot, fresh):
        def body(at):
            columns = span(at, TILE)
            left = jnp.concatenate([pool[which, m] for m in range(nm)], axis=1)
            right = jnp.concatenate([tile(slot, m)[columns, :] for m in range(nm)], axis=1)
            total = dot_nt(left, right)
            grad_in[:, columns] = total if fresh else grad_in[:, columns] + total

        each(D // TILE, body)

    def spread_unit(f):
        loads["w", 4 + 2 * f].wait()
        add_rows(f, 1, f == 0)
        load_tiles(6 + 2 * f if f < 3 else 2, 1)
        if f == 3:
            for part in range(3):
                load(("qkv", part), qkv.at[part], pool.at[QUERY + part])

    def norm_unit(which, after):
        def body(at):
            window, here = rows_of(at)
            normed, inverse = row_norm(xa[here, :])
            grad = grad_in[here, :]
            add_mod(window, which, grad)
            add_mod(window, which + 1, grad * normed)
            grad = grad * (1.0 + mod[window, which + 1 : which + 2, :])
            after(window, here, grad_rows[here, :] + norm_back(grad, normed, inverse))

        each(NBLOCK, body)

    def mid_unit():
        loads["middle2"].wait()
        loads["br_one"].wait()

        def after(window, here, grad):
            add_mod(window, 2, grad * xb[here, :])
            grad_rows[here, :] = grad
            grad_low[here, :] = (grad * mod[window, 2:3, :]).astype(BF)

        norm_unit(3, after)
        load("residual", residual, xa)
        loads["w", 3].wait()

        def body(m):
            pool[MIXED_GRAD, m] = dot_nn(grad_low[...], tile(0, m)[...]).astype(BF)

        each(nm, body)
        load_tiles(1, 0)

    def attend_unit(m):
        if m == 0:
            for part in range(3):
                loads["qkv", part].wait()

        def body(window):
            here = span(window, WTOK)
            query, key, value = (pool[QUERY + part, m, here, :] for part in range(3))
            grad_mixed = pool[MIXED_GRAD, m, here, :]
            grads = [jnp.zeros((WTOK, TILE), F32) for _ in range(3)]
            for head in range(TILE // HD):
                lanes = head_lanes(head, BF)
                scaled = lanes * HD ** (-0.5)
                own_query, own_grad = query * scaled, grad_mixed * lanes
                attn = soft_columns(key, own_query, row_mask[here, :])
                grads[2] = grads[2] + dot_nn(attn.astype(BF), own_grad)
                grad_attn = dot_nt(value, own_grad)
                inner = jnp.sum(attn * grad_attn, axis=0, keepdims=True)
                grad_scores = (attn * (grad_attn - inner)).astype(BF)
                grads[0] = grads[0] + dot_tn(grad_scores, key * scaled)
                grads[1] = grads[1] + dot_nn(grad_scores, own_query)
            pool[0, m, here, :] = grads[0].astype(BF)
            pool[1, m, here, :] = grads[1].astype(BF)
            pool[2, m, here, :] = grads[2].astype(BF)

        each(NMB, body)

    def inward_unit(j):
        slot = 1 if j != 1 else 0
        loads["w", j].wait()
        add_rows(j, slot, j == 2)
        if j == 2:
            load_tiles(0, 1)

    def last_unit():
        loads["residual"].wait()

        def after(window, here, grad):
            grad_low[here, :] = grad.astype(BF)

        norm_unit(0, after)
        embed_grad = jnp.zeros((PATCH, D), F32)
        for window in range(NMB):
            here = slice(window * WTOK, (window + 1) * WTOK)
            embed_grad = embed_grad + dot_nn(latents_in[window], grad_low[here, :])
        ends_rows[:PATCH, :] = embed_grad
        for index in range(nd):
            part = ends_rows[:, index * part_rows : (index + 1) * part_rows]
            ends[index // 2, index % 2] = part if part.shape == ends.shape[2:] else part.T
        mod_in[place.m] = grad_mod[...]
        swap.mp_gather(0, grad_mod, mod_in)
        swap.to_sibling(1, ends.at[:, 1 - core], ends_twin)

    own_copy = pltpu.make_async_copy(own_mod, all_mod.at[place.dp_id], own_sem)

    def swap_unit(step):
        if step == 0:
            swap.wait(0)
            for index in range(nm):
                for window in range(NMB):
                    for which in range(6):
                        row = index * NMB + window
                        mod_rows[which, row : row + 1, :] = mod_in[index, window, which : which + 1, :]
            for pair in range(3):
                both = mod_rows[2 * pair : 2 * pair + 2].reshape(2 * PER_INDEX, D)
                own_mod[pair] = both.astype(BF)
            own_copy.start()
            here = all_mod.at[place.dp_id]
            swap.chip_gather(2, own_mod, here)
            swap.to_sibling(3, own_mod, here, nd // 2 - 1)
            swap.wait(1)
            for chip in range(nd // 2):
                ends[chip, core] += ends_twin[chip]
            swap.chip_scatter(4, ends, ends_in)
        if step == 1:
            swap.wait(2)
            for hops in range(1, nd // 2):
                block = all_mod.at[place.chip(nd // 2 - hops) * 2 + core]
                swap.to_sibling(3, block, block, hops - 1)
            swap.wait(4)
            ends_z[place.m] = ends[place.dp_id // 2, core] + jnp.sum(ends_in[...], axis=0)
            swap.mp_gather(5, ends_z.at[place.m], ends_z)
        if step == 2:
            swap.wait(3)
            swap.wait(5)
            summed = jnp.sum(ends_z[...], axis=0)
            ends_sum[...] = summed if summed.shape == ends_sum.shape else summed.T
            squares[...] += square_sum(summed) * (1.0 / nm)
            own_copy.wait()
            swap.drain()

    units = {
        "head": head_unit,
        "slope": slope_unit,
        "spread": spread_unit,
        "mid": mid_unit,
        "attend": attend_unit,
        "inward": inward_unit,
        "last": last_unit,
        "swap": swap_unit,
    }

    def compute(turn):
        for when, (name, *args) in BACKWARD_TURNS:
            if when == turn:
                units[name](*args)

    last = max(when for when, _ in BACKWARD_TURNS)
    for turn in range(max(NJ + nb + 2, last + 1)):
        if turn == 0:
            compute(turn)
        if 0 < turn <= last and turn in (1, 5, 9):
            compute(turn)
        if turn == 8:
            transpose_rows(grad_low, grad_low_t)
        if turn < NJ:
            if turn == 1:
                loads["n_two"].wait()
            weight_grad(turn)
            begin(turn)
        for step in range(nb + 1):
            if 0 <= turn - 1 - step < NJ:
                stage(turn - 1 - step, step)
        if 0 <= turn - 2 - nb < NJ:
            finish(turn - 2 - nb)
        if turn not in (0, 1, 5, 9):
            compute(turn)


def backward_blocks(saved, residual, *in_vmem):
    nd, nm = lax.axis_size("dp"), lax.axis_size("mp")
    nb = nd.bit_length() - 2
    rows = D // nd
    bits = (2,) * nb
    slots = 2 * nb + nm
    stage_shapes = []
    for step in range(nb):
        high_first = tuple(1 if at <= step else 2 for at in range(nb))
        stage_shapes.append(pltpu.VMEM((NJ, nm // 2) + high_first + (rows, TILE), BF))
        stage_shapes.append(pltpu.VMEM((NJ, nm - nm // 2) + high_first[::-1] + (rows, TILE), BF))
    ends_part = (2 * PATCH, rows) if 2 * PATCH <= rows else (rows, 2 * PATCH)
    in_hbm = (*saved, residual)
    return pl.pallas_call(
        functools.partial(backward_kernel, nd, nm),
        out_shape=[
            jax.ShapeDtypeStruct((NJ, rows, TILE), F32),
            jax.ShapeDtypeStruct((1, 1), F32),
            jax.ShapeDtypeStruct((1, 1), F32),
            jax.ShapeDtypeStruct((2 * PATCH, rows), F32),
            jax.ShapeDtypeStruct((nd, 3, 2 * PER_INDEX, D), BF),
        ],
        in_specs=[pl.BlockSpec(memory_space=pl.ANY)] * len(in_hbm)
        + [pl.BlockSpec(memory_space=pltpu.VMEM)] * len(in_vmem),
        out_specs=[pl.BlockSpec(memory_space=pltpu.VMEM)] * 4 + [pl.BlockSpec(memory_space=pl.ANY)],
        scratch_shapes=[
            pltpu.VMEM((HELD, nm) + bits + (2, rows, TILE), BF),
            pltpu.VMEM((TWINS, nm) + bits + (rows, TILE), BF),
            pltpu.VMEM((ROWS, D), F32),
            pltpu.VMEM((ROWS, D), F32),
            pltpu.VMEM((ROWS, D), F32),
            pltpu.VMEM((ROWS, D), F32),
            pltpu.VMEM((ROWS, D), BF),
            pltpu.VMEM((D, ROWS), BF),
            pltpu.VMEM((D, ROWS), BF),
            pltpu.VMEM((9, nm, ROWS, TILE), BF),
            pltpu.VMEM((2, nm) + bits + (2, rows, TILE), BF),
            pltpu.VMEM((NJ, nm - 1, rows, TILE), BF),
            pltpu.VMEM((ROWS, PATCH), F32),
            pltpu.VMEM((ROWS, 1), F32),
            pltpu.VMEM((ROWS, 1), F32),
            pltpu.VMEM((2 * PATCH, D), F32),
            *stage_shapes,
            pltpu.SemaphoreType.DMA((NJ, slots)),
            pltpu.SemaphoreType.DMA((NJ, slots)),
            pltpu.SemaphoreType.REGULAR,
            pltpu.SemaphoreType.DMA((36,)),
            pltpu.VMEM((NMB, 6, D), F32),
            pltpu.VMEM((nm, NMB, 6, D), F32),
            pltpu.VMEM((6, PER_INDEX, D), F32),
            pltpu.VMEM((3, 2 * PER_INDEX, D), BF),
            pltpu.VMEM((nd // 2, 2) + ends_part, F32),
            pltpu.VMEM((nd // 2,) + ends_part, F32),
            pltpu.VMEM((nd // 2 - 1,) + ends_part, F32),
            pltpu.VMEM((nm,) + ends_part, F32),
            pltpu.SemaphoreType.DMA((6, max(nd // 2, nm - 1))),
            pltpu.SemaphoreType.DMA((6, max(nd // 2, nm - 1))),
            pltpu.SemaphoreType.DMA,
        ],
        compiler_params=pltpu.CompilerParams(
            collective_id=1, has_side_effects=True, vmem_limit_bytes=63 << 20
        ),
    )(*in_hbm, *in_vmem)


def tail_kernel(nd, nm, adaptive_state, loss, block_squares, all_mod_in, front, time_pre, condition, time_out, *refs):
    (adaptive_grad, time_in_grad, time_out_grad, classes_grad, sums) = refs[:5]
    (all_mod, act_rows, cond_all, terms, term_rows, adaptive) = refs[5:11]
    send_sems, recv_sems, load_sems = refs[11:]
    place = Place(nd, nm)
    swap = Exchange(place, send_sems, recv_sems)
    all_here = place.greet(everyone=True)
    loads = []
    pairs = ((all_mod_in, all_mod), (adaptive_state.at[0], adaptive))
    for at, (source, target) in enumerate(pairs):
        loads.append(pltpu.make_async_copy(source, target, load_sems.at[at]))
        loads[at].start()
    dp_id, m = place.dp_id, place.m
    windows, rows = time_pre.shape
    cond_act = silu(condition[...]).reshape(nd, PER_INDEX, rows)
    act_rows[...] = jnp.zeros_like(act_rows)
    for side in range(2):
        act_rows[side, :, side * PER_INDEX : (side + 1) * PER_INDEX, :] = cond_act
    features = front[:, :, :FREQ].reshape(windows, FREQ).astype(BF)
    time_hidden = silu(time_pre[...]).astype(BF)
    pick = label_pick(front, classes_grad.shape[0])
    squares = jnp.zeros((8, 128), F32)

    term_rows[m, 0] = jnp.zeros((8, 128), F32) + block_squares[...]
    term_rows[m, 1] = jnp.zeros((8, 128), F32) + loss[...]
    all_here()
    swap.mp_gather(2, term_rows.at[m], term_rows)
    loads[0].wait()
    loads[1].wait()
    grad_cond = jnp.zeros((windows, rows), F32)
    for which in range(6):
        pair, side = which // 2, which % 2
        block = all_mod[:, pair].reshape(nd * 2 * PER_INDEX, D)
        act = act_rows[side].reshape(nd * 2 * PER_INDEX, rows).astype(BF)
        gradient = dot_tn(act, block)
        adaptive_grad[which] = gradient
        squares = squares + square_sum(gradient)
        back = dot_nt(block, adaptive[which].astype(BF)).reshape(nd, 2, PER_INDEX, rows)
        grad_cond = grad_cond + back[:, side].reshape(windows, rows)
    grad_cond = (grad_cond * silu_slope(condition[...])).astype(BF)
    cond_all[dp_id] = grad_cond
    swap.dp_gather(0, cond_all.at[dp_id], cond_all)
    gradient = dot_tn(pick, grad_cond)
    classes_grad[...] = gradient
    squares = squares + square_sum(gradient)
    swap.wait(0)
    grad_time = jnp.zeros((windows, rows), F32)
    for index in range(nd):
        gradient = dot_tn(time_hidden, cond_all[index])
        time_out_grad[:, index * rows : (index + 1) * rows] = gradient
        squares = squares + square_sum(gradient)
        grad_time = grad_time + dot_nt(cond_all[index], time_out[index])
    grad_time = (grad_time * silu_slope(time_pre[...])).astype(BF)
    gradient = dot_tn(features, grad_time)
    time_in_grad[...] = gradient
    squares = squares + square_sum(gradient)

    swap.wait(2)
    term_sums = jnp.sum(term_rows[...], axis=0)
    terms[dp_id, 0] = squares + term_sums[0]
    terms[dp_id, 1] = term_sums[1]
    swap.dp_gather(1, terms.at[dp_id], terms)
    swap.wait(1)
    sums[...] = jnp.sum(terms[...], axis=0)
    swap.drain()


def tail_blocks(*operands):
    nd, nm = lax.axis_size("dp"), lax.axis_size("mp")
    rows = D // nd
    windows = nd * PER_INDEX
    classes = CLASSES + -CLASSES % 128
    shapes = [
        (6, rows, D),
        (FREQ, rows),
        (rows, D),
        (classes, rows),
        (2, 8, 128),
    ]
    return pl.pallas_call(
        functools.partial(tail_kernel, nd, nm),
        out_shape=[jax.ShapeDtypeStruct(shape, F32) for shape in shapes],
        in_specs=[
            pl.BlockSpec(memory_space=pl.ANY if at in (0, 3) else pltpu.VMEM)
            for at in range(len(operands))
        ],
        out_specs=[pl.BlockSpec(memory_space=pltpu.VMEM)] * len(shapes),
        scratch_shapes=[
            pltpu.VMEM((nd, 3, 2 * PER_INDEX, D), BF),
            pltpu.VMEM((2, nd, 2 * PER_INDEX, rows), F32),
            pltpu.VMEM((nd, windows, rows), BF),
            pltpu.VMEM((nd, 2, 8, 128), F32),
            pltpu.VMEM((nm, 2, 8, 128), F32),
            pltpu.VMEM((6, rows, D), F32),
            pltpu.SemaphoreType.DMA((3, max(nd, nm) - 1)),
            pltpu.SemaphoreType.DMA((3, max(nd, nm) - 1)),
            pltpu.SemaphoreType.DMA((2,)),
        ],
        compiler_params=pltpu.CompilerParams(
            collective_id=2, has_side_effects=True, vmem_limit_bytes=40 << 20
        ),
    )(*operands)


def adam_update(weight, first, root, gradient, factor):
    clipped = gradient * factor
    first = beta_one * first + (1.0 - beta_one) * clipped
    root = jnp.sqrt(beta_two * root * root + (1.0 - beta_two) * clipped * clipped)
    update = (
        first
        / (1.0 - beta_one**step_count)
        / (root / math.sqrt(1.0 - beta_two**step_count) + adam_eps)
    )
    return weight - learn_rate * (update + weight_decay * weight), first, root


def chunk_rows(rows, lanes):
    limit = max(16, 16384 // max(lanes, 128))
    return max(size for size in range(8, limit + 1, 8) if rows % size == 0)


def adam_kernel(names, *refs):
    count = len(names)
    states = dict(zip(names, refs[:count]))
    reduced, ends, time_in, time_out, classes, adaptive, sums = refs[count : count + 7]
    refs = refs[count + 7 :]
    targets = dict(zip(names, zip(refs[: 2 * count : 2], refs[1 : 2 * count : 2])))
    held = dict(zip(names, refs[2 * count : 3 * count]))
    load_sems, store_sems = refs[3 * count :]
    squares = sums[0, 0:1, 0:1]
    factor = jnp.minimum(1.0, threshold / jnp.sqrt(squares))
    loads, stores = {}, []

    def parts_of(name):
        lead = held[name].shape[1:-2]
        return [(at,) for at in range(lead[0])] if lead else [()]

    for name in names:
        for part in parts_of(name):
            every = (slice(None),) + part
            copy = pltpu.make_async_copy(
                states[name].at[every], held[name].at[every], load_sems.at[len(loads)]
            )
            copy.start()
            loads[name, part] = copy

    def apply(where, gradient):
        ref, part, rows, columns = where
        spot = lambda which: (which,) + part + (rows, columns)
        values = [ref[spot(which)] for which in range(3)]
        for which, value in enumerate(adam_update(*values, gradient, factor)):
            ref[spot(which)] = value

    def store(name, part):
        weight, moments = targets[name]
        copies = (
            (held[name].at[(0,) + part], weight.at[part] if part else weight),
            (held[name].at[(pl.ds(1, 2),) + part], moments.at[(slice(None),) + part]),
        )
        for source, target in copies:
            copy = pltpu.make_async_copy(source, target, store_sems.at[len(stores)])
            copy.start()
            stores.append(copy)

    def rowwise(name, part, source, first_row=0):
        rows, lanes = held[name].shape[-2:]
        size = chunk_rows(rows, lanes)

        def body(at):
            here = span(at, size)
            there = pl.ds(pl.multiple_of(first_row + at * size, 8), size)
            apply((held[name], part, here, slice(None)), source[there, :])

        each(rows // size, body)

    every = slice(None)
    for name in names:
        for part in parts_of(name):
            loads[name, part].wait()
            if name == "adapt":
                rowwise(name, part, adaptive.at[part[0]])
            elif name == "attn_in":
                rowwise(name, part, reduced.at[part[0]])
            elif name == "expand":
                for f in range(4):
                    columns = slice(f * TILE, (f + 1) * TILE)
                    apply((held[name], part, every, columns), reduced[4 + 2 * f])
            elif name == "contract":
                for f in range(4):
                    rows = slice(f * TILE, (f + 1) * TILE)
                    apply((held[name], part, rows, every), reduced[5 + 2 * f].T)
            elif name == "attn_out":
                apply((held[name], part, every, every), reduced[3].T)
            elif name == "embed":
                rowwise(name, part, ends)
            elif name == "head":
                rowwise(name, part, ends, PATCH)
            else:
                rowwise(name, part, {"time_in": time_in, "time_out": time_out, "classes": classes}[name])
            store(name, part)
    for copy in stores:
        copy.wait()


def adam_blocks(states, *gradients):
    names = list(states)
    shapes = [states[name].shape for name in names]
    outs = []
    for shape in shapes:
        outs += [shape[1:], (2,) + shape[1:]]
    pieces = sum(shape[1] if len(shape) == 4 else 1 for shape in shapes)
    return pl.pallas_call(
        functools.partial(adam_kernel, names),
        out_shape=[jax.ShapeDtypeStruct(shape, F32) for shape in outs],
        in_specs=[pl.BlockSpec(memory_space=pl.ANY)] * len(names)
        + [pl.BlockSpec(memory_space=pltpu.VMEM)] * len(gradients),
        out_specs=[pl.BlockSpec(memory_space=pl.ANY)] * len(outs),
        scratch_shapes=[pltpu.VMEM(shape, F32) for shape in shapes]
        + [pltpu.SemaphoreType.DMA((pieces,)), pltpu.SemaphoreType.DMA((2 * pieces,))],
        compiler_params=pltpu.CompilerParams(vmem_limit_bytes=40 << 20),
    )(*states.values(), *gradients)


def per_device(
    latents,
    noise_target,
    token_mask,
    timesteps,
    labels,
    state_embed,
    state_head,
    state_time_in,
    state_time_out,
    state_classes,
    state_adaptive,
    state_attention_in,
    state_attention_out,
    state_expand,
    state_contract,
):
    nd = lax.axis_size("dp")
    rows = state_attention_in.shape[1]
    states = {
        "adapt": state_adaptive.transpose(0, 2, 1, 3),
        "attn_in": state_attention_in.transpose(0, 2, 1, 3),
        "expand": state_expand,
        "contract": state_contract,
        "time_out": state_time_out,
        "classes": state_classes,
        "attn_out": state_attention_out,
        "time_in": state_time_in,
        "embed": state_embed,
        "head": state_head.transpose(0, 2, 1),
    }
    lanes = jnp.arange(FREQ + 128)[None, :]
    step_ids = timesteps[0].T.reshape(PER_INDEX, 1).astype(F32)
    label_ids = labels[0].T.reshape(PER_INDEX, 1).astype(F32)
    half_width = FREQ // 2
    frequency = jnp.exp(-math.log(10000.0) * (lanes % half_width).astype(F32) / half_width)
    angles = step_ids * frequency
    features = jnp.where(lanes < half_width, jnp.cos(angles), jnp.sin(angles))
    front = jnp.where(lanes < FREQ, features.astype(BF).astype(F32), label_ids)
    flags = token_mask.reshape(NMB, WTOK)
    latent_columns = latents[0].transpose(0, 2, 1)
    noise_columns = noise_target[0].transpose(0, 2, 1)
    residual, mod, ends, front_all, time_pre, condition, token_total, time_out_part, *saved = forward_blocks(
        states, flags, front, latent_columns, window_positions()
    )
    reduced, loss_local, squares, ends_sum, all_mod = backward_blocks(
        saved, residual, mod, flags, token_total, noise_columns, latent_columns, ends
    )
    adaptive_grad, time_in_grad, time_out_grad, classes_grad, sums = tail_blocks(
        states["adapt"],
        loss_local,
        squares,
        all_mod,
        front_all,
        time_pre,
        condition,
        time_out_part,
    )
    updated = adam_blocks(
        states,
        reduced,
        ends_sum,
        time_in_grad,
        time_out_grad,
        classes_grad,
        adaptive_grad,
        sums,
    )
    new = dict(zip(states, zip(updated[::2], updated[1::2])))
    back = {"adapt": (1, 0, 2), "attn_in": (1, 0, 2), "head": (1, 0)}
    results = [sums[1, 0, 0], jnp.sqrt(sums[0, 0, 0])]
    order = ("embed", "head", "time_in", "time_out", "classes", "adapt", "attn_in")
    for name in order + ("attn_out", "expand", "contract"):
        weight, moments = new[name]
        if name in back:
            axes = back[name]
            weight = weight.transpose(axes)
            moments = moments.transpose((0,) + tuple(1 + axis for axis in axes))
        results += [weight, moments]
    return tuple(results)


def solution(mesh):
    in_specs = (
        P("dp", None, "mp", None),
        P("dp", None, "mp", None),
        P("dp", None, "mp"),
        P("dp", None, None),
        P("dp", None, None),
        P(None, None, "dp"),
        P(None, "dp", None),
        P(None, None, "dp"),
        P(None, "dp", None),
        P(None, None, "dp"),
        P(None, "dp", None, None),
        P(None, "dp", None, "mp"),
        P(None, "mp", "dp"),
        P(None, "dp", "mp"),
        P(None, "mp", "dp"),
    )
    out_specs = (
        P(),
        P(),
        P(None, "dp"),
        P(None, None, "dp"),
        P("dp", None),
        P(None, "dp", None),
        P(None, "dp"),
        P(None, None, "dp"),
        P("dp", None),
        P(None, "dp", None),
        P(None, "dp"),
        P(None, None, "dp"),
        P("dp", None, None),
        P(None, "dp", None, None),
        P("dp", None, "mp"),
        P(None, "dp", None, "mp"),
        P("mp", "dp"),
        P(None, "mp", "dp"),
        P("dp", "mp"),
        P(None, "dp", "mp"),
        P("mp", "dp"),
        P(None, "mp", "dp"),
    )
    return jax.shard_map(
        per_device, mesh=mesh, in_specs=in_specs, out_specs=out_specs, check_vma=False
    )
```

```python
import functools
import math

import jax
import jax.numpy as jnp
import numpy as np
from jax import lax
from jax.experimental import pallas as pl
from jax.experimental.pallas import tpu as pltpu
from jax.sharding import PartitionSpec as P

D = 1024
HEADS = 16
HD = 64
PATCH = 32
FREQ = 256
CLASSES = 600
WTOK = 320
NMB = 2
WMB = 4
TILE = 256
NJ = 12
ROWS = NMB * WTOK
MESH = pl.DeviceIdType.MESH
BF = jnp.bfloat16
F32 = jnp.float32


beta_one = 0.9
beta_two = 0.999
adam_eps = 1e-08
learn_rate = 0.15
weight_decay = 0.1
threshold = 0.002
step_count = 10.0


def window_positions():
    half_width = D // 2
    steps = np.arange(half_width, dtype=np.float32)
    frequency = np.exp(np.float32(-math.log(10000.0)) * steps / np.float32(half_width))
    angles = np.arange(WTOK, dtype=np.float32)[:, None] * frequency.astype(np.float32)[None, :]
    table = np.concatenate([np.sin(angles), np.cos(angles)], axis=-1)
    return jnp.asarray(table.astype(np.float32))


def dot_general(a, b, a_dim, b_dim):
    return lax.dot_general(a, b, (((a_dim,), (b_dim,)), ((), ())), preferred_element_type=F32)


def dot_nn(a, b):
    return jnp.dot(a, b, preferred_element_type=F32)


def dot_nt(a, b):
    return dot_general(a, b, 1, 1)


def dot_tn(a, b):
    return dot_general(a, b, 0, 0)


def norm_back(grad, normed, inverse):
    mean_grad = jnp.mean(grad, axis=-1, keepdims=True)
    mean_prod = jnp.mean(grad * normed, axis=-1, keepdims=True)
    return inverse * (grad - mean_grad - normed * mean_prod)


def silu(values):
    return values * jax.nn.sigmoid(values)


def silu_slope(values):
    gate = jax.nn.sigmoid(values)
    return gate * (1.0 + values * (1.0 - gate))


def gelu_parts(up):
    cdf = 0.5 * (1.0 + lax.erf(up * math.sqrt(0.5)))
    pdf = jnp.exp(-0.5 * up * up) * (1.0 / math.sqrt(2.0 * math.pi))
    return up * cdf, cdf + up * pdf


def tokens3(values):
    return values.reshape(NMB, WTOK, -1)


def flip(bits, at):
    return [1 - bit if place == at else bit for place, bit in enumerate(bits)]


class Place:
    def __init__(self, nd, nm):
        self.nm = nm
        self.nb = nd.bit_length() - 2
        dp_id = lax.axis_index("dp")
        self.nd = nd
        self.dp_id = dp_id
        self.m = lax.axis_index("mp")
        self.core = dp_id % 2
        self.bits = [dp_id // (1 << (self.nb - at)) % 2 for at in range(self.nb)]
        self.sibling = {"dp": self.dp_of(self.bits, 1 - self.core), "mp": self.m}
        self.orders = (list(range(self.nb))[::-1], list(range(self.nb)))
        self.halves = (pl.ds(0, nm // 2), pl.ds(nm // 2, nm - nm // 2))

    def dp_of(self, bits, core):
        total = core
        for at, bit in enumerate(bits):
            total = total + bit * (1 << (self.nb - at))
        return total

    def across(self, at):
        return {"dp": self.dp_of(flip(self.bits, at), self.core), "mp": self.m}

    def along(self, hops):
        return {"dp": self.dp_of(self.bits, self.core), "mp": (self.m + hops) % self.nm}

    def facing(self, hops):
        return {"dp": self.chip(hops) * 2 + self.core, "mp": self.m}

    def chip(self, hops):
        return (self.dp_id // 2 + hops) % (self.nd // 2)

    def beside(self, hops):
        return {"dp": (self.dp_id + hops) % self.nd, "mp": self.m}

    def pick(self, half, done, flipped=None):
        where = flip(self.bits, flipped)
        return (self.halves[half],) + tuple(
            pl.ds(0, 2) if at in done else pl.ds(where[at], 1) for at in range(self.nb)
        )

    def mine(self, m=None):
        return (self.m if m is None else m,) + tuple(self.bits)

    def greet(self, everyone=False):
        barrier = pltpu.get_barrier_semaphore()
        if everyone:
            others = [self.beside(hops) for hops in range(1, self.nd)]
        else:
            others = [self.sibling] + [self.facing(hops) for hops in range(1, self.nd // 2)]
        others += [self.along(hops) for hops in range(1, self.nm)]
        for other in others:
            pl.semaphore_signal(barrier, inc=1, device_id=other, device_id_type=MESH)
        return lambda: pl.semaphore_wait(barrier, len(others))


class Copies:
    def __init__(self, send_sems, recv_sems):
        self.send_sems, self.recv_sems = send_sems, recv_sems
        self.started = {}

    def start(self, step, slot, source, target, device):
        copy = pltpu.make_async_remote_copy(
            src_ref=source,
            dst_ref=target,
            send_sem=self.send_sems.at[step, slot],
            recv_sem=self.recv_sems.at[step, slot],
            device_id=device,
            device_id_type=MESH,
        )
        copy.start()
        self.started[step, slot] = copy

    def arrived(self, step, slot):
        self.started[step, slot].wait_recv()

    def drain(self, step=None):
        for key in list(self.started):
            if step is None or key[0] == step:
                self.started.pop(key).wait_send()


class Exchange:
    def __init__(self, place, send_sems, recv_sems):
        self.place = place
        self.copies = Copies(send_sems, recv_sems)

    def dp_gather(self, group, source, target):
        for hops in range(1, self.place.nd):
            here = target.at[self.place.dp_id]
            self.copies.start(group, hops - 1, source, here, self.place.beside(hops))

    def to_sibling(self, group, source, target, slot=0):
        self.copies.start(group, slot, source, target, self.place.sibling)

    def chip_scatter(self, group, source, target):
        for hops in range(1, self.place.nd // 2):
            block = source.at[self.place.chip(hops), self.place.core]
            self.copies.start(group, hops - 1, block, target.at[hops - 1], self.place.facing(hops))

    def chip_gather(self, group, source, target):
        for hops in range(1, self.place.nd // 2):
            self.copies.start(group, hops - 1, source, target, self.place.facing(hops))

    def mp_gather(self, group, source, target):
        for hops in range(1, self.place.nm):
            here = target.at[self.place.m]
            self.copies.start(group, hops - 1, source, here, self.place.along(hops))

    def wait(self, group):
        for step, slot in list(self.copies.started):
            if step == group:
                self.copies.arrived(step, slot)

    def drain(self):
        self.copies.drain()


def gather_steps(
    place, shard, whole, send_sems, recv_sems, local_sems, all_here, prepare, load, compute, last
):
    nm, nb, core = place.nm, place.nb, place.core
    copies = Copies(send_sems, recv_sems)
    stage_slot = lambda stage, half: nm - 1 + 2 * stage + half
    twin = nm - 1 + 2 * nb
    wide = ARRIVALS[-1]
    count = NJ - 1
    late = 2 * twin + 1
    wide_z = lambda part, hops: (0 if part == 0 else late) + hops - 1
    wide_twin = lambda part, hops: (twin if part == 0 else late + nm - 1) + hops - 1
    locals_ = {}

    def begin_local(j):
        here = whole.at[(j,) + place.mine() + (core,)]
        locals_[j] = pltpu.make_async_copy(shard.at[j], here, local_sems.at[j])
        locals_[j].start()
        copies.start(j, 2 * twin, shard.at[j], here, place.sibling)

    def begin(j):
        here = whole.at[(j,) + place.mine() + (core,)]
        for hops in range(1, nm):
            copies.start(j, hops - 1, shard.at[j], here, place.along(hops))
        begin_local(j)

    def half_of_wide(half, bits):
        lanes = pl.ds(half * (TILE // 2), TILE // 2)
        return whole.at[(wide, place.m) + bits + (core, slice(None), lanes)]

    def wide_stage(step):
        if step == 1:
            locals_[wide].wait()
        for half in range(2):
            order = place.orders[half]
            if step > 0:
                copies.arrived(wide, stage_slot(step - 1, half))
            if step == 0:
                source = shard.at[wide, :, pl.ds(half * (TILE // 2), TILE // 2)]
                block = half_of_wide(half, tuple(place.bits))
                copies.start(wide, stage_slot(0, half), source, block, place.across(order[0]))
            elif step < nb:
                block = half_of_wide(half, place.pick(half, order[:step])[1:])
                copies.start(wide, stage_slot(step, half), block, block, place.across(order[step]))
            if step > 0:
                block = half_of_wide(half, place.pick(half, order[: step - 1], order[step - 1])[1:])
                copies.start(wide, twin + stage_slot(step - 1, half), block, block, place.sibling)

    def part_of_wide(part, m):
        return whole.at[(wide, m, pl.ds(part, 1)) + (pl.ds(0, 2),) * (nb - 1) + (core,)]

    def wide_send(part):
        block = part_of_wide(part, place.m)
        for hops in range(1, nm):
            copies.start(wide, wide_z(part, hops), block, block, place.along(hops))

    def wide_pass(part):
        for hops in range(1, nm):
            copies.arrived(wide, wide_z(part, hops))
            block = part_of_wide(part, (place.m + nm - hops) % nm)
            copies.start(wide, wide_twin(part, hops), block, block, place.sibling)

    def stage(j, step):
        if step == 0:
            locals_[j].wait()
            for hops in range(1, nm):
                copies.arrived(j, hops - 1)
        else:
            for half in range(2):
                copies.arrived(j, stage_slot(step - 1, half))
        if step < nb:
            for half in range(2):
                order = place.orders[half]
                block = whole.at[(j,) + place.pick(half, order[:step]) + (core,)]
                copies.start(j, stage_slot(step, half), block, block, place.across(order[step]))
        if step == 0:
            for hops in range(1, nm):
                block = whole.at[(j,) + place.mine((place.m + nm - hops) % nm) + (core,)]
                copies.start(j, twin + hops - 1, block, block, place.sibling)
        else:
            for half in range(2):
                order = place.orders[half]
                block = whole.at[
                    (j,) + place.pick(half, order[: step - 1], order[step - 1]) + (core,)
                ]
                copies.start(j, twin + stage_slot(step - 1, half), block, block, place.sibling)

    def finish(j):
        for slot in range(twin, 2 * twin + 1):
            copies.arrived(j, slot)
        if j == wide:
            for hops in range(1, nm):
                copies.arrived(j, wide_twin(1, hops))
        load(j)

    prepare(ARRIVALS[0])
    prepare(wide)
    all_here()
    begin(ARRIVALS[0])
    wide_stage(0)
    begin_local(wide)
    for at in range(1, 3):
        prepare(ARRIVALS[at])
        begin(ARRIVALS[at])
    prepare(ARRIVALS[3])
    for turn in range(max(NJ + nb + 1, last + nb - 1)):
        for step in range(nb + 1):
            if 0 <= turn - step < count:
                stage(ARRIVALS[turn - step], step)
        if 1 <= turn + 1 <= nb:
            wide_stage(turn + 1)
        if turn + 3 < count:
            begin(ARRIVALS[turn + 3])
        if turn in (nb, nb + 3):
            wide_send(0 if turn == nb else 1)
        if turn in (nb + 5, nb + 8):
            wide_pass(0 if turn == nb + 5 else 1)
        if turn == nb + 10:
            finish(wide)
        if 0 <= turn - 1 - nb < count:
            finish(ARRIVALS[turn - 1 - nb])
        if turn + 4 < count:
            prepare(ARRIVALS[turn + 4])
        compute(turn + 2 - nb)
    copies.drain()


def row_norm(values):
    center = values - jnp.mean(values, axis=-1, keepdims=True)
    inverse = lax.rsqrt(jnp.mean(center * center, axis=-1, keepdims=True) + 1e-06)
    return center * inverse, inverse


def each(count, body, unroll=1):
    lax.fori_loop(0, count, lambda at, carry: (body(at), carry)[1], 0, unroll=math.gcd(count, unroll))


def span(at, size):
    return pl.ds(pl.multiple_of(at * size, size), size)


def head_lanes(head, dtype=F32):
    lanes = lax.broadcasted_iota(jnp.int32, (1, TILE), 1) // HD
    return (lanes == head).astype(dtype)


def soft_rows(query, key, key_bias):
    scores = dot_nt(query, key)
    scores = jnp.where(key_bias > 0, scores, -1e30)
    exponents = jnp.exp(scores - jnp.max(scores, axis=-1, keepdims=True))
    return exponents * (1.0 / jnp.sum(exponents, axis=-1, keepdims=True))


def label_pick(front, count):
    labels = front[:, :, FREQ : FREQ + 1].reshape(-1, 1)
    lanes = lax.broadcasted_iota(jnp.int32, (labels.shape[0], count), 1).astype(F32)
    return (lanes == labels).astype(BF)


PER_INDEX = NMB * WMB
def soft_columns(key, query, key_mask):
    scores = dot_nt(key, query)
    scores = jnp.where(key_mask > 0, scores, -1e30)
    exponents = jnp.exp(scores - jnp.max(scores, axis=0, keepdims=True))
    return exponents * (1.0 / jnp.sum(exponents, axis=0, keepdims=True))


BLOCK = 64
PER_WINDOW = WTOK // BLOCK
NBLOCK = ROWS // BLOCK
LANE_BLOCK = 128


def token_rows(source, target):
    for window in range(NMB):
        target[window * WTOK : (window + 1) * WTOK, :] = source[window].T


def mask_column(source, target):
    for window in range(NMB):
        row = jnp.broadcast_to(source[window : window + 1, :].astype(F32), (8, WTOK))
        target[window * WTOK : (window + 1) * WTOK, :] = row.T[:, 0:1]


def square_sum(values):
    return jnp.sum(jnp.sum(values * values, axis=0, keepdims=True), axis=1, keepdims=True)


def transpose_rows(source, target):
    def body(at):
        target[:, span(at, LANE_BLOCK)] = source[span(at, LANE_BLOCK), :].T

    each(ROWS // LANE_BLOCK, body)


ARRIVALS = (0, 1, 2, 3, 4, 6, 8, 10, 5, 7, 9, 11)
FORWARD_TURNS = (
    (4, ("qkv", 0)),
    (5, ("qkv", 1)),
    (6, ("qkv", 2)),
    (6, ("attend", 0)),
    (7, ("attend", 1)),
    (7, ("attend", 2)),
    (7, ("attend", 3)),
    (8, ("out",)),
    (9, ("up", 0)),
    (9, ("up", 1)),
    (10, ("up", 2)),
    (11, ("up", 3)),
    (12, ("down", 0)),
    (13, ("down", 1)),
    (13, ("down", 3)),
    (14, ("down", 2)),
)


def forward_kernel(nd, nm, states, flags, times_in, latents_in, positions, *refs):
    (residual_out, mod, ends, front, time_pre, condition, token_total, time_out) = refs[:8]
    refs = refs[8:]
    (residual, parts, parts_twin, parts_in, mods, mods_twin, mods_in) = refs[-12:-5]
    (rows_ref, counts, ends_all, swap_send, swap_recv) = refs[-5:]
    (shard, held_in, held_out, held_up, held_down, adaptive, time_in, classes, held_embed, held_head, ends_in, front_in, latents, held_time, state_sems) = refs[-27:-12]
    refs = refs[:-27]
    place = Place(nd, nm)
    swap = Exchange(place, swap_send, swap_recv)
    all_here = place.greet(everyone=True)
    state_loads = {}
    class_pad = classes.shape[0] - CLASSES
    wanted_states = {
        "attn_in": held_in,
        "contract": held_down,
        "embed": held_embed,
        "head": held_head,
        "time_in": time_in,
        "time_out": held_time,
        "classes": classes.at[pl.ds(0, CLASSES)],
        "adapt": adaptive,
        "attn_out": held_out,
        "expand": held_up,
    }
    for at, (name, target) in enumerate(wanted_states.items()):
        state_loads[name] = pltpu.make_async_copy(states[name].at[0], target, state_sems.at[at])
        state_loads[name].start()

    def state_ready(name):
        if name in state_loads:
            state_loads.pop(name).wait()

    def prepare(j):
        if j < 3:
            state_ready("attn_in")
            values = held_in[j]
        elif j == 3:
            state_ready("attn_out")
            values = held_out[...].T
        elif j % 2 == 0:
            state_ready("expand")
            values = held_up[:, (j - 4) // 2 * TILE : (j - 2) // 2 * TILE]
        else:
            state_ready("contract")
            values = held_down[(j - 5) // 2 * TILE : (j - 3) // 2 * TILE, :].T
        shard[j] = values.astype(BF)

    dp_id = place.dp_id
    part_rows = D // nd
    windows = nd * PER_INDEX
    upright = parts.shape[2] == windows
    (whole, n_one_t, qkv_out, mixed_out, branch_one_out, middle_out, n_two_t, hidden_out, slope_out, branch_two_out) = refs[:10]
    (n_one, qkv, mixed, branch_one, middle, n_two, flipped, hidden, slope, branch_two, loaded) = refs[10:21]
    send_sems, recv_sems, local_sems, load_sems, spill_sems = refs[21:]
    spilled, spill_count = {}, []

    def spill(name, source, target):
        copy = pltpu.make_async_copy(source, target, spill_sems.at[len(spill_count)])
        copy.start()
        spill_count.append(name)
        spilled[name] = copy

    loads = {}
    slots = loaded.shape[0]

    def load(j):
        loads[j] = pltpu.make_async_copy(whole.at[j], loaded.at[ARRIVALS.index(j) % slots], load_sems.at[j])
        loads[j].start()

    def tile(j, m):
        return loaded.at[ARRIVALS.index(j) % slots, m].reshape(D, TILE)

    def first_swap():
        state_ready("embed")
        state_ready("head")
        ends_in[0] = held_embed[...].astype(BF)
        ends_in[1] = held_head[...].astype(BF)
        front_in[:, : FREQ + 128] = times_in[...]
        count = jnp.sum(jnp.sum(flags[...].astype(F32), axis=0, keepdims=True), axis=1, keepdims=True)
        front_in[:, FREQ + 128 :] = jnp.broadcast_to(count, (PER_INDEX, 128))
        classes[CLASSES:, :] = jnp.zeros((class_pad, classes.shape[1]), F32)
        token_rows(latents_in, latents)
        front[dp_id] = front_in[...]
        ends_all[dp_id] = ends_in[...]
        swap.dp_gather(0, front_in, front)
        swap.dp_gather(1, ends_in, ends_all)

    def time_layers():
        state_ready("time_out")
        for index in range(nd):
            time_out[index] = held_time[:, index * part_rows : (index + 1) * part_rows].astype(BF)
        swap.wait(0)
        features = front[:, :, :FREQ].reshape(windows, FREQ).astype(BF)
        state_ready("time_in")
        time_pre[...] = dot_nn(features, time_in[...].astype(BF))
        time_hidden = silu(time_pre[...]).astype(BF)
        for index in range(nd):
            if upright:
                parts[index // 2, index % 2] = dot_nn(time_hidden, time_out[index])
            else:
                parts[index // 2, index % 2] = dot_general(time_out[index], time_hidden, 0, 1)
        swap.to_sibling(2, parts.at[:, 1 - place.core], parts_twin)
        counts[place.m] = jnp.sum(front[:, :, FREQ + 128 :], axis=0)
        swap.mp_gather(5, counts.at[place.m], counts)
        swap.wait(2)
        for chip in range(nd // 2):
            parts[chip, place.core] += parts_twin[chip]
        swap.chip_scatter(3, parts, parts_in)

    def condition_layers():
        state_ready("classes")
        state_ready("adapt")
        swap.wait(3)
        total = parts[dp_id // 2, place.core] + jnp.sum(parts_in[...], axis=0)
        total = total if upright else total.T
        total = total + dot_nn(label_pick(front, classes.shape[0]), classes[...].astype(BF))
        condition[...] = total
        row_ids = lax.broadcasted_iota(jnp.int32, (nd * NMB, windows), 0)
        column_ids = lax.broadcasted_iota(jnp.int32, (nd * NMB, windows), 1)
        wanted = row_ids // NMB * PER_INDEX + place.m * NMB + row_ids % NMB
        own = dot_nn((wanted == column_ids).astype(BF), silu(total).astype(BF)).astype(BF)
        for which in range(6):
            rows_ref[...] = dot_nn(own, adaptive[which].astype(BF))

            def move(row):
                index, window = row // NMB, row % NMB
                spot = (index // 2, index % 2, window, slice(which, which + 1))
                mods[spot] = rows_ref[pl.ds(row, 1), :]

            each(nd * NMB, move)
        swap.to_sibling(6, mods.at[:, 1 - place.core], mods_twin)
        swap.wait(6)
        for chip in range(nd // 2):
            for window in range(NMB):
                mods[chip, place.core, window] += mods_twin[chip, window]
        swap.chip_scatter(4, mods, mods_in)

    def modulation():
        swap.wait(4)
        for window in range(NMB):
            mod[window] = mods[dp_id // 2, place.core, window] + jnp.sum(mods_in[:, window], axis=0)
        swap.wait(5)
        token_total[...] = jnp.sum(counts[...], axis=0)
        swap.wait(1)

        def turn_ends(index):
            for which in range(2):
                ends[which, index] = ends_all[index, which].astype(F32).T.astype(BF)

        each(nd, turn_ends)
        embed_mat = ends[0].reshape(D, PATCH)

        def body(window):
            here = span(window, WTOK)
            residual[here, :] = dot_nt(latents[here, :], embed_mat) + positions[...]

        each(NMB, body)
        spill("residual", residual, residual_out)

    def first_norm():
        def body(at):
            window, here = at // PER_WINDOW, span(at, BLOCK)
            normed, _ = row_norm(residual[here, :])
            normed = normed * (1.0 + mod[window, 1:2, :]) + mod[window, 0:1, :]
            n_one[here, :] = normed.astype(BF)

        each(NBLOCK, body)
        transpose_rows(n_one, flipped.at[0])
        spill("n_one", flipped.at[0], n_one_t)

    def qkv_unit(j):
        def body(m):
            qkv[j, m] = dot_nn(n_one[...], tile(j, m)[...]).astype(BF)

        each(nm, body)
        spill(("qkv", j), qkv.at[j], qkv_out.at[j])

    def attend_unit(m):
        def body(window):
            here = span(window, WTOK)
            query, key, value = qkv[0, m, here, :], qkv[1, m, here, :], qkv[2, m, here, :]
            total = jnp.zeros((WTOK, TILE), F32)
            for head in range(TILE // HD):
                lanes = head_lanes(head, BF)
                attn = soft_rows(query * (lanes * HD ** (-0.5)), key, flags[pl.ds(window, 1), :]).astype(BF)
                total = total + dot_nn(attn, value * lanes)
            mixed[m, here, :] = total.astype(BF)

        each(NMB, body)
        if m == nm - 1:
            spill("mixed", mixed, mixed_out)

    def add_nt(source, j, target, fresh):
        def body(at):
            columns = span(at, TILE)
            left = jnp.concatenate([source[m] for m in range(nm)], axis=1)
            right = jnp.concatenate([tile(j, m)[columns, :] for m in range(nm)], axis=1)
            total = dot_nt(left, right)
            target[:, columns] = total if fresh else target[:, columns] + total

        each(D // TILE, body)

    def out_unit():
        add_nt(mixed, 3, branch_one, True)
        spill("br_one", branch_one, branch_one_out)

        def body(at):
            window, here = at // PER_WINDOW, span(at, BLOCK)
            rows = residual[here, :] + mod[window, 2:3, :] * branch_one[here, :]
            middle[here, :] = rows
            normed, _ = row_norm(rows)
            normed = normed * (1.0 + mod[window, 4:5, :]) + mod[window, 3:4, :]
            n_two[here, :] = normed.astype(BF)

        each(NBLOCK, body)
        spill("middle", middle, middle_out)
        transpose_rows(n_two, flipped.at[1])
        spill("n_two", flipped.at[1], n_two_t)

    def up_unit(f):
        slot = f % 2
        if f >= 2:
            spilled.pop(("slope", f - 2)).wait()

        def body(m):
            up = dot_nn(n_two[...], tile(4 + 2 * f, m)[...])
            value, grad = gelu_parts(up)
            hidden[f, m] = value.astype(BF)
            slope[slot, :, span(m, TILE)] = grad

        each(nm, body)
        spill(("hidden", f), hidden.at[f], hidden_out.at[f])
        spill(("slope", f), slope.at[slot], slope_out.at[f])

    def down_unit(f):
        add_nt(hidden.at[f], 5 + 2 * f, branch_two, f == 0)
        if f == 2:
            spill("br_two", branch_two, branch_two_out)

    units = {"qkv": qkv_unit, "attend": attend_unit, "out": out_unit, "up": up_unit, "down": down_unit}
    need = {"qkv": lambda j: j, "out": lambda: 3, "up": lambda f: 4 + 2 * f, "down": lambda f: 5 + 2 * f}

    def compute(turn):
        early = (first_swap, time_layers, condition_layers, modulation, first_norm)
        if turn < len(early):
            early[turn]()
        for when, (name, *args) in FORWARD_TURNS:
            if when == turn:
                if name in need:
                    loads[need[name](*args)].wait()
                units[name](*args)

    last = max(when for when, _ in FORWARD_TURNS)
    gather_steps(
        place,
        shard,
        whole,
        send_sems,
        recv_sems,
        local_sems,
        all_here,
        prepare,
        load,
        compute,
        last,
    )
    for copy in spilled.values():
        copy.wait()
    swap.drain()


def forward_blocks(states, *others):
    nd, nm = lax.axis_size("dp"), lax.axis_size("mp")
    nb = nd.bit_length() - 2
    rows = D // nd
    names = list(states)
    slots = 2 * (nm - 1 + 2 * nb) + 1 + 2 * (nm - 1)
    windows = nd * PER_INDEX
    chips = nd // 2
    part = (windows, rows) if windows <= rows else (rows, windows)
    small = [
        ((NMB, 6, D), F32),
        ((2, nd, rows, PATCH), BF),
        ((nd, PER_INDEX, FREQ + 256), F32),
        ((windows, rows), F32),
        ((windows, rows), F32),
        ((PER_INDEX, 128), F32),
        ((nd, rows, rows), BF),
    ]
    shapes = [
        ((NJ, nm) + (2,) * nb + (2, rows, TILE), BF),
        ((D, ROWS), BF),
        ((3, nm, ROWS, TILE), BF),
        ((nm, ROWS, TILE), BF),
        ((ROWS, D), F32),
        ((ROWS, D), F32),
        ((D, ROWS), BF),
        ((4, nm, ROWS, TILE), BF),
        ((4, ROWS, D), F32),
        ((ROWS, D), F32),
    ]

    def kernel(*refs):
        named = dict(zip(names, refs))
        forward_kernel(nd, nm, named, *refs[len(names) :])

    return pl.pallas_call(
        kernel,
        out_shape=[
            jax.ShapeDtypeStruct(shape, dtype) for shape, dtype in [((ROWS, D), F32)] + small + shapes
        ],
        in_specs=[pl.BlockSpec(memory_space=pl.ANY)] * len(names)
        + [pl.BlockSpec(memory_space=pltpu.VMEM)] * len(others),
        out_specs=[pl.BlockSpec(memory_space=pl.ANY)]
        + [pl.BlockSpec(memory_space=pltpu.VMEM)] * len(small)
        + [pl.BlockSpec(memory_space=pl.ANY)] * len(shapes),
        scratch_shapes=[
            pltpu.VMEM((ROWS, D), BF),
            pltpu.VMEM((3, nm, ROWS, TILE), BF),
            pltpu.VMEM((nm, ROWS, TILE), BF),
            pltpu.VMEM((ROWS, D), F32),
            pltpu.VMEM((ROWS, D), F32),
            pltpu.VMEM((ROWS, D), BF),
            pltpu.VMEM((2, D, ROWS), BF),
            pltpu.VMEM((4, nm, ROWS, TILE), BF),
            pltpu.VMEM((2, ROWS, D), F32),
            pltpu.VMEM((ROWS, D), F32),
            pltpu.VMEM((4, nm) + (2,) * nb + (2, rows, TILE), BF),
            pltpu.SemaphoreType.DMA((NJ, slots)),
            pltpu.SemaphoreType.DMA((NJ, slots)),
            pltpu.SemaphoreType.DMA((NJ,)),
            pltpu.SemaphoreType.DMA((NJ,)),
            pltpu.SemaphoreType.DMA((24,)),
            pltpu.VMEM((NJ, rows, TILE), BF),
            pltpu.VMEM((3, rows, TILE), F32),
            pltpu.VMEM((TILE, rows), F32),
            pltpu.VMEM((rows, 4 * TILE), F32),
            pltpu.VMEM((4 * TILE, rows), F32),
            pltpu.VMEM((6, rows, D), F32),
            pltpu.VMEM((FREQ, rows), F32),
            pltpu.VMEM((CLASSES + -CLASSES % 128, rows), F32),
            pltpu.VMEM((PATCH, rows), F32),
            pltpu.VMEM((PATCH, rows), F32),
            pltpu.VMEM((2, PATCH, rows), BF),
            pltpu.VMEM((PER_INDEX, FREQ + 256), F32),
            pltpu.VMEM((ROWS, PATCH), BF),
            pltpu.VMEM((rows, D), F32),
            pltpu.SemaphoreType.DMA((10,)),
            pltpu.VMEM((ROWS, D), F32),
            pltpu.VMEM((chips, 2) + part, F32),
            pltpu.VMEM((chips,) + part, F32),
            pltpu.VMEM((chips - 1,) + part, F32),
            pltpu.VMEM((chips, 2, NMB, 6, D), F32),
            pltpu.VMEM((chips, NMB, 6, D), F32),
            pltpu.VMEM((chips - 1, NMB, 6, D), F32),
            pltpu.VMEM((nd * NMB, D), F32),
            pltpu.VMEM((nm, PER_INDEX, 128), F32),
            pltpu.VMEM((nd, 2, PATCH, rows), BF),
            pltpu.SemaphoreType.DMA((7, max(nd, nm) - 1)),
            pltpu.SemaphoreType.DMA((7, max(nd, nm) - 1)),
        ],
        compiler_params=pltpu.CompilerParams(
            collective_id=0, has_side_effects=True, vmem_limit_bytes=60 << 20
        ),
    )(*states.values(), *others)


PIECES = (5, 7, 4, 6, 9, 8, 11, 10, 3, 2, 1, 0)
BACKWARD_TURNS = (
    (0, ("head",)),
    (1, ("slope", 0)),
    (1, ("spread", 0)),
    (2, ("slope", 1)),
    (2, ("spread", 1)),
    (3, ("slope", 2)),
    (3, ("spread", 2)),
    (4, ("slope", 3)),
    (4, ("spread", 3)),
    (5, ("mid",)),
    (6, ("attend", 0)),
    (7, ("attend", 1)),
    (8, ("attend", 2)),
    (9, ("attend", 3)),
    (10, ("inward", 2)),
    (10, ("inward", 1)),
    (11, ("inward", 0)),
    (11, ("last",)),
    (12, ("swap", 0)),
    (13, ("swap", 1)),
    (14, ("swap", 2)),
)
HELD = 5
TWINS = 3


def backward_kernel(nd, nm, whole, n_one_t, qkv, mixed, branch_one, middle, n_two_t, hidden, slope, branch_two, residual, *refs):
    (mod, mask_in, token_total_in, noise_in, latents_in, both_ends) = refs[:6]
    token_total = token_total_in[0:1, 0:1]
    head_mat = both_ends[1].reshape(D, PATCH)
    (total, loss, squares, ends_sum, all_mod) = refs[6:11]
    (partial, twin_ref, xa, xb, grad_rows, grad_in, grad_low, grad_low_t, normed_t, pool, loaded, z_ref, noise, inverses, row_mask, ends_rows) = refs[11:27]
    rest = refs[27:]
    place = Place(nd, nm)
    nb, core = place.nb, place.core
    part_rows = D // nd
    stage_refs = [rest[2 * step : 2 * step + 2] for step in range(nb)]
    send_sems, recv_sems, free_sem, load_sems = rest[2 * nb : 2 * nb + 4]
    (grad_mod, mod_in, mod_rows, own_mod, ends, ends_twin, ends_in, ends_z) = rest[2 * nb + 4 : -3]
    swap_send, swap_recv, own_sem = rest[-3:]
    swap = Exchange(place, swap_send, swap_recv)
    copies = Copies(send_sems, recv_sems)
    orders = [order[::-1] for order in place.orders]
    all_here = place.greet()
    slot_of = lambda step, half: 1 + 2 * step + half
    z_slot = 1 + 2 * nb
    loads = {}

    def load(name, source, target):
        copy = pltpu.make_async_copy(source, target, load_sems.at[len(loads)])
        copy.start()
        loads[name] = copy

    def load_tiles(j, slot):
        load(("w", j), whole.at[j], loaded.at[slot])

    def tile(slot, m):
        return loaded.at[slot, m].reshape(D, TILE)

    HIDDEN, QUERY, MIXED_GRAD = 4, 5, 8

    load("br_two", branch_two, xb)
    load("middle", middle, xa)
    load(("hidden", 0), hidden.at[0], pool.at[HIDDEN])
    load("n_two", n_two_t, normed_t)
    load_tiles(5, 0)
    load_tiles(4, 1)
    token_rows(noise_in, noise)
    mask_column(mask_in, row_mask)

    def add_to(target, index, source):
        shape = source.shape[:-2]

        def body(at):
            inner, places = at, []
            for size in shape[::-1]:
                places.append(inner % size)
                inner = inner // size
            places = places[::-1]
            spot = tuple(
                base.start + offset if isinstance(base, pl.Slice) else base
                for base, offset in zip(index, places)
            ) + (core,)
            target[spot] = target[spot] + source[tuple(places)]

        each(math.prod(shape), body, 4)

    every = (slice(None),) * (nb + 1)

    def begin(s):
        if s == 0:
            all_here()
        if s >= TWINS:
            pl.semaphore_wait(free_sem, 1)
        source = partial.at[(s % HELD,) + every + (1 - core,)]
        copies.start(s, 0, source, twin_ref.at[s % TWINS], place.sibling)

    def stage(s, step):
        mine = partial.at[s % HELD]
        if step == 0:
            copies.arrived(s, 0)
            add_to(mine, (pl.ds(0, nm),) + (pl.ds(0, 2),) * nb, twin_ref.at[s % TWINS])
            if s + TWINS < NJ:
                pl.semaphore_signal(free_sem, inc=1, device_id=place.sibling, device_id_type=MESH)
        else:
            for half in range(2):
                copies.arrived(s, slot_of(step - 1, half))
                index = place.pick(half, orders[half][step:])
                add_to(mine, index, stage_refs[step - 1][half].at[s])
        if step < nb:
            for half in range(2):
                order = orders[half]
                block = mine.at[place.pick(half, order[step + 1 :], order[step]) + (core,)]
                target = stage_refs[step][half].at[s]
                copies.start(s, slot_of(step, half), block, target, place.across(order[step]))
        else:
            for hops in range(1, nm):
                block = mine.at[place.mine((place.m + hops) % nm) + (core,)]
                copies.start(s, z_slot + hops - 1, block, z_ref.at[s, hops - 1], place.along(hops))

    def finish(s):
        summed = partial[(s % HELD,) + place.mine() + (core,)].astype(F32)
        for hops in range(1, nm):
            copies.arrived(s, z_slot + hops - 1)
            summed = summed + z_ref[s, hops - 1].astype(F32)
        total[PIECES[s]] = summed
        squares[...] += square_sum(summed)
        copies.drain(s)

    def weight_grad(s):
        j = PIECES[s]
        if j >= 4 and j % 2 == 1:
            f = (j - 5) // 2
            loads["hidden", f].wait()
            left, right = grad_low_t, HIDDEN
        elif j >= 4:
            left, right = normed_t, (j - 4) // 2
        elif j == 3:
            loads["mixed"].wait()
            left, right = grad_low_t, HIDDEN
        else:
            if j == 2:
                loads["n_one"].wait()
            left, right = normed_t, j

        def body(m):
            grads = dot_nn(left[...], pool[right, m]).astype(BF)
            partial.at[s % HELD, m].reshape(D, TILE)[...] = grads

        each(nm, body)
        if j in (5, 7, 9):
            load(("hidden", f + 1), hidden.at[f + 1], pool.at[HIDDEN])
        if j == 11:
            load("mixed", mixed, pool.at[HIDDEN])
        if j == 10:
            load("n_one", n_one_t, normed_t)

    def rows_of(at):
        return at // PER_WINDOW, span(at, BLOCK)

    def add_mod(window, which, values):
        grad_mod[window, which : which + 1, :] += jnp.sum(values, axis=0, keepdims=True)

    def head_unit():
        loads["br_two"].wait()
        loads["middle"].wait()
        grad_mod[...] = jnp.zeros_like(grad_mod)
        squares[...] = jnp.zeros_like(squares)

        def norms(at):
            window, here = rows_of(at)
            normed, inverse = row_norm(xa[here, :] + mod[window, 5:6, :] * xb[here, :])
            grad_rows[here, :] = normed
            inverses[here, :] = inverse
            grad_low[here, :] = normed.astype(BF)

        each(NBLOCK, norms)
        error = dot_nn(grad_low[...], head_mat) - noise[...]
        mask = row_mask[...]
        share = jnp.sum(error * error, axis=-1, keepdims=True) * (1.0 / PATCH) * mask
        loss[...] = jnp.sum(share, axis=0, keepdims=True) / token_total
        grad_pred = (2.0 / PATCH * error * mask / token_total).astype(BF)
        ends_rows[PATCH:, :] = dot_tn(grad_pred, grad_low[...])
        grad_in[...] = dot_nt(grad_pred, head_mat)

        def grads(at):
            window, here = rows_of(at)
            grad = norm_back(grad_in[here, :], grad_rows[here, :], inverses[here, :])
            add_mod(window, 5, grad * xb[here, :])
            grad_rows[here, :] = grad
            grad_low[here, :] = (grad * mod[window, 5:6, :]).astype(BF)

        each(NBLOCK, grads)
        transpose_rows(grad_low, grad_low_t)
        load(("slope", 0), slope.at[0], xa)
        load(("slope", 1), slope.at[1], xb)

    def slope_unit(f):
        loads["slope", f].wait()
        loads["w", 5 + 2 * f].wait()
        slopes = xa if f % 2 == 0 else xb

        def body(m):
            grad = dot_nn(grad_low[...], tile(0, m)[...])
            pool[f, m] = (grad * slopes[:, span(m, TILE)]).astype(BF)

        each(nm, body)
        if f + 2 < 4:
            load(("slope", f + 2), slope.at[f + 2], slopes)
        elif f == 2:
            load("middle2", middle, xa)
        else:
            load("br_one", branch_one, xb)
        load_tiles(7 + 2 * f if f < 3 else 3, 0)

    def add_rows(which, slot, fresh):
        def body(at):
            columns = span(at, TILE)
            left = jnp.concatenate([pool[which, m] for m in range(nm)], axis=1)
            right = jnp.concatenate([tile(slot, m)[columns, :] for m in range(nm)], axis=1)
            total = dot_nt(left, right)
            grad_in[:, columns] = total if fresh else grad_in[:, columns] + total

        each(D // TILE, body)

    def spread_unit(f):
        loads["w", 4 + 2 * f].wait()
        add_rows(f, 1, f == 0)
        load_tiles(6 + 2 * f if f < 3 else 2, 1)
        if f == 3:
            for part in range(3):
                load(("qkv", part), qkv.at[part], pool.at[QUERY + part])

    def norm_unit(which, after):
        def body(at):
            window, here = rows_of(at)
            normed, inverse = row_norm(xa[here, :])
            grad = grad_in[here, :]
            add_mod(window, which, grad)
            add_mod(window, which + 1, grad * normed)
            grad = grad * (1.0 + mod[window, which + 1 : which + 2, :])
            after(window, here, grad_rows[here, :] + norm_back(grad, normed, inverse))

        each(NBLOCK, body)

    def mid_unit():
        loads["middle2"].wait()
        loads["br_one"].wait()

        def after(window, here, grad):
            add_mod(window, 2, grad * xb[here, :])
            grad_rows[here, :] = grad
            grad_low[here, :] = (grad * mod[window, 2:3, :]).astype(BF)

        norm_unit(3, after)
        load("residual", residual, xa)
        loads["w", 3].wait()

        def body(m):
            pool[MIXED_GRAD, m] = dot_nn(grad_low[...], tile(0, m)[...]).astype(BF)

        each(nm, body)
        load_tiles(1, 0)

    def attend_unit(m):
        if m == 0:
            for part in range(3):
                loads["qkv", part].wait()

        def body(window):
            here = span(window, WTOK)
            query, key, value = (pool[QUERY + part, m, here, :] for part in range(3))
            grad_mixed = pool[MIXED_GRAD, m, here, :]
            grads = [jnp.zeros((WTOK, TILE), F32) for _ in range(3)]
            for head in range(TILE // HD):
                lanes = head_lanes(head, BF)
                scaled = lanes * HD ** (-0.5)
                own_query, own_grad = query * scaled, grad_mixed * lanes
                attn = soft_columns(key, own_query, row_mask[here, :])
                grads[2] = grads[2] + dot_nn(attn.astype(BF), own_grad)
                grad_attn = dot_nt(value, own_grad)
                inner = jnp.sum(attn * grad_attn, axis=0, keepdims=True)
                grad_scores = (attn * (grad_attn - inner)).astype(BF)
                grads[0] = grads[0] + dot_tn(grad_scores, key * scaled)
                grads[1] = grads[1] + dot_nn(grad_scores, own_query)
            pool[0, m, here, :] = grads[0].astype(BF)
            pool[1, m, here, :] = grads[1].astype(BF)
            pool[2, m, here, :] = grads[2].astype(BF)

        each(NMB, body)

    def inward_unit(j):
        slot = 1 if j != 1 else 0
        loads["w", j].wait()
        add_rows(j, slot, j == 2)
        if j == 2:
            load_tiles(0, 1)

    def last_unit():
        loads["residual"].wait()

        def after(window, here, grad):
            grad_low[here, :] = grad.astype(BF)

        norm_unit(0, after)
        embed_grad = jnp.zeros((PATCH, D), F32)
        for window in range(NMB):
            here = slice(window * WTOK, (window + 1) * WTOK)
            embed_grad = embed_grad + dot_nn(latents_in[window], grad_low[here, :])
        ends_rows[:PATCH, :] = embed_grad
        for index in range(nd):
            part = ends_rows[:, index * part_rows : (index + 1) * part_rows]
            ends[index // 2, index % 2] = part if part.shape == ends.shape[2:] else part.T
        mod_in[place.m] = grad_mod[...]
        swap.mp_gather(0, grad_mod, mod_in)
        swap.to_sibling(1, ends.at[:, 1 - core], ends_twin)

    own_copy = pltpu.make_async_copy(own_mod, all_mod.at[place.dp_id], own_sem)

    def swap_unit(step):
        if step == 0:
            swap.wait(0)
            for index in range(nm):
                for window in range(NMB):
                    for which in range(6):
                        row = index * NMB + window
                        mod_rows[which, row : row + 1, :] = mod_in[index, window, which : which + 1, :]
            for pair in range(3):
                both = mod_rows[2 * pair : 2 * pair + 2].reshape(2 * PER_INDEX, D)
                own_mod[pair] = both.astype(BF)
            own_copy.start()
            here = all_mod.at[place.dp_id]
            swap.chip_gather(2, own_mod, here)
            swap.to_sibling(3, own_mod, here, nd // 2 - 1)
            swap.wait(1)
            for chip in range(nd // 2):
                ends[chip, core] += ends_twin[chip]
            swap.chip_scatter(4, ends, ends_in)
        if step == 1:
            swap.wait(2)
            for hops in range(1, nd // 2):
                block = all_mod.at[place.chip(nd // 2 - hops) * 2 + core]
                swap.to_sibling(3, block, block, hops - 1)
            swap.wait(4)
            ends_z[place.m] = ends[place.dp_id // 2, core] + jnp.sum(ends_in[...], axis=0)
            swap.mp_gather(5, ends_z.at[place.m], ends_z)
        if step == 2:
            swap.wait(3)
            swap.wait(5)
            summed = jnp.sum(ends_z[...], axis=0)
            ends_sum[...] = summed if summed.shape == ends_sum.shape else summed.T
            squares[...] += square_sum(summed) * (1.0 / nm)
            own_copy.wait()
            swap.drain()

    units = {
        "head": head_unit,
        "slope": slope_unit,
        "spread": spread_unit,
        "mid": mid_unit,
        "attend": attend_unit,
        "inward": inward_unit,
        "last": last_unit,
        "swap": swap_unit,
    }

    def compute(turn):
        for when, (name, *args) in BACKWARD_TURNS:
            if when == turn:
                units[name](*args)

    last = max(when for when, _ in BACKWARD_TURNS)
    for turn in range(max(NJ + nb + 2, last + 1)):
        if turn == 0:
            compute(turn)
        if turn == 9:
            compute(turn)
        if turn == 8:
            transpose_rows(grad_low, grad_low_t)
        if turn < NJ:
            if turn == 1:
                loads["n_two"].wait()
            weight_grad(turn)
            begin(turn)
        for step in range(nb + 1):
            if 0 <= turn - 1 - step < NJ:
                stage(turn - 1 - step, step)
        if 0 <= turn - 2 - nb < NJ:
            finish(turn - 2 - nb)
        if turn not in (0, 9):
            compute(turn)


def backward_blocks(saved, residual, *in_vmem):
    nd, nm = lax.axis_size("dp"), lax.axis_size("mp")
    nb = nd.bit_length() - 2
    rows = D // nd
    bits = (2,) * nb
    slots = 2 * nb + nm
    stage_shapes = []
    for step in range(nb):
        high_first = tuple(1 if at <= step else 2 for at in range(nb))
        stage_shapes.append(pltpu.VMEM((NJ, nm // 2) + high_first + (rows, TILE), BF))
        stage_shapes.append(pltpu.VMEM((NJ, nm - nm // 2) + high_first[::-1] + (rows, TILE), BF))
    ends_part = (2 * PATCH, rows) if 2 * PATCH <= rows else (rows, 2 * PATCH)
    in_hbm = (*saved, residual)
    return pl.pallas_call(
        functools.partial(backward_kernel, nd, nm),
        out_shape=[
            jax.ShapeDtypeStruct((NJ, rows, TILE), F32),
            jax.ShapeDtypeStruct((1, 1), F32),
            jax.ShapeDtypeStruct((1, 1), F32),
            jax.ShapeDtypeStruct((2 * PATCH, rows), F32),
            jax.ShapeDtypeStruct((nd, 3, 2 * PER_INDEX, D), BF),
        ],
        in_specs=[pl.BlockSpec(memory_space=pl.ANY)] * len(in_hbm)
        + [pl.BlockSpec(memory_space=pltpu.VMEM)] * len(in_vmem),
        out_specs=[pl.BlockSpec(memory_space=pltpu.VMEM)] * 4 + [pl.BlockSpec(memory_space=pl.ANY)],
        scratch_shapes=[
            pltpu.VMEM((HELD, nm) + bits + (2, rows, TILE), BF),
            pltpu.VMEM((TWINS, nm) + bits + (rows, TILE), BF),
            pltpu.VMEM((ROWS, D), F32),
            pltpu.VMEM((ROWS, D), F32),
            pltpu.VMEM((ROWS, D), F32),
            pltpu.VMEM((ROWS, D), F32),
            pltpu.VMEM((ROWS, D), BF),
            pltpu.VMEM((D, ROWS), BF),
            pltpu.VMEM((D, ROWS), BF),
            pltpu.VMEM((9, nm, ROWS, TILE), BF),
            pltpu.VMEM((2, nm) + bits + (2, rows, TILE), BF),
            pltpu.VMEM((NJ, nm - 1, rows, TILE), BF),
            pltpu.VMEM((ROWS, PATCH), F32),
            pltpu.VMEM((ROWS, 1), F32),
            pltpu.VMEM((ROWS, 1), F32),
            pltpu.VMEM((2 * PATCH, D), F32),
            *stage_shapes,
            pltpu.SemaphoreType.DMA((NJ, slots)),
            pltpu.SemaphoreType.DMA((NJ, slots)),
            pltpu.SemaphoreType.REGULAR,
            pltpu.SemaphoreType.DMA((36,)),
            pltpu.VMEM((NMB, 6, D), F32),
            pltpu.VMEM((nm, NMB, 6, D), F32),
            pltpu.VMEM((6, PER_INDEX, D), F32),
            pltpu.VMEM((3, 2 * PER_INDEX, D), BF),
            pltpu.VMEM((nd // 2, 2) + ends_part, F32),
            pltpu.VMEM((nd // 2,) + ends_part, F32),
            pltpu.VMEM((nd // 2 - 1,) + ends_part, F32),
            pltpu.VMEM((nm,) + ends_part, F32),
            pltpu.SemaphoreType.DMA((6, max(nd // 2, nm - 1))),
            pltpu.SemaphoreType.DMA((6, max(nd // 2, nm - 1))),
            pltpu.SemaphoreType.DMA,
        ],
        compiler_params=pltpu.CompilerParams(
            collective_id=1, has_side_effects=True, vmem_limit_bytes=63 << 20
        ),
    )(*in_hbm, *in_vmem)


def tail_kernel(nd, nm, adaptive_state, loss, block_squares, all_mod_in, front, time_pre, condition, time_out, *refs):
    (adaptive_grad, time_in_grad, time_out_grad, classes_grad, sums) = refs[:5]
    (all_mod, act_rows, cond_all, terms, term_rows, adaptive) = refs[5:11]
    send_sems, recv_sems, load_sems = refs[11:]
    place = Place(nd, nm)
    swap = Exchange(place, send_sems, recv_sems)
    all_here = place.greet(everyone=True)
    loads = []
    pairs = ((all_mod_in, all_mod), (adaptive_state.at[0], adaptive))
    for at, (source, target) in enumerate(pairs):
        loads.append(pltpu.make_async_copy(source, target, load_sems.at[at]))
        loads[at].start()
    dp_id, m = place.dp_id, place.m
    windows, rows = time_pre.shape
    cond_act = silu(condition[...]).reshape(nd, PER_INDEX, rows)
    act_rows[...] = jnp.zeros_like(act_rows)
    for side in range(2):
        act_rows[side, :, side * PER_INDEX : (side + 1) * PER_INDEX, :] = cond_act
    features = front[:, :, :FREQ].reshape(windows, FREQ).astype(BF)
    time_hidden = silu(time_pre[...]).astype(BF)
    pick = label_pick(front, classes_grad.shape[0])
    squares = jnp.zeros((8, 128), F32)

    term_rows[m, 0] = jnp.zeros((8, 128), F32) + block_squares[...]
    term_rows[m, 1] = jnp.zeros((8, 128), F32) + loss[...]
    all_here()
    swap.mp_gather(2, term_rows.at[m], term_rows)
    loads[0].wait()
    loads[1].wait()
    grad_cond = jnp.zeros((windows, rows), F32)
    for which in range(6):
        pair, side = which // 2, which % 2
        block = all_mod[:, pair].reshape(nd * 2 * PER_INDEX, D)
        act = act_rows[side].reshape(nd * 2 * PER_INDEX, rows).astype(BF)
        gradient = dot_tn(act, block)
        adaptive_grad[which] = gradient
        squares = squares + square_sum(gradient)
        back = dot_nt(block, adaptive[which].astype(BF)).reshape(nd, 2, PER_INDEX, rows)
        grad_cond = grad_cond + back[:, side].reshape(windows, rows)
    grad_cond = (grad_cond * silu_slope(condition[...])).astype(BF)
    cond_all[dp_id] = grad_cond
    swap.dp_gather(0, cond_all.at[dp_id], cond_all)
    gradient = dot_tn(pick, grad_cond)
    classes_grad[...] = gradient
    squares = squares + square_sum(gradient)
    swap.wait(0)
    grad_time = jnp.zeros((windows, rows), F32)
    for index in range(nd):
        gradient = dot_tn(time_hidden, cond_all[index])
        time_out_grad[:, index * rows : (index + 1) * rows] = gradient
        squares = squares + square_sum(gradient)
        grad_time = grad_time + dot_nt(cond_all[index], time_out[index])
    grad_time = (grad_time * silu_slope(time_pre[...])).astype(BF)
    gradient = dot_tn(features, grad_time)
    time_in_grad[...] = gradient
    squares = squares + square_sum(gradient)

    swap.wait(2)
    term_sums = jnp.sum(term_rows[...], axis=0)
    terms[dp_id, 0] = squares + term_sums[0]
    terms[dp_id, 1] = term_sums[1]
    swap.dp_gather(1, terms.at[dp_id], terms)
    swap.wait(1)
    sums[...] = jnp.sum(terms[...], axis=0)
    swap.drain()


def tail_blocks(*operands):
    nd, nm = lax.axis_size("dp"), lax.axis_size("mp")
    rows = D // nd
    windows = nd * PER_INDEX
    classes = CLASSES + -CLASSES % 128
    shapes = [
        (6, rows, D),
        (FREQ, rows),
        (rows, D),
        (classes, rows),
        (2, 8, 128),
    ]
    return pl.pallas_call(
        functools.partial(tail_kernel, nd, nm),
        out_shape=[jax.ShapeDtypeStruct(shape, F32) for shape in shapes],
        in_specs=[
            pl.BlockSpec(memory_space=pl.ANY if at in (0, 3) else pltpu.VMEM)
            for at in range(len(operands))
        ],
        out_specs=[pl.BlockSpec(memory_space=pltpu.VMEM)] * len(shapes),
        scratch_shapes=[
            pltpu.VMEM((nd, 3, 2 * PER_INDEX, D), BF),
            pltpu.VMEM((2, nd, 2 * PER_INDEX, rows), F32),
            pltpu.VMEM((nd, windows, rows), BF),
            pltpu.VMEM((nd, 2, 8, 128), F32),
            pltpu.VMEM((nm, 2, 8, 128), F32),
            pltpu.VMEM((6, rows, D), F32),
            pltpu.SemaphoreType.DMA((3, max(nd, nm) - 1)),
            pltpu.SemaphoreType.DMA((3, max(nd, nm) - 1)),
            pltpu.SemaphoreType.DMA((2,)),
        ],
        compiler_params=pltpu.CompilerParams(
            collective_id=2, has_side_effects=True, vmem_limit_bytes=40 << 20
        ),
    )(*operands)


def adam_update(weight, first, root, gradient, factor):
    clipped = gradient * factor
    first = beta_one * first + (1.0 - beta_one) * clipped
    root = jnp.sqrt(beta_two * root * root + (1.0 - beta_two) * clipped * clipped)
    update = (
        first
        / (1.0 - beta_one**step_count)
        / (root / math.sqrt(1.0 - beta_two**step_count) + adam_eps)
    )
    return weight - learn_rate * (update + weight_decay * weight), first, root


def chunk_rows(rows, lanes):
    limit = max(16, 16384 // max(lanes, 128))
    return max(size for size in range(8, limit + 1, 8) if rows % size == 0)


def adam_kernel(names, *refs):
    count = len(names)
    states = dict(zip(names, refs[:count]))
    reduced, ends, time_in, time_out, classes, adaptive, sums = refs[count : count + 7]
    refs = refs[count + 7 :]
    targets = dict(zip(names, zip(refs[: 2 * count : 2], refs[1 : 2 * count : 2])))
    held = dict(zip(names, refs[2 * count : 3 * count]))
    load_sems, store_sems = refs[3 * count :]
    squares = sums[0, 0:1, 0:1]
    factor = jnp.minimum(1.0, threshold / jnp.sqrt(squares))
    loads, stores = {}, []

    def parts_of(name):
        lead = held[name].shape[1:-2]
        return [(at,) for at in range(lead[0])] if lead else [()]

    for name in names:
        for part in parts_of(name):
            every = (slice(None),) + part
            copy = pltpu.make_async_copy(
                states[name].at[every], held[name].at[every], load_sems.at[len(loads)]
            )
            copy.start()
            loads[name, part] = copy

    def apply(where, gradient):
        ref, part, rows, columns = where
        spot = lambda which: (which,) + part + (rows, columns)
        values = [ref[spot(which)] for which in range(3)]
        for which, value in enumerate(adam_update(*values, gradient, factor)):
            ref[spot(which)] = value

    def store(name, part):
        weight, moments = targets[name]
        copies = (
            (held[name].at[(0,) + part], weight.at[part] if part else weight),
            (held[name].at[(pl.ds(1, 2),) + part], moments.at[(slice(None),) + part]),
        )
        for source, target in copies:
            copy = pltpu.make_async_copy(source, target, store_sems.at[len(stores)])
            copy.start()
            stores.append(copy)

    def rowwise(name, part, source, first_row=0):
        rows, lanes = held[name].shape[-2:]
        size = chunk_rows(rows, lanes)

        def body(at):
            here = span(at, size)
            there = pl.ds(pl.multiple_of(first_row + at * size, 8), size)
            apply((held[name], part, here, slice(None)), source[there, :])

        each(rows // size, body)

    every = slice(None)
    for name in names:
        for part in parts_of(name):
            loads[name, part].wait()
            if name == "adapt":
                rowwise(name, part, adaptive.at[part[0]])
            elif name == "attn_in":
                rowwise(name, part, reduced.at[part[0]])
            elif name == "expand":
                for f in range(4):
                    columns = slice(f * TILE, (f + 1) * TILE)
                    apply((held[name], part, every, columns), reduced[4 + 2 * f])
            elif name == "contract":
                for f in range(4):
                    rows = slice(f * TILE, (f + 1) * TILE)
                    apply((held[name], part, rows, every), reduced[5 + 2 * f].T)
            elif name == "attn_out":
                apply((held[name], part, every, every), reduced[3].T)
            elif name == "embed":
                rowwise(name, part, ends)
            elif name == "head":
                rowwise(name, part, ends, PATCH)
            else:
                rowwise(name, part, {"time_in": time_in, "time_out": time_out, "classes": classes}[name])
            store(name, part)
    for copy in stores:
        copy.wait()


def adam_blocks(states, *gradients):
    names = list(states)
    shapes = [states[name].shape for name in names]
    outs = []
    for shape in shapes:
        outs += [shape[1:], (2,) + shape[1:]]
    pieces = sum(shape[1] if len(shape) == 4 else 1 for shape in shapes)
    return pl.pallas_call(
        functools.partial(adam_kernel, names),
        out_shape=[jax.ShapeDtypeStruct(shape, F32) for shape in outs],
        in_specs=[pl.BlockSpec(memory_space=pl.ANY)] * len(names)
        + [pl.BlockSpec(memory_space=pltpu.VMEM)] * len(gradients),
        out_specs=[pl.BlockSpec(memory_space=pl.ANY)] * len(outs),
        scratch_shapes=[pltpu.VMEM(shape, F32) for shape in shapes]
        + [pltpu.SemaphoreType.DMA((pieces,)), pltpu.SemaphoreType.DMA((2 * pieces,))],
        compiler_params=pltpu.CompilerParams(vmem_limit_bytes=40 << 20),
    )(*states.values(), *gradients)


def per_device(
    latents,
    noise_target,
    token_mask,
    timesteps,
    labels,
    state_embed,
    state_head,
    state_time_in,
    state_time_out,
    state_classes,
    state_adaptive,
    state_attention_in,
    state_attention_out,
    state_expand,
    state_contract,
):
    nd = lax.axis_size("dp")
    rows = state_attention_in.shape[1]
    states = {
        "adapt": state_adaptive.transpose(0, 2, 1, 3),
        "attn_in": state_attention_in.transpose(0, 2, 1, 3),
        "expand": state_expand,
        "contract": state_contract,
        "time_out": state_time_out,
        "classes": state_classes,
        "attn_out": state_attention_out,
        "time_in": state_time_in,
        "embed": state_embed,
        "head": state_head.transpose(0, 2, 1),
    }
    lanes = jnp.arange(FREQ + 128)[None, :]
    step_ids = timesteps[0].T.reshape(PER_INDEX, 1).astype(F32)
    label_ids = labels[0].T.reshape(PER_INDEX, 1).astype(F32)
    half_width = FREQ // 2
    frequency = jnp.exp(-math.log(10000.0) * (lanes % half_width).astype(F32) / half_width)
    angles = step_ids * frequency
    features = jnp.where(lanes < half_width, jnp.cos(angles), jnp.sin(angles))
    front = jnp.where(lanes < FREQ, features.astype(BF).astype(F32), label_ids)
    flags = token_mask.reshape(NMB, WTOK)
    latent_columns = latents[0].transpose(0, 2, 1)
    noise_columns = noise_target[0].transpose(0, 2, 1)
    residual, mod, ends, front_all, time_pre, condition, token_total, time_out_part, *saved = forward_blocks(
        states, flags, front, latent_columns, window_positions()
    )
    reduced, loss_local, squares, ends_sum, all_mod = backward_blocks(
        saved, residual, mod, flags, token_total, noise_columns, latent_columns, ends
    )
    adaptive_grad, time_in_grad, time_out_grad, classes_grad, sums = tail_blocks(
        states["adapt"],
        loss_local,
        squares,
        all_mod,
        front_all,
        time_pre,
        condition,
        time_out_part,
    )
    updated = adam_blocks(
        states,
        reduced,
        ends_sum,
        time_in_grad,
        time_out_grad,
        classes_grad,
        adaptive_grad,
        sums,
    )
    new = dict(zip(states, zip(updated[::2], updated[1::2])))
    back = {"adapt": (1, 0, 2), "attn_in": (1, 0, 2), "head": (1, 0)}
    results = [sums[1, 0, 0], jnp.sqrt(sums[0, 0, 0])]
    order = ("embed", "head", "time_in", "time_out", "classes", "adapt", "attn_in")
    for name in order + ("attn_out", "expand", "contract"):
        weight, moments = new[name]
        if name in back:
            axes = back[name]
            weight = weight.transpose(axes)
            moments = moments.transpose((0,) + tuple(1 + axis for axis in axes))
        results += [weight, moments]
    return tuple(results)


def solution(mesh):
    in_specs = (
        P("dp", None, "mp", None),
        P("dp", None, "mp", None),
        P("dp", None, "mp"),
        P("dp", None, None),
        P("dp", None, None),
        P(None, None, "dp"),
        P(None, "dp", None),
        P(None, None, "dp"),
        P(None, "dp", None),
        P(None, None, "dp"),
        P(None, "dp", None, None),
        P(None, "dp", None, "mp"),
        P(None, "mp", "dp"),
        P(None, "dp", "mp"),
        P(None, "mp", "dp"),
    )
    out_specs = (
        P(),
        P(),
        P(None, "dp"),
        P(None, None, "dp"),
        P("dp", None),
        P(None, "dp", None),
        P(None, "dp"),
        P(None, None, "dp"),
        P("dp", None),
        P(None, "dp", None),
        P(None, "dp"),
        P(None, None, "dp"),
        P("dp", None, None),
        P(None, "dp", None, None),
        P("dp", None, "mp"),
        P(None, "dp", None, "mp"),
        P("mp", "dp"),
        P(None, "mp", "dp"),
        P("dp", "mp"),
        P(None, "dp", "mp"),
        P("mp", "dp"),
        P(None, "mp", "dp"),
    )
    return jax.shard_map(
        per_device, mesh=mesh, in_specs=in_specs, out_specs=out_specs, check_vma=False
    )
```

```python
import functools
import math

import jax
import jax.numpy as jnp
import numpy as np
from jax import lax
from jax.experimental import pallas as pl
from jax.experimental.pallas import tpu as pltpu
from jax.sharding import PartitionSpec as P

D = 1024
HEADS = 16
HD = 64
PATCH = 32
FREQ = 256
CLASSES = 600
WTOK = 320
NMB = 2
WMB = 4
TILE = 256
NJ = 12
ROWS = NMB * WTOK
MESH = pl.DeviceIdType.MESH
BF = jnp.bfloat16
F32 = jnp.float32


beta_one = 0.9
beta_two = 0.999
adam_eps = 1e-08
learn_rate = 0.15
weight_decay = 0.1
threshold = 0.002
step_count = 10.0


def window_positions():
    half_width = D // 2
    steps = np.arange(half_width, dtype=np.float32)
    frequency = np.exp(np.float32(-math.log(10000.0)) * steps / np.float32(half_width))
    angles = np.arange(WTOK, dtype=np.float32)[:, None] * frequency.astype(np.float32)[None, :]
    table = np.concatenate([np.sin(angles), np.cos(angles)], axis=-1)
    return jnp.asarray(table.astype(np.float32))


def dot_general(a, b, a_dim, b_dim):
    return lax.dot_general(a, b, (((a_dim,), (b_dim,)), ((), ())), preferred_element_type=F32)


def dot_nn(a, b):
    return jnp.dot(a, b, preferred_element_type=F32)


def dot_nt(a, b):
    return dot_general(a, b, 1, 1)


def dot_tn(a, b):
    return dot_general(a, b, 0, 0)


def norm_back(grad, normed, inverse):
    mean_grad = jnp.mean(grad, axis=-1, keepdims=True)
    mean_prod = jnp.mean(grad * normed, axis=-1, keepdims=True)
    return inverse * (grad - mean_grad - normed * mean_prod)


def silu(values):
    return values * jax.nn.sigmoid(values)


def silu_slope(values):
    gate = jax.nn.sigmoid(values)
    return gate * (1.0 + values * (1.0 - gate))


def gelu_parts(up):
    cdf = 0.5 * (1.0 + lax.erf(up * math.sqrt(0.5)))
    pdf = jnp.exp(-0.5 * up * up) * (1.0 / math.sqrt(2.0 * math.pi))
    return up * cdf, cdf + up * pdf


def tokens3(values):
    return values.reshape(NMB, WTOK, -1)


def flip(bits, at):
    return [1 - bit if place == at else bit for place, bit in enumerate(bits)]


class Place:
    def __init__(self, nd, nm):
        self.nm = nm
        self.nb = nd.bit_length() - 2
        dp_id = lax.axis_index("dp")
        self.nd = nd
        self.dp_id = dp_id
        self.m = lax.axis_index("mp")
        self.core = dp_id % 2
        self.bits = [dp_id // (1 << (self.nb - at)) % 2 for at in range(self.nb)]
        self.sibling = {"dp": self.dp_of(self.bits, 1 - self.core), "mp": self.m}
        self.orders = (list(range(self.nb))[::-1], list(range(self.nb)))
        self.halves = (pl.ds(0, nm // 2), pl.ds(nm // 2, nm - nm // 2))

    def dp_of(self, bits, core):
        total = core
        for at, bit in enumerate(bits):
            total = total + bit * (1 << (self.nb - at))
        return total

    def across(self, at):
        return {"dp": self.dp_of(flip(self.bits, at), self.core), "mp": self.m}

    def along(self, hops):
        return {"dp": self.dp_of(self.bits, self.core), "mp": (self.m + hops) % self.nm}

    def facing(self, hops):
        return {"dp": self.chip(hops) * 2 + self.core, "mp": self.m}

    def chip(self, hops):
        return (self.dp_id // 2 + hops) % (self.nd // 2)

    def beside(self, hops):
        return {"dp": (self.dp_id + hops) % self.nd, "mp": self.m}

    def pick(self, half, done, flipped=None):
        where = flip(self.bits, flipped)
        return (self.halves[half],) + tuple(
            pl.ds(0, 2) if at in done else pl.ds(where[at], 1) for at in range(self.nb)
        )

    def mine(self, m=None):
        return (self.m if m is None else m,) + tuple(self.bits)

    def greet(self, everyone=False):
        barrier = pltpu.get_barrier_semaphore()
        if everyone:
            others = [self.beside(hops) for hops in range(1, self.nd)]
        else:
            others = [self.sibling] + [self.facing(hops) for hops in range(1, self.nd // 2)]
        others += [self.along(hops) for hops in range(1, self.nm)]
        for other in others:
            pl.semaphore_signal(barrier, inc=1, device_id=other, device_id_type=MESH)
        return lambda: pl.semaphore_wait(barrier, len(others))


class Copies:
    def __init__(self, send_sems, recv_sems):
        self.send_sems, self.recv_sems = send_sems, recv_sems
        self.started = {}

    def start(self, step, slot, source, target, device):
        copy = pltpu.make_async_remote_copy(
            src_ref=source,
            dst_ref=target,
            send_sem=self.send_sems.at[step, slot],
            recv_sem=self.recv_sems.at[step, slot],
            device_id=device,
            device_id_type=MESH,
        )
        copy.start()
        self.started[step, slot] = copy

    def arrived(self, step, slot):
        self.started[step, slot].wait_recv()

    def drain(self, step=None):
        for key in list(self.started):
            if step is None or key[0] == step:
                self.started.pop(key).wait_send()


class Exchange:
    def __init__(self, place, send_sems, recv_sems):
        self.place = place
        self.copies = Copies(send_sems, recv_sems)

    def dp_gather(self, group, source, target):
        for hops in range(1, self.place.nd):
            here = target.at[self.place.dp_id]
            self.copies.start(group, hops - 1, source, here, self.place.beside(hops))

    def to_sibling(self, group, source, target, slot=0):
        self.copies.start(group, slot, source, target, self.place.sibling)

    def chip_scatter(self, group, source, target):
        for hops in range(1, self.place.nd // 2):
            block = source.at[self.place.chip(hops), self.place.core]
            self.copies.start(group, hops - 1, block, target.at[hops - 1], self.place.facing(hops))

    def chip_gather(self, group, source, target):
        for hops in range(1, self.place.nd // 2):
            self.copies.start(group, hops - 1, source, target, self.place.facing(hops))

    def mp_gather(self, group, source, target):
        for hops in range(1, self.place.nm):
            here = target.at[self.place.m]
            self.copies.start(group, hops - 1, source, here, self.place.along(hops))

    def wait(self, group):
        for step, slot in list(self.copies.started):
            if step == group:
                self.copies.arrived(step, slot)

    def drain(self):
        self.copies.drain()


def gather_steps(
    place, shard, whole, send_sems, recv_sems, local_sems, all_here, prepare, load, compute, last
):
    nm, nb, core = place.nm, place.nb, place.core
    copies = Copies(send_sems, recv_sems)
    stage_slot = lambda stage, half: nm - 1 + 2 * stage + half
    twin = nm - 1 + 2 * nb
    wide = ARRIVALS[-1]
    count = NJ - 1
    late = 2 * twin + 1
    wide_z = lambda part, hops: (0 if part == 0 else late) + hops - 1
    wide_twin = lambda part, hops: (twin if part == 0 else late + nm - 1) + hops - 1
    locals_ = {}

    def begin_local(j):
        here = whole.at[(j,) + place.mine() + (core,)]
        locals_[j] = pltpu.make_async_copy(shard.at[j], here, local_sems.at[j])
        locals_[j].start()
        copies.start(j, 2 * twin, shard.at[j], here, place.sibling)

    def begin(j):
        here = whole.at[(j,) + place.mine() + (core,)]
        for hops in range(1, nm):
            copies.start(j, hops - 1, shard.at[j], here, place.along(hops))
        begin_local(j)

    def half_of_wide(half, bits):
        lanes = pl.ds(half * (TILE // 2), TILE // 2)
        return whole.at[(wide, place.m) + bits + (core, slice(None), lanes)]

    def wide_stage(step):
        if step == 1:
            locals_[wide].wait()
        for half in range(2):
            order = place.orders[half]
            if step > 0:
                copies.arrived(wide, stage_slot(step - 1, half))
            if step == 0:
                source = shard.at[wide, :, pl.ds(half * (TILE // 2), TILE // 2)]
                block = half_of_wide(half, tuple(place.bits))
                copies.start(wide, stage_slot(0, half), source, block, place.across(order[0]))
            elif step < nb:
                block = half_of_wide(half, place.pick(half, order[:step])[1:])
                copies.start(wide, stage_slot(step, half), block, block, place.across(order[step]))
            if step > 0:
                block = half_of_wide(half, place.pick(half, order[: step - 1], order[step - 1])[1:])
                copies.start(wide, twin + stage_slot(step - 1, half), block, block, place.sibling)

    def part_of_wide(part, m):
        return whole.at[(wide, m, pl.ds(part, 1)) + (pl.ds(0, 2),) * (nb - 1) + (core,)]

    def wide_send(part):
        block = part_of_wide(part, place.m)
        for hops in range(1, nm):
            copies.start(wide, wide_z(part, hops), block, block, place.along(hops))

    def wide_pass(part):
        for hops in range(1, nm):
            copies.arrived(wide, wide_z(part, hops))
            block = part_of_wide(part, (place.m + nm - hops) % nm)
            copies.start(wide, wide_twin(part, hops), block, block, place.sibling)

    def stage(j, step):
        if step == 0:
            locals_[j].wait()
            for hops in range(1, nm):
                copies.arrived(j, hops - 1)
        else:
            for half in range(2):
                copies.arrived(j, stage_slot(step - 1, half))
        if step < nb:
            for half in range(2):
                order = place.orders[half]
                block = whole.at[(j,) + place.pick(half, order[:step]) + (core,)]
                copies.start(j, stage_slot(step, half), block, block, place.across(order[step]))
        if step == 0:
            for hops in range(1, nm):
                block = whole.at[(j,) + place.mine((place.m + nm - hops) % nm) + (core,)]
                copies.start(j, twin + hops - 1, block, block, place.sibling)
        else:
            for half in range(2):
                order = place.orders[half]
                block = whole.at[
                    (j,) + place.pick(half, order[: step - 1], order[step - 1]) + (core,)
                ]
                copies.start(j, twin + stage_slot(step - 1, half), block, block, place.sibling)

    def finish(j):
        for slot in range(twin, 2 * twin + 1):
            copies.arrived(j, slot)
        if j == wide:
            for hops in range(1, nm):
                copies.arrived(j, wide_twin(1, hops))
        load(j)

    prepare(ARRIVALS[0])
    prepare(wide)
    all_here()
    begin(ARRIVALS[0])
    wide_stage(0)
    begin_local(wide)
    for at in range(1, 3):
        prepare(ARRIVALS[at])
        begin(ARRIVALS[at])
    prepare(ARRIVALS[3])
    for turn in range(max(NJ + nb + 1, last + nb - 1)):
        for step in range(nb + 1):
            if 0 <= turn - step < count:
                stage(ARRIVALS[turn - step], step)
        if 1 <= turn + 1 <= nb:
            wide_stage(turn + 1)
        if turn + 3 < count:
            begin(ARRIVALS[turn + 3])
        if turn in (nb, nb + 3):
            wide_send(0 if turn == nb else 1)
        if turn in (nb + 5, nb + 8):
            wide_pass(0 if turn == nb + 5 else 1)
        if turn == nb + 10:
            finish(wide)
        if 0 <= turn - 1 - nb < count:
            finish(ARRIVALS[turn - 1 - nb])
        if turn + 4 < count:
            prepare(ARRIVALS[turn + 4])
        compute(turn + 2 - nb)
    copies.drain()


def row_norm(values):
    center = values - jnp.mean(values, axis=-1, keepdims=True)
    inverse = lax.rsqrt(jnp.mean(center * center, axis=-1, keepdims=True) + 1e-06)
    return center * inverse, inverse


def each(count, body, unroll=1):
    lax.fori_loop(0, count, lambda at, carry: (body(at), carry)[1], 0, unroll=math.gcd(count, unroll))


def span(at, size):
    return pl.ds(pl.multiple_of(at * size, size), size)


def head_lanes(head, dtype=F32):
    lanes = lax.broadcasted_iota(jnp.int32, (1, TILE), 1) // HD
    return (lanes == head).astype(dtype)


def soft_rows(query, key, key_bias):
    scores = dot_nt(query, key)
    scores = jnp.where(key_bias > 0, scores, -1e30)
    exponents = jnp.exp(scores - jnp.max(scores, axis=-1, keepdims=True))
    return exponents * (1.0 / jnp.sum(exponents, axis=-1, keepdims=True))


def label_pick(front, count):
    labels = front[:, :, FREQ : FREQ + 1].reshape(-1, 1)
    lanes = lax.broadcasted_iota(jnp.int32, (labels.shape[0], count), 1).astype(F32)
    return (lanes == labels).astype(BF)


PER_INDEX = NMB * WMB
def soft_columns(key, query, key_mask):
    scores = dot_nt(key, query)
    scores = jnp.where(key_mask > 0, scores, -1e30)
    exponents = jnp.exp(scores - jnp.max(scores, axis=0, keepdims=True))
    return exponents * (1.0 / jnp.sum(exponents, axis=0, keepdims=True))


BLOCK = 64
PER_WINDOW = WTOK // BLOCK
NBLOCK = ROWS // BLOCK
LANE_BLOCK = 128


def token_rows(source, target):
    for window in range(NMB):
        target[window * WTOK : (window + 1) * WTOK, :] = source[window].T


def mask_column(source, target):
    for window in range(NMB):
        row = jnp.broadcast_to(source[window : window + 1, :].astype(F32), (8, WTOK))
        target[window * WTOK : (window + 1) * WTOK, :] = row.T[:, 0:1]


def square_sum(values):
    return jnp.sum(jnp.sum(values * values, axis=0, keepdims=True), axis=1, keepdims=True)


def transpose_rows(source, target):
    def body(at):
        target[:, span(at, LANE_BLOCK)] = source[span(at, LANE_BLOCK), :].T

    each(ROWS // LANE_BLOCK, body)


ARRIVALS = (0, 1, 2, 3, 4, 6, 8, 10, 5, 7, 9, 11)
FORWARD_TURNS = (
    (4, ("qkv", 0)),
    (5, ("qkv", 1)),
    (6, ("qkv", 2)),
    (6, ("attend", 0)),
    (7, ("attend", 1)),
    (7, ("attend", 2)),
    (7, ("attend", 3)),
    (8, ("out",)),
    (9, ("up", 0)),
    (9, ("up", 1)),
    (10, ("up", 2)),
    (11, ("up", 3)),
    (12, ("down", 0)),
    (13, ("down", 1)),
    (13, ("down", 3)),
    (14, ("down", 2)),
)


def forward_kernel(nd, nm, states, flags, times_in, latents_in, positions, *refs):
    (residual_out, mod, ends, front, time_pre, condition, token_total, time_out) = refs[:8]
    refs = refs[8:]
    (residual, parts, parts_twin, parts_in, mods, mods_twin, mods_in) = refs[-12:-5]
    (rows_ref, counts, ends_all, swap_send, swap_recv) = refs[-5:]
    (shard, held_in, held_out, held_up, held_down, adaptive, time_in, classes, held_embed, held_head, ends_in, front_in, latents, held_time, state_sems) = refs[-27:-12]
    refs = refs[:-27]
    place = Place(nd, nm)
    swap = Exchange(place, swap_send, swap_recv)
    all_here = place.greet(everyone=True)
    state_loads = {}
    class_pad = classes.shape[0] - CLASSES
    wanted_states = {
        "attn_in": held_in,
        "contract": held_down,
        "embed": held_embed,
        "head": held_head,
        "time_in": time_in,
        "time_out": held_time,
        "classes": classes.at[pl.ds(0, CLASSES)],
        "adapt": adaptive,
        "attn_out": held_out,
        "expand": held_up,
    }
    for at, (name, target) in enumerate(wanted_states.items()):
        state_loads[name] = pltpu.make_async_copy(states[name].at[0], target, state_sems.at[at])
        state_loads[name].start()

    def state_ready(name):
        if name in state_loads:
            state_loads.pop(name).wait()

    def prepare(j):
        if j < 3:
            state_ready("attn_in")
            values = held_in[j]
        elif j == 3:
            state_ready("attn_out")
            values = held_out[...].T
        elif j % 2 == 0:
            state_ready("expand")
            values = held_up[:, (j - 4) // 2 * TILE : (j - 2) // 2 * TILE]
        else:
            state_ready("contract")
            values = held_down[(j - 5) // 2 * TILE : (j - 3) // 2 * TILE, :].T
        shard[j] = values.astype(BF)

    dp_id = place.dp_id
    part_rows = D // nd
    windows = nd * PER_INDEX
    upright = parts.shape[2] == windows
    (whole, n_one_t, qkv_out, mixed_out, branch_one_out, middle_out, n_two_t, hidden_out, slope_out, branch_two_out) = refs[:10]
    (n_one, qkv, mixed, branch_one, middle, n_two, flipped, hidden, slope, branch_two, loaded) = refs[10:21]
    send_sems, recv_sems, local_sems, load_sems, spill_sems = refs[21:]
    spilled, spill_count = {}, []

    def spill(name, source, target):
        copy = pltpu.make_async_copy(source, target, spill_sems.at[len(spill_count)])
        copy.start()
        spill_count.append(name)
        spilled[name] = copy

    loads = {}
    slots = loaded.shape[0]

    def load(j):
        loads[j] = pltpu.make_async_copy(whole.at[j], loaded.at[ARRIVALS.index(j) % slots], load_sems.at[j])
        loads[j].start()

    def tile(j, m):
        return loaded.at[ARRIVALS.index(j) % slots, m].reshape(D, TILE)

    def first_swap():
        state_ready("embed")
        state_ready("head")
        ends_in[0] = held_embed[...].astype(BF)
        ends_in[1] = held_head[...].astype(BF)
        front_in[:, : FREQ + 128] = times_in[...]
        count = jnp.sum(jnp.sum(flags[...].astype(F32), axis=0, keepdims=True), axis=1, keepdims=True)
        front_in[:, FREQ + 128 :] = jnp.broadcast_to(count, (PER_INDEX, 128))
        classes[CLASSES:, :] = jnp.zeros((class_pad, classes.shape[1]), F32)
        token_rows(latents_in, latents)
        front[dp_id] = front_in[...]
        ends_all[dp_id] = ends_in[...]
        swap.dp_gather(0, front_in, front)
        swap.dp_gather(1, ends_in, ends_all)

    def time_layers():
        state_ready("time_out")
        for index in range(nd):
            time_out[index] = held_time[:, index * part_rows : (index + 1) * part_rows].astype(BF)
        swap.wait(0)
        features = front[:, :, :FREQ].reshape(windows, FREQ).astype(BF)
        state_ready("time_in")
        time_pre[...] = dot_nn(features, time_in[...].astype(BF))
        time_hidden = silu(time_pre[...]).astype(BF)
        for index in range(nd):
            if upright:
                parts[index // 2, index % 2] = dot_nn(time_hidden, time_out[index])
            else:
                parts[index // 2, index % 2] = dot_general(time_out[index], time_hidden, 0, 1)
        swap.to_sibling(2, parts.at[:, 1 - place.core], parts_twin)
        counts[place.m] = jnp.sum(front[:, :, FREQ + 128 :], axis=0)
        swap.mp_gather(5, counts.at[place.m], counts)
        swap.wait(2)
        for chip in range(nd // 2):
            parts[chip, place.core] += parts_twin[chip]
        swap.chip_scatter(3, parts, parts_in)

    def condition_layers():
        state_ready("classes")
        state_ready("adapt")
        swap.wait(3)
        total = parts[dp_id // 2, place.core] + jnp.sum(parts_in[...], axis=0)
        total = total if upright else total.T
        total = total + dot_nn(label_pick(front, classes.shape[0]), classes[...].astype(BF))
        condition[...] = total
        row_ids = lax.broadcasted_iota(jnp.int32, (nd * NMB, windows), 0)
        column_ids = lax.broadcasted_iota(jnp.int32, (nd * NMB, windows), 1)
        wanted = row_ids // NMB * PER_INDEX + place.m * NMB + row_ids % NMB
        own = dot_nn((wanted == column_ids).astype(BF), silu(total).astype(BF)).astype(BF)
        for which in range(6):
            rows_ref[...] = dot_nn(own, adaptive[which].astype(BF))

            def move(row):
                index, window = row // NMB, row % NMB
                spot = (index // 2, index % 2, window, slice(which, which + 1))
                mods[spot] = rows_ref[pl.ds(row, 1), :]

            each(nd * NMB, move)
        swap.to_sibling(6, mods.at[:, 1 - place.core], mods_twin)
        swap.wait(6)
        for chip in range(nd // 2):
            for window in range(NMB):
                mods[chip, place.core, window] += mods_twin[chip, window]
        swap.chip_scatter(4, mods, mods_in)

    def modulation():
        swap.wait(4)
        for window in range(NMB):
            mod[window] = mods[dp_id // 2, place.core, window] + jnp.sum(mods_in[:, window], axis=0)
        swap.wait(5)
        token_total[...] = jnp.sum(counts[...], axis=0)
        swap.wait(1)

        def turn_ends(index):
            for which in range(2):
                ends[which, index] = ends_all[index, which].astype(F32).T.astype(BF)

        each(nd, turn_ends)
        embed_mat = ends[0].reshape(D, PATCH)

        def body(window):
            here = span(window, WTOK)
            residual[here, :] = dot_nt(latents[here, :], embed_mat) + positions[...]

        each(NMB, body)
        spill("residual", residual, residual_out)

    def first_norm():
        def body(at):
            window, here = at // PER_WINDOW, span(at, BLOCK)
            normed, _ = row_norm(residual[here, :])
            normed = normed * (1.0 + mod[window, 1:2, :]) + mod[window, 0:1, :]
            n_one[here, :] = normed.astype(BF)

        each(NBLOCK, body)
        transpose_rows(n_one, flipped.at[0])
        spill("n_one", flipped.at[0], n_one_t)

    def qkv_unit(j):
        def body(m):
            qkv[j, m] = dot_nn(n_one[...], tile(j, m)[...]).astype(BF)

        each(nm, body)
        spill(("qkv", j), qkv.at[j], qkv_out.at[j])

    def attend_unit(m):
        def body(window):
            here = span(window, WTOK)
            query, key, value = qkv[0, m, here, :], qkv[1, m, here, :], qkv[2, m, here, :]
            total = jnp.zeros((WTOK, TILE), F32)
            for head in range(TILE // HD):
                lanes = head_lanes(head, BF)
                attn = soft_rows(query * (lanes * HD ** (-0.5)), key, flags[pl.ds(window, 1), :]).astype(BF)
                total = total + dot_nn(attn, value * lanes)
            mixed[m, here, :] = total.astype(BF)

        each(NMB, body)
        if m == nm - 1:
            spill("mixed", mixed, mixed_out)

    def add_nt(source, j, target, fresh):
        def body(at):
            columns = span(at, TILE)
            left = jnp.concatenate([source[m] for m in range(nm)], axis=1)
            right = jnp.concatenate([tile(j, m)[columns, :] for m in range(nm)], axis=1)
            total = dot_nt(left, right)
            target[:, columns] = total if fresh else target[:, columns] + total

        each(D // TILE, body)

    def out_unit():
        add_nt(mixed, 3, branch_one, True)
        spill("br_one", branch_one, branch_one_out)

        def body(at):
            window, here = at // PER_WINDOW, span(at, BLOCK)
            rows = residual[here, :] + mod[window, 2:3, :] * branch_one[here, :]
            middle[here, :] = rows
            normed, _ = row_norm(rows)
            normed = normed * (1.0 + mod[window, 4:5, :]) + mod[window, 3:4, :]
            n_two[here, :] = normed.astype(BF)

        each(NBLOCK, body)
        spill("middle", middle, middle_out)
        transpose_rows(n_two, flipped.at[1])
        spill("n_two", flipped.at[1], n_two_t)

    def up_unit(f):
        slot = f % 2
        if f >= 2:
            spilled.pop(("slope", f - 2)).wait()

        def body(m):
            up = dot_nn(n_two[...], tile(4 + 2 * f, m)[...])
            value, grad = gelu_parts(up)
            hidden[f, m] = value.astype(BF)
            slope[slot, :, span(m, TILE)] = grad

        each(nm, body)
        spill(("hidden", f), hidden.at[f], hidden_out.at[f])
        spill(("slope", f), slope.at[slot], slope_out.at[f])

    def down_unit(f):
        add_nt(hidden.at[f], 5 + 2 * f, branch_two, f == 0)
        if f == 2:
            spill("br_two", branch_two, branch_two_out)

    units = {"qkv": qkv_unit, "attend": attend_unit, "out": out_unit, "up": up_unit, "down": down_unit}
    need = {"qkv": lambda j: j, "out": lambda: 3, "up": lambda f: 4 + 2 * f, "down": lambda f: 5 + 2 * f}

    def compute(turn):
        early = (first_swap, time_layers, condition_layers, modulation, first_norm)
        if turn < len(early):
            early[turn]()
        for when, (name, *args) in FORWARD_TURNS:
            if when == turn:
                if name in need:
                    loads[need[name](*args)].wait()
                units[name](*args)

    last = max(when for when, _ in FORWARD_TURNS)
    gather_steps(
        place,
        shard,
        whole,
        send_sems,
        recv_sems,
        local_sems,
        all_here,
        prepare,
        load,
        compute,
        last,
    )
    for copy in spilled.values():
        copy.wait()
    swap.drain()


def forward_blocks(states, *others):
    nd, nm = lax.axis_size("dp"), lax.axis_size("mp")
    nb = nd.bit_length() - 2
    rows = D // nd
    names = list(states)
    slots = 2 * (nm - 1 + 2 * nb) + 1 + 2 * (nm - 1)
    windows = nd * PER_INDEX
    chips = nd // 2
    part = (windows, rows) if windows <= rows else (rows, windows)
    small = [
        ((NMB, 6, D), F32),
        ((2, nd, rows, PATCH), BF),
        ((nd, PER_INDEX, FREQ + 256), F32),
        ((windows, rows), F32),
        ((windows, rows), F32),
        ((PER_INDEX, 128), F32),
        ((nd, rows, rows), BF),
    ]
    shapes = [
        ((NJ, nm) + (2,) * nb + (2, rows, TILE), BF),
        ((D, ROWS), BF),
        ((3, nm, ROWS, TILE), BF),
        ((nm, ROWS, TILE), BF),
        ((ROWS, D), F32),
        ((ROWS, D), F32),
        ((D, ROWS), BF),
        ((4, nm, ROWS, TILE), BF),
        ((4, ROWS, D), F32),
        ((ROWS, D), F32),
    ]

    def kernel(*refs):
        named = dict(zip(names, refs))
        forward_kernel(nd, nm, named, *refs[len(names) :])

    return pl.pallas_call(
        kernel,
        out_shape=[
            jax.ShapeDtypeStruct(shape, dtype) for shape, dtype in [((ROWS, D), F32)] + small + shapes
        ],
        in_specs=[pl.BlockSpec(memory_space=pl.ANY)] * len(names)
        + [pl.BlockSpec(memory_space=pltpu.VMEM)] * len(others),
        out_specs=[pl.BlockSpec(memory_space=pl.ANY)]
        + [pl.BlockSpec(memory_space=pltpu.VMEM)] * len(small)
        + [pl.BlockSpec(memory_space=pl.ANY)] * len(shapes),
        scratch_shapes=[
            pltpu.VMEM((ROWS, D), BF),
            pltpu.VMEM((3, nm, ROWS, TILE), BF),
            pltpu.VMEM((nm, ROWS, TILE), BF),
            pltpu.VMEM((ROWS, D), F32),
            pltpu.VMEM((ROWS, D), F32),
            pltpu.VMEM((ROWS, D), BF),
            pltpu.VMEM((2, D, ROWS), BF),
            pltpu.VMEM((4, nm, ROWS, TILE), BF),
            pltpu.VMEM((2, ROWS, D), F32),
            pltpu.VMEM((ROWS, D), F32),
            pltpu.VMEM((4, nm) + (2,) * nb + (2, rows, TILE), BF),
            pltpu.SemaphoreType.DMA((NJ, slots)),
            pltpu.SemaphoreType.DMA((NJ, slots)),
            pltpu.SemaphoreType.DMA((NJ,)),
            pltpu.SemaphoreType.DMA((NJ,)),
            pltpu.SemaphoreType.DMA((24,)),
            pltpu.VMEM((NJ, rows, TILE), BF),
            pltpu.VMEM((3, rows, TILE), F32),
            pltpu.VMEM((TILE, rows), F32),
            pltpu.VMEM((rows, 4 * TILE), F32),
            pltpu.VMEM((4 * TILE, rows), F32),
            pltpu.VMEM((6, rows, D), F32),
            pltpu.VMEM((FREQ, rows), F32),
            pltpu.VMEM((CLASSES + -CLASSES % 128, rows), F32),
            pltpu.VMEM((PATCH, rows), F32),
            pltpu.VMEM((PATCH, rows), F32),
            pltpu.VMEM((2, PATCH, rows), BF),
            pltpu.VMEM((PER_INDEX, FREQ + 256), F32),
            pltpu.VMEM((ROWS, PATCH), BF),
            pltpu.VMEM((rows, D), F32),
            pltpu.SemaphoreType.DMA((10,)),
            pltpu.VMEM((ROWS, D), F32),
            pltpu.VMEM((chips, 2) + part, F32),
            pltpu.VMEM((chips,) + part, F32),
            pltpu.VMEM((chips - 1,) + part, F32),
            pltpu.VMEM((chips, 2, NMB, 6, D), F32),
            pltpu.VMEM((chips, NMB, 6, D), F32),
            pltpu.VMEM((chips - 1, NMB, 6, D), F32),
            pltpu.VMEM((nd * NMB, D), F32),
            pltpu.VMEM((nm, PER_INDEX, 128), F32),
            pltpu.VMEM((nd, 2, PATCH, rows), BF),
            pltpu.SemaphoreType.DMA((7, max(nd, nm) - 1)),
            pltpu.SemaphoreType.DMA((7, max(nd, nm) - 1)),
        ],
        compiler_params=pltpu.CompilerParams(
            collective_id=0, has_side_effects=True, vmem_limit_bytes=60 << 20
        ),
    )(*states.values(), *others)


PIECES = (5, 7, 4, 6, 9, 8, 11, 10, 3, 2, 1, 0)
BACKWARD_TURNS = (
    (0, ("head",)),
    (1, ("slope", 0)),
    (1, ("spread", 0)),
    (2, ("slope", 1)),
    (2, ("spread", 1)),
    (3, ("slope", 2)),
    (3, ("spread", 2)),
    (4, ("slope", 3)),
    (4, ("spread", 3)),
    (5, ("mid",)),
    (6, ("attend", 0)),
    (7, ("attend", 1)),
    (7, ("attend", 2)),
    (8, ("attend", 3)),
    (9, ("inward", 2)),
    (10, ("inward", 1)),
    (10, ("inward", 0)),
    (11, ("last",)),
    (12, ("swap", 0)),
    (13, ("swap", 1)),
    (14, ("swap", 2)),
)
HELD = 5
TWINS = 3


def backward_kernel(nd, nm, whole, n_one_t, qkv, mixed, branch_one, middle, n_two_t, hidden, slope, branch_two, residual, *refs):
    (mod, mask_in, token_total_in, noise_in, latents_in, both_ends) = refs[:6]
    token_total = token_total_in[0:1, 0:1]
    head_mat = both_ends[1].reshape(D, PATCH)
    (total, loss, squares, ends_sum, all_mod) = refs[6:11]
    (partial, twin_ref, xa, xb, grad_rows, grad_in, grad_low, grad_low_t, normed_t, pool, loaded, z_ref, noise, inverses, row_mask, ends_rows) = refs[11:27]
    rest = refs[27:]
    place = Place(nd, nm)
    nb, core = place.nb, place.core
    part_rows = D // nd
    stage_refs = [rest[2 * step : 2 * step + 2] for step in range(nb)]
    send_sems, recv_sems, free_sem, load_sems = rest[2 * nb : 2 * nb + 4]
    (grad_mod, mod_in, mod_rows, own_mod, ends, ends_twin, ends_in, ends_z) = rest[2 * nb + 4 : -3]
    swap_send, swap_recv, own_sem = rest[-3:]
    swap = Exchange(place, swap_send, swap_recv)
    copies = Copies(send_sems, recv_sems)
    orders = [order[::-1] for order in place.orders]
    all_here = place.greet()
    slot_of = lambda step, half: 1 + 2 * step + half
    z_slot = 1 + 2 * nb
    loads = {}

    def load(name, source, target):
        copy = pltpu.make_async_copy(source, target, load_sems.at[len(loads)])
        copy.start()
        loads[name] = copy

    def load_tiles(j, slot):
        load(("w", j), whole.at[j], loaded.at[slot])

    def tile(slot, m):
        return loaded.at[slot, m].reshape(D, TILE)

    HIDDEN, QUERY, MIXED_GRAD = 4, 5, 8

    load("br_two", branch_two, xb)
    load("middle", middle, xa)
    load(("hidden", 0), hidden.at[0], pool.at[HIDDEN])
    load("n_two", n_two_t, normed_t)
    load_tiles(5, 0)
    load_tiles(4, 1)
    token_rows(noise_in, noise)
    mask_column(mask_in, row_mask)

    def add_to(target, index, source):
        shape = source.shape[:-2]

        def body(at):
            inner, places = at, []
            for size in shape[::-1]:
                places.append(inner % size)
                inner = inner // size
            places = places[::-1]
            spot = tuple(
                base.start + offset if isinstance(base, pl.Slice) else base
                for base, offset in zip(index, places)
            ) + (core,)
            target[spot] = target[spot] + source[tuple(places)]

        each(math.prod(shape), body, 4)

    every = (slice(None),) * (nb + 1)

    def begin(s):
        if s == 0:
            all_here()
        if s >= TWINS:
            pl.semaphore_wait(free_sem, 1)
        source = partial.at[(s % HELD,) + every + (1 - core,)]
        copies.start(s, 0, source, twin_ref.at[s % TWINS], place.sibling)

    def stage(s, step):
        mine = partial.at[s % HELD]
        if step == 0:
            copies.arrived(s, 0)
            add_to(mine, (pl.ds(0, nm),) + (pl.ds(0, 2),) * nb, twin_ref.at[s % TWINS])
            if s + TWINS < NJ:
                pl.semaphore_signal(free_sem, inc=1, device_id=place.sibling, device_id_type=MESH)
        else:
            for half in range(2):
                copies.arrived(s, slot_of(step - 1, half))
                index = place.pick(half, orders[half][step:])
                add_to(mine, index, stage_refs[step - 1][half].at[s])
        if step < nb:
            for half in range(2):
                order = orders[half]
                block = mine.at[place.pick(half, order[step + 1 :], order[step]) + (core,)]
                target = stage_refs[step][half].at[s]
                copies.start(s, slot_of(step, half), block, target, place.across(order[step]))
        else:
            for hops in range(1, nm):
                block = mine.at[place.mine((place.m + hops) % nm) + (core,)]
                copies.start(s, z_slot + hops - 1, block, z_ref.at[s, hops - 1], place.along(hops))

    def finish(s):
        summed = partial[(s % HELD,) + place.mine() + (core,)].astype(F32)
        for hops in range(1, nm):
            copies.arrived(s, z_slot + hops - 1)
            summed = summed + z_ref[s, hops - 1].astype(F32)
        total[PIECES[s]] = summed
        squares[...] += square_sum(summed)
        copies.drain(s)

    def weight_grad(s):
        j = PIECES[s]
        if j >= 4 and j % 2 == 1:
            f = (j - 5) // 2
            loads["hidden", f].wait()
            left, right = grad_low_t, HIDDEN
        elif j >= 4:
            left, right = normed_t, (j - 4) // 2
        elif j == 3:
            loads["mixed"].wait()
            left, right = grad_low_t, HIDDEN
        else:
            if j == 2:
                loads["n_one"].wait()
            left, right = normed_t, j

        def body(m):
            grads = dot_nn(left[...], pool[right, m]).astype(BF)
            partial.at[s % HELD, m].reshape(D, TILE)[...] = grads

        each(nm, body)
        if j in (5, 7, 9):
            load(("hidden", f + 1), hidden.at[f + 1], pool.at[HIDDEN])
        if j == 11:
            load("mixed", mixed, pool.at[HIDDEN])
        if j == 10:
            load("n_one", n_one_t, normed_t)

    def rows_of(at):
        return at // PER_WINDOW, span(at, BLOCK)

    def add_mod(window, which, values):
        grad_mod[window, which : which + 1, :] += jnp.sum(values, axis=0, keepdims=True)

    def head_unit():
        loads["br_two"].wait()
        loads["middle"].wait()
        grad_mod[...] = jnp.zeros_like(grad_mod)
        squares[...] = jnp.zeros_like(squares)

        def norms(at):
            window, here = rows_of(at)
            normed, inverse = row_norm(xa[here, :] + mod[window, 5:6, :] * xb[here, :])
            grad_rows[here, :] = normed
            inverses[here, :] = inverse
            grad_low[here, :] = normed.astype(BF)

        each(NBLOCK, norms)
        error = dot_nn(grad_low[...], head_mat) - noise[...]
        mask = row_mask[...]
        share = jnp.sum(error * error, axis=-1, keepdims=True) * (1.0 / PATCH) * mask
        loss[...] = jnp.sum(share, axis=0, keepdims=True) / token_total
        grad_pred = (2.0 / PATCH * error * mask / token_total).astype(BF)
        ends_rows[PATCH:, :] = dot_tn(grad_pred, grad_low[...])
        grad_in[...] = dot_nt(grad_pred, head_mat)

        def grads(at):
            window, here = rows_of(at)
            grad = norm_back(grad_in[here, :], grad_rows[here, :], inverses[here, :])
            add_mod(window, 5, grad * xb[here, :])
            grad_rows[here, :] = grad
            grad_low[here, :] = (grad * mod[window, 5:6, :]).astype(BF)

        each(NBLOCK, grads)
        transpose_rows(grad_low, grad_low_t)
        load(("slope", 0), slope.at[0], xa)
        load(("slope", 1), slope.at[1], xb)

    def slope_unit(f):
        loads["slope", f].wait()
        loads["w", 5 + 2 * f].wait()
        slopes = xa if f % 2 == 0 else xb

        def body(m):
            grad = dot_nn(grad_low[...], tile(0, m)[...])
            pool[f, m] = (grad * slopes[:, span(m, TILE)]).astype(BF)

        each(nm, body)
        if f + 2 < 4:
            load(("slope", f + 2), slope.at[f + 2], slopes)
        elif f == 2:
            load("middle2", middle, xa)
        else:
            load("br_one", branch_one, xb)
        load_tiles(7 + 2 * f if f < 3 else 3, 0)

    def add_rows(which, slot, fresh):
        def body(at):
            columns = span(at, TILE)
            left = jnp.concatenate([pool[which, m] for m in range(nm)], axis=1)
            right = jnp.concatenate([tile(slot, m)[columns, :] for m in range(nm)], axis=1)
            total = dot_nt(left, right)
            grad_in[:, columns] = total if fresh else grad_in[:, columns] + total

        each(D // TILE, body)

    def spread_unit(f):
        loads["w", 4 + 2 * f].wait()
        add_rows(f, 1, f == 0)
        load_tiles(6 + 2 * f if f < 3 else 2, 1)
        if f == 3:
            for part in range(3):
                load(("qkv", part), qkv.at[part], pool.at[QUERY + part])

    def norm_unit(which, after):
        def body(at):
            window, here = rows_of(at)
            normed, inverse = row_norm(xa[here, :])
            grad = grad_in[here, :]
            add_mod(window, which, grad)
            add_mod(window, which + 1, grad * normed)
            grad = grad * (1.0 + mod[window, which + 1 : which + 2, :])
            after(window, here, grad_rows[here, :] + norm_back(grad, normed, inverse))

        each(NBLOCK, body)

    def mid_unit():
        loads["middle2"].wait()
        loads["br_one"].wait()

        def after(window, here, grad):
            add_mod(window, 2, grad * xb[here, :])
            grad_rows[here, :] = grad
            grad_low[here, :] = (grad * mod[window, 2:3, :]).astype(BF)

        norm_unit(3, after)
        load("residual", residual, xa)
        loads["w", 3].wait()

        def body(m):
            pool[MIXED_GRAD, m] = dot_nn(grad_low[...], tile(0, m)[...]).astype(BF)

        each(nm, body)
        load_tiles(1, 0)

    def attend_unit(m):
        if m == 0:
            for part in range(3):
                loads["qkv", part].wait()

        def body(window):
            here = span(window, WTOK)
            query, key, value = (pool[QUERY + part, m, here, :] for part in range(3))
            grad_mixed = pool[MIXED_GRAD, m, here, :]
            grads = [jnp.zeros((WTOK, TILE), F32) for _ in range(3)]
            for head in range(TILE // HD):
                lanes = head_lanes(head, BF)
                scaled = lanes * HD ** (-0.5)
                own_query, own_grad = query * scaled, grad_mixed * lanes
                attn = soft_columns(key, own_query, row_mask[here, :])
                grads[2] = grads[2] + dot_nn(attn.astype(BF), own_grad)
                grad_attn = dot_nt(value, own_grad)
                inner = jnp.sum(attn * grad_attn, axis=0, keepdims=True)
                grad_scores = (attn * (grad_attn - inner)).astype(BF)
                grads[0] = grads[0] + dot_tn(grad_scores, key * scaled)
                grads[1] = grads[1] + dot_nn(grad_scores, own_query)
            pool[0, m, here, :] = grads[0].astype(BF)
            pool[1, m, here, :] = grads[1].astype(BF)
            pool[2, m, here, :] = grads[2].astype(BF)

        each(NMB, body)

    def inward_unit(j):
        slot = 1 if j != 1 else 0
        loads["w", j].wait()
        add_rows(j, slot, j == 2)
        if j == 2:
            load_tiles(0, 1)

    def last_unit():
        loads["residual"].wait()

        def after(window, here, grad):
            grad_low[here, :] = grad.astype(BF)

        norm_unit(0, after)
        embed_grad = jnp.zeros((PATCH, D), F32)
        for window in range(NMB):
            here = slice(window * WTOK, (window + 1) * WTOK)
            embed_grad = embed_grad + dot_nn(latents_in[window], grad_low[here, :])
        ends_rows[:PATCH, :] = embed_grad
        for index in range(nd):
            part = ends_rows[:, index * part_rows : (index + 1) * part_rows]
            ends[index // 2, index % 2] = part if part.shape == ends.shape[2:] else part.T
        mod_in[place.m] = grad_mod[...]
        swap.mp_gather(0, grad_mod, mod_in)
        swap.to_sibling(1, ends.at[:, 1 - core], ends_twin)

    own_copy = pltpu.make_async_copy(own_mod, all_mod.at[place.dp_id], own_sem)

    def swap_unit(step):
        if step == 0:
            swap.wait(0)
            for index in range(nm):
                for window in range(NMB):
                    for which in range(6):
                        row = index * NMB + window
                        mod_rows[which, row : row + 1, :] = mod_in[index, window, which : which + 1, :]
            for pair in range(3):
                both = mod_rows[2 * pair : 2 * pair + 2].reshape(2 * PER_INDEX, D)
                own_mod[pair] = both.astype(BF)
            own_copy.start()
            here = all_mod.at[place.dp_id]
            swap.chip_gather(2, own_mod, here)
            swap.to_sibling(3, own_mod, here, nd // 2 - 1)
            swap.wait(1)
            for chip in range(nd // 2):
                ends[chip, core] += ends_twin[chip]
            swap.chip_scatter(4, ends, ends_in)
        if step == 1:
            swap.wait(2)
            for hops in range(1, nd // 2):
                block = all_mod.at[place.chip(nd // 2 - hops) * 2 + core]
                swap.to_sibling(3, block, block, hops - 1)
            swap.wait(4)
            ends_z[place.m] = ends[place.dp_id // 2, core] + jnp.sum(ends_in[...], axis=0)
            swap.mp_gather(5, ends_z.at[place.m], ends_z)
        if step == 2:
            swap.wait(3)
            swap.wait(5)
            summed = jnp.sum(ends_z[...], axis=0)
            ends_sum[...] = summed if summed.shape == ends_sum.shape else summed.T
            squares[...] += square_sum(summed) * (1.0 / nm)
            own_copy.wait()
            swap.drain()

    units = {
        "head": head_unit,
        "slope": slope_unit,
        "spread": spread_unit,
        "mid": mid_unit,
        "attend": attend_unit,
        "inward": inward_unit,
        "last": last_unit,
        "swap": swap_unit,
    }

    def compute(turn):
        for when, (name, *args) in BACKWARD_TURNS:
            if when == turn:
                units[name](*args)

    last = max(when for when, _ in BACKWARD_TURNS)
    for turn in range(max(NJ + nb + 2, last + 1)):
        if turn == 0:
            compute(turn)
        if turn == 8:
            transpose_rows(grad_low, grad_low_t)
        if turn < NJ:
            if turn == 1:
                loads["n_two"].wait()
            weight_grad(turn)
            begin(turn)
        for step in range(nb + 1):
            if 0 <= turn - 1 - step < NJ:
                stage(turn - 1 - step, step)
        if 0 <= turn - 2 - nb < NJ:
            finish(turn - 2 - nb)
        if turn > 0:
            compute(turn)


def backward_blocks(saved, residual, *in_vmem):
    nd, nm = lax.axis_size("dp"), lax.axis_size("mp")
    nb = nd.bit_length() - 2
    rows = D // nd
    bits = (2,) * nb
    slots = 2 * nb + nm
    stage_shapes = []
    for step in range(nb):
        high_first = tuple(1 if at <= step else 2 for at in range(nb))
        stage_shapes.append(pltpu.VMEM((NJ, nm // 2) + high_first + (rows, TILE), BF))
        stage_shapes.append(pltpu.VMEM((NJ, nm - nm // 2) + high_first[::-1] + (rows, TILE), BF))
    ends_part = (2 * PATCH, rows) if 2 * PATCH <= rows else (rows, 2 * PATCH)
    in_hbm = (*saved, residual)
    return pl.pallas_call(
        functools.partial(backward_kernel, nd, nm),
        out_shape=[
            jax.ShapeDtypeStruct((NJ, rows, TILE), F32),
            jax.ShapeDtypeStruct((1, 1), F32),
            jax.ShapeDtypeStruct((1, 1), F32),
            jax.ShapeDtypeStruct((2 * PATCH, rows), F32),
            jax.ShapeDtypeStruct((nd, 3, 2 * PER_INDEX, D), BF),
        ],
        in_specs=[pl.BlockSpec(memory_space=pl.ANY)] * len(in_hbm)
        + [pl.BlockSpec(memory_space=pltpu.VMEM)] * len(in_vmem),
        out_specs=[pl.BlockSpec(memory_space=pltpu.VMEM)] * 4 + [pl.BlockSpec(memory_space=pl.ANY)],
        scratch_shapes=[
            pltpu.VMEM((HELD, nm) + bits + (2, rows, TILE), BF),
            pltpu.VMEM((TWINS, nm) + bits + (rows, TILE), BF),
            pltpu.VMEM((ROWS, D), F32),
            pltpu.VMEM((ROWS, D), F32),
            pltpu.VMEM((ROWS, D), F32),
            pltpu.VMEM((ROWS, D), F32),
            pltpu.VMEM((ROWS, D), BF),
            pltpu.VMEM((D, ROWS), BF),
            pltpu.VMEM((D, ROWS), BF),
            pltpu.VMEM((9, nm, ROWS, TILE), BF),
            pltpu.VMEM((2, nm) + bits + (2, rows, TILE), BF),
            pltpu.VMEM((NJ, nm - 1, rows, TILE), BF),
            pltpu.VMEM((ROWS, PATCH), F32),
            pltpu.VMEM((ROWS, 1), F32),
            pltpu.VMEM((ROWS, 1), F32),
            pltpu.VMEM((2 * PATCH, D), F32),
            *stage_shapes,
            pltpu.SemaphoreType.DMA((NJ, slots)),
            pltpu.SemaphoreType.DMA((NJ, slots)),
            pltpu.SemaphoreType.REGULAR,
            pltpu.SemaphoreType.DMA((36,)),
            pltpu.VMEM((NMB, 6, D), F32),
            pltpu.VMEM((nm, NMB, 6, D), F32),
            pltpu.VMEM((6, PER_INDEX, D), F32),
            pltpu.VMEM((3, 2 * PER_INDEX, D), BF),
            pltpu.VMEM((nd // 2, 2) + ends_part, F32),
            pltpu.VMEM((nd // 2,) + ends_part, F32),
            pltpu.VMEM((nd // 2 - 1,) + ends_part, F32),
            pltpu.VMEM((nm,) + ends_part, F32),
            pltpu.SemaphoreType.DMA((6, max(nd // 2, nm - 1))),
            pltpu.SemaphoreType.DMA((6, max(nd // 2, nm - 1))),
            pltpu.SemaphoreType.DMA,
        ],
        compiler_params=pltpu.CompilerParams(
            collective_id=1, has_side_effects=True, vmem_limit_bytes=63 << 20
        ),
    )(*in_hbm, *in_vmem)


def tail_kernel(nd, nm, adaptive_state, loss, block_squares, all_mod_in, front, time_pre, condition, time_out, *refs):
    (adaptive_grad, time_in_grad, time_out_grad, classes_grad, sums) = refs[:5]
    (all_mod, act_rows, cond_all, terms, term_rows, adaptive) = refs[5:11]
    send_sems, recv_sems, load_sems = refs[11:]
    place = Place(nd, nm)
    swap = Exchange(place, send_sems, recv_sems)
    all_here = place.greet(everyone=True)
    loads = []
    pairs = ((all_mod_in, all_mod), (adaptive_state.at[0], adaptive))
    for at, (source, target) in enumerate(pairs):
        loads.append(pltpu.make_async_copy(source, target, load_sems.at[at]))
        loads[at].start()
    dp_id, m = place.dp_id, place.m
    windows, rows = time_pre.shape
    cond_act = silu(condition[...]).reshape(nd, PER_INDEX, rows)
    act_rows[...] = jnp.zeros_like(act_rows)
    for side in range(2):
        act_rows[side, :, side * PER_INDEX : (side + 1) * PER_INDEX, :] = cond_act
    features = front[:, :, :FREQ].reshape(windows, FREQ).astype(BF)
    time_hidden = silu(time_pre[...]).astype(BF)
    pick = label_pick(front, classes_grad.shape[0])
    squares = jnp.zeros((8, 128), F32)

    term_rows[m, 0] = jnp.zeros((8, 128), F32) + block_squares[...]
    term_rows[m, 1] = jnp.zeros((8, 128), F32) + loss[...]
    all_here()
    swap.mp_gather(2, term_rows.at[m], term_rows)
    loads[0].wait()
    loads[1].wait()
    grad_cond = jnp.zeros((windows, rows), F32)
    for which in range(6):
        pair, side = which // 2, which % 2
        block = all_mod[:, pair].reshape(nd * 2 * PER_INDEX, D)
        act = act_rows[side].reshape(nd * 2 * PER_INDEX, rows).astype(BF)
        gradient = dot_tn(act, block)
        adaptive_grad[which] = gradient
        squares = squares + square_sum(gradient)
        back = dot_nt(block, adaptive[which].astype(BF)).reshape(nd, 2, PER_INDEX, rows)
        grad_cond = grad_cond + back[:, side].reshape(windows, rows)
    grad_cond = (grad_cond * silu_slope(condition[...])).astype(BF)
    cond_all[dp_id] = grad_cond
    swap.dp_gather(0, cond_all.at[dp_id], cond_all)
    gradient = dot_tn(pick, grad_cond)
    classes_grad[...] = gradient
    squares = squares + square_sum(gradient)
    swap.wait(0)
    grad_time = jnp.zeros((windows, rows), F32)
    for index in range(nd):
        gradient = dot_tn(time_hidden, cond_all[index])
        time_out_grad[:, index * rows : (index + 1) * rows] = gradient
        squares = squares + square_sum(gradient)
        grad_time = grad_time + dot_nt(cond_all[index], time_out[index])
    grad_time = (grad_time * silu_slope(time_pre[...])).astype(BF)
    gradient = dot_tn(features, grad_time)
    time_in_grad[...] = gradient
    squares = squares + square_sum(gradient)

    swap.wait(2)
    term_sums = jnp.sum(term_rows[...], axis=0)
    terms[dp_id, 0] = squares + term_sums[0]
    terms[dp_id, 1] = term_sums[1]
    swap.dp_gather(1, terms.at[dp_id], terms)
    swap.wait(1)
    sums[...] = jnp.sum(terms[...], axis=0)
    swap.drain()


def tail_blocks(*operands):
    nd, nm = lax.axis_size("dp"), lax.axis_size("mp")
    rows = D // nd
    windows = nd * PER_INDEX
    classes = CLASSES + -CLASSES % 128
    shapes = [
        (6, rows, D),
        (FREQ, rows),
        (rows, D),
        (classes, rows),
        (2, 8, 128),
    ]
    return pl.pallas_call(
        functools.partial(tail_kernel, nd, nm),
        out_shape=[jax.ShapeDtypeStruct(shape, F32) for shape in shapes],
        in_specs=[
            pl.BlockSpec(memory_space=pl.ANY if at in (0, 3) else pltpu.VMEM)
            for at in range(len(operands))
        ],
        out_specs=[pl.BlockSpec(memory_space=pltpu.VMEM)] * len(shapes),
        scratch_shapes=[
            pltpu.VMEM((nd, 3, 2 * PER_INDEX, D), BF),
            pltpu.VMEM((2, nd, 2 * PER_INDEX, rows), F32),
            pltpu.VMEM((nd, windows, rows), BF),
            pltpu.VMEM((nd, 2, 8, 128), F32),
            pltpu.VMEM((nm, 2, 8, 128), F32),
            pltpu.VMEM((6, rows, D), F32),
            pltpu.SemaphoreType.DMA((3, max(nd, nm) - 1)),
            pltpu.SemaphoreType.DMA((3, max(nd, nm) - 1)),
            pltpu.SemaphoreType.DMA((2,)),
        ],
        compiler_params=pltpu.CompilerParams(
            collective_id=2, has_side_effects=True, vmem_limit_bytes=40 << 20
        ),
    )(*operands)


def adam_update(weight, first, root, gradient, factor):
    clipped = gradient * factor
    first = beta_one * first + (1.0 - beta_one) * clipped
    root = jnp.sqrt(beta_two * root * root + (1.0 - beta_two) * clipped * clipped)
    update = (
        first
        / (1.0 - beta_one**step_count)
        / (root / math.sqrt(1.0 - beta_two**step_count) + adam_eps)
    )
    return weight - learn_rate * (update + weight_decay * weight), first, root


def chunk_rows(rows, lanes):
    limit = max(16, 16384 // max(lanes, 128))
    return max(size for size in range(8, limit + 1, 8) if rows % size == 0)


def adam_kernel(names, *refs):
    count = len(names)
    states = dict(zip(names, refs[:count]))
    reduced, ends, time_in, time_out, classes, adaptive, sums = refs[count : count + 7]
    refs = refs[count + 7 :]
    targets = dict(zip(names, zip(refs[: 2 * count : 2], refs[1 : 2 * count : 2])))
    held = dict(zip(names, refs[2 * count : 3 * count]))
    load_sems, store_sems = refs[3 * count :]
    squares = sums[0, 0:1, 0:1]
    factor = jnp.minimum(1.0, threshold / jnp.sqrt(squares))
    loads, stores = {}, []

    def parts_of(name):
        lead = held[name].shape[1:-2]
        return [(at,) for at in range(lead[0])] if lead else [()]

    for name in names:
        for part in parts_of(name):
            every = (slice(None),) + part
            copy = pltpu.make_async_copy(
                states[name].at[every], held[name].at[every], load_sems.at[len(loads)]
            )
            copy.start()
            loads[name, part] = copy

    def apply(where, gradient):
        ref, part, rows, columns = where
        spot = lambda which: (which,) + part + (rows, columns)
        values = [ref[spot(which)] for which in range(3)]
        for which, value in enumerate(adam_update(*values, gradient, factor)):
            ref[spot(which)] = value

    def store(name, part):
        weight, moments = targets[name]
        copies = (
            (held[name].at[(0,) + part], weight.at[part] if part else weight),
            (held[name].at[(pl.ds(1, 2),) + part], moments.at[(slice(None),) + part]),
        )
        for source, target in copies:
            copy = pltpu.make_async_copy(source, target, store_sems.at[len(stores)])
            copy.start()
            stores.append(copy)

    def rowwise(name, part, source, first_row=0):
        rows, lanes = held[name].shape[-2:]
        size = chunk_rows(rows, lanes)

        def body(at):
            here = span(at, size)
            there = pl.ds(pl.multiple_of(first_row + at * size, 8), size)
            apply((held[name], part, here, slice(None)), source[there, :])

        each(rows // size, body)

    every = slice(None)
    for name in names:
        for part in parts_of(name):
            loads[name, part].wait()
            if name == "adapt":
                rowwise(name, part, adaptive.at[part[0]])
            elif name == "attn_in":
                rowwise(name, part, reduced.at[part[0]])
            elif name == "expand":
                for f in range(4):
                    columns = slice(f * TILE, (f + 1) * TILE)
                    apply((held[name], part, every, columns), reduced[4 + 2 * f])
            elif name == "contract":
                for f in range(4):
                    rows = slice(f * TILE, (f + 1) * TILE)
                    apply((held[name], part, rows, every), reduced[5 + 2 * f].T)
            elif name == "attn_out":
                apply((held[name], part, every, every), reduced[3].T)
            elif name == "embed":
                rowwise(name, part, ends)
            elif name == "head":
                rowwise(name, part, ends, PATCH)
            else:
                rowwise(name, part, {"time_in": time_in, "time_out": time_out, "classes": classes}[name])
            store(name, part)
    for copy in stores:
        copy.wait()


def adam_blocks(states, *gradients):
    names = list(states)
    shapes = [states[name].shape for name in names]
    outs = []
    for shape in shapes:
        outs += [shape[1:], (2,) + shape[1:]]
    pieces = sum(shape[1] if len(shape) == 4 else 1 for shape in shapes)
    return pl.pallas_call(
        functools.partial(adam_kernel, names),
        out_shape=[jax.ShapeDtypeStruct(shape, F32) for shape in outs],
        in_specs=[pl.BlockSpec(memory_space=pl.ANY)] * len(names)
        + [pl.BlockSpec(memory_space=pltpu.VMEM)] * len(gradients),
        out_specs=[pl.BlockSpec(memory_space=pl.ANY)] * len(outs),
        scratch_shapes=[pltpu.VMEM(shape, F32) for shape in shapes]
        + [pltpu.SemaphoreType.DMA((pieces,)), pltpu.SemaphoreType.DMA((2 * pieces,))],
        compiler_params=pltpu.CompilerParams(vmem_limit_bytes=40 << 20),
    )(*states.values(), *gradients)


def per_device(
    latents,
    noise_target,
    token_mask,
    timesteps,
    labels,
    state_embed,
    state_head,
    state_time_in,
    state_time_out,
    state_classes,
    state_adaptive,
    state_attention_in,
    state_attention_out,
    state_expand,
    state_contract,
):
    nd = lax.axis_size("dp")
    rows = state_attention_in.shape[1]
    states = {
        "adapt": state_adaptive.transpose(0, 2, 1, 3),
        "attn_in": state_attention_in.transpose(0, 2, 1, 3),
        "expand": state_expand,
        "contract": state_contract,
        "time_out": state_time_out,
        "classes": state_classes,
        "attn_out": state_attention_out,
        "time_in": state_time_in,
        "embed": state_embed,
        "head": state_head.transpose(0, 2, 1),
    }
    lanes = jnp.arange(FREQ + 128)[None, :]
    step_ids = timesteps[0].T.reshape(PER_INDEX, 1).astype(F32)
    label_ids = labels[0].T.reshape(PER_INDEX, 1).astype(F32)
    half_width = FREQ // 2
    frequency = jnp.exp(-math.log(10000.0) * (lanes % half_width).astype(F32) / half_width)
    angles = step_ids * frequency
    features = jnp.where(lanes < half_width, jnp.cos(angles), jnp.sin(angles))
    front = jnp.where(lanes < FREQ, features.astype(BF).astype(F32), label_ids)
    flags = token_mask.reshape(NMB, WTOK)
    latent_columns = latents[0].transpose(0, 2, 1)
    noise_columns = noise_target[0].transpose(0, 2, 1)
    residual, mod, ends, front_all, time_pre, condition, token_total, time_out_part, *saved = forward_blocks(
        states, flags, front, latent_columns, window_positions()
    )
    reduced, loss_local, squares, ends_sum, all_mod = backward_blocks(
        saved, residual, mod, flags, token_total, noise_columns, latent_columns, ends
    )
    adaptive_grad, time_in_grad, time_out_grad, classes_grad, sums = tail_blocks(
        states["adapt"],
        loss_local,
        squares,
        all_mod,
        front_all,
        time_pre,
        condition,
        time_out_part,
    )
    updated = adam_blocks(
        states,
        reduced,
        ends_sum,
        time_in_grad,
        time_out_grad,
        classes_grad,
        adaptive_grad,
        sums,
    )
    new = dict(zip(states, zip(updated[::2], updated[1::2])))
    back = {"adapt": (1, 0, 2), "attn_in": (1, 0, 2), "head": (1, 0)}
    results = [sums[1, 0, 0], jnp.sqrt(sums[0, 0, 0])]
    order = ("embed", "head", "time_in", "time_out", "classes", "adapt", "attn_in")
    for name in order + ("attn_out", "expand", "contract"):
        weight, moments = new[name]
        if name in back:
            axes = back[name]
            weight = weight.transpose(axes)
            moments = moments.transpose((0,) + tuple(1 + axis for axis in axes))
        results += [weight, moments]
    return tuple(results)


def solution(mesh):
    in_specs = (
        P("dp", None, "mp", None),
        P("dp", None, "mp", None),
        P("dp", None, "mp"),
        P("dp", None, None),
        P("dp", None, None),
        P(None, None, "dp"),
        P(None, "dp", None),
        P(None, None, "dp"),
        P(None, "dp", None),
        P(None, None, "dp"),
        P(None, "dp", None, None),
        P(None, "dp", None, "mp"),
        P(None, "mp", "dp"),
        P(None, "dp", "mp"),
        P(None, "mp", "dp"),
    )
    out_specs = (
        P(),
        P(),
        P(None, "dp"),
        P(None, None, "dp"),
        P("dp", None),
        P(None, "dp", None),
        P(None, "dp"),
        P(None, None, "dp"),
        P("dp", None),
        P(None, "dp", None),
        P(None, "dp"),
        P(None, None, "dp"),
        P("dp", None, None),
        P(None, "dp", None, None),
        P("dp", None, "mp"),
        P(None, "dp", None, "mp"),
        P("mp", "dp"),
        P(None, "mp", "dp"),
        P("dp", "mp"),
        P(None, "dp", "mp"),
        P("mp", "dp"),
        P(None, "mp", "dp"),
    )
    return jax.shard_map(
        per_device, mesh=mesh, in_specs=in_specs, out_specs=out_specs, check_vma=False
    )
```
